512 devices in a mesh: seq: 64 (over y, z), head: 8 (over x, core).
Axes of the slice: x: 4, y: 8, z: 8, core: 2. Of those that a mesh axis runs over, the one named last changes fastest.
Arguments:
- queries: bfloat16 [32768, 1024], P('seq', 'head'), may hold values from -6 to 6
- key_rows: bfloat16 [32768, 1024], P('seq', 'head'), may hold values from -6 to 6
- value_rows: bfloat16 [32768, 1024], P('seq', 'head'), may hold values from -6 to 6
- query_gain: float32 [1024], P('head'), may hold values from 1.2 to 2.4
- key_gain: float32 [1024], P('head'), may hold values from 1.2 to 2.4
- out_grad: bfloat16 [32768, 1024], P('seq', 'head'), may hold values from -6 to 6
Outputs:
- attended: bfloat16 [32768, 1024], P('seq', 'head')
- query_grad: bfloat16 [32768, 1024], P('seq', 'head')
- key_grad: bfloat16 [32768, 1024], P('seq', 'head')
- value_grad: bfloat16 [32768, 1024], P('seq', 'head')
The draws below stay inside these ranges and needn't reach their ends.
All inputs are finite; a program needn't handle non-finite values.
Results may differ from the reference program's by a relative error of at most 0.007.
The reference program's roundings to bfloat16 on the way count: a program that leaves them out, or rounds other values in their place, can miss the bound.
Values may be sent and summed in bfloat16 or wider, within the bound.
No kernel may reach another device: no remote copies, remote signals or barrier semaphores. Data moves between devices by JAX's collectives and lax.ppermute only.
A program may use at most 64 MiB of HBM per device.

```python
import math
import jax
import jax.numpy as jnp
from jax import lax

HEADS = 16
DH = 64
NR = 128
TOK_DEV = 512
TOKENS = 32768
WIDTH = 1024


def column_scale(feat_width, rise_factor):
    position = jnp.arange(feat_width, dtype=jnp.float32) / float(feat_width - 1)
    return jnp.exp(position * math.log(rise_factor))


def draw_queries(key, part):
    key = jax.random.fold_in(key, 11)
    drawn = jnp.clip(jax.random.normal(key, (TOKENS, HEADS * DH)) * column_scale(HEADS * DH, math.sqrt(3.0)), -6.0, 6.0)
    return drawn.astype(jnp.bfloat16)


def draw_key_rows(key, part):
    key = jax.random.fold_in(key, 12)
    drawn = jnp.clip(jax.random.normal(key, (TOKENS, HEADS * DH)) * column_scale(HEADS * DH, math.sqrt(3.0)), -6.0, 6.0)
    return drawn.astype(jnp.bfloat16)


def draw_value_rows(key, part):
    key = jax.random.fold_in(key, 13)
    noise_key = jax.random.fold_in(key, 1)
    level_key = jax.random.fold_in(key, 2)
    stretch_count = TOKENS // TOK_DEV
    levels = jax.random.uniform(level_key, (stretch_count, 1, HEADS * DH), minval=-2.0, maxval=2.0)
    noise = jax.random.normal(noise_key, (stretch_count, TOK_DEV, HEADS * DH))
    drawn = jnp.clip(noise + levels, -6.0, 6.0).reshape(TOKENS, HEADS * DH)
    return drawn.astype(jnp.bfloat16)


def block_scale(own_key, shape, shards, low, high):
    level, own = 1.0, jax.random.fold_in(own_key, 6)
    for axis_at, shards_of in shards:
        steps = jnp.exp(jax.random.uniform(jax.random.fold_in(own, axis_at), (shards_of,), jnp.float32, low / len(shards), high / len(shards)))
        level = level * jnp.repeat(steps, shape[axis_at] // shards_of).reshape([-1 if axis == axis_at else 1 for axis in range(len(shape))])
    return level


def bell_draw(stream_key, dims, deviation, most, cuts=(), kind=jnp.bfloat16):
    result = deviation * jax.random.normal(stream_key, dims, jnp.float32)
    if cuts:
        result = result * block_scale(stream_key, dims, cuts, -0.22, 0.18)
    return jnp.clip(result, -most, most).astype(kind)


def setup_inputs(seed: int = 0) -> dict:
    key_list = jax.random.split(jax.random.key(seed), 7)
    queries = draw_queries(jax.random.fold_in(key_list[6], 71), 0)
    key_rows = draw_key_rows(jax.random.fold_in(key_list[6], 71), 0)
    value_rows = draw_value_rows(jax.random.fold_in(key_list[6], 71), 0)
    query_gain = jnp.clip(jnp.exp(math.log(2.4) - 0.6931472 * jax.random.uniform(key_list[3], (WIDTH,), jnp.float32) ** block_scale(key_list[3], (WIDTH,), ((0, 8),), -0.2, 0.2)), 1.2, 2.4)
    key_gain = jnp.clip(jnp.exp(math.log(2.4) - 0.6931472 * jax.random.uniform(key_list[4], (WIDTH,), jnp.float32) ** block_scale(key_list[4], (WIDTH,), ((0, 8),), -0.2, 0.2)), 1.2, 2.4)
    out_grad = bell_draw(key_list[5], (TOKENS, WIDTH), 1.0, 6.0, ((0, 64), (1, 8)))
    return dict(queries=queries, key_rows=key_rows, value_rows=value_rows, query_gain=query_gain, key_gain=key_gain, out_grad=out_grad)


EPS = 1e-06

def coarsen(array_in, level_index):
    row_count, feat_width = array_in.shape
    grouped = array_in.astype(jnp.float32).reshape(row_count >> level_index, 1 << level_index, feat_width)
    return lax.optimization_barrier(jnp.mean(grouped, axis=1)).astype(jnp.bfloat16)

def swap_pairs(blocked):
    shape_in = blocked.shape
    paired = blocked.reshape(shape_in[:-3] + (shape_in[-3] // 2, 2) + shape_in[-2:])
    return jnp.flip(paired, axis=-3).reshape(shape_in)

def spread_rows(coarse_rows, level_index):
    lead = coarse_rows.shape[:-2]
    row_count, feat_width = coarse_rows.shape[-2:]
    wide = jnp.broadcast_to(coarse_rows[..., :, None, :], lead + (row_count, 1 << level_index, feat_width))
    return wide.reshape(lead + (row_count << level_index, feat_width)) / float(1 << level_index)

def normalize(array_in, gain):
    as_float = array_in.astype(jnp.float32)
    norm_rate = lax.rsqrt(lax.optimization_barrier(jnp.mean(as_float * as_float, axis=1, keepdims=True)) + EPS)
    return ((as_float * norm_rate * gain).astype(jnp.bfloat16), norm_rate)

def restore(array_in, norm_rate, gain, grad_in):
    as_float = array_in.astype(jnp.float32)
    inner = lax.optimization_barrier(jnp.mean(as_float * gain * grad_in, axis=1, keepdims=True))
    return (norm_rate * gain * grad_in - as_float * norm_rate * norm_rate * norm_rate * inner).astype(jnp.bfloat16)

def add_at(target, update, start):
    current = lax.dynamic_slice_in_dim(target, start, update.shape[0], 0)
    return lax.dynamic_update_slice_in_dim(target, current + update, start, 0)

def reference(queries, key_rows, value_rows, query_gain, key_gain, out_grad):
    token_count, feat_width = queries.shape
    leaf_size = NR
    head_size = DH
    head_count = HEADS
    leaf_count = token_count // leaf_size
    level_count = (token_count // (2 * leaf_size)).bit_length() - 1
    score_scale = 1.0 / math.sqrt(head_size)
    query_norm, query_rate = normalize(queries, query_gain)
    key_norm, key_rate = normalize(key_rows, key_gain)
    coarse_keys = []
    coarse_values = []
    for level_index in range(1, level_count + 1):
        block_count = (token_count >> level_index) // leaf_size
        coarse_keys.append(swap_pairs(coarsen(key_norm, level_index).reshape(block_count, leaf_size, feat_width)).reshape(-1, feat_width))
        coarse_values.append(swap_pairs(coarsen(value_rows, level_index).reshape(block_count, leaf_size, feat_width)).reshape(-1, feat_width))
    padding = ((leaf_size, leaf_size), (0, 0))
    key_padded = jnp.pad(key_norm, padding)
    value_padded = jnp.pad(value_rows, padding)
    offsets = jnp.arange(3 * leaf_size, dtype=jnp.int32) - leaf_size
    far_bias = [jnp.full((leaf_size,), level_index * math.log(2.0), jnp.float32) for level_index in range(1, level_count + 1)]
    near_rows = 3 * leaf_size

    def visit(carry, leaf_index):
        key_pad_grad, value_pad_grad, key_coarse_grad, value_coarse_grad = carry
        start = leaf_index * leaf_size
        query_block = lax.dynamic_slice_in_dim(query_norm, start, leaf_size, 0).reshape(leaf_size, head_count, head_size)
        grad_block = lax.dynamic_slice_in_dim(out_grad, start, leaf_size, 0).reshape(leaf_size, head_count, head_size)
        key_parts = [lax.dynamic_slice_in_dim(key_padded, start, near_rows, 0)]
        value_parts = [lax.dynamic_slice_in_dim(value_padded, start, near_rows, 0)]
        coarse_starts = []
        for i in range(level_count):
            coarse_start = jnp.right_shift(leaf_index, i + 1) * leaf_size
            coarse_starts.append(coarse_start)
            key_parts.append(lax.dynamic_slice_in_dim(coarse_keys[i], coarse_start, leaf_size, 0))
            value_parts.append(lax.dynamic_slice_in_dim(coarse_values[i], coarse_start, leaf_size, 0))
        key_set = jnp.concatenate(key_parts, axis=0).reshape(-1, head_count, head_size)
        value_set = jnp.concatenate(value_parts, axis=0).reshape(-1, head_count, head_size)
        inside = (start + offsets >= 0) & (start + offsets < token_count)
        bias = jnp.concatenate([jnp.where(inside, 0.0, -jnp.inf).astype(jnp.float32)] + far_bias)
        scores = jnp.einsum('qhe,khe->hqk', query_block.astype(jnp.float32), key_set.astype(jnp.float32)) * score_scale + bias
        top_score = lax.optimization_barrier(jnp.max(scores, axis=-1, keepdims=True))
        weights = jnp.exp(scores - top_score)
        probs = weights / lax.optimization_barrier(jnp.sum(weights, axis=-1, keepdims=True))
        probs_low = probs.astype(jnp.bfloat16)
        mixed = jnp.einsum('hqk,khe->qhe', probs_low.astype(jnp.float32), value_set.astype(jnp.float32))
        prob_grad = jnp.einsum('qhe,khe->hqk', grad_block.astype(jnp.float32), value_set.astype(jnp.float32))
        delta = lax.optimization_barrier(jnp.sum(probs * prob_grad, axis=-1, keepdims=True))
        score_grad = (probs * (prob_grad - delta)).astype(jnp.bfloat16)
        query_part = jnp.einsum('hqk,khe->qhe', score_grad.astype(jnp.float32), key_set.astype(jnp.float32)) * score_scale
        key_part = jnp.einsum('hqk,qhe->khe', score_grad.astype(jnp.float32), query_block.astype(jnp.float32)) * score_scale
        value_part = jnp.einsum('hqk,qhe->khe', probs_low.astype(jnp.float32), grad_block.astype(jnp.float32))
        key_part = key_part.reshape(-1, feat_width)
        value_part = value_part.reshape(-1, feat_width)
        key_pad_grad = add_at(key_pad_grad, key_part[:near_rows], start)
        value_pad_grad = add_at(value_pad_grad, value_part[:near_rows], start)
        new_key_coarse = []
        new_value_coarse = []
        for i in range(level_count):
            lower = near_rows + i * leaf_size
            new_key_coarse.append(add_at(key_coarse_grad[i], key_part[lower:lower + leaf_size], coarse_starts[i]))
            new_value_coarse.append(add_at(value_coarse_grad[i], value_part[lower:lower + leaf_size], coarse_starts[i]))
        outputs = (mixed.reshape(leaf_size, feat_width).astype(jnp.bfloat16), query_part.reshape(leaf_size, feat_width))
        return ((key_pad_grad, value_pad_grad, new_key_coarse, new_value_coarse), outputs)
    initial = (jnp.zeros((token_count + 2 * leaf_size, feat_width), jnp.float32), jnp.zeros((token_count + 2 * leaf_size, feat_width), jnp.float32), [jnp.zeros((token_count >> i + 1, feat_width), jnp.float32) for i in range(level_count)], [jnp.zeros((token_count >> i + 1, feat_width), jnp.float32) for i in range(level_count)])
    final, stacked = lax.scan(visit, initial, jnp.arange(leaf_count, dtype=jnp.int32))
    key_pad_grad, value_pad_grad, key_coarse_grad, value_coarse_grad = final
    attended_rows, query_parts = stacked
    attended = attended_rows.reshape(token_count, feat_width)
    key_grad_norm = key_pad_grad[leaf_size:leaf_size + token_count]
    value_total = value_pad_grad[leaf_size:leaf_size + token_count]
    for i in range(level_count):
        level_index = i + 1
        block_count = (token_count >> level_index) // leaf_size
        owner_keys = swap_pairs(key_coarse_grad[i].reshape(block_count, leaf_size, feat_width)).reshape(-1, feat_width)
        owner_values = swap_pairs(value_coarse_grad[i].reshape(block_count, leaf_size, feat_width)).reshape(-1, feat_width)
        key_grad_norm = key_grad_norm + spread_rows(owner_keys, level_index)
        value_total = value_total + spread_rows(owner_values, level_index)
    query_grad = restore(queries, query_rate, query_gain, query_parts.reshape(token_count, feat_width))
    key_grad = restore(key_rows, key_rate, key_gain, key_grad_norm)
    return (attended, query_grad, key_grad, value_total.astype(jnp.bfloat16))
```

```python
import math

import jax
import jax.numpy as jnp
from jax import lax
from jax.experimental import pallas as pl
from jax.experimental.pallas import tpu as pltpu
from jax.sharding import PartitionSpec as P

ROWS = 512
FEAT = 128
LEAF = 128
LEAVES = 4
HEAD = 64
KEYS = 1280
EPS = 1e-06
LN2 = math.log(2.0)
F32 = jnp.float32
BF16 = jnp.bfloat16
PARAMS = pltpu.CompilerParams(vmem_limit_bytes=40 * 1024 * 1024)
ROW_LEVEL = {1: 2, 2: 3, 3: 3, 4: 4, 5: 4, 6: 4, 7: 4}
COLUMN_LEVEL = {1: 5, 2: 6, 3: 6, 4: 7, 5: 7, 6: 7, 7: 7}
FAR = 48
SLOT = 112


def dot(a, b, dims):
    return lax.dot_general(a, b, ((dims[:1], dims[1:]), ((), ())), preferred_element_type=F32)


def iota(shape, axis):
    return lax.broadcasted_iota(jnp.int32, shape, axis)


def pooling(rows, level):
    token = iota((rows, ROWS), 1)
    hit = jnp.right_shift(token, level) == iota((rows, ROWS), 0)
    return jnp.where(hit, 2.0**-level, 0.0)


def spreading(first, rows, level):
    token = iota((ROWS, rows), 0)
    hit = jnp.right_shift(token, level) == iota((ROWS, rows), 1) + first
    return jnp.where(hit, 2.0**-level, 0.0)


def far_pick(shape, far_axis):
    far = iota(shape, far_axis)
    slot_row = iota(shape, 1 - far_axis)
    mid = far - 16
    low = far - 32
    column = jnp.where(
        far < 16,
        far,
        jnp.where(
            far < 32,
            (1 + jnp.right_shift(mid, 3)) * 16 + jnp.bitwise_and(mid, 7),
            (3 + jnp.right_shift(low, 2)) * 16 + jnp.bitwise_and(low, 3),
        ),
    )
    return jnp.where(column == slot_row, 1.0, 0.0).astype(BF16)


def token_sums(x):
    return [
        jnp.sum(x[i * LEAF : (i + 1) * LEAF].T, axis=0, keepdims=True) for i in range(LEAVES)
    ]


def spread_tokens(tile, first):
    return jnp.concatenate(
        [
            jnp.broadcast_to(tile[first + i : first + i + 1], (LEAF, LEAF)).T
            for i in range(LEAVES)
        ],
        axis=0,
    )


def squares_kernel(q_ref, k_ref, out_ref):
    q = q_ref[...].astype(F32)
    k = k_ref[...].astype(F32)
    tile = jnp.concatenate(token_sums(q * q) + token_sums(k * k), axis=0)
    for i in range(out_ref.shape[0]):
        out_ref[i] = tile


def norm_kernel(width, sum_ref, q_ref, k_ref, v_ref, qg_ref, kg_ref, qn_ref, kv_ref, one_ref, lv_ref, y_ref, p1_ref, p2_ref):
    index = lax.axis_index("seq")
    column = jnp.right_shift(index, 3)
    odd = jnp.bitwise_and(index, 1)
    total = jnp.sum(sum_ref[...], axis=0)
    rate = lax.rsqrt(total / width + EPS)
    qn_ref[...] = (
        q_ref[...].astype(F32) * spread_tokens(rate, 0) * qg_ref[...]
    ).astype(BF16)
    kv_ref[:, :FEAT] = (
        k_ref[...].astype(F32) * spread_tokens(rate, 4) * kg_ref[...]
    ).astype(BF16)
    kv_ref[:, FEAT:] = v_ref[...]
    pool = jnp.concatenate(
        [pooling(ROWS >> level, level) for level in (1, 2, 3, 4)]
        + [pooling(16, COLUMN_LEVEL[d]) for d in range(1, 8)],
        axis=0,
    ).astype(BF16)
    coarse = dot(pool, kv_ref[...], (1, 0)).astype(BF16)
    one_ref[...] = coarse[:256]
    lv_ref[...] = coarse[256:480]
    y_ref[column] = jnp.zeros((16, 2 * FEAT), BF16)
    for d in range(1, 8):
        y_ref[jnp.bitwise_xor(column, d)] = coarse[464 + 16 * d : 480 + 16 * d]
    p1_ref[:LEAF] = kv_ref[pl.ds(pl.multiple_of((1 - odd) * 384, LEAF), LEAF)]
    p1_ref[LEAF:] = coarse[320:384]
    p2_ref[...] = kv_ref[pl.ds(pl.multiple_of(odd * 384, LEAF), LEAF)]


def row_kernel(y_ref, lv_ref, out_ref):
    index = lax.axis_index("seq")
    column = jnp.right_shift(index, 3)
    place = jnp.bitwise_and(index, 7)
    slots = jnp.concatenate([y_ref[jnp.bitwise_xor(column, d)] for d in range(1, 8)], axis=0)
    far = dot(far_pick((FAR, 112), 0), slots, (1, 0)).astype(BF16)
    for s in range(8):
        out_ref[s, :FAR] = far
    out_ref[place, FAR:] = jnp.zeros((64, 2 * FEAT), BF16)
    for d in range(1, 8):
        other = jnp.bitwise_xor(place, d)
        if d == 1:
            out_ref[other, FAR:] = lv_ref[:64]
        elif d < 4:
            out_ref[other, FAR:] = lv_ref[128:192]
        else:
            out_ref[other, FAR : FAR + 32] = lv_ref[192:224]
            out_ref[other, FAR + 32 :] = jnp.zeros((32, 2 * FEAT), BF16)


def attend_kernel(
    qn_ref, kv_ref, one_ref, g_ref, p1_ref, p2_ref, z_ref,
    att_ref, nqg_ref, tok_ref, p1o_ref, p2o_ref, zo_ref,
    near, cross, near_grad, one_grad, cross_grad,
):
    index = lax.axis_index("seq")
    last = lax.axis_size("seq") - 1
    place = jnp.bitwise_and(index, 7)
    odd = jnp.bitwise_and(index, 1)
    peer_side = pl.multiple_of((1 - odd) * 640, LEAF)
    other_side = pl.multiple_of(odd * 640, LEAF)
    near[LEAF : LEAF + ROWS] = kv_ref[...]
    near[pl.ds(peer_side, LEAF)] = p1_ref[:LEAF]
    near[pl.ds(other_side, LEAF)] = p2_ref[...]
    cross[:64] = z_ref[jnp.bitwise_xor(place, 1), FAR:]
    cross[64:128] = p1_ref[LEAF:]
    cross[128:192] = z_ref[jnp.bitwise_xor(place, 2), FAR:]
    cross[192:256] = z_ref[jnp.bitwise_xor(place, 3), FAR:]
    for i in range(4):
        cross[256 + 32 * i : 288 + 32 * i] = z_ref[jnp.bitwise_xor(place, 4 + i), FAR : FAR + 32]
    for s in range(8):
        cross[384 + FAR * s : 384 + FAR * (s + 1)] = z_ref[s, :FAR]

    def level_bias(rows, level):
        return jnp.full((rows, 2 * LEAF), level * LN2, F32)

    bias = jnp.concatenate(
        [level_bias(LEAF, level) for level in (1, 2, 3, 4)]
        + [level_bias(16, level) for _ in range(8) for level in (5, 6, 7)],
        axis=0,
    )
    left = jnp.where(index > 0, 0.0, -jnp.inf).astype(F32)
    right = jnp.where(index < last, 0.0, -jnp.inf).astype(F32)
    lane = iota((LEAF, FEAT), 1)
    feature = iota((FEAT, LEAF), 0)
    zero = jnp.zeros((LEAF, FEAT), BF16)

    def by_head(block):
        return jnp.concatenate(
            [jnp.where(lane < HEAD, block, zero), jnp.where(lane < HEAD, zero, block)], axis=0
        )

    def merge_heads(transposed):
        return jnp.where(feature < HEAD, transposed[:, :LEAF], transposed[:, LEAF:]).T

    near_grad[...] = jnp.zeros_like(near_grad)
    one_grad[...] = jnp.zeros_like(one_grad)
    for b in range(LEAVES):
        rows = slice(b * LEAF, (b + 1) * LEAF)
        near_rows = slice(b * LEAF, (b + 3) * LEAF)
        half = (1 - b // 2) * LEAF
        q2 = by_head(qn_ref[rows]) * jnp.asarray(0.125, BF16)
        g2 = by_head(g_ref[rows])
        kv = jnp.concatenate([near[near_rows], one_ref[half : half + LEAF], cross[...]], axis=0)
        keys = kv[:, :FEAT]
        values = kv[:, FEAT:]
        raw = dot(keys, q2, (1, 1))
        before, after = raw[:LEAF], raw[2 * LEAF : 3 * LEAF]
        if b == 0:
            before = before + left
        if b == LEAVES - 1:
            after = after + right
        scores = jnp.concatenate(
            [before, raw[LEAF : 2 * LEAF], after, raw[3 * LEAF :] + bias], axis=0
        )
        weights = jnp.exp(scores - jnp.max(scores, axis=0, keepdims=True))
        probs = weights * (1.0 / jnp.sum(weights, axis=0, keepdims=True))
        low = probs.astype(BF16)
        prob_grad = dot(values, g2, (1, 1))
        delta = jnp.sum(probs * prob_grad, axis=0, keepdims=True)
        score_grad = (probs * (prob_grad - delta)).astype(BF16)
        att_ref[rows] = merge_heads(dot(values, low, (0, 0))).astype(BF16)
        nqg_ref[rows] = merge_heads(dot(keys, score_grad, (0, 0))) * 0.125
        key_part = dot(score_grad, q2, (1, 0))
        value_part = dot(low, g2, (1, 0))
        for part, lanes in ((key_part, slice(0, FEAT)), (value_part, slice(FEAT, 2 * FEAT))):
            near_grad[near_rows, lanes] += part[: 3 * LEAF]
            one_grad[half : half + LEAF, lanes] += part[3 * LEAF : 4 * LEAF]
            if b == 0:
                cross_grad[:, lanes] = part[4 * LEAF :]
            else:
                cross_grad[:, lanes] += part[4 * LEAF :]

    spread = spreading(0, 256, 1).astype(BF16)
    high = one_grad[...].astype(BF16)
    rest = (one_grad[...] - high.astype(F32)).astype(BF16)
    tok_ref[...] = near_grad[LEAF : LEAF + ROWS] + dot(spread, high, (1, 0)) + dot(spread, rest, (1, 0))
    p1o_ref[:LEAF] = near_grad[pl.ds(peer_side, LEAF)].astype(BF16)
    p1o_ref[LEAF:] = cross_grad[64:128].astype(BF16)
    p2o_ref[...] = near_grad[pl.ds(other_side, LEAF)].astype(BF16)
    for s in range(8):
        zo_ref[s, :FAR] = cross_grad[384 + FAR * s : 384 + FAR * (s + 1)].astype(BF16)
    zo_ref[place, FAR:] = jnp.zeros((64, 2 * FEAT), BF16)
    zo_ref[jnp.bitwise_xor(place, 1), FAR:] = cross_grad[:64].astype(BF16)
    zo_ref[jnp.bitwise_xor(place, 2), FAR:] = cross_grad[128:192].astype(BF16)
    zo_ref[jnp.bitwise_xor(place, 3), FAR:] = cross_grad[192:256].astype(BF16)
    for i in range(4):
        other = jnp.bitwise_xor(place, 4 + i)
        zo_ref[other, FAR : FAR + 32] = cross_grad[256 + 32 * i : 288 + 32 * i].astype(BF16)
        zo_ref[other, FAR + 32 :] = jnp.zeros((32, 2 * FEAT), BF16)


def column_kernel(z_ref, *out_refs):
    far = jnp.sum(z_ref[:, :FAR].astype(F32), axis=0).astype(BF16)
    slots = dot(far_pick((112, FAR), 1), far, (1, 0)).astype(BF16)
    for d in range(1, 8):
        out_refs[d - 1][...] = slots[16 * (d - 1) : 16 * d]


def total_kernel(
    tok_ref, p1_ref, p2_ref, z_ref, y1, y2, y3, y4, y5, y6, y7,
    q_ref, k_ref, qg_ref, kg_ref, nqg_ref, nkg_ref, vg_ref, sum_ref, acc,
):
    index = lax.axis_index("seq")
    place = jnp.bitwise_and(index, 7)
    odd = jnp.bitwise_and(index, 1)
    pieces = [z_ref[jnp.bitwise_xor(place, 1), FAR:], p1_ref[LEAF:]]
    maps = [spreading(0, 64, 2), spreading(64, 64, 2)]
    for d in range(2, 8):
        rows = ROWS >> ROW_LEVEL[d]
        pieces.append(z_ref[jnp.bitwise_xor(place, d), FAR : FAR + rows])
        maps.append(spreading(0, rows, ROW_LEVEL[d]))
    for d, y_ref in zip(range(1, 8), (y1, y2, y3, y4, y5, y6, y7)):
        pieces.append(y_ref[...])
        maps.append(spreading(0, 16, COLUMN_LEVEL[d]))
    spread = jnp.concatenate(maps, axis=1).astype(BF16)
    acc[...] = tok_ref[...] + dot(spread, jnp.concatenate(pieces, axis=0), (1, 0))
    acc[pl.ds(pl.multiple_of((1 - odd) * 384, LEAF), LEAF)] += p1_ref[:LEAF].astype(F32)
    acc[pl.ds(pl.multiple_of(odd * 384, LEAF), LEAF)] += p2_ref[...].astype(F32)
    vg_ref[...] = acc[:, FEAT:].astype(BF16)
    key_total = acc[:, :FEAT]
    nkg_ref[...] = key_total
    tile = jnp.concatenate(
        token_sums(q_ref[...].astype(F32) * qg_ref[...] * nqg_ref[...])
        + token_sums(k_ref[...].astype(F32) * kg_ref[...] * key_total),
        axis=0,
    )
    sum_ref[...] = tile


def finish_kernel(width, sq_ref, inner_ref, q_ref, k_ref, qg_ref, kg_ref, nqg_ref, nkg_ref, dq_ref, dk_ref):
    rate = lax.rsqrt(jnp.sum(sq_ref[...], axis=0) / width + EPS)
    inner = jnp.sum(inner_ref[...], axis=0) / width
    cubed = rate * rate * rate * inner
    for first, x_ref, gain_ref, grad_ref, out_ref in (
        (0, q_ref, qg_ref, nqg_ref, dq_ref),
        (4, k_ref, kg_ref, nkg_ref, dk_ref),
    ):
        out_ref[...] = (
            spread_tokens(rate, first) * gain_ref[...] * grad_ref[...]
            - x_ref[...].astype(F32) * spread_tokens(cubed, first)
        ).astype(BF16)


def call(kernel, outs, args, scratch=(), flops=0, name=None):
    many = isinstance(outs, list)
    moved = sum(math.prod(x.shape) * x.dtype.itemsize for x in list(args) + (outs if many else [outs]))
    return pl.pallas_call(
        kernel,
        out_shape=outs,
        scratch_shapes=list(scratch),
        compiler_params=PARAMS,
        cost_estimate=pl.CostEstimate(flops=flops, bytes_accessed=moved, transcendentals=0),
        name=name,
    )(*args)


def sds(*shape, dtype=BF16):
    return jax.ShapeDtypeStruct(shape, dtype)


ROW_GROUPS = [[8 * y + z for z in range(8)] for y in range(8)]
COLUMN_GROUPS = [[8 * y + z for y in range(8)] for z in range(8)]


def exchange(x, axis, groups=None):
    return lax.all_to_all(x, axis, 0, 0, axis_index_groups=groups, tiled=True)


def local(queries, key_rows, value_rows, query_gain, key_gain, out_grad):
    seq = lax.axis_size("seq")
    heads = lax.axis_size("head")
    width = float(heads * FEAT)
    qg = query_gain.reshape(1, FEAT)
    kg = key_gain.reshape(1, FEAT)
    peer = [(i, i ^ 1) for i in range(seq)]
    beside = [(i, i + 1) for i in range(1, seq - 1, 2)] + [(i + 1, i) for i in range(1, seq - 1, 2)]

    squares = call(squares_kernel, sds(heads, 8, FEAT, dtype=F32), (queries, key_rows), name="squares")
    squares = exchange(squares, "head")
    qn, kv, one, lv, ysend, p1, p2 = call(
        lambda *refs: norm_kernel(width, *refs),
        [sds(ROWS, FEAT), sds(ROWS, 256), sds(256, 256), sds(224, 256), sds(8, 16, 256), sds(192, 256), sds(LEAF, 256)],
        (squares, queries, key_rows, value_rows, qg, kg),
        name="norm",
    )
    p1 = lax.ppermute(p1, "seq", peer)
    p2 = lax.ppermute(p2, "seq", beside)
    yrecv = exchange(ysend, "seq", COLUMN_GROUPS)
    zsend = call(row_kernel, sds(8, SLOT, 256), (yrecv, lv), name="rows")
    zrecv = exchange(zsend, "seq", ROW_GROUPS)
    attended, nqg, tok, p1, p2, zsend = call(
        attend_kernel,
        [sds(ROWS, FEAT), sds(ROWS, FEAT, dtype=F32), sds(ROWS, 256, dtype=F32), sds(192, 256), sds(LEAF, 256), sds(8, SLOT, 256)],
        (qn, kv, one, out_grad, p1, p2, zrecv),
        scratch=[
            pltpu.VMEM((768, 256), BF16),
            pltpu.VMEM((768, 256), BF16),
            pltpu.VMEM((768, 256), F32),
            pltpu.VMEM((256, 256), F32),
            pltpu.VMEM((768, 256), F32),
        ],
        flops=4 * 6 * 2 * 256 * KEYS * FEAT,
        name="attend",
    )
    p1 = lax.ppermute(p1, "seq", peer)
    p2 = lax.ppermute(p2, "seq", beside)
    zrecv = exchange(zsend, "seq", ROW_GROUPS)
    ysend = call(column_kernel, [sds(16, 256) for _ in range(7)], (zrecv,), name="columns")
    yrecv = [
        lax.ppermute(ysend[d - 1], "seq", [(i, i ^ (8 * d)) for i in range(seq)]) for d in range(1, 8)
    ]
    nkg, value_grad, inner = call(
        total_kernel,
        [sds(ROWS, FEAT, dtype=F32), sds(ROWS, FEAT), sds(8, FEAT, dtype=F32)],
        (tok, p1, p2, zrecv, *yrecv, queries, key_rows, qg, kg, nqg),
        scratch=[pltpu.VMEM((ROWS, 256), F32)],
        name="total",
    )
    inner = lax.all_gather(inner, "head", axis=0)
    query_grad, key_grad = call(
        lambda *refs: finish_kernel(width, *refs),
        [sds(ROWS, FEAT), sds(ROWS, FEAT)],
        (squares, inner, queries, key_rows, qg, kg, nqg, nkg),
        name="finish",
    )
    return (attended, query_grad, key_grad, value_grad)


def solution(mesh):
    placed = (
        P("seq", "head"),
        P("seq", "head"),
        P("seq", "head"),
        P("head"),
        P("head"),
        P("seq", "head"),
    )
    return jax.shard_map(
        local,
        mesh=mesh,
        in_specs=placed,
        out_specs=(P("seq", "head"), P("seq", "head"), P("seq", "head"), P("seq", "head")),
        check_vma=False,
    )
```

```python
import math

import jax
import jax.numpy as jnp
from jax import lax
from jax.experimental import pallas as pl
from jax.experimental.pallas import tpu as pltpu
from jax.sharding import PartitionSpec as P

ROWS = 512
FEAT = 128
LEAF = 128
LEAVES = 4
HEAD = 64
KEYS = 1280
EPS = 1e-06
LN2 = math.log(2.0)
F32 = jnp.float32
BF16 = jnp.bfloat16
PARAMS = pltpu.CompilerParams(vmem_limit_bytes=40 * 1024 * 1024)
ROW_LEVEL = {1: 2, 2: 3, 3: 3, 4: 4, 5: 4, 6: 4, 7: 4}
COLUMN_LEVEL = {1: 5, 2: 6, 3: 6, 4: 7, 5: 7, 6: 7, 7: 7}
FAR = 48
SLOT = 112


def dot(a, b, dims):
    return lax.dot_general(a, b, ((dims[:1], dims[1:]), ((), ())), preferred_element_type=F32)


def iota(shape, axis):
    return lax.broadcasted_iota(jnp.int32, shape, axis)


def pooling(rows, level):
    token = iota((rows, ROWS), 1)
    hit = jnp.right_shift(token, level) == iota((rows, ROWS), 0)
    return jnp.where(hit, 2.0**-level, 0.0)


def spreading(first, rows, level):
    token = iota((ROWS, rows), 0)
    hit = jnp.right_shift(token, level) == iota((ROWS, rows), 1) + first
    return jnp.where(hit, 2.0**-level, 0.0)


def far_pick(shape, far_axis):
    far = iota(shape, far_axis)
    slot_row = iota(shape, 1 - far_axis)
    mid = far - 16
    low = far - 32
    column = jnp.where(
        far < 16,
        far,
        jnp.where(
            far < 32,
            (1 + jnp.right_shift(mid, 3)) * 16 + jnp.bitwise_and(mid, 7),
            (3 + jnp.right_shift(low, 2)) * 16 + jnp.bitwise_and(low, 3),
        ),
    )
    return jnp.where(column == slot_row, 1.0, 0.0).astype(BF16)


def token_sums(x):
    return [
        jnp.sum(x[i * LEAF : (i + 1) * LEAF].T, axis=0, keepdims=True) for i in range(LEAVES)
    ]


def spread_tokens(tile, first):
    return jnp.concatenate(
        [
            jnp.broadcast_to(tile[first + i : first + i + 1], (LEAF, LEAF)).T
            for i in range(LEAVES)
        ],
        axis=0,
    )


def squares_kernel(q_ref, k_ref, out_ref):
    q = q_ref[...].astype(F32)
    k = k_ref[...].astype(F32)
    tile = jnp.concatenate(token_sums(q * q) + token_sums(k * k), axis=0)
    for i in range(out_ref.shape[0]):
        out_ref[i] = tile


def norm_kernel(width, sum_ref, q_ref, k_ref, v_ref, qg_ref, kg_ref, qn_ref, kv_ref, one_ref, lv_ref, y_ref, p1_ref, p2_ref):
    index = lax.axis_index("seq")
    column = jnp.right_shift(index, 3)
    odd = jnp.bitwise_and(index, 1)
    total = jnp.sum(sum_ref[...], axis=0)
    rate = lax.rsqrt(total / width + EPS)
    qn_ref[...] = (
        q_ref[...].astype(F32) * spread_tokens(rate, 0) * qg_ref[...]
    ).astype(BF16)
    kv_ref[:, :FEAT] = (
        k_ref[...].astype(F32) * spread_tokens(rate, 4) * kg_ref[...]
    ).astype(BF16)
    kv_ref[:, FEAT:] = v_ref[...]
    pool = jnp.concatenate(
        [pooling(ROWS >> level, level) for level in (1, 2, 3, 4)]
        + [pooling(16, COLUMN_LEVEL[d]) for d in range(1, 8)],
        axis=0,
    ).astype(BF16)
    coarse = dot(pool, kv_ref[...], (1, 0)).astype(BF16)
    one_ref[...] = coarse[:256]
    lv_ref[...] = coarse[256:480]
    y_ref[column] = jnp.zeros((16, 2 * FEAT), BF16)
    for d in range(1, 8):
        y_ref[jnp.bitwise_xor(column, d)] = coarse[464 + 16 * d : 480 + 16 * d]
    p1_ref[:LEAF] = kv_ref[pl.ds(pl.multiple_of((1 - odd) * 384, LEAF), LEAF)]
    p1_ref[LEAF:] = coarse[320:384]
    p2_ref[...] = kv_ref[pl.ds(pl.multiple_of(odd * 384, LEAF), LEAF)]


def row_kernel(y_ref, lv_ref, out_ref):
    index = lax.axis_index("seq")
    column = jnp.right_shift(index, 3)
    place = jnp.bitwise_and(index, 7)
    slots = jnp.concatenate([y_ref[jnp.bitwise_xor(column, d)] for d in range(1, 8)], axis=0)
    far = dot(far_pick((FAR, 112), 0), slots, (1, 0)).astype(BF16)
    for s in range(8):
        out_ref[s, :FAR] = far
    out_ref[place, FAR:] = jnp.zeros((64, 2 * FEAT), BF16)
    for d in range(1, 8):
        other = jnp.bitwise_xor(place, d)
        if d == 1:
            out_ref[other, FAR:] = lv_ref[:64]
        elif d < 4:
            out_ref[other, FAR:] = lv_ref[128:192]
        else:
            out_ref[other, FAR : FAR + 32] = lv_ref[192:224]
            out_ref[other, FAR + 32 :] = jnp.zeros((32, 2 * FEAT), BF16)


def attend_kernel(
    qn_ref, kv_ref, one_ref, g_ref, p1_ref, p2_ref, z_ref,
    att_ref, nqg_ref, tok_ref, p1o_ref, p2o_ref, zo_ref,
    near, cross, near_grad, one_grad, cross_grad,
):
    index = lax.axis_index("seq")
    last = lax.axis_size("seq") - 1
    place = jnp.bitwise_and(index, 7)
    odd = jnp.bitwise_and(index, 1)
    peer_side = pl.multiple_of((1 - odd) * 640, LEAF)
    other_side = pl.multiple_of(odd * 640, LEAF)
    near[LEAF : LEAF + ROWS] = kv_ref[...]
    near[pl.ds(peer_side, LEAF)] = p1_ref[:LEAF]
    near[pl.ds(other_side, LEAF)] = p2_ref[...]
    cross[:64] = z_ref[jnp.bitwise_xor(place, 1), FAR:]
    cross[64:128] = p1_ref[LEAF:]
    cross[128:192] = z_ref[jnp.bitwise_xor(place, 2), FAR:]
    cross[192:256] = z_ref[jnp.bitwise_xor(place, 3), FAR:]
    for i in range(4):
        cross[256 + 32 * i : 288 + 32 * i] = z_ref[jnp.bitwise_xor(place, 4 + i), FAR : FAR + 32]
    for s in range(8):
        cross[384 + FAR * s : 384 + FAR * (s + 1)] = z_ref[s, :FAR]

    def level_bias(rows, level):
        return jnp.full((rows, 2 * LEAF), level * LN2, F32)

    bias = jnp.concatenate(
        [level_bias(LEAF, level) for level in (1, 2, 3, 4)]
        + [level_bias(16, level) for _ in range(8) for level in (5, 6, 7)],
        axis=0,
    )
    left = jnp.where(index > 0, 0.0, -jnp.inf).astype(F32)
    right = jnp.where(index < last, 0.0, -jnp.inf).astype(F32)
    lane = iota((LEAF, FEAT), 1)
    feature = iota((FEAT, LEAF), 0)
    zero = jnp.zeros((LEAF, FEAT), BF16)

    def by_head(block):
        return jnp.concatenate(
            [jnp.where(lane < HEAD, block, zero), jnp.where(lane < HEAD, zero, block)], axis=0
        )

    def merge_heads(transposed):
        return jnp.where(feature < HEAD, transposed[:, :LEAF], transposed[:, LEAF:]).T

    near_grad[...] = jnp.zeros_like(near_grad)
    one_grad[...] = jnp.zeros_like(one_grad)
    for b in range(LEAVES):
        rows = slice(b * LEAF, (b + 1) * LEAF)
        near_rows = slice(b * LEAF, (b + 3) * LEAF)
        half = (1 - b // 2) * LEAF
        q2 = by_head(qn_ref[rows]) * jnp.asarray(0.125, BF16)
        g2 = by_head(g_ref[rows])
        kv = jnp.concatenate([near[near_rows], one_ref[half : half + LEAF], cross[...]], axis=0)
        keys = kv[:, :FEAT]
        values = kv[:, FEAT:]
        raw = dot(keys, q2, (1, 1))
        before, after = raw[:LEAF], raw[2 * LEAF : 3 * LEAF]
        if b == 0:
            before = before + left
        if b == LEAVES - 1:
            after = after + right
        scores = jnp.concatenate(
            [before, raw[LEAF : 2 * LEAF], after, raw[3 * LEAF :] + bias], axis=0
        )
        weights = jnp.exp(scores - jnp.max(scores, axis=0, keepdims=True))
        probs = weights * (1.0 / jnp.sum(weights, axis=0, keepdims=True))
        low = probs.astype(BF16)
        prob_grad = dot(values, g2, (1, 1))
        delta = jnp.sum(probs * prob_grad, axis=0, keepdims=True)
        score_grad = (probs * (prob_grad - delta)).astype(BF16)
        att_ref[rows] = merge_heads(dot(values, low, (0, 0))).astype(BF16)
        nqg_ref[rows] = merge_heads(dot(keys, score_grad, (0, 0))) * 0.125
        key_part = dot(score_grad, q2, (1, 0))
        value_part = dot(low, g2, (1, 0))
        for part, lanes in ((key_part, slice(0, FEAT)), (value_part, slice(FEAT, 2 * FEAT))):
            near_grad[near_rows, lanes] += part[: 3 * LEAF]
            one_grad[half : half + LEAF, lanes] += part[3 * LEAF : 4 * LEAF]
            if b == 0:
                cross_grad[:, lanes] = part[4 * LEAF :]
            else:
                cross_grad[:, lanes] += part[4 * LEAF :]

    spread = spreading(0, 256, 1).astype(BF16)
    high = one_grad[...].astype(BF16)
    rest = (one_grad[...] - high.astype(F32)).astype(BF16)
    tok_ref[...] = near_grad[LEAF : LEAF + ROWS] + dot(spread, high, (1, 0)) + dot(spread, rest, (1, 0))
    p1o_ref[:LEAF] = near_grad[pl.ds(peer_side, LEAF)].astype(BF16)
    p1o_ref[LEAF:] = cross_grad[64:128].astype(BF16)
    p2o_ref[...] = near_grad[pl.ds(other_side, LEAF)].astype(BF16)
    for s in range(8):
        zo_ref[s, :FAR] = cross_grad[384 + FAR * s : 384 + FAR * (s + 1)].astype(BF16)
    zo_ref[place, FAR:] = jnp.zeros((64, 2 * FEAT), BF16)
    zo_ref[jnp.bitwise_xor(place, 1), FAR:] = cross_grad[:64].astype(BF16)
    zo_ref[jnp.bitwise_xor(place, 2), FAR:] = cross_grad[128:192].astype(BF16)
    zo_ref[jnp.bitwise_xor(place, 3), FAR:] = cross_grad[192:256].astype(BF16)
    for i in range(4):
        other = jnp.bitwise_xor(place, 4 + i)
        zo_ref[other, FAR : FAR + 32] = cross_grad[256 + 32 * i : 288 + 32 * i].astype(BF16)
        zo_ref[other, FAR + 32 :] = jnp.zeros((32, 2 * FEAT), BF16)


def column_kernel(z_ref, out_ref):
    column = jnp.right_shift(lax.axis_index("seq"), 3)
    far = jnp.sum(z_ref[:, :FAR].astype(F32), axis=0).astype(BF16)
    slots = dot(far_pick((112, FAR), 1), far, (1, 0)).astype(BF16)
    out_ref[column] = jnp.zeros((16, 2 * FEAT), BF16)
    for d in range(1, 8):
        out_ref[jnp.bitwise_xor(column, d)] = slots[16 * (d - 1) : 16 * d]


def total_kernel(
    tok_ref, p1_ref, p2_ref, z_ref, y_ref,
    q_ref, k_ref, qg_ref, kg_ref, nqg_ref, nkg_ref, vg_ref, sum_ref, acc,
):
    index = lax.axis_index("seq")
    column = jnp.right_shift(index, 3)
    place = jnp.bitwise_and(index, 7)
    odd = jnp.bitwise_and(index, 1)
    pieces = [z_ref[jnp.bitwise_xor(place, 1), FAR:], p1_ref[LEAF:]]
    maps = [spreading(0, 64, 2), spreading(64, 64, 2)]
    for d in range(2, 8):
        rows = ROWS >> ROW_LEVEL[d]
        pieces.append(z_ref[jnp.bitwise_xor(place, d), FAR : FAR + rows])
        maps.append(spreading(0, rows, ROW_LEVEL[d]))
    for d in range(1, 8):
        pieces.append(y_ref[jnp.bitwise_xor(column, d)])
        maps.append(spreading(0, 16, COLUMN_LEVEL[d]))
    spread = jnp.concatenate(maps, axis=1).astype(BF16)
    acc[...] = tok_ref[...] + dot(spread, jnp.concatenate(pieces, axis=0), (1, 0))
    acc[pl.ds(pl.multiple_of((1 - odd) * 384, LEAF), LEAF)] += p1_ref[:LEAF].astype(F32)
    acc[pl.ds(pl.multiple_of(odd * 384, LEAF), LEAF)] += p2_ref[...].astype(F32)
    vg_ref[...] = acc[:, FEAT:].astype(BF16)
    key_total = acc[:, :FEAT]
    nkg_ref[...] = key_total
    tile = jnp.concatenate(
        token_sums(q_ref[...].astype(F32) * qg_ref[...] * nqg_ref[...])
        + token_sums(k_ref[...].astype(F32) * kg_ref[...] * key_total),
        axis=0,
    )
    for i in range(sum_ref.shape[0]):
        sum_ref[i] = tile


def finish_kernel(width, sq_ref, inner_ref, q_ref, k_ref, qg_ref, kg_ref, nqg_ref, nkg_ref, dq_ref, dk_ref):
    rate = lax.rsqrt(jnp.sum(sq_ref[...], axis=0) / width + EPS)
    inner = jnp.sum(inner_ref[...], axis=0) / width
    cubed = rate * rate * rate * inner
    for first, x_ref, gain_ref, grad_ref, out_ref in (
        (0, q_ref, qg_ref, nqg_ref, dq_ref),
        (4, k_ref, kg_ref, nkg_ref, dk_ref),
    ):
        out_ref[...] = (
            spread_tokens(rate, first) * gain_ref[...] * grad_ref[...]
            - x_ref[...].astype(F32) * spread_tokens(cubed, first)
        ).astype(BF16)


def call(kernel, outs, args, scratch=(), flops=0, name=None):
    many = isinstance(outs, list)
    moved = sum(math.prod(x.shape) * x.dtype.itemsize for x in list(args) + (outs if many else [outs]))
    return pl.pallas_call(
        kernel,
        out_shape=outs,
        scratch_shapes=list(scratch),
        compiler_params=PARAMS,
        cost_estimate=pl.CostEstimate(flops=flops, bytes_accessed=moved, transcendentals=0),
        name=name,
    )(*args)


def sds(*shape, dtype=BF16):
    return jax.ShapeDtypeStruct(shape, dtype)


ROW_GROUPS = [[8 * y + z for z in range(8)] for y in range(8)]
COLUMN_GROUPS = [[8 * y + z for y in range(8)] for z in range(8)]


def exchange(x, axis, groups=None):
    return lax.all_to_all(x, axis, 0, 0, axis_index_groups=groups, tiled=True)


def local(queries, key_rows, value_rows, query_gain, key_gain, out_grad):
    seq = lax.axis_size("seq")
    heads = lax.axis_size("head")
    width = float(heads * FEAT)
    qg = query_gain.reshape(1, FEAT)
    kg = key_gain.reshape(1, FEAT)
    peer = [(i, i ^ 1) for i in range(seq)]
    beside = [(i, i + 1) for i in range(1, seq - 1, 2)] + [(i + 1, i) for i in range(1, seq - 1, 2)]

    squares = call(squares_kernel, sds(heads, 8, FEAT, dtype=F32), (queries, key_rows), name="squares")
    squares = exchange(squares, "head")
    qn, kv, one, lv, ysend, p1, p2 = call(
        lambda *refs: norm_kernel(width, *refs),
        [sds(ROWS, FEAT), sds(ROWS, 256), sds(256, 256), sds(224, 256), sds(8, 16, 256), sds(192, 256), sds(LEAF, 256)],
        (squares, queries, key_rows, value_rows, qg, kg),
        name="norm",
    )
    p1 = lax.ppermute(p1, "seq", peer)
    p2 = lax.ppermute(p2, "seq", beside)
    yrecv = exchange(ysend, "seq", COLUMN_GROUPS)
    zsend = call(row_kernel, sds(8, SLOT, 256), (yrecv, lv), name="rows")
    zrecv = exchange(zsend, "seq", ROW_GROUPS)
    attended, nqg, tok, p1, p2, zsend = call(
        attend_kernel,
        [sds(ROWS, FEAT), sds(ROWS, FEAT, dtype=F32), sds(ROWS, 256, dtype=F32), sds(192, 256), sds(LEAF, 256), sds(8, SLOT, 256)],
        (qn, kv, one, out_grad, p1, p2, zrecv),
        scratch=[
            pltpu.VMEM((768, 256), BF16),
            pltpu.VMEM((768, 256), BF16),
            pltpu.VMEM((768, 256), F32),
            pltpu.VMEM((256, 256), F32),
            pltpu.VMEM((768, 256), F32),
        ],
        flops=4 * 6 * 2 * 256 * KEYS * FEAT,
        name="attend",
    )
    p1 = lax.ppermute(p1, "seq", peer)
    p2 = lax.ppermute(p2, "seq", beside)
    zrecv = exchange(zsend, "seq", ROW_GROUPS)
    ysend = call(column_kernel, sds(8, 16, 256), (zrecv,), name="columns")
    yrecv = exchange(ysend, "seq", COLUMN_GROUPS)
    nkg, value_grad, inner = call(
        total_kernel,
        [sds(ROWS, FEAT, dtype=F32), sds(ROWS, FEAT), sds(heads, 8, FEAT, dtype=F32)],
        (tok, p1, p2, zrecv, yrecv, queries, key_rows, qg, kg, nqg),
        scratch=[pltpu.VMEM((ROWS, 256), F32)],
        name="total",
    )
    inner = exchange(inner, "head")
    query_grad, key_grad = call(
        lambda *refs: finish_kernel(width, *refs),
        [sds(ROWS, FEAT), sds(ROWS, FEAT)],
        (squares, inner, queries, key_rows, qg, kg, nqg, nkg),
        name="finish",
    )
    return (attended, query_grad, key_grad, value_grad)


def solution(mesh):
    placed = (
        P("seq", "head"),
        P("seq", "head"),
        P("seq", "head"),
        P("head"),
        P("head"),
        P("seq", "head"),
    )
    return jax.shard_map(
        local,
        mesh=mesh,
        in_specs=placed,
        out_specs=(P("seq", "head"), P("seq", "head"), P("seq", "head"), P("seq", "head")),
        check_vma=False,
    )
```

```python
import math

import jax
import jax.numpy as jnp
from jax import lax
from jax.experimental import pallas as pl
from jax.experimental.pallas import tpu as pltpu
from jax.sharding import PartitionSpec as P

ROWS = 512
FEAT = 128
LEAF = 128
LEAVES = 4
HEAD = 64
KEYS = 1280
EPS = 1e-06
LN2 = math.log(2.0)
F32 = jnp.float32
BF16 = jnp.bfloat16
PARAMS = pltpu.CompilerParams(vmem_limit_bytes=40 * 1024 * 1024)
ROW_LEVEL = {1: 2, 2: 3, 3: 3, 4: 4, 5: 4, 6: 4, 7: 4}
COLUMN_LEVEL = {1: 5, 2: 6, 3: 6, 4: 7, 5: 7, 6: 7, 7: 7}
FAR = 48
SLOT = 112


def dot(a, b, dims):
    return lax.dot_general(a, b, ((dims[:1], dims[1:]), ((), ())), preferred_element_type=F32)


def iota(shape, axis):
    return lax.broadcasted_iota(jnp.int32, shape, axis)


def pooling(rows, level):
    token = iota((rows, ROWS), 1)
    hit = jnp.right_shift(token, level) == iota((rows, ROWS), 0)
    return jnp.where(hit, 2.0**-level, 0.0)


def spreading(first, rows, level):
    token = iota((ROWS, rows), 0)
    hit = jnp.right_shift(token, level) == iota((ROWS, rows), 1) + first
    return jnp.where(hit, 2.0**-level, 0.0)


def far_pick(shape, far_axis):
    far = iota(shape, far_axis)
    slot_row = iota(shape, 1 - far_axis)
    mid = far - 16
    low = far - 32
    column = jnp.where(
        far < 16,
        far,
        jnp.where(
            far < 32,
            (1 + jnp.right_shift(mid, 3)) * 16 + jnp.bitwise_and(mid, 7),
            (3 + jnp.right_shift(low, 2)) * 16 + jnp.bitwise_and(low, 3),
        ),
    )
    return jnp.where(column == slot_row, 1.0, 0.0).astype(BF16)


def token_sums(x):
    return [
        jnp.sum(x[i * LEAF : (i + 1) * LEAF].T, axis=0, keepdims=True) for i in range(LEAVES)
    ]


def spread_tokens(tile, first):
    return jnp.concatenate(
        [
            jnp.broadcast_to(tile[first + i : first + i + 1], (LEAF, LEAF)).T
            for i in range(LEAVES)
        ],
        axis=0,
    )


def squares_kernel(q_ref, k_ref, out_ref):
    q = q_ref[...].astype(F32)
    k = k_ref[...].astype(F32)
    tile = jnp.concatenate(token_sums(q * q) + token_sums(k * k), axis=0)
    for i in range(out_ref.shape[0]):
        out_ref[i] = tile


def norm_kernel(width, sum_ref, q_ref, k_ref, v_ref, qg_ref, kg_ref, qn_ref, kv_ref, one_ref, lv_ref, y_ref, p1_ref, p2_ref):
    index = lax.axis_index("seq")
    place = jnp.bitwise_and(index, 7)
    odd = jnp.bitwise_and(index, 1)
    total = jnp.sum(sum_ref[...], axis=0)
    rate = lax.rsqrt(total / width + EPS)
    qn_ref[...] = (
        q_ref[...].astype(F32) * spread_tokens(rate, 0) * qg_ref[...]
    ).astype(BF16)
    kv_ref[:, :FEAT] = (
        k_ref[...].astype(F32) * spread_tokens(rate, 4) * kg_ref[...]
    ).astype(BF16)
    kv_ref[:, FEAT:] = v_ref[...]
    pool = jnp.concatenate(
        [pooling(ROWS >> level, level) for level in (1, 2, 3, 4)]
        + [pooling(16, COLUMN_LEVEL[d]) for d in range(1, 8)],
        axis=0,
    ).astype(BF16)
    coarse = dot(pool, kv_ref[...], (1, 0)).astype(BF16)
    one_ref[...] = coarse[:256]
    lv_ref[place] = jnp.zeros((64, 2 * FEAT), BF16)
    for d in range(1, 8):
        other = jnp.bitwise_xor(place, d)
        if d == 1:
            lv_ref[other] = coarse[256:320]
        elif d < 4:
            lv_ref[other] = coarse[384:448]
        else:
            lv_ref[other, :32] = coarse[448:480]
            lv_ref[other, 32:] = jnp.zeros((32, 2 * FEAT), BF16)
    for m in range(64):
        d = m >> 3
        piece = coarse[464 + 16 * d : 480 + 16 * d] if d else jnp.zeros((16, 2 * FEAT), BF16)
        y_ref[jnp.bitwise_xor(index, m)] = piece
    p1_ref[:LEAF] = kv_ref[pl.ds(pl.multiple_of((1 - odd) * 384, LEAF), LEAF)]
    p1_ref[LEAF:] = coarse[320:384]
    p2_ref[...] = kv_ref[pl.ds(pl.multiple_of(odd * 384, LEAF), LEAF)]


def far_kernel(y_ref, out_ref):
    index = lax.axis_index("seq")
    pick = far_pick((FAR, 112), 0)
    for d in range(8):
        slots = jnp.concatenate(
            [y_ref[jnp.bitwise_xor(index, 8 * c + d)] for c in range(1, 8)], axis=0
        )
        out_ref[d] = dot(pick, slots, (1, 0)).astype(BF16)


def attend_kernel(
    qn_ref, kv_ref, one_ref, g_ref, p1_ref, p2_ref, z_ref, far_ref,
    att_ref, nqg_ref, tok_ref, p1o_ref, p2o_ref, zo_ref,
    near, cross, near_grad, one_grad, cross_grad,
):
    index = lax.axis_index("seq")
    last = lax.axis_size("seq") - 1
    place = jnp.bitwise_and(index, 7)
    odd = jnp.bitwise_and(index, 1)
    peer_side = pl.multiple_of((1 - odd) * 640, LEAF)
    other_side = pl.multiple_of(odd * 640, LEAF)
    near[LEAF : LEAF + ROWS] = kv_ref[...]
    near[pl.ds(peer_side, LEAF)] = p1_ref[:LEAF]
    near[pl.ds(other_side, LEAF)] = p2_ref[...]
    cross[:64] = z_ref[jnp.bitwise_xor(place, 1)]
    cross[64:128] = p1_ref[LEAF:]
    cross[128:192] = z_ref[jnp.bitwise_xor(place, 2)]
    cross[192:256] = z_ref[jnp.bitwise_xor(place, 3)]
    for i in range(4):
        cross[256 + 32 * i : 288 + 32 * i] = z_ref[jnp.bitwise_xor(place, 4 + i), :32]
    for d in range(8):
        cross[384 + FAR * d : 384 + FAR * (d + 1)] = far_ref[d]

    def level_bias(rows, level):
        return jnp.full((rows, 2 * LEAF), level * LN2, F32)

    bias = jnp.concatenate(
        [level_bias(LEAF, level) for level in (1, 2, 3, 4)]
        + [level_bias(16, level) for _ in range(8) for level in (5, 6, 7)],
        axis=0,
    )
    left = jnp.where(index > 0, 0.0, -jnp.inf).astype(F32)
    right = jnp.where(index < last, 0.0, -jnp.inf).astype(F32)
    lane = iota((LEAF, FEAT), 1)
    feature = iota((FEAT, LEAF), 0)
    zero = jnp.zeros((LEAF, FEAT), BF16)

    def by_head(block):
        return jnp.concatenate(
            [jnp.where(lane < HEAD, block, zero), jnp.where(lane < HEAD, zero, block)], axis=0
        )

    def merge_heads(transposed):
        return jnp.where(feature < HEAD, transposed[:, :LEAF], transposed[:, LEAF:]).T

    near_grad[...] = jnp.zeros_like(near_grad)
    one_grad[...] = jnp.zeros_like(one_grad)
    for b in range(LEAVES):
        rows = slice(b * LEAF, (b + 1) * LEAF)
        near_rows = slice(b * LEAF, (b + 3) * LEAF)
        half = (1 - b // 2) * LEAF
        q2 = by_head(qn_ref[rows]) * jnp.asarray(0.125, BF16)
        g2 = by_head(g_ref[rows])
        kv = jnp.concatenate([near[near_rows], one_ref[half : half + LEAF], cross[...]], axis=0)
        keys = kv[:, :FEAT]
        values = kv[:, FEAT:]
        raw = dot(keys, q2, (1, 1))
        before, after = raw[:LEAF], raw[2 * LEAF : 3 * LEAF]
        if b == 0:
            before = before + left
        if b == LEAVES - 1:
            after = after + right
        scores = jnp.concatenate(
            [before, raw[LEAF : 2 * LEAF], after, raw[3 * LEAF :] + bias], axis=0
        )
        weights = jnp.exp(scores - jnp.max(scores, axis=0, keepdims=True))
        probs = weights * (1.0 / jnp.sum(weights, axis=0, keepdims=True))
        low = probs.astype(BF16)
        prob_grad = dot(values, g2, (1, 1))
        delta = jnp.sum(probs * prob_grad, axis=0, keepdims=True)
        score_grad = (probs * (prob_grad - delta)).astype(BF16)
        att_ref[rows] = merge_heads(dot(values, low, (0, 0))).astype(BF16)
        nqg_ref[rows] = merge_heads(dot(keys, score_grad, (0, 0))) * 0.125
        key_part = dot(score_grad, q2, (1, 0))
        value_part = dot(low, g2, (1, 0))
        for part, lanes in ((key_part, slice(0, FEAT)), (value_part, slice(FEAT, 2 * FEAT))):
            near_grad[near_rows, lanes] += part[: 3 * LEAF]
            one_grad[half : half + LEAF, lanes] += part[3 * LEAF : 4 * LEAF]
            if b == 0:
                cross_grad[:, lanes] = part[4 * LEAF :]
            else:
                cross_grad[:, lanes] += part[4 * LEAF :]

    spread = spreading(0, 256, 1).astype(BF16)
    high = one_grad[...].astype(BF16)
    rest = (one_grad[...] - high.astype(F32)).astype(BF16)
    tok_ref[...] = near_grad[LEAF : LEAF + ROWS] + dot(spread, high, (1, 0)) + dot(spread, rest, (1, 0))
    p1o_ref[:LEAF] = near_grad[pl.ds(peer_side, LEAF)].astype(BF16)
    p1o_ref[LEAF:] = cross_grad[64:128].astype(BF16)
    p2o_ref[...] = near_grad[pl.ds(other_side, LEAF)].astype(BF16)
    for d in range(8):
        rows = slice(384 + FAR * d, 384 + FAR * (d + 1))
        zo_ref[jnp.bitwise_xor(place, d), :FAR] = cross_grad[rows].astype(BF16)
    zo_ref[place, FAR:] = jnp.zeros((64, 2 * FEAT), BF16)
    zo_ref[jnp.bitwise_xor(place, 1), FAR:] = cross_grad[:64].astype(BF16)
    zo_ref[jnp.bitwise_xor(place, 2), FAR:] = cross_grad[128:192].astype(BF16)
    zo_ref[jnp.bitwise_xor(place, 3), FAR:] = cross_grad[192:256].astype(BF16)
    for i in range(4):
        other = jnp.bitwise_xor(place, 4 + i)
        zo_ref[other, FAR : FAR + 32] = cross_grad[256 + 32 * i : 288 + 32 * i].astype(BF16)
        zo_ref[other, FAR + 32 :] = jnp.zeros((32, 2 * FEAT), BF16)


def column_kernel(z_ref, out_ref):
    column = jnp.right_shift(lax.axis_index("seq"), 3)
    far = jnp.sum(z_ref[:, :FAR].astype(F32), axis=0).astype(BF16)
    slots = dot(far_pick((112, FAR), 1), far, (1, 0)).astype(BF16)
    out_ref[column] = jnp.zeros((16, 2 * FEAT), BF16)
    for d in range(1, 8):
        out_ref[jnp.bitwise_xor(column, d)] = slots[16 * (d - 1) : 16 * d]


def total_kernel(
    tok_ref, p1_ref, p2_ref, z_ref, y_ref,
    q_ref, k_ref, qg_ref, kg_ref, nqg_ref, nkg_ref, vg_ref, sum_ref, acc,
):
    index = lax.axis_index("seq")
    column = jnp.right_shift(index, 3)
    place = jnp.bitwise_and(index, 7)
    odd = jnp.bitwise_and(index, 1)
    pieces = [z_ref[jnp.bitwise_xor(place, 1), FAR:], p1_ref[LEAF:]]
    maps = [spreading(0, 64, 2), spreading(64, 64, 2)]
    for d in range(2, 8):
        rows = ROWS >> ROW_LEVEL[d]
        pieces.append(z_ref[jnp.bitwise_xor(place, d), FAR : FAR + rows])
        maps.append(spreading(0, rows, ROW_LEVEL[d]))
    for d in range(1, 8):
        pieces.append(y_ref[jnp.bitwise_xor(column, d)])
        maps.append(spreading(0, 16, COLUMN_LEVEL[d]))
    spread = jnp.concatenate(maps, axis=1).astype(BF16)
    acc[...] = tok_ref[...] + dot(spread, jnp.concatenate(pieces, axis=0), (1, 0))
    acc[pl.ds(pl.multiple_of((1 - odd) * 384, LEAF), LEAF)] += p1_ref[:LEAF].astype(F32)
    acc[pl.ds(pl.multiple_of(odd * 384, LEAF), LEAF)] += p2_ref[...].astype(F32)
    vg_ref[...] = acc[:, FEAT:].astype(BF16)
    key_total = acc[:, :FEAT]
    nkg_ref[...] = key_total
    tile = jnp.concatenate(
        token_sums(q_ref[...].astype(F32) * qg_ref[...] * nqg_ref[...])
        + token_sums(k_ref[...].astype(F32) * kg_ref[...] * key_total),
        axis=0,
    )
    for i in range(sum_ref.shape[0]):
        sum_ref[i] = tile


def finish_kernel(width, sq_ref, inner_ref, q_ref, k_ref, qg_ref, kg_ref, nqg_ref, nkg_ref, dq_ref, dk_ref):
    rate = lax.rsqrt(jnp.sum(sq_ref[...], axis=0) / width + EPS)
    inner = jnp.sum(inner_ref[...], axis=0) / width
    cubed = rate * rate * rate * inner
    for first, x_ref, gain_ref, grad_ref, out_ref in (
        (0, q_ref, qg_ref, nqg_ref, dq_ref),
        (4, k_ref, kg_ref, nkg_ref, dk_ref),
    ):
        out_ref[...] = (
            spread_tokens(rate, first) * gain_ref[...] * grad_ref[...]
            - x_ref[...].astype(F32) * spread_tokens(cubed, first)
        ).astype(BF16)


def call(kernel, outs, args, scratch=(), flops=0, name=None):
    many = isinstance(outs, list)
    moved = sum(math.prod(x.shape) * x.dtype.itemsize for x in list(args) + (outs if many else [outs]))
    return pl.pallas_call(
        kernel,
        out_shape=outs,
        scratch_shapes=list(scratch),
        compiler_params=PARAMS,
        cost_estimate=pl.CostEstimate(flops=flops, bytes_accessed=moved, transcendentals=0),
        name=name,
    )(*args)


def sds(*shape, dtype=BF16):
    return jax.ShapeDtypeStruct(shape, dtype)


ROW_GROUPS = [[8 * y + z for z in range(8)] for y in range(8)]
COLUMN_GROUPS = [[8 * y + z for y in range(8)] for z in range(8)]


def exchange(x, axis, groups=None):
    return lax.all_to_all(x, axis, 0, 0, axis_index_groups=groups, tiled=True)


def local(queries, key_rows, value_rows, query_gain, key_gain, out_grad):
    seq = lax.axis_size("seq")
    heads = lax.axis_size("head")
    width = float(heads * FEAT)
    qg = query_gain.reshape(1, FEAT)
    kg = key_gain.reshape(1, FEAT)
    peer = [(i, i ^ 1) for i in range(seq)]
    beside = [(i, i + 1) for i in range(1, seq - 1, 2)] + [(i + 1, i) for i in range(1, seq - 1, 2)]

    squares = call(squares_kernel, sds(heads, 8, FEAT, dtype=F32), (queries, key_rows), name="squares")
    squares = exchange(squares, "head")
    qn, kv, one, lv, ysend, p1, p2 = call(
        lambda *refs: norm_kernel(width, *refs),
        [sds(ROWS, FEAT), sds(ROWS, 256), sds(256, 256), sds(8, 64, 256), sds(seq, 16, 256), sds(192, 256), sds(LEAF, 256)],
        (squares, queries, key_rows, value_rows, qg, kg),
        name="norm",
    )
    p1 = lax.ppermute(p1, "seq", peer)
    p2 = lax.ppermute(p2, "seq", beside)
    yrecv = exchange(ysend, "seq")
    zrecv = exchange(lv, "seq", ROW_GROUPS)
    far = call(far_kernel, sds(8, FAR, 256), (yrecv,), name="far")
    attended, nqg, tok, p1, p2, zsend = call(
        attend_kernel,
        [sds(ROWS, FEAT), sds(ROWS, FEAT, dtype=F32), sds(ROWS, 256, dtype=F32), sds(192, 256), sds(LEAF, 256), sds(8, SLOT, 256)],
        (qn, kv, one, out_grad, p1, p2, zrecv, far),
        scratch=[
            pltpu.VMEM((768, 256), BF16),
            pltpu.VMEM((768, 256), BF16),
            pltpu.VMEM((768, 256), F32),
            pltpu.VMEM((256, 256), F32),
            pltpu.VMEM((768, 256), F32),
        ],
        flops=4 * 6 * 2 * 256 * KEYS * FEAT,
        name="attend",
    )
    p1 = lax.ppermute(p1, "seq", peer)
    p2 = lax.ppermute(p2, "seq", beside)
    zrecv = exchange(zsend, "seq", ROW_GROUPS)
    ysend = call(column_kernel, sds(8, 16, 256), (zrecv,), name="columns")
    yrecv = exchange(ysend, "seq", COLUMN_GROUPS)
    nkg, value_grad, inner = call(
        total_kernel,
        [sds(ROWS, FEAT, dtype=F32), sds(ROWS, FEAT), sds(heads, 8, FEAT, dtype=F32)],
        (tok, p1, p2, zrecv, yrecv, queries, key_rows, qg, kg, nqg),
        scratch=[pltpu.VMEM((ROWS, 256), F32)],
        name="total",
    )
    inner = exchange(inner, "head")
    query_grad, key_grad = call(
        lambda *refs: finish_kernel(width, *refs),
        [sds(ROWS, FEAT), sds(ROWS, FEAT)],
        (squares, inner, queries, key_rows, qg, kg, nqg, nkg),
        name="finish",
    )
    return (attended, query_grad, key_grad, value_grad)


def solution(mesh):
    placed = (
        P("seq", "head"),
        P("seq", "head"),
        P("seq", "head"),
        P("head"),
        P("head"),
        P("seq", "head"),
    )
    return jax.shard_map(
        local,
        mesh=mesh,
        in_specs=placed,
        out_specs=(P("seq", "head"), P("seq", "head"), P("seq", "head"), P("seq", "head")),
        check_vma=False,
    )
```

```python
import math

import jax
import jax.numpy as jnp
from jax import lax
from jax.experimental import pallas as pl
from jax.experimental.pallas import tpu as pltpu
from jax.sharding import PartitionSpec as P

ROWS = 512
FEAT = 128
LEAF = 128
LEAVES = 4
HEAD = 64
KEYS = 1280
EPS = 1e-06
LN2 = math.log(2.0)
F32 = jnp.float32
BF16 = jnp.bfloat16
MIB = 1024 * 1024
ROW_LEVEL = {1: 2, 2: 3, 3: 3, 4: 4, 5: 4, 6: 4, 7: 4}
COLUMN_LEVEL = {1: 5, 2: 6, 3: 6, 4: 7, 5: 7, 6: 7, 7: 7}
FAR = 48
SLOT = 112


def dot(a, b, dims):
    return lax.dot_general(a, b, ((dims[:1], dims[1:]), ((), ())), preferred_element_type=F32)


def iota(shape, axis):
    return lax.broadcasted_iota(jnp.int32, shape, axis)


def pooling(rows, level):
    token = iota((rows, ROWS), 1)
    hit = jnp.right_shift(token, level) == iota((rows, ROWS), 0)
    return jnp.where(hit, 2.0**-level, 0.0)


def spreading(first, rows, level):
    token = iota((ROWS, rows), 0)
    hit = jnp.right_shift(token, level) == iota((ROWS, rows), 1) + first
    return jnp.where(hit, 2.0**-level, 0.0)


def far_pick(shape, far_axis):
    far = iota(shape, far_axis)
    slot_row = iota(shape, 1 - far_axis)
    mid = far - 16
    low = far - 32
    column = jnp.where(
        far < 16,
        far,
        jnp.where(
            far < 32,
            (1 + jnp.right_shift(mid, 3)) * 16 + jnp.bitwise_and(mid, 7),
            (3 + jnp.right_shift(low, 2)) * 16 + jnp.bitwise_and(low, 3),
        ),
    )
    return jnp.where(column == slot_row, 1.0, 0.0).astype(BF16)


def token_sums(x):
    return [
        jnp.sum(x[i * LEAF : (i + 1) * LEAF].T, axis=0, keepdims=True) for i in range(LEAVES)
    ]


def spread_tokens(tile, first):
    return jnp.concatenate(
        [
            jnp.broadcast_to(tile[first + i : first + i + 1], (LEAF, LEAF)).T
            for i in range(LEAVES)
        ],
        axis=0,
    )


def squares_kernel(q_ref, k_ref, out_ref):
    q = q_ref[...].astype(F32)
    k = k_ref[...].astype(F32)
    tile = jnp.concatenate(token_sums(q * q) + token_sums(k * k), axis=0)
    for i in range(out_ref.shape[0]):
        out_ref[i] = tile


def norm_kernel(width, sum_ref, q_ref, k_ref, v_ref, qg_ref, kg_ref, qn_ref, kv_ref, one_ref, lv_ref, y_ref, p1_ref, p2_ref):
    index = lax.axis_index("seq")
    column = jnp.right_shift(index, 3)
    odd = jnp.bitwise_and(index, 1)
    total = jnp.sum(sum_ref[...], axis=0)
    rate = lax.rsqrt(total / width + EPS)
    qn_ref[...] = (
        q_ref[...].astype(F32) * spread_tokens(rate, 0) * qg_ref[...]
    ).astype(BF16)
    kv_ref[:, :FEAT] = (
        k_ref[...].astype(F32) * spread_tokens(rate, 4) * kg_ref[...]
    ).astype(BF16)
    kv_ref[:, FEAT:] = v_ref[...]
    pool = jnp.concatenate(
        [pooling(ROWS >> level, level) for level in (1, 2, 3, 4)]
        + [pooling(16, COLUMN_LEVEL[d]) for d in range(1, 8)],
        axis=0,
    ).astype(BF16)
    coarse = dot(pool, kv_ref[...], (1, 0)).astype(BF16)
    one_ref[...] = coarse[:256]
    lv_ref[...] = coarse[256:480]
    y_ref[column] = jnp.zeros((16, 2 * FEAT), BF16)
    for d in range(1, 8):
        y_ref[jnp.bitwise_xor(column, d)] = coarse[464 + 16 * d : 480 + 16 * d]
    p1_ref[:LEAF] = kv_ref[pl.ds(pl.multiple_of((1 - odd) * 384, LEAF), LEAF)]
    p1_ref[LEAF:] = coarse[320:384]
    p2_ref[...] = kv_ref[pl.ds(pl.multiple_of(odd * 384, LEAF), LEAF)]


def row_kernel(y_ref, lv_ref, out_ref):
    index = lax.axis_index("seq")
    column = jnp.right_shift(index, 3)
    place = jnp.bitwise_and(index, 7)
    slots = jnp.concatenate([y_ref[jnp.bitwise_xor(column, d)] for d in range(1, 8)], axis=0)
    far = dot(far_pick((FAR, 112), 0), slots, (1, 0)).astype(BF16)
    for s in range(8):
        out_ref[s, :FAR] = far
    out_ref[place, FAR:] = jnp.zeros((64, 2 * FEAT), BF16)
    for d in range(1, 8):
        other = jnp.bitwise_xor(place, d)
        if d == 1:
            out_ref[other, FAR:] = lv_ref[:64]
        elif d < 4:
            out_ref[other, FAR:] = lv_ref[128:192]
        else:
            out_ref[other, FAR : FAR + 32] = lv_ref[192:224]
            out_ref[other, FAR + 32 :] = jnp.zeros((32, 2 * FEAT), BF16)


def by_head(block):
    lane = iota((LEAF, FEAT), 1)
    zero = jnp.zeros((LEAF, FEAT), BF16)
    return jnp.concatenate(
        [jnp.where(lane < HEAD, block, zero), jnp.where(lane < HEAD, zero, block)], axis=0
    )


def peak(x):
    return jnp.max(x, axis=0, keepdims=True)


def add_up(x):
    return jnp.sum(x, axis=0, keepdims=True)


HALO_PIECE = {0: 0, LEAVES - 1: 2}


def near_kernel(qn_ref, kv_ref, one_ref, g_ref, q2_ref, g2_ref, weight_ref, pgrad_ref, stat_ref):
    for b in range(LEAVES):
        rows = slice(b * LEAF, (b + 1) * LEAF)
        q2 = by_head(qn_ref[rows]) * jnp.asarray(0.125, BF16)
        g2 = by_head(g_ref[rows])
        q2_ref[b] = q2
        g2_ref[b] = g2
        half = (1 - b // 2) * LEAF
        kv = [
            None if HALO_PIECE.get(b) == i else kv_ref[(b + i - 1) * LEAF : (b + i) * LEAF]
            for i in range(3)
        ] + [one_ref[half : half + LEAF]]
        scores = {
            i: dot(x[:, :FEAT], q2, (1, 1)) + (LN2 if i == 3 else 0.0)
            for i, x in enumerate(kv)
            if x is not None
        }
        top = peak(jnp.concatenate([peak(x) for x in scores.values()], axis=0))
        total = jnp.zeros((1, 2 * LEAF), F32)
        mixed = jnp.zeros((1, 2 * LEAF), F32)
        for i, score in scores.items():
            weight = jnp.exp(score - top)
            pgrad = dot(kv[i][:, FEAT:], g2, (1, 1))
            weight_ref[b, i * LEAF : (i + 1) * LEAF] = weight
            pgrad_ref[b, i * LEAF : (i + 1) * LEAF] = pgrad
            total = total + add_up(weight)
            mixed = mixed + add_up(weight * pgrad)
        stat_ref[b] = jnp.concatenate([top, total, mixed, jnp.zeros((5, 2 * LEAF), F32)], axis=0)


def attend_kernel(
    q2_ref, g2_ref, weight_ref, pgrad_ref, stat_ref, p1_ref, p2_ref, z_ref,
    low_ref, sgrad_ref, cross, halo, p1o_ref, p2o_ref, zo_ref,
    score_scr, pgrad_scr, cross_grad, rims,
):
    index = lax.axis_index("seq")
    last = lax.axis_size("seq") - 1
    place = jnp.bitwise_and(index, 7)
    odd = jnp.bitwise_and(index, 1)
    peer_side = 1 - odd
    halo[peer_side] = p1_ref[:LEAF]
    halo[odd] = p2_ref[...]
    cross[:64] = z_ref[jnp.bitwise_xor(place, 1), FAR:]
    cross[64:128] = p1_ref[LEAF:]
    cross[128:192] = z_ref[jnp.bitwise_xor(place, 2), FAR:]
    cross[192:256] = z_ref[jnp.bitwise_xor(place, 3), FAR:]
    for i in range(4):
        cross[256 + 32 * i : 288 + 32 * i] = z_ref[jnp.bitwise_xor(place, 4 + i), FAR : FAR + 32]
    for s in range(8):
        cross[384 + FAR * s : 384 + FAR * (s + 1)] = z_ref[s, :FAR]

    def level_bias(rows, level):
        return jnp.full((rows, 2 * LEAF), level * LN2, F32)

    bias = jnp.concatenate(
        [level_bias(LEAF, level) for level in (2, 3, 4)]
        + [level_bias(16, level) for _ in range(8) for level in (5, 6, 7)],
        axis=0,
    )
    outside = {
        0: jnp.where(index > 0, 0.0, -jnp.inf).astype(F32),
        LEAVES - 1: jnp.where(index < last, 0.0, -jnp.inf).astype(F32),
    }
    for b in range(LEAVES):
        q2 = q2_ref[b]
        g2 = g2_ref[b]
        near_top = stat_ref[b, 0:1]
        top = near_top
        pieces = []
        if b in HALO_PIECE:
            side = halo[0 if b == 0 else 1]
            score = dot(side[:, :FEAT], q2, (1, 1)) + outside[b]
            top = jnp.maximum(top, peak(score))
            score_scr[6 * LEAF :] = score
            pgrad_scr[6 * LEAF :] = dot(side[:, FEAT:], g2, (1, 1))
            pieces.append((6 * LEAF, HALO_PIECE[b] * LEAF))
        for i in range(6):
            rows = slice(i * LEAF, (i + 1) * LEAF)
            score = dot(cross[rows, :FEAT], q2, (1, 1)) + bias[rows]
            top = jnp.maximum(top, peak(score))
            score_scr[rows] = score
            pgrad_scr[rows] = dot(cross[rows, FEAT:], g2, (1, 1))
            pieces.append((i * LEAF, (4 + i) * LEAF))
        shrink = jnp.exp(near_top - top)
        total = stat_ref[b, 1:2] * shrink
        mixed = stat_ref[b, 2:3] * shrink
        for at, _ in pieces:
            weight = jnp.exp(score_scr[at : at + LEAF] - top)
            score_scr[at : at + LEAF] = weight
            total = total + add_up(weight)
            mixed = mixed + add_up(weight * pgrad_scr[at : at + LEAF])
        inverse = 1.0 / total
        delta = mixed * inverse
        near_scale = shrink * inverse
        for at, to in pieces:
            prob = score_scr[at : at + LEAF] * inverse
            low_ref[b, to : to + LEAF] = prob.astype(BF16)
            sgrad_ref[b, to : to + LEAF] = (prob * (pgrad_scr[at : at + LEAF] - delta)).astype(BF16)
        for i in range(4):
            if HALO_PIECE.get(b) == i:
                continue
            rows = slice(i * LEAF, (i + 1) * LEAF)
            prob = weight_ref[b, rows] * near_scale
            low_ref[b, rows] = prob.astype(BF16)
            sgrad_ref[b, rows] = (prob * (pgrad_ref[b, rows] - delta)).astype(BF16)
        for source, other, lanes in (
            (sgrad_ref, q2, slice(0, FEAT)),
            (low_ref, g2, slice(FEAT, 2 * FEAT)),
        ):
            part = dot(source[b, 4 * LEAF :], other, (1, 0))
            if b == 0:
                cross_grad[:, lanes] = part
            else:
                cross_grad[:, lanes] += part
            if b in HALO_PIECE:
                at = HALO_PIECE[b] * LEAF
                rims[0 if b == 0 else 1, :, lanes] = dot(
                    source[b, at : at + LEAF], other, (1, 0)
                ).astype(BF16)

    p1o_ref[:LEAF] = rims[peer_side]
    p1o_ref[LEAF:] = cross_grad[64:128].astype(BF16)
    p2o_ref[...] = rims[odd]
    for s in range(8):
        zo_ref[s, :FAR] = cross_grad[384 + FAR * s : 384 + FAR * (s + 1)].astype(BF16)
    zo_ref[place, FAR:] = jnp.zeros((64, 2 * FEAT), BF16)
    zo_ref[jnp.bitwise_xor(place, 1), FAR:] = cross_grad[:64].astype(BF16)
    zo_ref[jnp.bitwise_xor(place, 2), FAR:] = cross_grad[128:192].astype(BF16)
    zo_ref[jnp.bitwise_xor(place, 3), FAR:] = cross_grad[192:256].astype(BF16)
    for i in range(4):
        other = jnp.bitwise_xor(place, 4 + i)
        zo_ref[other, FAR : FAR + 32] = cross_grad[256 + 32 * i : 288 + 32 * i].astype(BF16)
        zo_ref[other, FAR + 32 :] = jnp.zeros((32, 2 * FEAT), BF16)


def after_kernel(
    low_ref, sgrad_ref, q2_ref, g2_ref, kv_ref, one_ref, halo, cross,
    att_ref, nqg_ref, tok_ref, near, near_grad, one_grad,
):
    near[:LEAF] = halo[0]
    near[LEAF : LEAF + ROWS] = kv_ref[...]
    near[LEAF + ROWS :] = halo[1]
    near_grad[...] = jnp.zeros_like(near_grad)
    one_grad[...] = jnp.zeros_like(one_grad)
    feature = iota((FEAT, LEAF), 0)

    def merge_heads(transposed):
        return jnp.where(feature < HEAD, transposed[:, :LEAF], transposed[:, LEAF:]).T

    for b in range(LEAVES):
        rows = slice(b * LEAF, (b + 1) * LEAF)
        near_rows = slice(b * LEAF, (b + 3) * LEAF)
        half = (1 - b // 2) * LEAF
        low = low_ref[b]
        score_grad = sgrad_ref[b]
        kv = jnp.concatenate([near[near_rows], one_ref[half : half + LEAF], cross[...]], axis=0)
        att_ref[rows] = merge_heads(dot(kv[:, FEAT:], low, (0, 0))).astype(BF16)
        nqg_ref[rows] = merge_heads(dot(kv[:, :FEAT], score_grad, (0, 0))) * 0.125
        for part, lanes in (
            (dot(score_grad[: 4 * LEAF], q2_ref[b], (1, 0)), slice(0, FEAT)),
            (dot(low[: 4 * LEAF], g2_ref[b], (1, 0)), slice(FEAT, 2 * FEAT)),
        ):
            near_grad[near_rows, lanes] += part[: 3 * LEAF]
            one_grad[half : half + LEAF, lanes] += part[3 * LEAF :]
    spread = spreading(0, 256, 1).astype(BF16)
    high = one_grad[...].astype(BF16)
    rest = (one_grad[...] - high.astype(F32)).astype(BF16)
    tok_ref[...] = near_grad[LEAF : LEAF + ROWS] + dot(spread, high, (1, 0)) + dot(spread, rest, (1, 0))


def column_kernel(z_ref, p1_ref, p2_ref, tok_ref, out_ref):
    column = jnp.right_shift(lax.axis_index("seq"), 3)
    far = jnp.sum(z_ref[:, :FAR].astype(F32), axis=0).astype(BF16)
    slots = dot(far_pick((112, FAR), 1), far, (1, 0)).astype(BF16)
    out_ref[column] = jnp.zeros((16, 2 * FEAT), BF16)
    for d in range(1, 8):
        out_ref[jnp.bitwise_xor(column, d)] = slots[16 * (d - 1) : 16 * d]


def total_kernel(
    tok_ref, p1_ref, p2_ref, z_ref, y_ref,
    q_ref, k_ref, qg_ref, kg_ref, nqg_ref, nkg_ref, vg_ref, sum_ref, acc,
):
    index = lax.axis_index("seq")
    column = jnp.right_shift(index, 3)
    place = jnp.bitwise_and(index, 7)
    odd = jnp.bitwise_and(index, 1)
    pieces = [z_ref[jnp.bitwise_xor(place, 1), FAR:], p1_ref[LEAF:]]
    maps = [spreading(0, 64, 2), spreading(64, 64, 2)]
    for d in range(2, 8):
        rows = ROWS >> ROW_LEVEL[d]
        pieces.append(z_ref[jnp.bitwise_xor(place, d), FAR : FAR + rows])
        maps.append(spreading(0, rows, ROW_LEVEL[d]))
    for d in range(1, 8):
        pieces.append(y_ref[jnp.bitwise_xor(column, d)])
        maps.append(spreading(0, 16, COLUMN_LEVEL[d]))
    spread = jnp.concatenate(maps, axis=1).astype(BF16)
    acc[...] = tok_ref[...] + dot(spread, jnp.concatenate(pieces, axis=0), (1, 0))
    acc[pl.ds(pl.multiple_of((1 - odd) * 384, LEAF), LEAF)] += p1_ref[:LEAF].astype(F32)
    acc[pl.ds(pl.multiple_of(odd * 384, LEAF), LEAF)] += p2_ref[...].astype(F32)
    vg_ref[...] = acc[:, FEAT:].astype(BF16)
    key_total = acc[:, :FEAT]
    nkg_ref[...] = key_total
    tile = jnp.concatenate(
        token_sums(q_ref[...].astype(F32) * qg_ref[...] * nqg_ref[...])
        + token_sums(k_ref[...].astype(F32) * kg_ref[...] * key_total),
        axis=0,
    )
    for i in range(sum_ref.shape[0]):
        sum_ref[i] = tile


def finish_kernel(width, sq_ref, inner_ref, q_ref, k_ref, qg_ref, kg_ref, nqg_ref, nkg_ref, dq_ref, dk_ref):
    rate = lax.rsqrt(jnp.sum(sq_ref[...], axis=0) / width + EPS)
    inner = jnp.sum(inner_ref[...], axis=0) / width
    cubed = rate * rate * rate * inner
    for first, x_ref, gain_ref, grad_ref, out_ref in (
        (0, q_ref, qg_ref, nqg_ref, dq_ref),
        (4, k_ref, kg_ref, nkg_ref, dk_ref),
    ):
        out_ref[...] = (
            spread_tokens(rate, first) * gain_ref[...] * grad_ref[...]
            - x_ref[...].astype(F32) * spread_tokens(cubed, first)
        ).astype(BF16)


def call(kernel, outs, args, scratch=(), flops=0, name=None, spaces=None, vmem=24 * MIB):
    many = isinstance(outs, list)
    moved = sum(math.prod(x.shape) * x.dtype.itemsize for x in list(args) + (outs if many else [outs]))
    return pl.pallas_call(
        kernel,
        out_shape=outs,
        in_specs=[pl.BlockSpec(memory_space=space) for space in spaces or [pltpu.VMEM] * len(args)],
        scratch_shapes=list(scratch),
        compiler_params=pltpu.CompilerParams(vmem_limit_bytes=int(vmem)),
        cost_estimate=pl.CostEstimate(flops=flops, bytes_accessed=moved, transcendentals=0),
        name=name,
    )(*args)


def sds(*shape, dtype=BF16):
    return jax.ShapeDtypeStruct(shape, dtype)


ROW_GROUPS = [[8 * y + z for z in range(8)] for y in range(8)]
COLUMN_GROUPS = [[8 * y + z for y in range(8)] for z in range(8)]


def exchange(x, axis, groups=None):
    return lax.all_to_all(x, axis, 0, 0, axis_index_groups=groups, tiled=True)


def local(queries, key_rows, value_rows, query_gain, key_gain, out_grad):
    seq = lax.axis_size("seq")
    heads = lax.axis_size("head")
    width = float(heads * FEAT)
    qg = query_gain.reshape(1, FEAT)
    kg = key_gain.reshape(1, FEAT)
    peer = [(i, i ^ 1) for i in range(seq)]
    beside = [(i, i + 1) for i in range(1, seq - 1, 2)] + [(i + 1, i) for i in range(1, seq - 1, 2)]

    squares = call(squares_kernel, sds(heads, 8, FEAT, dtype=F32), (queries, key_rows), name="squares")
    squares = exchange(squares, "head")
    qn, kv, one, lv, ysend, p1, p2 = call(
        lambda *refs: norm_kernel(width, *refs),
        [sds(ROWS, FEAT), sds(ROWS, 256), sds(256, 256), sds(224, 256), sds(8, 16, 256), sds(192, 256), sds(LEAF, 256)],
        (squares, queries, key_rows, value_rows, qg, kg),
        name="norm",
    )
    p1 = lax.ppermute(p1, "seq", peer)
    p2 = lax.ppermute(p2, "seq", beside)
    yrecv = exchange(ysend, "seq", COLUMN_GROUPS)
    zsend = call(row_kernel, sds(8, SLOT, 256), (yrecv, lv), name="rows")
    zrecv = exchange(zsend, "seq", ROW_GROUPS)
    q2, g2, weight, pgrad, stat = call(
        near_kernel,
        [sds(LEAVES, 256, FEAT), sds(LEAVES, 256, FEAT)]
        + [sds(LEAVES, 512, 256, dtype=F32), sds(LEAVES, 512, 256, dtype=F32), sds(LEAVES, 8, 256, dtype=F32)],
        (qn, kv, one, out_grad),
        flops=4 * 2 * 2 * 256 * 512 * FEAT,
        name="near",
    )
    low, sgrad, cross, halo, p1, p2, zsend = call(
        attend_kernel,
        [sds(LEAVES, KEYS, 256), sds(LEAVES, KEYS, 256), sds(768, 256), sds(2, LEAF, 256)]
        + [sds(192, 256), sds(LEAF, 256), sds(8, SLOT, 256)],
        (q2, g2, weight, pgrad, stat, p1, p2, zrecv),
        scratch=[
            pltpu.VMEM((896, 256), F32),
            pltpu.VMEM((896, 256), F32),
            pltpu.VMEM((768, 256), F32),
            pltpu.VMEM((2, LEAF, 256), BF16),
        ],
        flops=4 * 4 * 2 * 256 * 768 * FEAT,
        name="attend",
    )
    p1 = lax.ppermute(p1, "seq", peer)
    p2 = lax.ppermute(p2, "seq", beside)
    zrecv = exchange(zsend, "seq", ROW_GROUPS)
    attended, nqg, tok = call(
        after_kernel,
        [sds(ROWS, FEAT), sds(ROWS, FEAT, dtype=F32), sds(ROWS, 256, dtype=F32)],
        (low, sgrad, q2, g2, kv, one, halo, cross),
        scratch=[
            pltpu.VMEM((768, 256), BF16),
            pltpu.VMEM((768, 256), F32),
            pltpu.VMEM((256, 256), F32),
        ],
        flops=4 * 2 * 2 * 256 * (KEYS + 512) * FEAT,
        name="after",
    )
    ysend = call(
        column_kernel,
        sds(8, 16, 256),
        (zrecv, p1, p2, tok),
        spaces=[pltpu.VMEM, pl.ANY, pl.ANY, pl.ANY],
        name="columns",
    )
    yrecv = exchange(ysend, "seq", COLUMN_GROUPS)
    nkg, value_grad, inner = call(
        total_kernel,
        [sds(ROWS, FEAT, dtype=F32), sds(ROWS, FEAT), sds(heads, 8, FEAT, dtype=F32)],
        (tok, p1, p2, zrecv, yrecv, queries, key_rows, qg, kg, nqg),
        scratch=[pltpu.VMEM((ROWS, 256), F32)],
        name="total",
    )
    inner = exchange(inner, "head")
    query_grad, key_grad = call(
        lambda *refs: finish_kernel(width, *refs),
        [sds(ROWS, FEAT), sds(ROWS, FEAT)],
        (squares, inner, queries, key_rows, qg, kg, nqg, nkg),
        name="finish",
    )
    return (attended, query_grad, key_grad, value_grad)


def solution(mesh):
    placed = (
        P("seq", "head"),
        P("seq", "head"),
        P("seq", "head"),
        P("head"),
        P("head"),
        P("seq", "head"),
    )
    return jax.shard_map(
        local,
        mesh=mesh,
        in_specs=placed,
        out_specs=(P("seq", "head"), P("seq", "head"), P("seq", "head"), P("seq", "head")),
        check_vma=False,
    )
```

```python
import math

import jax
import jax.numpy as jnp
from jax import lax
from jax.experimental import pallas as pl
from jax.experimental.pallas import tpu as pltpu
from jax.sharding import PartitionSpec as P

ROWS = 512
FEAT = 128
LEAF = 128
LEAVES = 4
HEAD = 64
KEYS = 1280
EPS = 1e-06
LN2 = math.log(2.0)
F32 = jnp.float32
BF16 = jnp.bfloat16
PARAMS = pltpu.CompilerParams(vmem_limit_bytes=40 * 1024 * 1024)
COLUMN_LEVEL = {1: 5, 2: 6, 3: 6, 4: 7, 5: 7, 6: 7, 7: 7}
FAR = 48
MID = 96


def dot(a, b, dims):
    return lax.dot_general(a, b, ((dims[:1], dims[1:]), ((), ())), preferred_element_type=F32)


def iota(shape, axis):
    return lax.broadcasted_iota(jnp.int32, shape, axis)


def pooling(rows, level):
    token = iota((rows, ROWS), 1)
    hit = jnp.right_shift(token, level) == iota((rows, ROWS), 0)
    return jnp.where(hit, 2.0**-level, 0.0)


def spreading(first, rows, level):
    token = iota((ROWS, rows), 0)
    hit = jnp.right_shift(token, level) == iota((ROWS, rows), 1) + first
    return jnp.where(hit, 2.0**-level, 0.0)


def far_pick(shape, far_axis):
    far = iota(shape, far_axis)
    slot_row = iota(shape, 1 - far_axis)
    mid = far - 16
    low = far - 32
    column = jnp.where(
        far < 16,
        far,
        jnp.where(
            far < 32,
            (1 + jnp.right_shift(mid, 3)) * 16 + jnp.bitwise_and(mid, 7),
            (3 + jnp.right_shift(low, 2)) * 16 + jnp.bitwise_and(low, 3),
        ),
    )
    return jnp.where(column == slot_row, 1.0, 0.0).astype(BF16)


def token_sums(x):
    return [
        jnp.sum(x[i * LEAF : (i + 1) * LEAF].T, axis=0, keepdims=True) for i in range(LEAVES)
    ]


def spread_tokens(tile, first):
    return jnp.concatenate(
        [
            jnp.broadcast_to(tile[first + i : first + i + 1], (LEAF, LEAF)).T
            for i in range(LEAVES)
        ],
        axis=0,
    )


def squares_kernel(q_ref, k_ref, out_ref):
    q = q_ref[...].astype(F32)
    k = k_ref[...].astype(F32)
    tile = jnp.concatenate(token_sums(q * q) + token_sums(k * k), axis=0)
    for i in range(out_ref.shape[0]):
        out_ref[i] = tile


def norm_kernel(width, sum_ref, q_ref, k_ref, v_ref, qg_ref, kg_ref, qn_ref, kv_ref, one_ref, lv_ref, y_ref, p1_ref, p2_ref):
    index = lax.axis_index("seq")
    column = jnp.right_shift(index, 3)
    odd = jnp.bitwise_and(index, 1)
    total = jnp.sum(sum_ref[...], axis=0)
    rate = lax.rsqrt(total / width + EPS)
    qn_ref[...] = (
        q_ref[...].astype(F32) * spread_tokens(rate, 0) * qg_ref[...]
    ).astype(BF16)
    kv_ref[:, :FEAT] = (
        k_ref[...].astype(F32) * spread_tokens(rate, 4) * kg_ref[...]
    ).astype(BF16)
    kv_ref[:, FEAT:] = v_ref[...]
    pool = jnp.concatenate(
        [pooling(ROWS >> level, level) for level in (1, 2, 3, 4)]
        + [pooling(16, COLUMN_LEVEL[d]) for d in range(1, 8)],
        axis=0,
    ).astype(BF16)
    coarse = dot(pool, kv_ref[...], (1, 0)).astype(BF16)
    one_ref[...] = coarse[:256]
    lv_ref[...] = coarse[384:480]
    y_ref[column] = jnp.zeros((16, 2 * FEAT), BF16)
    for d in range(1, 8):
        y_ref[jnp.bitwise_xor(column, d)] = coarse[464 + 16 * d : 480 + 16 * d]
    p1_ref[:LEAF] = kv_ref[pl.ds(pl.multiple_of((1 - odd) * 384, LEAF), LEAF)]
    p1_ref[LEAF:] = coarse[256:384]
    p2_ref[...] = kv_ref[pl.ds(pl.multiple_of(odd * 384, LEAF), LEAF)]


def row_kernel(y_ref, out_ref):
    column = jnp.right_shift(lax.axis_index("seq"), 3)
    slots = jnp.concatenate([y_ref[jnp.bitwise_xor(column, d)] for d in range(1, 8)], axis=0)
    far = dot(far_pick((FAR, 112), 0), slots, (1, 0)).astype(BF16)
    for s in range(8):
        out_ref[s] = far


def attend_kernel(
    qn_ref, kv_ref, one_ref, g_ref, p1_ref, p2_ref, z_ref, lv_ref,
    att_ref, nqg_ref, tok_ref, p1o_ref, p2o_ref, zo_ref, lo_ref,
    near, cross, near_grad, one_grad, cross_grad,
):
    index = lax.axis_index("seq")
    last = lax.axis_size("seq") - 1
    place = jnp.bitwise_and(index, 7)
    odd = jnp.bitwise_and(index, 1)
    peer_side = pl.multiple_of((1 - odd) * 640, LEAF)
    other_side = pl.multiple_of(odd * 640, LEAF)
    near[LEAF : LEAF + ROWS] = kv_ref[...]
    near[pl.ds(peer_side, LEAF)] = p1_ref[:LEAF]
    near[pl.ds(other_side, LEAF)] = p2_ref[...]
    cross[:128] = p1_ref[LEAF:]
    cross[128:192] = lv_ref[jnp.bitwise_xor(place, 2), :64]
    cross[192:256] = lv_ref[jnp.bitwise_xor(place, 3), :64]
    for i in range(4):
        cross[256 + 32 * i : 288 + 32 * i] = lv_ref[jnp.bitwise_xor(place, 4 + i), 64:]
    for s in range(8):
        cross[384 + FAR * s : 384 + FAR * (s + 1)] = z_ref[s]

    def level_bias(rows, level):
        return jnp.full((rows, 2 * LEAF), level * LN2, F32)

    bias = jnp.concatenate(
        [level_bias(LEAF, level) for level in (1, 2, 3, 4)]
        + [level_bias(16, level) for _ in range(8) for level in (5, 6, 7)],
        axis=0,
    )
    left = jnp.where(index > 0, 0.0, -jnp.inf).astype(F32)
    right = jnp.where(index < last, 0.0, -jnp.inf).astype(F32)
    lane = iota((LEAF, FEAT), 1)
    feature = iota((FEAT, LEAF), 0)
    zero = jnp.zeros((LEAF, FEAT), BF16)

    def by_head(block):
        return jnp.concatenate(
            [jnp.where(lane < HEAD, block, zero), jnp.where(lane < HEAD, zero, block)], axis=0
        )

    def merge_heads(transposed):
        return jnp.where(feature < HEAD, transposed[:, :LEAF], transposed[:, LEAF:]).T

    near_grad[...] = jnp.zeros_like(near_grad)
    one_grad[...] = jnp.zeros_like(one_grad)
    for b in range(LEAVES):
        rows = slice(b * LEAF, (b + 1) * LEAF)
        near_rows = slice(b * LEAF, (b + 3) * LEAF)
        half = (1 - b // 2) * LEAF
        q2 = by_head(qn_ref[rows]) * jnp.asarray(0.125, BF16)
        g2 = by_head(g_ref[rows])
        kv = jnp.concatenate([near[near_rows], one_ref[half : half + LEAF], cross[...]], axis=0)
        keys = kv[:, :FEAT]
        values = kv[:, FEAT:]
        raw = dot(keys, q2, (1, 1))
        before, after = raw[:LEAF], raw[2 * LEAF : 3 * LEAF]
        if b == 0:
            before = before + left
        if b == LEAVES - 1:
            after = after + right
        scores = jnp.concatenate(
            [before, raw[LEAF : 2 * LEAF], after, raw[3 * LEAF :] + bias], axis=0
        )
        weights = jnp.exp(scores - jnp.max(scores, axis=0, keepdims=True))
        probs = weights * (1.0 / jnp.sum(weights, axis=0, keepdims=True))
        low = probs.astype(BF16)
        prob_grad = dot(values, g2, (1, 1))
        delta = jnp.sum(probs * prob_grad, axis=0, keepdims=True)
        score_grad = (probs * (prob_grad - delta)).astype(BF16)
        att_ref[rows] = merge_heads(dot(values, low, (0, 0))).astype(BF16)
        nqg_ref[rows] = merge_heads(dot(keys, score_grad, (0, 0))) * 0.125
        key_part = dot(score_grad, q2, (1, 0))
        value_part = dot(low, g2, (1, 0))
        for part, lanes in ((key_part, slice(0, FEAT)), (value_part, slice(FEAT, 2 * FEAT))):
            near_grad[near_rows, lanes] += part[: 3 * LEAF]
            one_grad[half : half + LEAF, lanes] += part[3 * LEAF : 4 * LEAF]
            if b == 0:
                cross_grad[:, lanes] = part[4 * LEAF :]
            else:
                cross_grad[:, lanes] += part[4 * LEAF :]

    spread = spreading(0, 256, 1).astype(BF16)
    high = one_grad[...].astype(BF16)
    rest = (one_grad[...] - high.astype(F32)).astype(BF16)
    tok_ref[...] = near_grad[LEAF : LEAF + ROWS] + dot(spread, high, (1, 0)) + dot(spread, rest, (1, 0))
    p1o_ref[:LEAF] = near_grad[pl.ds(peer_side, LEAF)].astype(BF16)
    p1o_ref[LEAF:] = cross_grad[:128].astype(BF16)
    p2o_ref[...] = near_grad[pl.ds(other_side, LEAF)].astype(BF16)
    for s in range(8):
        zo_ref[s] = cross_grad[384 + FAR * s : 384 + FAR * (s + 1)].astype(BF16)
    for d in range(8):
        other = jnp.bitwise_xor(place, d)
        high_rows = jnp.zeros((64, 2 * FEAT), BF16)
        low_rows = jnp.zeros((32, 2 * FEAT), BF16)
        if d in (2, 3):
            high_rows = cross_grad[64 * d : 64 * (d + 1)].astype(BF16)
        if d >= 4:
            low_rows = cross_grad[128 + 32 * d : 160 + 32 * d].astype(BF16)
        lo_ref[other, :64] = high_rows
        lo_ref[other, 64:] = low_rows


def column_kernel(z_ref, p1_ref, p2_ref, out_ref):
    column = jnp.right_shift(lax.axis_index("seq"), 3)
    far = jnp.sum(z_ref[...].astype(F32), axis=0).astype(BF16)
    slots = dot(far_pick((112, FAR), 1), far, (1, 0)).astype(BF16)
    out_ref[column] = jnp.zeros((16, 2 * FEAT), BF16)
    for d in range(1, 8):
        out_ref[jnp.bitwise_xor(column, d)] = slots[16 * (d - 1) : 16 * d]


def total_kernel(
    tok_ref, p1_ref, p2_ref, lv_ref, y_ref,
    q_ref, k_ref, qg_ref, kg_ref, nqg_ref, nkg_ref, vg_ref, sum_ref, acc,
):
    index = lax.axis_index("seq")
    column = jnp.right_shift(index, 3)
    odd = jnp.bitwise_and(index, 1)
    pieces = [p1_ref[LEAF:], lv_ref[...]]
    maps = [spreading(0, 128, 2), spreading(0, 64, 3), spreading(0, 32, 4)]
    for d in range(1, 8):
        pieces.append(y_ref[jnp.bitwise_xor(column, d)])
        maps.append(spreading(0, 16, COLUMN_LEVEL[d]))
    spread = jnp.concatenate(maps, axis=1).astype(BF16)
    acc[...] = tok_ref[...] + dot(spread, jnp.concatenate(pieces, axis=0), (1, 0))
    acc[pl.ds(pl.multiple_of((1 - odd) * 384, LEAF), LEAF)] += p1_ref[:LEAF].astype(F32)
    acc[pl.ds(pl.multiple_of(odd * 384, LEAF), LEAF)] += p2_ref[...].astype(F32)
    vg_ref[...] = acc[:, FEAT:].astype(BF16)
    key_total = acc[:, :FEAT]
    nkg_ref[...] = key_total
    tile = jnp.concatenate(
        token_sums(q_ref[...].astype(F32) * qg_ref[...] * nqg_ref[...])
        + token_sums(k_ref[...].astype(F32) * kg_ref[...] * key_total),
        axis=0,
    )
    for i in range(sum_ref.shape[0]):
        sum_ref[i] = tile


def finish_kernel(width, sq_ref, inner_ref, q_ref, k_ref, qg_ref, kg_ref, nqg_ref, nkg_ref, dq_ref, dk_ref):
    rate = lax.rsqrt(jnp.sum(sq_ref[...], axis=0) / width + EPS)
    inner = jnp.sum(inner_ref[...], axis=0) / width
    cubed = rate * rate * rate * inner
    for first, x_ref, gain_ref, grad_ref, out_ref in (
        (0, q_ref, qg_ref, nqg_ref, dq_ref),
        (4, k_ref, kg_ref, nkg_ref, dk_ref),
    ):
        out_ref[...] = (
            spread_tokens(rate, first) * gain_ref[...] * grad_ref[...]
            - x_ref[...].astype(F32) * spread_tokens(cubed, first)
        ).astype(BF16)


def call(kernel, outs, args, scratch=(), flops=0, name=None, spaces=None):
    many = isinstance(outs, list)
    moved = sum(math.prod(x.shape) * x.dtype.itemsize for x in list(args) + (outs if many else [outs]))
    return pl.pallas_call(
        kernel,
        out_shape=outs,
        in_specs=[pl.BlockSpec(memory_space=space) for space in spaces or [pltpu.VMEM] * len(args)],
        scratch_shapes=list(scratch),
        compiler_params=PARAMS,
        cost_estimate=pl.CostEstimate(flops=flops, bytes_accessed=moved, transcendentals=0),
        name=name,
    )(*args)


def sds(*shape, dtype=BF16):
    return jax.ShapeDtypeStruct(shape, dtype)


ROW_GROUPS = [[8 * y + z for z in range(8)] for y in range(8)]
COLUMN_GROUPS = [[8 * y + z for y in range(8)] for z in range(8)]


def exchange(x, axis, groups=None):
    return lax.all_to_all(x, axis, 0, 0, axis_index_groups=groups, tiled=True)


def local(queries, key_rows, value_rows, query_gain, key_gain, out_grad):
    seq = lax.axis_size("seq")
    heads = lax.axis_size("head")
    width = float(heads * FEAT)
    qg = query_gain.reshape(1, FEAT)
    kg = key_gain.reshape(1, FEAT)
    peer = [(i, i ^ 1) for i in range(seq)]
    beside = [(i, i + 1) for i in range(1, seq - 1, 2)] + [(i + 1, i) for i in range(1, seq - 1, 2)]

    squares = call(squares_kernel, sds(heads, 8, FEAT, dtype=F32), (queries, key_rows), name="squares")
    squares = exchange(squares, "head")
    qn, kv, one, lv, ysend, p1, p2 = call(
        lambda *refs: norm_kernel(width, *refs),
        [sds(ROWS, FEAT), sds(ROWS, 256), sds(256, 256), sds(MID, 256), sds(8, 16, 256), sds(256, 256), sds(LEAF, 256)],
        (squares, queries, key_rows, value_rows, qg, kg),
        name="norm",
    )
    p1 = lax.ppermute(p1, "seq", peer)
    p2 = lax.ppermute(p2, "seq", beside)
    lv = lax.all_gather(lv, "seq", axis=0, axis_index_groups=ROW_GROUPS)
    yrecv = exchange(ysend, "seq", COLUMN_GROUPS)
    zsend = call(row_kernel, sds(8, FAR, 256), (yrecv,), name="rows")
    zrecv = exchange(zsend, "seq", ROW_GROUPS)
    attended, nqg, tok, p1, p2, zsend, lv = call(
        attend_kernel,
        [sds(ROWS, FEAT), sds(ROWS, FEAT, dtype=F32), sds(ROWS, 256, dtype=F32), sds(256, 256), sds(LEAF, 256), sds(8, FAR, 256), sds(8, MID, 256)],
        (qn, kv, one, out_grad, p1, p2, zrecv, lv),
        scratch=[
            pltpu.VMEM((768, 256), BF16),
            pltpu.VMEM((768, 256), BF16),
            pltpu.VMEM((768, 256), F32),
            pltpu.VMEM((256, 256), F32),
            pltpu.VMEM((768, 256), F32),
        ],
        flops=4 * 6 * 2 * 256 * KEYS * FEAT,
        name="attend",
    )
    p1 = lax.ppermute(p1, "seq", peer)
    p2 = lax.ppermute(p2, "seq", beside)
    lv = lax.psum_scatter(lv, "seq", scatter_dimension=0, axis_index_groups=ROW_GROUPS)
    zrecv = exchange(zsend, "seq", ROW_GROUPS)
    ysend = call(
        column_kernel,
        sds(8, 16, 256),
        (zrecv, p1, p2),
        spaces=[pltpu.VMEM, pl.ANY, pl.ANY],
        name="columns",
    )
    yrecv = exchange(ysend, "seq", COLUMN_GROUPS)
    nkg, value_grad, inner = call(
        total_kernel,
        [sds(ROWS, FEAT, dtype=F32), sds(ROWS, FEAT), sds(heads, 8, FEAT, dtype=F32)],
        (tok, p1, p2, lv, yrecv, queries, key_rows, qg, kg, nqg),
        scratch=[pltpu.VMEM((ROWS, 256), F32)],
        name="total",
    )
    inner = exchange(inner, "head")
    query_grad, key_grad = call(
        lambda *refs: finish_kernel(width, *refs),
        [sds(ROWS, FEAT), sds(ROWS, FEAT)],
        (squares, inner, queries, key_rows, qg, kg, nqg, nkg),
        name="finish",
    )
    return (attended, query_grad, key_grad, value_grad)


def solution(mesh):
    placed = (
        P("seq", "head"),
        P("seq", "head"),
        P("seq", "head"),
        P("head"),
        P("head"),
        P("seq", "head"),
    )
    return jax.shard_map(
        local,
        mesh=mesh,
        in_specs=placed,
        out_specs=(P("seq", "head"), P("seq", "head"), P("seq", "head"), P("seq", "head")),
        check_vma=False,
    )
```

```python
import math

import jax
import jax.numpy as jnp
from jax import lax
from jax.experimental import pallas as pl
from jax.experimental.pallas import tpu as pltpu
from jax.sharding import PartitionSpec as P

ROWS = 512
FEAT = 128
LEAF = 128
LEAVES = 4
HEAD = 64
KEYS = 1280
EPS = 1e-06
LN2 = math.log(2.0)
F32 = jnp.float32
BF16 = jnp.bfloat16
PARAMS = pltpu.CompilerParams(vmem_limit_bytes=40 * 1024 * 1024)
ROW_LEVEL = {1: 2, 2: 3, 3: 3, 4: 4, 5: 4, 6: 4, 7: 4}
COLUMN_LEVEL = {1: 5, 2: 6, 3: 6, 4: 7, 5: 7, 6: 7, 7: 7}
FAR = 48
SLOT = 112


def dot(a, b, dims):
    return lax.dot_general(a, b, ((dims[:1], dims[1:]), ((), ())), preferred_element_type=F32)


def iota(shape, axis):
    return lax.broadcasted_iota(jnp.int32, shape, axis)


def pooling(rows, level):
    token = iota((rows, ROWS), 1)
    hit = jnp.right_shift(token, level) == iota((rows, ROWS), 0)
    return jnp.where(hit, 2.0**-level, 0.0)


def spreading(first, rows, level):
    token = iota((ROWS, rows), 0)
    hit = jnp.right_shift(token, level) == iota((ROWS, rows), 1) + first
    return jnp.where(hit, 2.0**-level, 0.0)


def far_pick(shape, far_axis):
    far = iota(shape, far_axis)
    slot_row = iota(shape, 1 - far_axis)
    mid = far - 16
    low = far - 32
    column = jnp.where(
        far < 16,
        far,
        jnp.where(
            far < 32,
            (1 + jnp.right_shift(mid, 3)) * 16 + jnp.bitwise_and(mid, 7),
            (3 + jnp.right_shift(low, 2)) * 16 + jnp.bitwise_and(low, 3),
        ),
    )
    return jnp.where(column == slot_row, 1.0, 0.0).astype(BF16)


def token_sums(x):
    return [
        jnp.sum(x[i * LEAF : (i + 1) * LEAF].T, axis=0, keepdims=True) for i in range(LEAVES)
    ]


def spread_tokens(tile, first):
    return jnp.concatenate(
        [
            jnp.broadcast_to(tile[first + i : first + i + 1], (LEAF, LEAF)).T
            for i in range(LEAVES)
        ],
        axis=0,
    )


def squares_kernel(q_ref, k_ref, out_ref):
    q = q_ref[...].astype(F32)
    k = k_ref[...].astype(F32)
    tile = jnp.concatenate(token_sums(q * q) + token_sums(k * k), axis=0)
    for i in range(out_ref.shape[0]):
        out_ref[i] = tile


def norm_kernel(width, sum_ref, q_ref, k_ref, v_ref, qg_ref, kg_ref, qn_ref, kv_ref, one_ref, lv_ref, y_ref, p1_ref, p2_ref):
    index = lax.axis_index("seq")
    column = jnp.right_shift(index, 3)
    odd = jnp.bitwise_and(index, 1)
    total = jnp.sum(sum_ref[...], axis=0)
    rate = lax.rsqrt(total / width + EPS)
    qn_ref[...] = (
        q_ref[...].astype(F32) * spread_tokens(rate, 0) * qg_ref[...]
    ).astype(BF16)
    kv_ref[:, :FEAT] = (
        k_ref[...].astype(F32) * spread_tokens(rate, 4) * kg_ref[...]
    ).astype(BF16)
    kv_ref[:, FEAT:] = v_ref[...]
    pool = jnp.concatenate(
        [pooling(ROWS >> level, level) for level in (1, 2, 3, 4)]
        + [pooling(16, COLUMN_LEVEL[d]) for d in range(1, 8)],
        axis=0,
    ).astype(BF16)
    coarse = dot(pool, kv_ref[...], (1, 0)).astype(BF16)
    one_ref[...] = coarse[:256]
    lv_ref[...] = coarse[256:480]
    y_ref[column] = jnp.zeros((16, 2 * FEAT), BF16)
    for d in range(1, 8):
        y_ref[jnp.bitwise_xor(column, d)] = coarse[464 + 16 * d : 480 + 16 * d]
    p1_ref[:LEAF] = kv_ref[pl.ds(pl.multiple_of((1 - odd) * 384, LEAF), LEAF)]
    p1_ref[LEAF:] = coarse[320:384]
    p2_ref[...] = kv_ref[pl.ds(pl.multiple_of(odd * 384, LEAF), LEAF)]


def row_kernel(y_ref, lv_ref, out_ref):
    index = lax.axis_index("seq")
    column = jnp.right_shift(index, 3)
    place = jnp.bitwise_and(index, 7)
    slots = jnp.concatenate([y_ref[jnp.bitwise_xor(column, d)] for d in range(1, 8)], axis=0)
    far = dot(far_pick((FAR, 112), 0), slots, (1, 0)).astype(BF16)
    for s in range(8):
        out_ref[s, :FAR] = far
    out_ref[place, FAR:] = jnp.zeros((64, 2 * FEAT), BF16)
    for d in range(1, 8):
        other = jnp.bitwise_xor(place, d)
        if d == 1:
            out_ref[other, FAR:] = lv_ref[:64]
        elif d < 4:
            out_ref[other, FAR:] = lv_ref[128:192]
        else:
            out_ref[other, FAR : FAR + 32] = lv_ref[192:224]
            out_ref[other, FAR + 32 :] = jnp.zeros((32, 2 * FEAT), BF16)


def by_head(block):
    lane = iota((LEAF, FEAT), 1)
    zero = jnp.zeros((LEAF, FEAT), BF16)
    return jnp.concatenate(
        [jnp.where(lane < HEAD, block, zero), jnp.where(lane < HEAD, zero, block)], axis=0
    )


def peak(x):
    return jnp.max(x, axis=0, keepdims=True)


def add_up(x):
    return jnp.sum(x, axis=0, keepdims=True)


HALO_PIECE = {0: 0, LEAVES - 1: 2}


def level_bias(rows, level):
    return jnp.full((rows, 2 * LEAF), level * LN2, F32)


def far_bias():
    return jnp.concatenate(
        [level_bias(LEAF, level) for level in (2, 3, 4)]
        + [level_bias(16, level) for _ in range(8) for level in (5, 6, 7)],
        axis=0,
    )


def outside_bias():
    index = lax.axis_index("seq")
    last = lax.axis_size("seq") - 1
    return {
        0: jnp.where(index > 0, 0.0, -jnp.inf).astype(F32),
        LEAVES - 1: jnp.where(index < last, 0.0, -jnp.inf).astype(F32),
    }


def attend_kernel(
    qn_ref, kv_ref, one_ref, g_ref, p1_ref, p2_ref, z_ref,
    stat_ref, cross, halo, p1o_ref, p2o_ref, zo_ref,
    q2_scr, g2_scr, score_scr, pgrad_scr, low_scr, sgrad_scr, rims, cross_grad,
):
    index = lax.axis_index("seq")
    place = jnp.bitwise_and(index, 7)
    odd = jnp.bitwise_and(index, 1)
    peer_side = 1 - odd
    halo[peer_side] = p1_ref[:LEAF]
    halo[odd] = p2_ref[...]
    cross[:64] = z_ref[jnp.bitwise_xor(place, 1), FAR:]
    cross[64:128] = p1_ref[LEAF:]
    cross[128:192] = z_ref[jnp.bitwise_xor(place, 2), FAR:]
    cross[192:256] = z_ref[jnp.bitwise_xor(place, 3), FAR:]
    for i in range(4):
        cross[256 + 32 * i : 288 + 32 * i] = z_ref[jnp.bitwise_xor(place, 4 + i), FAR : FAR + 32]
    for s in range(8):
        cross[384 + FAR * s : 384 + FAR * (s + 1)] = z_ref[s, :FAR]

    bias = far_bias()
    outside = outside_bias()
    for b in range(LEAVES):
        block = slice(b * LEAF, (b + 1) * LEAF)
        lanes = slice(2 * b * LEAF, 2 * (b + 1) * LEAF)
        q2 = by_head(qn_ref[block]) * jnp.asarray(0.125, BF16)
        g2 = by_head(g_ref[block])
        q2_scr[lanes] = q2
        g2_scr[lanes] = g2
        half = (1 - b // 2) * LEAF
        top = None
        for i in range(10):
            rows = slice(i * LEAF, (i + 1) * LEAF)
            if HALO_PIECE.get(b) == i:
                kv = halo[0 if b == 0 else 1]
                extra = outside[b]
            elif i < 3:
                kv = kv_ref[(b + i - 1) * LEAF : (b + i) * LEAF]
                extra = None
            elif i == 3:
                kv = one_ref[half : half + LEAF]
                extra = LN2
            else:
                kv = cross[(i - 4) * LEAF : (i - 3) * LEAF]
                extra = bias[(i - 4) * LEAF : (i - 3) * LEAF]
            score = dot(kv[:, :FEAT], q2, (1, 1))
            if extra is not None:
                score = score + extra
            top = peak(score) if top is None else jnp.maximum(top, peak(score))
            score_scr[b, rows] = score
            pgrad_scr[b, rows] = dot(kv[:, FEAT:], g2, (1, 1))
        total = jnp.zeros((1, 2 * LEAF), F32)
        mixed = jnp.zeros((1, 2 * LEAF), F32)
        for i in range(10):
            rows = slice(i * LEAF, (i + 1) * LEAF)
            weight = jnp.exp(score_scr[b, rows] - top)
            total = total + add_up(weight)
            mixed = mixed + add_up(weight * pgrad_scr[b, rows])
            if i > 3 or HALO_PIECE.get(b) == i:
                score_scr[b, rows] = weight
        inverse = 1.0 / total
        delta = mixed * inverse
        stat_ref[b] = jnp.concatenate(
            [top, inverse, delta, jnp.zeros((5, 2 * LEAF), F32)], axis=0
        )
        for i in range(10):
            rows = slice(i * LEAF, (i + 1) * LEAF)
            if i < 4 and HALO_PIECE.get(b) != i:
                continue
            prob = score_scr[b, rows] * inverse
            low = prob.astype(BF16)
            sgrad = (prob * (pgrad_scr[b, rows] - delta)).astype(BF16)
            if i < 4:
                rims[0 if b == 0 else 1, :, :FEAT] = dot(sgrad, q2, (1, 0)).astype(BF16)
                rims[0 if b == 0 else 1, :, FEAT:] = dot(low, g2, (1, 0)).astype(BF16)
            else:
                low_scr[(i - 4) * LEAF : (i - 3) * LEAF, lanes] = low
                sgrad_scr[(i - 4) * LEAF : (i - 3) * LEAF, lanes] = sgrad

    cross_grad[:, :FEAT] = dot(sgrad_scr[...], q2_scr[...], (1, 0)).astype(BF16)
    cross_grad[:, FEAT:] = dot(low_scr[...], g2_scr[...], (1, 0)).astype(BF16)
    p1o_ref[:LEAF] = rims[peer_side]
    p1o_ref[LEAF:] = cross_grad[64:128]
    p2o_ref[...] = rims[odd]
    for s in range(8):
        zo_ref[s, :FAR] = cross_grad[384 + FAR * s : 384 + FAR * (s + 1)]
    zo_ref[place, FAR:] = jnp.zeros((64, 2 * FEAT), BF16)
    zo_ref[jnp.bitwise_xor(place, 1), FAR:] = cross_grad[:64]
    zo_ref[jnp.bitwise_xor(place, 2), FAR:] = cross_grad[128:192]
    zo_ref[jnp.bitwise_xor(place, 3), FAR:] = cross_grad[192:256]
    for i in range(4):
        other = jnp.bitwise_xor(place, 4 + i)
        zo_ref[other, FAR : FAR + 32] = cross_grad[256 + 32 * i : 288 + 32 * i]
        zo_ref[other, FAR + 32 :] = jnp.zeros((32, 2 * FEAT), BF16)


def after_kernel(
    stat_ref, qn_ref, kv_ref, one_ref, g_ref, halo, cross,
    att_ref, nqg_ref, tok_ref, near, near_grad, one_grad,
):
    near[:LEAF] = halo[0]
    near[LEAF : LEAF + ROWS] = kv_ref[...]
    near[LEAF + ROWS :] = halo[1]
    near_grad[...] = jnp.zeros_like(near_grad)
    one_grad[...] = jnp.zeros_like(one_grad)
    feature = iota((FEAT, LEAF), 0)
    bias = jnp.concatenate([level_bias(LEAF, 1), far_bias()], axis=0)
    outside = outside_bias()

    def merge_heads(transposed):
        return jnp.where(feature < HEAD, transposed[:, :LEAF], transposed[:, LEAF:]).T

    for b in range(LEAVES):
        rows = slice(b * LEAF, (b + 1) * LEAF)
        near_rows = slice(b * LEAF, (b + 3) * LEAF)
        half = (1 - b // 2) * LEAF
        q2 = by_head(qn_ref[rows]) * jnp.asarray(0.125, BF16)
        g2 = by_head(g_ref[rows])
        kv = jnp.concatenate([near[near_rows], one_ref[half : half + LEAF], cross[...]], axis=0)
        keys = kv[:, :FEAT]
        values = kv[:, FEAT:]
        raw = dot(keys, q2, (1, 1))
        before, after = raw[:LEAF], raw[2 * LEAF : 3 * LEAF]
        if b == 0:
            before = before + outside[b]
        if b == LEAVES - 1:
            after = after + outside[b]
        scores = jnp.concatenate(
            [before, raw[LEAF : 2 * LEAF], after, raw[3 * LEAF :] + bias], axis=0
        )
        probs = jnp.exp(scores - stat_ref[b, 0:1]) * stat_ref[b, 1:2]
        low = probs.astype(BF16)
        score_grad = (probs * (dot(values, g2, (1, 1)) - stat_ref[b, 2:3])).astype(BF16)
        att_ref[rows] = merge_heads(dot(values, low, (0, 0))).astype(BF16)
        nqg_ref[rows] = merge_heads(dot(keys, score_grad, (0, 0))) * 0.125
        for part, lanes in (
            (dot(score_grad[: 4 * LEAF], q2, (1, 0)), slice(0, FEAT)),
            (dot(low[: 4 * LEAF], g2, (1, 0)), slice(FEAT, 2 * FEAT)),
        ):
            near_grad[near_rows, lanes] += part[: 3 * LEAF]
            one_grad[half : half + LEAF, lanes] += part[3 * LEAF :]
    spread = spreading(0, 256, 1).astype(BF16)
    high = one_grad[...].astype(BF16)
    rest = (one_grad[...] - high.astype(F32)).astype(BF16)
    tok_ref[...] = near_grad[LEAF : LEAF + ROWS] + dot(spread, high, (1, 0)) + dot(spread, rest, (1, 0))


def column_kernel(z_ref, p1_ref, p2_ref, tok_ref, out_ref, far_rows, sem):
    column = jnp.right_shift(lax.axis_index("seq"), 3)
    copy = pltpu.make_async_copy(z_ref.at[:, pl.ds(0, FAR)], far_rows, sem)
    copy.start()
    copy.wait()
    far = jnp.sum(far_rows[...].astype(F32), axis=0).astype(BF16)
    slots = dot(far_pick((112, FAR), 1), far, (1, 0)).astype(BF16)
    out_ref[column] = jnp.zeros((16, 2 * FEAT), BF16)
    for d in range(1, 8):
        out_ref[jnp.bitwise_xor(column, d)] = slots[16 * (d - 1) : 16 * d]


def total_kernel(
    tok_ref, p1_ref, p2_ref, z_ref, y_ref,
    q_ref, k_ref, qg_ref, kg_ref, nqg_ref, nkg_ref, vg_ref, sum_ref, acc,
):
    index = lax.axis_index("seq")
    column = jnp.right_shift(index, 3)
    place = jnp.bitwise_and(index, 7)
    odd = jnp.bitwise_and(index, 1)
    pieces = [z_ref[jnp.bitwise_xor(place, 1), FAR:], p1_ref[LEAF:]]
    maps = [spreading(0, 64, 2), spreading(64, 64, 2)]
    for d in range(2, 8):
        rows = ROWS >> ROW_LEVEL[d]
        pieces.append(z_ref[jnp.bitwise_xor(place, d), FAR : FAR + rows])
        maps.append(spreading(0, rows, ROW_LEVEL[d]))
    for d in range(1, 8):
        pieces.append(y_ref[jnp.bitwise_xor(column, d)])
        maps.append(spreading(0, 16, COLUMN_LEVEL[d]))
    spread = jnp.concatenate(maps, axis=1).astype(BF16)
    acc[...] = tok_ref[...] + dot(spread, jnp.concatenate(pieces, axis=0), (1, 0))
    acc[pl.ds(pl.multiple_of((1 - odd) * 384, LEAF), LEAF)] += p1_ref[:LEAF].astype(F32)
    acc[pl.ds(pl.multiple_of(odd * 384, LEAF), LEAF)] += p2_ref[...].astype(F32)
    vg_ref[...] = acc[:, FEAT:].astype(BF16)
    key_total = acc[:, :FEAT]
    nkg_ref[...] = key_total
    tile = jnp.concatenate(
        token_sums(q_ref[...].astype(F32) * qg_ref[...] * nqg_ref[...])
        + token_sums(k_ref[...].astype(F32) * kg_ref[...] * key_total),
        axis=0,
    )
    for i in range(sum_ref.shape[0]):
        sum_ref[i] = tile


def finish_kernel(width, sq_ref, inner_ref, q_ref, k_ref, qg_ref, kg_ref, nqg_ref, nkg_ref, dq_ref, dk_ref):
    rate = lax.rsqrt(jnp.sum(sq_ref[...], axis=0) / width + EPS)
    inner = jnp.sum(inner_ref[...], axis=0) / width
    cubed = rate * rate * rate * inner
    for first, x_ref, gain_ref, grad_ref, out_ref in (
        (0, q_ref, qg_ref, nqg_ref, dq_ref),
        (4, k_ref, kg_ref, nkg_ref, dk_ref),
    ):
        out_ref[...] = (
            spread_tokens(rate, first) * gain_ref[...] * grad_ref[...]
            - x_ref[...].astype(F32) * spread_tokens(cubed, first)
        ).astype(BF16)


def call(kernel, outs, args, scratch=(), flops=0, name=None, spaces=None):
    many = isinstance(outs, list)
    moved = sum(math.prod(x.shape) * x.dtype.itemsize for x in list(args) + (outs if many else [outs]))
    return pl.pallas_call(
        kernel,
        out_shape=outs,
        in_specs=[pl.BlockSpec(memory_space=space) for space in spaces or [pltpu.VMEM] * len(args)],
        scratch_shapes=list(scratch),
        compiler_params=PARAMS,
        cost_estimate=pl.CostEstimate(flops=flops, bytes_accessed=moved, transcendentals=0),
        name=name,
    )(*args)


def sds(*shape, dtype=BF16):
    return jax.ShapeDtypeStruct(shape, dtype)


ROW_GROUPS = [[8 * y + z for z in range(8)] for y in range(8)]
COLUMN_GROUPS = [[8 * y + z for y in range(8)] for z in range(8)]


def exchange(x, axis, groups=None):
    return lax.all_to_all(x, axis, 0, 0, axis_index_groups=groups, tiled=True)


def local(queries, key_rows, value_rows, query_gain, key_gain, out_grad):
    seq = lax.axis_size("seq")
    heads = lax.axis_size("head")
    width = float(heads * FEAT)
    qg = query_gain.reshape(1, FEAT)
    kg = key_gain.reshape(1, FEAT)
    peer = [(i, i ^ 1) for i in range(seq)]
    beside = [(i, i + 1) for i in range(1, seq - 1, 2)] + [(i + 1, i) for i in range(1, seq - 1, 2)]

    squares = call(squares_kernel, sds(heads, 8, FEAT, dtype=F32), (queries, key_rows), name="squares")
    squares = exchange(squares, "head")
    qn, kv, one, lv, ysend, p1, p2 = call(
        lambda *refs: norm_kernel(width, *refs),
        [sds(ROWS, FEAT), sds(ROWS, 256), sds(256, 256), sds(224, 256), sds(8, 16, 256), sds(192, 256), sds(LEAF, 256)],
        (squares, queries, key_rows, value_rows, qg, kg),
        name="norm",
    )
    p1 = lax.ppermute(p1, "seq", peer)
    p2 = lax.ppermute(p2, "seq", beside)
    yrecv = exchange(ysend, "seq", COLUMN_GROUPS)
    zsend = call(row_kernel, sds(8, SLOT, 256), (yrecv, lv), name="rows")
    zrecv = exchange(zsend, "seq", ROW_GROUPS)
    stat, cross, halo, p1, p2, zsend = call(
        attend_kernel,
        [sds(LEAVES, 8, 256, dtype=F32), sds(768, 256), sds(2, LEAF, 256)]
        + [sds(192, 256), sds(LEAF, 256), sds(8, SLOT, 256)],
        (qn, kv, one, out_grad, p1, p2, zrecv),
        scratch=[
            pltpu.VMEM((1024, FEAT), BF16),
            pltpu.VMEM((1024, FEAT), BF16),
            pltpu.VMEM((LEAVES, KEYS, 256), F32),
            pltpu.VMEM((LEAVES, KEYS, 256), F32),
            pltpu.VMEM((768, 1024), BF16),
            pltpu.VMEM((768, 1024), BF16),
            pltpu.VMEM((2, LEAF, 256), BF16),
            pltpu.VMEM((768, 256), BF16),
        ],
        flops=4 * 4 * 2 * 256 * KEYS * FEAT,
        name="attend",
    )
    p1 = lax.ppermute(p1, "seq", peer)
    p2 = lax.ppermute(p2, "seq", beside)
    zrecv = exchange(zsend, "seq", ROW_GROUPS)
    attended, nqg, tok = call(
        after_kernel,
        [sds(ROWS, FEAT), sds(ROWS, FEAT, dtype=F32), sds(ROWS, 256, dtype=F32)],
        (stat, qn, kv, one, out_grad, halo, cross),
        scratch=[
            pltpu.VMEM((768, 256), BF16),
            pltpu.VMEM((768, 256), F32),
            pltpu.VMEM((256, 256), F32),
        ],
        flops=4 * 5 * 2 * 256 * KEYS * FEAT,
        name="after",
    )
    ysend = call(
        column_kernel,
        sds(8, 16, 256),
        (zrecv, p1, p2, tok),
        scratch=[pltpu.VMEM((8, FAR, 256), BF16), pltpu.SemaphoreType.DMA],
        spaces=[pl.ANY] * 4,
        name="columns",
    )
    yrecv = exchange(ysend, "seq", COLUMN_GROUPS)
    nkg, value_grad, inner = call(
        total_kernel,
        [sds(ROWS, FEAT, dtype=F32), sds(ROWS, FEAT), sds(heads, 8, FEAT, dtype=F32)],
        (tok, p1, p2, zrecv, yrecv, queries, key_rows, qg, kg, nqg),
        scratch=[pltpu.VMEM((ROWS, 256), F32)],
        name="total",
    )
    inner = exchange(inner, "head")
    query_grad, key_grad = call(
        lambda *refs: finish_kernel(width, *refs),
        [sds(ROWS, FEAT), sds(ROWS, FEAT)],
        (squares, inner, queries, key_rows, qg, kg, nqg, nkg),
        name="finish",
    )
    return (attended, query_grad, key_grad, value_grad)


def solution(mesh):
    placed = (
        P("seq", "head"),
        P("seq", "head"),
        P("seq", "head"),
        P("head"),
        P("head"),
        P("seq", "head"),
    )
    return jax.shard_map(
        local,
        mesh=mesh,
        in_specs=placed,
        out_specs=(P("seq", "head"), P("seq", "head"), P("seq", "head"), P("seq", "head")),
        check_vma=False,
    )
```

```python
import math

import jax
import jax.numpy as jnp
from jax import lax
from jax.experimental import pallas as pl
from jax.experimental.pallas import tpu as pltpu
from jax.sharding import PartitionSpec as P

ROWS = 512
FEAT = 128
LEAF = 128
LEAVES = 4
HEAD = 64
KEYS = 1280
EPS = 1e-06
LN2 = math.log(2.0)
F32 = jnp.float32
BF16 = jnp.bfloat16
PARAMS = pltpu.CompilerParams(vmem_limit_bytes=40 * 1024 * 1024)
ROW_LEVEL = {1: 2, 2: 3, 3: 3, 4: 4, 5: 4, 6: 4, 7: 4}
COLUMN_LEVEL = {1: 5, 2: 6, 3: 6, 4: 7, 5: 7, 6: 7, 7: 7}
FAR = 48
SLOT = 112


def dot(a, b, dims):
    return lax.dot_general(a, b, ((dims[:1], dims[1:]), ((), ())), preferred_element_type=F32)


def iota(shape, axis):
    return lax.broadcasted_iota(jnp.int32, shape, axis)


def pooling(rows, level):
    token = iota((rows, ROWS), 1)
    hit = jnp.right_shift(token, level) == iota((rows, ROWS), 0)
    return jnp.where(hit, 2.0**-level, 0.0)


def spreading(first, rows, level):
    token = iota((ROWS, rows), 0)
    hit = jnp.right_shift(token, level) == iota((ROWS, rows), 1) + first
    return jnp.where(hit, 2.0**-level, 0.0)


def far_pick(shape, far_axis):
    far = iota(shape, far_axis)
    slot_row = iota(shape, 1 - far_axis)
    mid = far - 16
    low = far - 32
    column = jnp.where(
        far < 16,
        far,
        jnp.where(
            far < 32,
            (1 + jnp.right_shift(mid, 3)) * 16 + jnp.bitwise_and(mid, 7),
            (3 + jnp.right_shift(low, 2)) * 16 + jnp.bitwise_and(low, 3),
        ),
    )
    return jnp.where(column == slot_row, 1.0, 0.0).astype(BF16)


def token_sums(x):
    return [
        jnp.sum(x[i * LEAF : (i + 1) * LEAF].T, axis=0, keepdims=True) for i in range(LEAVES)
    ]


def spread_tokens(tile, first):
    return jnp.concatenate(
        [
            jnp.broadcast_to(tile[first + i : first + i + 1], (LEAF, LEAF)).T
            for i in range(LEAVES)
        ],
        axis=0,
    )


def squares_kernel(q_ref, k_ref, out_ref):
    q = q_ref[...].astype(F32)
    k = k_ref[...].astype(F32)
    tile = jnp.concatenate(token_sums(q * q) + token_sums(k * k), axis=0)
    for i in range(out_ref.shape[0]):
        out_ref[i] = tile


def norm_kernel(width, sum_ref, q_ref, k_ref, v_ref, qg_ref, kg_ref, qn_ref, kv_ref, one_ref, lv_ref, y_ref, p1_ref, p2_ref):
    index = lax.axis_index("seq")
    column = jnp.right_shift(index, 3)
    odd = jnp.bitwise_and(index, 1)
    total = jnp.sum(sum_ref[...], axis=0)
    rate = lax.rsqrt(total / width + EPS)
    qn_ref[...] = (
        q_ref[...].astype(F32) * spread_tokens(rate, 0) * qg_ref[...]
    ).astype(BF16)
    kv_ref[:, :FEAT] = (
        k_ref[...].astype(F32) * spread_tokens(rate, 4) * kg_ref[...]
    ).astype(BF16)
    kv_ref[:, FEAT:] = v_ref[...]
    pool = jnp.concatenate(
        [pooling(ROWS >> level, level) for level in (1, 2, 3, 4)]
        + [pooling(16, COLUMN_LEVEL[d]) for d in range(1, 8)],
        axis=0,
    ).astype(BF16)
    coarse = dot(pool, kv_ref[...], (1, 0)).astype(BF16)
    one_ref[...] = coarse[:256]
    lv_ref[...] = coarse[256:480]
    y_ref[column] = jnp.zeros((16, 2 * FEAT), BF16)
    for d in range(1, 8):
        y_ref[jnp.bitwise_xor(column, d)] = coarse[464 + 16 * d : 480 + 16 * d]
    p1_ref[:LEAF] = kv_ref[pl.ds(pl.multiple_of((1 - odd) * 384, LEAF), LEAF)]
    p1_ref[LEAF:] = coarse[320:384]
    p2_ref[...] = kv_ref[pl.ds(pl.multiple_of(odd * 384, LEAF), LEAF)]


def row_kernel(y_ref, lv_ref, out_ref):
    index = lax.axis_index("seq")
    column = jnp.right_shift(index, 3)
    place = jnp.bitwise_and(index, 7)
    slots = jnp.concatenate([y_ref[jnp.bitwise_xor(column, d)] for d in range(1, 8)], axis=0)
    far = dot(far_pick((FAR, 112), 0), slots, (1, 0)).astype(BF16)
    for s in range(8):
        out_ref[s, :FAR] = far
    out_ref[place, FAR:] = jnp.zeros((64, 2 * FEAT), BF16)
    for d in range(1, 8):
        other = jnp.bitwise_xor(place, d)
        if d == 1:
            out_ref[other, FAR:] = lv_ref[:64]
        elif d < 4:
            out_ref[other, FAR:] = lv_ref[128:192]
        else:
            out_ref[other, FAR : FAR + 32] = lv_ref[192:224]
            out_ref[other, FAR + 32 :] = jnp.zeros((32, 2 * FEAT), BF16)


def by_head(block):
    lane = iota((LEAF, FEAT), 1)
    zero = jnp.zeros((LEAF, FEAT), BF16)
    return jnp.concatenate(
        [jnp.where(lane < HEAD, block, zero), jnp.where(lane < HEAD, zero, block)], axis=0
    )


def peak(x):
    return jnp.max(x, axis=0, keepdims=True)


def add_up(x):
    return jnp.sum(x, axis=0, keepdims=True)


HALO_PIECE = {0: 0, LEAVES - 1: 2}


def far_bias():
    return jnp.concatenate(
        [jnp.full((LEAF, 2 * LEAF), level * LN2, F32) for level in range(1, 8)], axis=0
    )


def outside_bias():
    index = lax.axis_index("seq")
    last = lax.axis_size("seq") - 1
    return {
        0: jnp.where(index > 0, 0.0, -1e30).astype(F32),
        LEAVES - 1: jnp.where(index < last, 0.0, -1e30).astype(F32),
    }


def weigh(kv, q2, g2):
    score = dot(kv[:, :FEAT], q2, (1, 1))
    top = peak(score)
    weight = jnp.exp(score - top)
    pgrad = dot(kv[:, FEAT:], g2, (1, 1))
    return weight, pgrad, (top, add_up(weight), add_up(weight * pgrad))


def combine(stats):
    top = stats[0][0]
    for stat in stats[1:]:
        top = jnp.maximum(top, stat[0])
    factors = [jnp.exp(stat[0] - top) for stat in stats]
    total = sum(factor * stat[1] for factor, stat in zip(factors, stats))
    mixed = sum(factor * stat[2] for factor, stat in zip(factors, stats))
    return top, total, mixed, factors


def scaled_queries(block):
    return by_head(block) * jnp.asarray(0.125, BF16)


def near_kernel(qn_ref, kv_ref, one_ref, g_ref, stat_ref):
    for b in range(LEAVES):
        block = slice(b * LEAF, (b + 1) * LEAF)
        q2 = scaled_queries(qn_ref[block])
        g2 = by_head(g_ref[block])
        half = (1 - b // 2) * LEAF
        stats = [
            weigh(kv_ref[(b + i - 1) * LEAF : (b + i) * LEAF], q2, g2)[2]
            for i in range(3)
            if HALO_PIECE.get(b) != i
        ]
        top, total, mixed = weigh(one_ref[half : half + LEAF], q2, g2)[2]
        stats.append((top + LN2, total, mixed))
        top, total, mixed, _ = combine(stats)
        stat_ref[b] = jnp.concatenate([top, total, mixed, jnp.zeros((5, 2 * LEAF), F32)], axis=0)


def attend_kernel(
    qn_ref, g_ref, near_ref, p1_ref, p2_ref, z_ref,
    stat_ref, cross, halo, p1o_ref, p2o_ref, zo_ref,
    q2_scr, g2_scr, weight_scr, pgrad_scr, low_scr, sgrad_scr, rims, cross_grad,
):
    index = lax.axis_index("seq")
    place = jnp.bitwise_and(index, 7)
    odd = jnp.bitwise_and(index, 1)
    peer_side = 1 - odd
    halo[peer_side] = p1_ref[:LEAF]
    halo[odd] = p2_ref[...]
    cross[:64] = z_ref[jnp.bitwise_xor(place, 1), FAR:]
    cross[64:128] = p1_ref[LEAF:]
    cross[128:192] = z_ref[jnp.bitwise_xor(place, 2), FAR:]
    cross[192:256] = z_ref[jnp.bitwise_xor(place, 3), FAR:]
    for i in range(4):
        cross[256 + 32 * i : 288 + 32 * i] = z_ref[jnp.bitwise_xor(place, 4 + i), FAR : FAR + 32]
    for s in range(8):
        for j in range(3):
            at = 384 + LEAF * j + 16 * s
            cross[at : at + 16] = z_ref[s, 16 * j : 16 * (j + 1)]

    outside = outside_bias()
    for b in range(LEAVES):
        block = slice(b * LEAF, (b + 1) * LEAF)
        lanes = slice(2 * b * LEAF, 2 * (b + 1) * LEAF)
        q2 = scaled_queries(qn_ref[block])
        g2 = by_head(g_ref[block])
        q2_scr[lanes] = q2
        g2_scr[lanes] = g2
        side = 0 if b == 0 else 1
        pieces = list(range(7 if b in HALO_PIECE else 6))
        stats = [(near_ref[b, 0:1], near_ref[b, 1:2], near_ref[b, 2:3])]
        for i in pieces:
            kv = cross[i * LEAF : (i + 1) * LEAF] if i < 6 else halo[side]
            weight, pgrad, (top, total, mixed) = weigh(kv, q2, g2)
            weight_scr[b, i] = weight
            pgrad_scr[b, i] = pgrad
            bias = (i + 2) * LN2 if i < 6 else outside[b]
            stats.append((top + bias, total, mixed))
        top, total, mixed, factors = combine(stats)
        inverse = 1.0 / total
        delta = mixed * inverse
        stat_ref[b] = jnp.concatenate(
            [top, inverse, delta, jnp.zeros((5, 2 * LEAF), F32)], axis=0
        )
        for i in pieces:
            prob = weight_scr[b, i] * (factors[i + 1] * inverse)
            low = prob.astype(BF16)
            sgrad = (prob * (pgrad_scr[b, i] - delta)).astype(BF16)
            if i < 6:
                low_scr[i * LEAF : (i + 1) * LEAF, lanes] = low
                sgrad_scr[i * LEAF : (i + 1) * LEAF, lanes] = sgrad
            else:
                rims[side, :, :FEAT] = dot(sgrad, q2, (1, 0)).astype(BF16)
                rims[side, :, FEAT:] = dot(low, g2, (1, 0)).astype(BF16)

    cross_grad[:, :FEAT] = dot(sgrad_scr[...], q2_scr[...], (1, 0)).astype(BF16)
    cross_grad[:, FEAT:] = dot(low_scr[...], g2_scr[...], (1, 0)).astype(BF16)
    p1o_ref[:LEAF] = rims[peer_side]
    p1o_ref[LEAF:] = cross_grad[64:128]
    p2o_ref[...] = rims[odd]
    for s in range(8):
        for j in range(3):
            at = 384 + LEAF * j + 16 * s
            zo_ref[s, 16 * j : 16 * (j + 1)] = cross_grad[at : at + 16]
    zo_ref[place, FAR:] = jnp.zeros((64, 2 * FEAT), BF16)
    zo_ref[jnp.bitwise_xor(place, 1), FAR:] = cross_grad[:64]
    zo_ref[jnp.bitwise_xor(place, 2), FAR:] = cross_grad[128:192]
    zo_ref[jnp.bitwise_xor(place, 3), FAR:] = cross_grad[192:256]
    for i in range(4):
        other = jnp.bitwise_xor(place, 4 + i)
        zo_ref[other, FAR : FAR + 32] = cross_grad[256 + 32 * i : 288 + 32 * i]
        zo_ref[other, FAR + 32 :] = jnp.zeros((32, 2 * FEAT), BF16)


def after_kernel(
    stat_ref, qn_ref, kv_ref, one_ref, g_ref, halo, cross,
    att_ref, nqg_ref, tok_ref, near, near_grad, one_grad,
):
    near[:LEAF] = halo[0]
    near[LEAF : LEAF + ROWS] = kv_ref[...]
    near[LEAF + ROWS :] = halo[1]
    near_grad[...] = jnp.zeros_like(near_grad)
    one_grad[...] = jnp.zeros_like(one_grad)
    feature = iota((FEAT, LEAF), 0)
    bias = far_bias()
    outside = outside_bias()

    def merge_heads(transposed):
        return jnp.where(feature < HEAD, transposed[:, :LEAF], transposed[:, LEAF:]).T

    for b in range(LEAVES):
        rows = slice(b * LEAF, (b + 1) * LEAF)
        near_rows = slice(b * LEAF, (b + 3) * LEAF)
        half = (1 - b // 2) * LEAF
        q2 = scaled_queries(qn_ref[rows])
        g2 = by_head(g_ref[rows])
        kv = jnp.concatenate([near[near_rows], one_ref[half : half + LEAF], cross[...]], axis=0)
        keys = kv[:, :FEAT]
        values = kv[:, FEAT:]
        raw = dot(keys, q2, (1, 1))
        before, after = raw[:LEAF], raw[2 * LEAF : 3 * LEAF]
        if b == 0:
            before = before + outside[b]
        if b == LEAVES - 1:
            after = after + outside[b]
        scores = jnp.concatenate(
            [before, raw[LEAF : 2 * LEAF], after, raw[3 * LEAF :] + bias], axis=0
        )
        probs = jnp.exp(scores - stat_ref[b, 0:1]) * stat_ref[b, 1:2]
        low = probs.astype(BF16)
        score_grad = (probs * (dot(values, g2, (1, 1)) - stat_ref[b, 2:3])).astype(BF16)
        att_ref[rows] = merge_heads(dot(values, low, (0, 0))).astype(BF16)
        nqg_ref[rows] = merge_heads(dot(keys, score_grad, (0, 0))) * 0.125
        for part, lanes in (
            (dot(score_grad[: 4 * LEAF], q2, (1, 0)), slice(0, FEAT)),
            (dot(low[: 4 * LEAF], g2, (1, 0)), slice(FEAT, 2 * FEAT)),
        ):
            near_grad[near_rows, lanes] += part[: 3 * LEAF]
            one_grad[half : half + LEAF, lanes] += part[3 * LEAF :]
    spread = spreading(0, 256, 1).astype(BF16)
    high = one_grad[...].astype(BF16)
    rest = (one_grad[...] - high.astype(F32)).astype(BF16)
    tok_ref[...] = near_grad[LEAF : LEAF + ROWS] + dot(spread, high, (1, 0)) + dot(spread, rest, (1, 0))


def column_kernel(z_ref, p1_ref, p2_ref, tok_ref, out_ref, far_rows, sem):
    column = jnp.right_shift(lax.axis_index("seq"), 3)
    copy = pltpu.make_async_copy(z_ref.at[:, pl.ds(0, FAR)], far_rows, sem)
    copy.start()
    copy.wait()
    far = jnp.sum(far_rows[...].astype(F32), axis=0).astype(BF16)
    slots = dot(far_pick((112, FAR), 1), far, (1, 0)).astype(BF16)
    out_ref[column] = jnp.zeros((16, 2 * FEAT), BF16)
    for d in range(1, 8):
        out_ref[jnp.bitwise_xor(column, d)] = slots[16 * (d - 1) : 16 * d]


def middle_kernel(tok_ref, p1_ref, p2_ref, z_ref, q_ref, qg_ref, nqg_ref, acc_ref, sum_ref):
    index = lax.axis_index("seq")
    place = jnp.bitwise_and(index, 7)
    odd = jnp.bitwise_and(index, 1)
    pieces = [z_ref[jnp.bitwise_xor(place, 1), FAR:], p1_ref[LEAF:]]
    maps = [spreading(0, 64, 2), spreading(64, 64, 2)]
    for d in range(2, 8):
        rows = ROWS >> ROW_LEVEL[d]
        pieces.append(z_ref[jnp.bitwise_xor(place, d), FAR : FAR + rows])
        maps.append(spreading(0, rows, ROW_LEVEL[d]))
    spread = jnp.concatenate(maps, axis=1).astype(BF16)
    acc_ref[...] = tok_ref[...] + dot(spread, jnp.concatenate(pieces, axis=0), (1, 0))
    acc_ref[pl.ds(pl.multiple_of((1 - odd) * 384, LEAF), LEAF)] += p1_ref[:LEAF].astype(F32)
    acc_ref[pl.ds(pl.multiple_of(odd * 384, LEAF), LEAF)] += p2_ref[...].astype(F32)
    sums = token_sums(q_ref[...].astype(F32) * qg_ref[...] * nqg_ref[...])
    sum_ref[...] = jnp.concatenate(sums + [jnp.zeros((LEAVES, FEAT), F32)], axis=0)


def total_kernel(acc_ref, y_ref, k_ref, kg_ref, qsum_ref, nkg_ref, vg_ref, sum_ref):
    column = jnp.right_shift(lax.axis_index("seq"), 3)
    pieces = [y_ref[jnp.bitwise_xor(column, d)] for d in range(1, 8)]
    maps = [spreading(0, 16, COLUMN_LEVEL[d]) for d in range(1, 8)]
    spread = jnp.concatenate(maps, axis=1).astype(BF16)
    grads = acc_ref[...] + dot(spread, jnp.concatenate(pieces, axis=0), (1, 0))
    vg_ref[...] = grads[:, FEAT:].astype(BF16)
    key_total = grads[:, :FEAT]
    nkg_ref[...] = key_total
    sums = token_sums(k_ref[...].astype(F32) * kg_ref[...] * key_total)
    tile = jnp.concatenate([qsum_ref[:LEAVES]] + sums, axis=0)
    for i in range(sum_ref.shape[0]):
        sum_ref[i] = tile


def finish_kernel(width, sq_ref, inner_ref, q_ref, k_ref, qg_ref, kg_ref, nqg_ref, nkg_ref, dq_ref, dk_ref):
    rate = lax.rsqrt(jnp.sum(sq_ref[...], axis=0) / width + EPS)
    inner = jnp.sum(inner_ref[...], axis=0) / width
    cubed = rate * rate * rate * inner
    for first, x_ref, gain_ref, grad_ref, out_ref in (
        (0, q_ref, qg_ref, nqg_ref, dq_ref),
        (4, k_ref, kg_ref, nkg_ref, dk_ref),
    ):
        out_ref[...] = (
            spread_tokens(rate, first) * gain_ref[...] * grad_ref[...]
            - x_ref[...].astype(F32) * spread_tokens(cubed, first)
        ).astype(BF16)


def call(kernel, outs, args, scratch=(), flops=0, name=None, spaces=None):
    many = isinstance(outs, list)
    moved = sum(math.prod(x.shape) * x.dtype.itemsize for x in list(args) + (outs if many else [outs]))
    return pl.pallas_call(
        kernel,
        out_shape=outs,
        in_specs=[pl.BlockSpec(memory_space=space) for space in spaces or [pltpu.VMEM] * len(args)],
        scratch_shapes=list(scratch),
        compiler_params=PARAMS,
        cost_estimate=pl.CostEstimate(flops=flops, bytes_accessed=moved, transcendentals=0),
        name=name,
    )(*args)


def sds(*shape, dtype=BF16):
    return jax.ShapeDtypeStruct(shape, dtype)


ROW_GROUPS = [[8 * y + z for z in range(8)] for y in range(8)]
COLUMN_GROUPS = [[8 * y + z for y in range(8)] for z in range(8)]


def exchange(x, axis, groups=None):
    return lax.all_to_all(x, axis, 0, 0, axis_index_groups=groups, tiled=True)


def local(queries, key_rows, value_rows, query_gain, key_gain, out_grad):
    seq = lax.axis_size("seq")
    heads = lax.axis_size("head")
    width = float(heads * FEAT)
    qg = query_gain.reshape(1, FEAT)
    kg = key_gain.reshape(1, FEAT)
    peer = [(i, i ^ 1) for i in range(seq)]
    beside = [(i, i + 1) for i in range(1, seq - 1, 2)] + [(i + 1, i) for i in range(1, seq - 1, 2)]

    squares = call(squares_kernel, sds(heads, 8, FEAT, dtype=F32), (queries, key_rows), name="squares")
    squares = exchange(squares, "head")
    qn, kv, one, lv, ysend, p1, p2 = call(
        lambda *refs: norm_kernel(width, *refs),
        [sds(ROWS, FEAT), sds(ROWS, 256), sds(256, 256), sds(224, 256), sds(8, 16, 256), sds(192, 256), sds(LEAF, 256)],
        (squares, queries, key_rows, value_rows, qg, kg),
        name="norm",
    )
    p1 = lax.ppermute(p1, "seq", peer)
    p2 = lax.ppermute(p2, "seq", beside)
    yrecv = exchange(ysend, "seq", COLUMN_GROUPS)
    zsend = call(row_kernel, sds(8, SLOT, 256), (yrecv, lv), name="rows")
    zrecv = exchange(zsend, "seq", ROW_GROUPS)
    near = call(
        near_kernel,
        sds(LEAVES, 8, 256, dtype=F32),
        (qn, kv, one, out_grad),
        flops=14 * 2 * 2 * 256 * LEAF * FEAT,
        name="near",
    )
    stat, cross, halo, p1, p2, zsend = call(
        attend_kernel,
        [sds(LEAVES, 8, 256, dtype=F32), sds(768, 256), sds(2, LEAF, 256)]
        + [sds(192, 256), sds(LEAF, 256), sds(8, SLOT, 256)],
        (qn, out_grad, near, p1, p2, zrecv),
        scratch=[
            pltpu.VMEM((1024, FEAT), BF16),
            pltpu.VMEM((1024, FEAT), BF16),
            pltpu.VMEM((LEAVES, 7, LEAF, 256), F32),
            pltpu.VMEM((LEAVES, 7, LEAF, 256), F32),
            pltpu.VMEM((768, 1024), BF16),
            pltpu.VMEM((768, 1024), BF16),
            pltpu.VMEM((2, LEAF, 256), BF16),
            pltpu.VMEM((768, 256), BF16),
        ],
        flops=4 * 4 * 2 * 256 * 768 * FEAT,
        name="attend",
    )
    p1 = lax.ppermute(p1, "seq", peer)
    p2 = lax.ppermute(p2, "seq", beside)
    zrecv = exchange(zsend, "seq", ROW_GROUPS)
    attended, nqg, tok = call(
        after_kernel,
        [sds(ROWS, FEAT), sds(ROWS, FEAT, dtype=F32), sds(ROWS, 256, dtype=F32)],
        (stat, qn, kv, one, out_grad, halo, cross),
        scratch=[
            pltpu.VMEM((768, 256), BF16),
            pltpu.VMEM((768, 256), F32),
            pltpu.VMEM((256, 256), F32),
        ],
        flops=4 * 5 * 2 * 256 * KEYS * FEAT,
        name="after",
    )
    ysend = call(
        column_kernel,
        sds(8, 16, 256),
        (zrecv, p1, p2, tok),
        scratch=[pltpu.VMEM((8, FAR, 256), BF16), pltpu.SemaphoreType.DMA],
        spaces=[pl.ANY] * 4,
        name="columns",
    )
    yrecv = exchange(ysend, "seq", COLUMN_GROUPS)
    acc, qsum = call(
        middle_kernel,
        [sds(ROWS, 256, dtype=F32), sds(8, FEAT, dtype=F32)],
        (tok, p1, p2, zrecv, queries, qg, nqg),
        flops=2 * ROWS * 384 * 256,
        name="middle",
    )
    nkg, value_grad, inner = call(
        total_kernel,
        [sds(ROWS, FEAT, dtype=F32), sds(ROWS, FEAT), sds(heads, 8, FEAT, dtype=F32)],
        (acc, yrecv, key_rows, kg, qsum),
        name="total",
    )
    inner = exchange(inner, "head")
    query_grad, key_grad = call(
        lambda *refs: finish_kernel(width, *refs),
        [sds(ROWS, FEAT), sds(ROWS, FEAT)],
        (squares, inner, queries, key_rows, qg, kg, nqg, nkg),
        name="finish",
    )
    return (attended, query_grad, key_grad, value_grad)


def solution(mesh):
    placed = (
        P("seq", "head"),
        P("seq", "head"),
        P("seq", "head"),
        P("head"),
        P("head"),
        P("seq", "head"),
    )
    return jax.shard_map(
        local,
        mesh=mesh,
        in_specs=placed,
        out_specs=(P("seq", "head"), P("seq", "head"), P("seq", "head"), P("seq", "head")),
        check_vma=False,
    )
```

```python
import math

import jax
import jax.numpy as jnp
from jax import lax
from jax.experimental import pallas as pl
from jax.experimental.pallas import tpu as pltpu
from jax.sharding import PartitionSpec as P

ROWS = 512
FEAT = 128
LEAF = 128
LEAVES = 4
HEAD = 64
KEYS = 1280
EPS = 1e-06
LN2 = math.log(2.0)
F32 = jnp.float32
BF16 = jnp.bfloat16
PARAMS = pltpu.CompilerParams(vmem_limit_bytes=40 * 1024 * 1024)
ROW_LEVEL = {1: 2, 2: 3, 3: 3, 4: 4, 5: 4, 6: 4, 7: 4}
MID_ROWS = {1: (0, 64), 2: (64, 64), 3: (128, 64), 4: (192, 32), 5: (224, 32), 6: (256, 32), 7: (288, 32)}
COLUMN_LEVEL = {1: 5, 2: 6, 3: 6, 4: 7, 5: 7, 6: 7, 7: 7}
FAR = 48
SLOT = 112


def dot(a, b, dims):
    return lax.dot_general(a, b, ((dims[:1], dims[1:]), ((), ())), preferred_element_type=F32)


def iota(shape, axis):
    return lax.broadcasted_iota(jnp.int32, shape, axis)


def pooling(rows, level):
    token = iota((rows, ROWS), 1)
    hit = jnp.right_shift(token, level) == iota((rows, ROWS), 0)
    return jnp.where(hit, 2.0**-level, 0.0)


def spreading(first, rows, level):
    token = iota((ROWS, rows), 0)
    hit = jnp.right_shift(token, level) == iota((ROWS, rows), 1) + first
    return jnp.where(hit, 2.0**-level, 0.0)


def far_pick(shape, far_axis):
    far = iota(shape, far_axis)
    slot_row = iota(shape, 1 - far_axis)
    mid = far - 16
    low = far - 32
    column = jnp.where(
        far < 16,
        far,
        jnp.where(
            far < 32,
            (1 + jnp.right_shift(mid, 3)) * 16 + jnp.bitwise_and(mid, 7),
            (3 + jnp.right_shift(low, 2)) * 16 + jnp.bitwise_and(low, 3),
        ),
    )
    return jnp.where(column == slot_row, 1.0, 0.0).astype(BF16)


def token_sums(x):
    return [
        jnp.sum(x[i * LEAF : (i + 1) * LEAF].T, axis=0, keepdims=True) for i in range(LEAVES)
    ]


def spread_tokens(tile, first):
    return jnp.concatenate(
        [
            jnp.broadcast_to(tile[first + i : first + i + 1], (LEAF, LEAF)).T
            for i in range(LEAVES)
        ],
        axis=0,
    )


def squares_kernel(qk_ref, out_ref):
    q = qk_ref[0].astype(F32)
    k = qk_ref[1].astype(F32)
    tile = jnp.concatenate(token_sums(q * q) + token_sums(k * k), axis=0)
    for i in range(out_ref.shape[0]):
        out_ref[i] = tile


def norm_kernel(width, sum_ref, qk_ref, v_ref, qg_ref, kg_ref, qn_ref, kv_ref, one_ref, lv_ref, y_ref, p1_ref, p2_ref):
    index = lax.axis_index("seq")
    column = jnp.right_shift(index, 3)
    odd = jnp.bitwise_and(index, 1)
    total = jnp.sum(sum_ref[...], axis=0)
    rate = lax.rsqrt(total / width + EPS)
    qn_ref[...] = (
        qk_ref[0].astype(F32) * spread_tokens(rate, 0) * qg_ref[...]
    ).astype(BF16)
    kv_ref[:, :FEAT] = (
        qk_ref[1].astype(F32) * spread_tokens(rate, 4) * kg_ref[...]
    ).astype(BF16)
    kv_ref[:, FEAT:] = v_ref[...]
    pool = jnp.concatenate(
        [pooling(ROWS >> level, level) for level in (1, 2, 3, 4)]
        + [pooling(16, COLUMN_LEVEL[d]) for d in range(1, 8)],
        axis=0,
    ).astype(BF16)
    coarse = dot(pool, kv_ref[...], (1, 0)).astype(BF16)
    one_ref[...] = coarse[:256]
    lv_ref[...] = coarse[256:480]
    y_ref[column] = jnp.zeros((16, 2 * FEAT), BF16)
    for d in range(1, 8):
        y_ref[jnp.bitwise_xor(column, d)] = coarse[464 + 16 * d : 480 + 16 * d]
    p1_ref[:LEAF] = kv_ref[pl.ds(pl.multiple_of((1 - odd) * 384, LEAF), LEAF)]
    p1_ref[LEAF:] = coarse[320:384]
    p2_ref[...] = kv_ref[pl.ds(pl.multiple_of(odd * 384, LEAF), LEAF)]


def row_kernel(y_ref, lv_ref, p2_ref, out_ref):
    index = lax.axis_index("seq")
    column = jnp.right_shift(index, 3)
    place = jnp.bitwise_and(index, 7)
    slots = jnp.concatenate([y_ref[jnp.bitwise_xor(column, d)] for d in range(1, 8)], axis=0)
    far = dot(far_pick((FAR, 112), 0), slots, (1, 0)).astype(BF16)
    for s in range(8):
        out_ref[s, :FAR] = far
    out_ref[place, FAR:] = jnp.zeros((64, 2 * FEAT), BF16)
    for d in range(1, 8):
        other = jnp.bitwise_xor(place, d)
        if d == 1:
            out_ref[other, FAR:] = lv_ref[:64]
        elif d < 4:
            out_ref[other, FAR:] = lv_ref[128:192]
        else:
            out_ref[other, FAR : FAR + 32] = lv_ref[192:224]
            out_ref[other, FAR + 32 :] = jnp.zeros((32, 2 * FEAT), BF16)


def by_head(block):
    lane = iota((LEAF, FEAT), 1)
    zero = jnp.zeros((LEAF, FEAT), BF16)
    return jnp.concatenate(
        [jnp.where(lane < HEAD, block, zero), jnp.where(lane < HEAD, zero, block)], axis=0
    )


def peak(x):
    return jnp.max(x, axis=0, keepdims=True)


def add_up(x):
    return jnp.sum(x, axis=0, keepdims=True)


HALO_PIECE = {0: 0, LEAVES - 1: 2}


def far_bias():
    return jnp.concatenate(
        [jnp.full((LEAF, 2 * LEAF), level * LN2, F32) for level in range(1, 8)], axis=0
    )


def outside_bias():
    index = lax.axis_index("seq")
    last = lax.axis_size("seq") - 1
    return {
        0: jnp.where(index > 0, 0.0, -1e30).astype(F32),
        LEAVES - 1: jnp.where(index < last, 0.0, -1e30).astype(F32),
    }


def weigh(kv, q2, g2):
    score = dot(kv[:, :FEAT], q2, (1, 1))
    top = peak(score)
    weight = jnp.exp(score - top)
    pgrad = dot(kv[:, FEAT:], g2, (1, 1))
    return weight, pgrad, (top, add_up(weight), add_up(weight * pgrad))


def combine(stats):
    top = stats[0][0]
    for stat in stats[1:]:
        top = jnp.maximum(top, stat[0])
    factors = [jnp.exp(stat[0] - top) for stat in stats]
    total = sum(factor * stat[1] for factor, stat in zip(factors, stats))
    mixed = sum(factor * stat[2] for factor, stat in zip(factors, stats))
    return top, total, mixed, factors


def scaled_queries(block):
    return by_head(block) * jnp.asarray(0.125, BF16)


def near_kernel(qn_ref, kv_ref, one_ref, g_ref, stat_ref):
    for b in range(LEAVES):
        block = slice(b * LEAF, (b + 1) * LEAF)
        q2 = scaled_queries(qn_ref[block])
        g2 = by_head(g_ref[block])
        half = (1 - b // 2) * LEAF
        stats = [
            weigh(kv_ref[(b + i - 1) * LEAF : (b + i) * LEAF], q2, g2)[2]
            for i in range(3)
            if HALO_PIECE.get(b) != i
        ]
        top, total, mixed = weigh(one_ref[half : half + LEAF], q2, g2)[2]
        stats.append((top + LN2, total, mixed))
        top, total, mixed, _ = combine(stats)
        stat_ref[b] = jnp.concatenate([top, total, mixed, jnp.zeros((5, 2 * LEAF), F32)], axis=0)


def attend_kernel(
    qn_ref, g_ref, near_ref, p1_ref, p2_ref, z_ref,
    stat_ref, cross, halo, p1o_ref, p2o_ref, zo_ref,
    q2_scr, g2_scr, weight_scr, pgrad_scr, low_scr, sgrad_scr, rims, cross_grad,
):
    index = lax.axis_index("seq")
    place = jnp.bitwise_and(index, 7)
    odd = jnp.bitwise_and(index, 1)
    peer_side = 1 - odd
    halo[peer_side] = p1_ref[:LEAF]
    halo[odd] = p2_ref[...]
    cross[:64] = z_ref[jnp.bitwise_xor(place, 1), FAR:]
    cross[64:128] = p1_ref[LEAF:]
    cross[128:192] = z_ref[jnp.bitwise_xor(place, 2), FAR:]
    cross[192:256] = z_ref[jnp.bitwise_xor(place, 3), FAR:]
    for i in range(4):
        cross[256 + 32 * i : 288 + 32 * i] = z_ref[jnp.bitwise_xor(place, 4 + i), FAR : FAR + 32]
    for s in range(8):
        for j in range(3):
            at = 384 + LEAF * j + 16 * s
            cross[at : at + 16] = z_ref[s, 16 * j : 16 * (j + 1)]

    outside = outside_bias()
    for b in range(LEAVES):
        block = slice(b * LEAF, (b + 1) * LEAF)
        lanes = slice(2 * b * LEAF, 2 * (b + 1) * LEAF)
        q2 = scaled_queries(qn_ref[block])
        g2 = by_head(g_ref[block])
        q2_scr[lanes] = q2
        g2_scr[lanes] = g2
        side = 0 if b == 0 else 1
        pieces = list(range(7 if b in HALO_PIECE else 6))
        stats = [(near_ref[b, 0:1], near_ref[b, 1:2], near_ref[b, 2:3])]
        for i in pieces:
            kv = cross[i * LEAF : (i + 1) * LEAF] if i < 6 else halo[side]
            weight, pgrad, (top, total, mixed) = weigh(kv, q2, g2)
            weight_scr[b, i] = weight
            pgrad_scr[b, i] = pgrad
            bias = (i + 2) * LN2 if i < 6 else outside[b]
            stats.append((top + bias, total, mixed))
        top, total, mixed, factors = combine(stats)
        inverse = 1.0 / total
        delta = mixed * inverse
        stat_ref[b] = jnp.concatenate(
            [top, inverse, delta, jnp.zeros((5, 2 * LEAF), F32)], axis=0
        )
        for i in pieces:
            prob = weight_scr[b, i] * (factors[i + 1] * inverse)
            low = prob.astype(BF16)
            sgrad = (prob * (pgrad_scr[b, i] - delta)).astype(BF16)
            if i < 6:
                low_scr[i * LEAF : (i + 1) * LEAF, lanes] = low
                sgrad_scr[i * LEAF : (i + 1) * LEAF, lanes] = sgrad
            else:
                rims[side, :, :FEAT] = dot(sgrad, q2, (1, 0)).astype(BF16)
                rims[side, :, FEAT:] = dot(low, g2, (1, 0)).astype(BF16)

    cross_grad[:, :FEAT] = dot(sgrad_scr[...], q2_scr[...], (1, 0)).astype(BF16)
    cross_grad[:, FEAT:] = dot(low_scr[...], g2_scr[...], (1, 0)).astype(BF16)
    p1o_ref[:LEAF] = rims[peer_side]
    p1o_ref[LEAF:] = cross_grad[64:128]
    p2o_ref[...] = rims[odd]
    for s in range(8):
        for j in range(3):
            at = 384 + LEAF * j + 16 * s
            zo_ref[s, 16 * j : 16 * (j + 1)] = cross_grad[at : at + 16]
    zo_ref[place, FAR:] = jnp.zeros((64, 2 * FEAT), BF16)
    zo_ref[jnp.bitwise_xor(place, 1), FAR:] = cross_grad[:64]
    zo_ref[jnp.bitwise_xor(place, 2), FAR:] = cross_grad[128:192]
    zo_ref[jnp.bitwise_xor(place, 3), FAR:] = cross_grad[192:256]
    for i in range(4):
        other = jnp.bitwise_xor(place, 4 + i)
        zo_ref[other, FAR : FAR + 32] = cross_grad[256 + 32 * i : 288 + 32 * i]
        zo_ref[other, FAR + 32 :] = jnp.zeros((32, 2 * FEAT), BF16)


def after_kernel(
    stat_ref, qn_ref, kv_ref, one_ref, g_ref, halo, cross,
    att_ref, nqg_ref, tok_ref, near, near_grad, one_grad,
):
    near[:LEAF] = halo[0]
    near[LEAF : LEAF + ROWS] = kv_ref[...]
    near[LEAF + ROWS :] = halo[1]
    near_grad[...] = jnp.zeros_like(near_grad)
    one_grad[...] = jnp.zeros_like(one_grad)
    feature = iota((FEAT, LEAF), 0)
    bias = far_bias()
    outside = outside_bias()

    def merge_heads(transposed):
        return jnp.where(feature < HEAD, transposed[:, :LEAF], transposed[:, LEAF:]).T

    for b in range(LEAVES):
        rows = slice(b * LEAF, (b + 1) * LEAF)
        near_rows = slice(b * LEAF, (b + 3) * LEAF)
        half = (1 - b // 2) * LEAF
        q2 = scaled_queries(qn_ref[rows])
        g2 = by_head(g_ref[rows])
        kv = jnp.concatenate([near[near_rows], one_ref[half : half + LEAF], cross[...]], axis=0)
        keys = kv[:, :FEAT]
        values = kv[:, FEAT:]
        raw = dot(keys, q2, (1, 1))
        before, after = raw[:LEAF], raw[2 * LEAF : 3 * LEAF]
        if b == 0:
            before = before + outside[b]
        if b == LEAVES - 1:
            after = after + outside[b]
        scores = jnp.concatenate(
            [before, raw[LEAF : 2 * LEAF], after, raw[3 * LEAF :] + bias], axis=0
        )
        probs = jnp.exp(scores - stat_ref[b, 0:1]) * stat_ref[b, 1:2]
        low = probs.astype(BF16)
        score_grad = (probs * (dot(values, g2, (1, 1)) - stat_ref[b, 2:3])).astype(BF16)
        att_ref[rows] = merge_heads(dot(values, low, (0, 0))).astype(BF16)
        nqg_ref[rows] = merge_heads(dot(keys, score_grad, (0, 0))) * 0.125
        for part, lanes in (
            (dot(score_grad[: 4 * LEAF], q2, (1, 0)), slice(0, FEAT)),
            (dot(low[: 4 * LEAF], g2, (1, 0)), slice(FEAT, 2 * FEAT)),
        ):
            near_grad[near_rows, lanes] += part[: 3 * LEAF]
            one_grad[half : half + LEAF, lanes] += part[3 * LEAF :]
    spread = spreading(0, 256, 1).astype(BF16)
    high = one_grad[...].astype(BF16)
    rest = (one_grad[...] - high.astype(F32)).astype(BF16)
    tok_ref[...] = near_grad[LEAF : LEAF + ROWS] + dot(spread, high, (1, 0)) + dot(spread, rest, (1, 0))


def column_kernel(z_ref, p1_ref, tok_ref, out_ref, mid_ref):
    index = lax.axis_index("seq")
    column = jnp.right_shift(index, 3)
    place = jnp.bitwise_and(index, 7)
    far = jnp.sum(z_ref[:, :FAR].astype(F32), axis=0).astype(BF16)
    slots = dot(far_pick((112, FAR), 1), far, (1, 0)).astype(BF16)
    out_ref[column] = jnp.zeros((16, 2 * FEAT), BF16)
    for d in range(1, 8):
        out_ref[jnp.bitwise_xor(column, d)] = slots[16 * (d - 1) : 16 * d]
    for d in range(1, 8):
        at, rows = MID_ROWS[d]
        mid_ref[at : at + rows] = z_ref[jnp.bitwise_xor(place, d), FAR : FAR + rows]


def middle_kernel(tok_ref, p1_ref, mid_ref, qk_ref, qg_ref, nqg_ref, acc_ref, sum_ref):
    odd = jnp.bitwise_and(lax.axis_index("seq"), 1)
    maps = [spreading(0, MID_ROWS[d][1], ROW_LEVEL[d]) for d in range(1, 8)]
    spread = jnp.concatenate(maps + [spreading(64, 64, 2)], axis=1).astype(BF16)
    rows = jnp.concatenate([mid_ref[...], p1_ref[LEAF:]], axis=0)
    acc_ref[...] = tok_ref[...] + dot(spread, rows, (1, 0))
    acc_ref[pl.ds(pl.multiple_of((1 - odd) * 384, LEAF), LEAF)] += p1_ref[:LEAF].astype(F32)
    sums = token_sums(qk_ref[0].astype(F32) * qg_ref[...] * nqg_ref[...])
    sum_ref[...] = jnp.concatenate(sums + [jnp.zeros((LEAVES, FEAT), F32)], axis=0)


def total_kernel(acc_ref, p2_ref, y_ref, qk_ref, kg_ref, qsum_ref, nkg_ref, vg_ref, sum_ref, grads):
    index = lax.axis_index("seq")
    column = jnp.right_shift(index, 3)
    odd = jnp.bitwise_and(index, 1)
    pieces = [y_ref[jnp.bitwise_xor(column, d)] for d in range(1, 8)]
    maps = [spreading(0, 16, COLUMN_LEVEL[d]) for d in range(1, 8)]
    spread = jnp.concatenate(maps, axis=1).astype(BF16)
    grads[...] = acc_ref[...] + dot(spread, jnp.concatenate(pieces, axis=0), (1, 0))
    grads[pl.ds(pl.multiple_of(odd * 384, LEAF), LEAF)] += p2_ref[...].astype(F32)
    vg_ref[...] = grads[:, FEAT:].astype(BF16)
    key_total = grads[:, :FEAT]
    nkg_ref[...] = key_total
    sums = token_sums(qk_ref[1].astype(F32) * kg_ref[...] * key_total)
    tile = jnp.concatenate([qsum_ref[:LEAVES]] + sums, axis=0)
    for i in range(sum_ref.shape[0]):
        sum_ref[i] = tile


def finish_kernel(width, sq_ref, inner_ref, qk_ref, qg_ref, kg_ref, nqg_ref, nkg_ref, dq_ref, dk_ref):
    rate = lax.rsqrt(jnp.sum(sq_ref[...], axis=0) / width + EPS)
    inner = jnp.sum(inner_ref[...], axis=0) / width
    cubed = rate * rate * rate * inner
    for first, x_ref, gain_ref, grad_ref, out_ref in (
        (0, qk_ref.at[0], qg_ref, nqg_ref, dq_ref),
        (4, qk_ref.at[1], kg_ref, nkg_ref, dk_ref),
    ):
        out_ref[...] = (
            spread_tokens(rate, first) * gain_ref[...] * grad_ref[...]
            - x_ref[...].astype(F32) * spread_tokens(cubed, first)
        ).astype(BF16)


def call(kernel, outs, args, scratch=(), flops=0, name=None, spaces=None):
    many = isinstance(outs, list)
    moved = sum(math.prod(x.shape) * x.dtype.itemsize for x in list(args) + (outs if many else [outs]))
    return pl.pallas_call(
        kernel,
        out_shape=outs,
        in_specs=[pl.BlockSpec(memory_space=space) for space in spaces or [pltpu.VMEM] * len(args)],
        scratch_shapes=list(scratch),
        compiler_params=PARAMS,
        cost_estimate=pl.CostEstimate(flops=flops, bytes_accessed=moved, transcendentals=0),
        name=name,
    )(*args)


def sds(*shape, dtype=BF16):
    return jax.ShapeDtypeStruct(shape, dtype)


ROW_GROUPS = [[8 * y + z for z in range(8)] for y in range(8)]
COLUMN_GROUPS = [[8 * y + z for y in range(8)] for z in range(8)]


def exchange(x, axis, groups=None):
    return lax.all_to_all(x, axis, 0, 0, axis_index_groups=groups, tiled=True)


def local(queries, key_rows, value_rows, query_gain, key_gain, out_grad):
    seq = lax.axis_size("seq")
    heads = lax.axis_size("head")
    width = float(heads * FEAT)
    qg = query_gain.reshape(1, FEAT)
    kg = key_gain.reshape(1, FEAT)
    peer = [(i, i ^ 1) for i in range(seq)]
    beside = [(i, i + 1) for i in range(1, seq - 1, 2)] + [(i + 1, i) for i in range(1, seq - 1, 2)]

    qk = jnp.stack([queries, key_rows])
    squares = call(squares_kernel, sds(heads, 8, FEAT, dtype=F32), (qk,), name="squares")
    squares = exchange(squares, "head")
    qn, kv, one, lv, ysend, p1, p2 = call(
        lambda *refs: norm_kernel(width, *refs),
        [sds(ROWS, FEAT), sds(ROWS, 256), sds(256, 256), sds(224, 256), sds(8, 16, 256), sds(192, 256), sds(LEAF, 256)],
        (squares, qk, value_rows, qg, kg),
        name="norm",
    )
    p1 = lax.ppermute(p1, "seq", peer)
    p2 = lax.ppermute(p2, "seq", beside)
    yrecv = exchange(ysend, "seq", COLUMN_GROUPS)
    zsend = call(
        row_kernel,
        sds(8, SLOT, 256),
        (yrecv, lv, p2),
        spaces=[pltpu.VMEM, pltpu.VMEM, pl.ANY],
        name="rows",
    )
    zrecv = exchange(zsend, "seq", ROW_GROUPS)
    near = call(
        near_kernel,
        sds(LEAVES, 8, 256, dtype=F32),
        (qn, kv, one, out_grad),
        flops=14 * 2 * 2 * 256 * LEAF * FEAT,
        name="near",
    )
    stat, cross, halo, p1, p2, zsend = call(
        attend_kernel,
        [sds(LEAVES, 8, 256, dtype=F32), sds(768, 256), sds(2, LEAF, 256)]
        + [sds(192, 256), sds(LEAF, 256), sds(8, SLOT, 256)],
        (qn, out_grad, near, p1, p2, zrecv),
        scratch=[
            pltpu.VMEM((1024, FEAT), BF16),
            pltpu.VMEM((1024, FEAT), BF16),
            pltpu.VMEM((LEAVES, 7, LEAF, 256), F32),
            pltpu.VMEM((LEAVES, 7, LEAF, 256), F32),
            pltpu.VMEM((768, 1024), BF16),
            pltpu.VMEM((768, 1024), BF16),
            pltpu.VMEM((2, LEAF, 256), BF16),
            pltpu.VMEM((768, 256), BF16),
        ],
        flops=4 * 4 * 2 * 256 * 768 * FEAT,
        name="attend",
    )
    p1 = lax.ppermute(p1, "seq", peer)
    p2 = lax.ppermute(p2, "seq", beside)
    zrecv = exchange(zsend, "seq", ROW_GROUPS)
    attended, nqg, tok = call(
        after_kernel,
        [sds(ROWS, FEAT), sds(ROWS, FEAT, dtype=F32), sds(ROWS, 256, dtype=F32)],
        (stat, qn, kv, one, out_grad, halo, cross),
        scratch=[
            pltpu.VMEM((768, 256), BF16),
            pltpu.VMEM((768, 256), F32),
            pltpu.VMEM((256, 256), F32),
        ],
        flops=4 * 5 * 2 * 256 * KEYS * FEAT,
        name="after",
    )
    ysend, mid = call(
        column_kernel,
        [sds(8, 16, 256), sds(320, 256)],
        (zrecv, p1, tok),
        spaces=[pltpu.VMEM, pl.ANY, pl.ANY],
        name="columns",
    )
    yrecv = exchange(ysend, "seq", COLUMN_GROUPS)
    acc, qsum = call(
        middle_kernel,
        [sds(ROWS, 256, dtype=F32), sds(8, FEAT, dtype=F32)],
        (tok, p1, mid, qk, qg, nqg),
        flops=2 * ROWS * 384 * 256,
        name="middle",
    )
    nkg, value_grad, inner = call(
        total_kernel,
        [sds(ROWS, FEAT, dtype=F32), sds(ROWS, FEAT), sds(heads, 8, FEAT, dtype=F32)],
        (acc, p2, yrecv, qk, kg, qsum),
        scratch=[pltpu.VMEM((ROWS, 256), F32)],
        name="total",
    )
    inner = exchange(inner, "head")
    query_grad, key_grad = call(
        lambda *refs: finish_kernel(width, *refs),
        [sds(ROWS, FEAT), sds(ROWS, FEAT)],
        (squares, inner, qk, qg, kg, nqg, nkg),
        name="finish",
    )
    return (attended, query_grad, key_grad, value_grad)


def solution(mesh):
    placed = (
        P("seq", "head"),
        P("seq", "head"),
        P("seq", "head"),
        P("head"),
        P("head"),
        P("seq", "head"),
    )
    return jax.shard_map(
        local,
        mesh=mesh,
        in_specs=placed,
        out_specs=(P("seq", "head"), P("seq", "head"), P("seq", "head"), P("seq", "head")),
        check_vma=False,
    )
```

```python
import math

import jax
import jax.numpy as jnp
from jax import lax
from jax.experimental import pallas as pl
from jax.experimental.pallas import tpu as pltpu
from jax.sharding import PartitionSpec as P

ROWS = 512
FEAT = 128
LEAF = 128
LEAVES = 4
HEAD = 64
KEYS = 1280
EPS = 1e-06
LN2 = math.log(2.0)
F32 = jnp.float32
BF16 = jnp.bfloat16
BLOCKS = [pl.ds(i * LEAF, LEAF) for i in range(LEAVES)]
ROW_LEVEL = {1: 2, 2: 3, 3: 3, 4: 4, 5: 4, 6: 4, 7: 4}
COLUMN_LEVEL = {1: 5, 2: 6, 3: 6, 4: 7, 5: 7, 6: 7, 7: 7}
FAR = 48
SLOT = 112


def dot(a, b, dims):
    return lax.dot_general(a, b, ((dims[:1], dims[1:]), ((), ())), preferred_element_type=F32)


def iota(shape, axis):
    return lax.broadcasted_iota(jnp.int32, shape, axis)


def pooling(rows, level):
    token = iota((rows, ROWS), 1)
    hit = jnp.right_shift(token, level) == iota((rows, ROWS), 0)
    return jnp.where(hit, 2.0**-level, 0.0)


def spreading(first, rows, level):
    token = iota((ROWS, rows), 0)
    hit = jnp.right_shift(token, level) == iota((ROWS, rows), 1) + first
    return jnp.where(hit, 2.0**-level, 0.0)


def far_pick(shape, far_axis):
    far = iota(shape, far_axis)
    slot_row = iota(shape, 1 - far_axis)
    mid = far - 16
    low = far - 32
    column = jnp.where(
        far < 16,
        far,
        jnp.where(
            far < 32,
            (1 + jnp.right_shift(mid, 3)) * 16 + jnp.bitwise_and(mid, 7),
            (3 + jnp.right_shift(low, 2)) * 16 + jnp.bitwise_and(low, 3),
        ),
    )
    return jnp.where(column == slot_row, 1.0, 0.0).astype(BF16)


def token_sums(x):
    return [
        jnp.sum(x[i * LEAF : (i + 1) * LEAF].T, axis=0, keepdims=True) for i in range(LEAVES)
    ]


def spread_tokens(tile, first):
    return jnp.concatenate(
        [
            jnp.broadcast_to(tile[first + i : first + i + 1], (LEAF, LEAF)).T
            for i in range(LEAVES)
        ],
        axis=0,
    )


def squares_kernel(q_in, k_in, qg_in, kg_in, out_ref, rows, gains, sems):
    copies = []
    for i in range(2 * LEAVES):
        source = (q_in if i < LEAVES else k_in).at[pl.ds((i % LEAVES) * LEAF, LEAF)]
        copies.append(pltpu.make_async_copy(source, rows.at[i], sems.at[i]))
    for i, source in enumerate((qg_in, kg_in)):
        copies.append(pltpu.make_async_copy(source, gains.at[i], sems.at[2 * LEAVES + i]))
    for copy in copies:
        copy.start()
    sums = []
    for i in range(2 * LEAVES):
        copies[i].wait()
        x = rows[i].astype(F32)
        sums.append(jnp.sum((x * x).T, axis=0, keepdims=True))
    for copy in copies[2 * LEAVES :]:
        copy.wait()
    tile = jnp.concatenate(sums + [gains[0], gains[1], jnp.zeros((6, FEAT), F32)], axis=0)
    for i in range(out_ref.shape[0]):
        out_ref[i] = tile


def rates(width, sum_ref):
    return lax.rsqrt(jnp.sum(sum_ref[:, :8], axis=0) / width + EPS)


def norm_kernel(width, sum_ref, k_ref, v_ref, kv_ref, one_ref, lv_ref, y_ref, p1_ref, p2_ref):
    index = lax.axis_index("seq")
    column = jnp.right_shift(index, 3)
    odd = jnp.bitwise_and(index, 1)
    gain = sum_ref[lax.axis_index("head"), 9:10]
    kv_ref[:, :FEAT] = (
        k_ref[...].astype(F32) * spread_tokens(rates(width, sum_ref), 4) * gain
    ).astype(BF16)
    kv_ref[:, FEAT:] = v_ref[...]
    pool = jnp.concatenate(
        [pooling(ROWS >> level, level) for level in (1, 2, 3, 4)]
        + [pooling(16, COLUMN_LEVEL[d]) for d in range(1, 8)],
        axis=0,
    ).astype(BF16)
    coarse = dot(pool, kv_ref[...], (1, 0)).astype(BF16)
    one_ref[...] = coarse[:256]
    lv_ref[...] = coarse[256:480]
    y_ref[column] = jnp.zeros((16, 2 * FEAT), BF16)
    for d in range(1, 8):
        y_ref[jnp.bitwise_xor(column, d)] = coarse[464 + 16 * d : 480 + 16 * d]
    p1_ref[:LEAF] = kv_ref[pl.ds(pl.multiple_of((1 - odd) * 384, LEAF), LEAF)]
    p1_ref[LEAF:] = coarse[320:384]
    p2_ref[...] = kv_ref[pl.ds(pl.multiple_of(odd * 384, LEAF), LEAF)]


def start_all(copies):
    for copy in copies:
        copy.start()
    return copies


def wait_all(copies):
    for copy in copies:
        copy.wait()


def row_kernel(y_ref, lv_ref, out_ref, slots_scr, sems):
    index = lax.axis_index("seq")
    column = jnp.right_shift(index, 3)
    place = jnp.bitwise_and(index, 7)
    slots = jnp.concatenate([y_ref[jnp.bitwise_xor(column, d)] for d in range(1, 8)], axis=0)
    far = dot(far_pick((FAR, 112), 0), slots, (1, 0)).astype(BF16)
    copies = []
    for d in range(8):
        slots_scr[d, :FAR] = far
        if d == 0:
            slots_scr[d, FAR:] = jnp.zeros((64, 2 * FEAT), BF16)
        elif d == 1:
            slots_scr[d, FAR:] = lv_ref[:64]
        elif d < 4:
            slots_scr[d, FAR:] = lv_ref[128:192]
        else:
            slots_scr[d, FAR : FAR + 32] = lv_ref[192:224]
            slots_scr[d, FAR + 32 :] = jnp.zeros((32, 2 * FEAT), BF16)
        target = out_ref.at[jnp.bitwise_xor(place, d)]
        copies += start_all([pltpu.make_async_copy(slots_scr.at[d], target, sems.at[d])])
    wait_all(copies)


def by_head(block):
    lane = iota((LEAF, FEAT), 1)
    zero = jnp.zeros((LEAF, FEAT), BF16)
    return jnp.concatenate(
        [jnp.where(lane < HEAD, block, zero), jnp.where(lane < HEAD, zero, block)], axis=0
    )


def peak(x):
    return jnp.max(x, axis=0, keepdims=True)


def add_up(x):
    return jnp.sum(x, axis=0, keepdims=True)


HALO_PIECE = {0: 0, LEAVES - 1: 2}


def far_bias():
    return jnp.concatenate(
        [jnp.full((LEAF, 2 * LEAF), level * LN2, F32) for level in range(1, 8)], axis=0
    )


def outside_bias():
    index = lax.axis_index("seq")
    last = lax.axis_size("seq") - 1
    return {
        0: jnp.where(index > 0, 0.0, -1e30).astype(F32),
        LEAVES - 1: jnp.where(index < last, 0.0, -1e30).astype(F32),
    }


def weigh(kv, q2, g2):
    score = dot(kv[:, :FEAT], q2, (1, 1))
    top = peak(score)
    weight = jnp.exp(score - top)
    pgrad = dot(kv[:, FEAT:], g2, (1, 1))
    return weight, pgrad, (top, add_up(weight), add_up(weight * pgrad))


def combine(stats):
    top = stats[0][0]
    for stat in stats[1:]:
        top = jnp.maximum(top, stat[0])
    factors = [jnp.exp(stat[0] - top) for stat in stats]
    total = sum(factor * stat[1] for factor, stat in zip(factors, stats))
    mixed = sum(factor * stat[2] for factor, stat in zip(factors, stats))
    return top, total, mixed, factors


def scaled_queries(block):
    return by_head(block) * jnp.asarray(0.125, BF16)


def near_kernel(width, sum_ref, q_ref, kv_ref, one_ref, g_ref, qn_ref, stat_ref):
    gain = sum_ref[lax.axis_index("head"), 8:9]
    qn_ref[...] = (
        q_ref[...].astype(F32) * spread_tokens(rates(width, sum_ref), 0) * gain
    ).astype(BF16)
    for b in range(LEAVES):
        block = slice(b * LEAF, (b + 1) * LEAF)
        q2 = scaled_queries(qn_ref[block])
        g2 = by_head(g_ref[block])
        half = (1 - b // 2) * LEAF
        stats = [
            weigh(kv_ref[(b + i - 1) * LEAF : (b + i) * LEAF], q2, g2)[2]
            for i in range(3)
            if HALO_PIECE.get(b) != i
        ]
        top, total, mixed = weigh(one_ref[half : half + LEAF], q2, g2)[2]
        stats.append((top + LN2, total, mixed))
        top, total, mixed, _ = combine(stats)
        stat_ref[b] = jnp.concatenate([top, total, mixed, jnp.zeros((5, 2 * LEAF), F32)], axis=0)


def attend_kernel(
    qn_ref, g_ref, near_ref, p1_ref, p2_ref, z_ref,
    stat_ref, cross, halo, p1o_ref, p2o_ref, zo_ref,
    q2_scr, g2_scr, weight_scr, pgrad_scr, low_scr, sgrad_scr, rims, mid_grad, far_scr, mid_scr, sems,
):
    index = lax.axis_index("seq")
    place = jnp.bitwise_and(index, 7)
    odd = jnp.bitwise_and(index, 1)
    peer_side = 1 - odd
    halo[peer_side] = p1_ref[:LEAF]
    halo[odd] = p2_ref[...]
    cross[:64] = z_ref[jnp.bitwise_xor(place, 1), FAR:]
    cross[64:128] = p1_ref[LEAF:]
    cross[128:192] = z_ref[jnp.bitwise_xor(place, 2), FAR:]
    cross[192:256] = z_ref[jnp.bitwise_xor(place, 3), FAR:]
    for i in range(4):
        cross[256 + 32 * i : 288 + 32 * i] = z_ref[jnp.bitwise_xor(place, 4 + i), FAR : FAR + 32]
    for s in range(8):
        for j in range(3):
            at = 384 + LEAF * j + 16 * s
            cross[at : at + 16] = z_ref[s, 16 * j : 16 * (j + 1)]

    outside = outside_bias()
    for b in range(LEAVES):
        block = slice(b * LEAF, (b + 1) * LEAF)
        lanes = slice(2 * b * LEAF, 2 * (b + 1) * LEAF)
        q2 = scaled_queries(qn_ref[block])
        g2 = by_head(g_ref[block])
        q2_scr[lanes] = q2
        g2_scr[lanes] = g2
        side = 0 if b == 0 else 1
        pieces = list(range(7 if b in HALO_PIECE else 6))
        stats = [(near_ref[b, 0:1], near_ref[b, 1:2], near_ref[b, 2:3])]
        for i in pieces:
            kv = cross[i * LEAF : (i + 1) * LEAF] if i < 6 else halo[side]
            weight, pgrad, (top, total, mixed) = weigh(kv, q2, g2)
            weight_scr[b, i] = weight
            pgrad_scr[b, i] = pgrad
            bias = (i + 2) * LN2 if i < 6 else outside[b]
            stats.append((top + bias, total, mixed))
        top, total, mixed, factors = combine(stats)
        inverse = 1.0 / total
        delta = mixed * inverse
        stat_ref[b] = jnp.concatenate(
            [top, inverse, delta, jnp.zeros((5, 2 * LEAF), F32)], axis=0
        )
        for i in pieces:
            prob = weight_scr[b, i] * (factors[i + 1] * inverse)
            low = prob.astype(BF16)
            sgrad = (prob * (pgrad_scr[b, i] - delta)).astype(BF16)
            if i < 6:
                low_scr[i * LEAF : (i + 1) * LEAF, lanes] = low
                sgrad_scr[i * LEAF : (i + 1) * LEAF, lanes] = sgrad
            else:
                rims[side, :, :FEAT] = dot(sgrad, q2, (1, 0)).astype(BF16)
                rims[side, :, FEAT:] = dot(low, g2, (1, 0)).astype(BF16)

    def grads(rows):
        keys = dot(sgrad_scr[rows], q2_scr[...], (1, 0))
        values = dot(low_scr[rows], g2_scr[...], (1, 0))
        return jnp.concatenate([keys, values], axis=1).astype(BF16)

    for j in range(3):
        far = grads(slice(384 + LEAF * j, 384 + LEAF * (j + 1)))
        for s in range(8):
            far_scr[s, 16 * j : 16 * (j + 1)] = far[16 * s : 16 * (s + 1)]
    copies = start_all(
        [
            pltpu.make_async_copy(far_scr.at[s], zo_ref.at[s, pl.ds(0, FAR)], sems.at[s])
            for s in range(8)
        ]
    )
    mid_grad[...] = grads(slice(0, 384))
    mid_scr[...] = jnp.zeros_like(mid_scr)
    mid_scr[1] = mid_grad[:64]
    mid_scr[2] = mid_grad[128:192]
    mid_scr[3] = mid_grad[192:256]
    for i in range(4):
        mid_scr[4 + i, :32] = mid_grad[256 + 32 * i : 288 + 32 * i]
    copies += start_all(
        [
            pltpu.make_async_copy(
                mid_scr.at[d],
                zo_ref.at[jnp.bitwise_xor(place, d), pl.ds(FAR, 64)],
                sems.at[8 + d],
            )
            for d in range(8)
        ]
    )
    p1o_ref[:LEAF] = rims[peer_side]
    p1o_ref[LEAF:] = mid_grad[64:128]
    p2o_ref[...] = rims[odd]
    wait_all(copies)


def after_kernel(
    stat_ref, qn_ref, kv_ref, one_ref, g_ref, halo, cross, sum_ref, q_ref,
    att_ref, nqg_ref, tok_ref, qsum_ref, near, near_grad, one_grad,
):
    near[:LEAF] = halo[0]
    near[LEAF : LEAF + ROWS] = kv_ref[...]
    near[LEAF + ROWS :] = halo[1]
    near_grad[...] = jnp.zeros_like(near_grad)
    one_grad[...] = jnp.zeros_like(one_grad)
    feature = iota((FEAT, LEAF), 0)
    bias = far_bias()
    outside = outside_bias()

    def merge_heads(transposed):
        return jnp.where(feature < HEAD, transposed[:, :LEAF], transposed[:, LEAF:]).T

    for b in range(LEAVES):
        rows = slice(b * LEAF, (b + 1) * LEAF)
        near_rows = slice(b * LEAF, (b + 3) * LEAF)
        half = (1 - b // 2) * LEAF
        q2 = scaled_queries(qn_ref[rows])
        g2 = by_head(g_ref[rows])
        kv = jnp.concatenate([near[near_rows], one_ref[half : half + LEAF], cross[...]], axis=0)
        keys = kv[:, :FEAT]
        values = kv[:, FEAT:]
        raw = dot(keys, q2, (1, 1))
        before, after = raw[:LEAF], raw[2 * LEAF : 3 * LEAF]
        if b == 0:
            before = before + outside[b]
        if b == LEAVES - 1:
            after = after + outside[b]
        scores = jnp.concatenate(
            [before, raw[LEAF : 2 * LEAF], after, raw[3 * LEAF :] + bias], axis=0
        )
        probs = jnp.exp(scores - stat_ref[b, 0:1]) * stat_ref[b, 1:2]
        low = probs.astype(BF16)
        score_grad = (probs * (dot(values, g2, (1, 1)) - stat_ref[b, 2:3])).astype(BF16)
        att_ref[rows] = merge_heads(dot(values, low, (0, 0))).astype(BF16)
        nqg_ref[rows] = merge_heads(dot(keys, score_grad, (0, 0))) * 0.125
        for part, lanes in (
            (dot(score_grad[: 4 * LEAF], q2, (1, 0)), slice(0, FEAT)),
            (dot(low[: 4 * LEAF], g2, (1, 0)), slice(FEAT, 2 * FEAT)),
        ):
            near_grad[near_rows, lanes] += part[: 3 * LEAF]
            one_grad[half : half + LEAF, lanes] += part[3 * LEAF :]
    spread = spreading(0, 256, 1).astype(BF16)
    high = one_grad[...].astype(BF16)
    rest = (one_grad[...] - high.astype(F32)).astype(BF16)
    tok_ref[...] = near_grad[LEAF : LEAF + ROWS] + dot(spread, high, (1, 0)) + dot(spread, rest, (1, 0))
    gains = sum_ref[lax.axis_index("head"), 8:16]
    sums = token_sums(q_ref[...].astype(F32) * gains[0:1] * nqg_ref[...])
    qsum_ref[...] = jnp.concatenate(sums + [gains[1:2], jnp.zeros((3, FEAT), F32)], axis=0)


def column_kernel(z_ref, p1_ref, p2_ref, tok_ref, out_ref, far_rows, sem):
    column = jnp.right_shift(lax.axis_index("seq"), 3)
    copy = pltpu.make_async_copy(z_ref.at[:, pl.ds(0, FAR)], far_rows, sem)
    copy.start()
    copy.wait()
    far = jnp.sum(far_rows[...].astype(F32), axis=0).astype(BF16)
    slots = dot(far_pick((112, FAR), 1), far, (1, 0)).astype(BF16)
    out_ref[column] = jnp.zeros((16, 2 * FEAT), BF16)
    for d in range(1, 8):
        out_ref[jnp.bitwise_xor(column, d)] = slots[16 * (d - 1) : 16 * d]


def total_kernel(
    tok_ref, p1_ref, p2_ref, z_ref, y_ref, k_ref, qsum_ref,
    nkg_ref, vg_ref, sum_ref, acc, value_rows, sems,
):
    index = lax.axis_index("seq")
    column = jnp.right_shift(index, 3)
    place = jnp.bitwise_and(index, 7)
    odd = jnp.bitwise_and(index, 1)
    pieces = [z_ref[jnp.bitwise_xor(place, 1), FAR:], p1_ref[LEAF:]]
    maps = [spreading(0, 64, 2), spreading(64, 64, 2)]
    for d in range(2, 8):
        rows = ROWS >> ROW_LEVEL[d]
        pieces.append(z_ref[jnp.bitwise_xor(place, d), FAR : FAR + rows])
        maps.append(spreading(0, rows, ROW_LEVEL[d]))
    for d in range(1, 8):
        pieces.append(y_ref[jnp.bitwise_xor(column, d)])
        maps.append(spreading(0, 16, COLUMN_LEVEL[d]))
    spread = jnp.concatenate(maps, axis=1).astype(BF16)
    acc[...] = tok_ref[...] + dot(spread, jnp.concatenate(pieces, axis=0), (1, 0))
    acc[pl.ds(pl.multiple_of((1 - odd) * 384, LEAF), LEAF)] += p1_ref[:LEAF].astype(F32)
    acc[pl.ds(pl.multiple_of(odd * 384, LEAF), LEAF)] += p2_ref[...].astype(F32)
    value_rows[...] = acc[:, FEAT:].astype(BF16)
    copies = start_all(
        [
            pltpu.make_async_copy(value_rows.at[rows], vg_ref.at[rows], sems.at[i])
            for i, rows in enumerate(BLOCKS)
        ]
    )
    key_total = acc[:, :FEAT]
    nkg_ref[...] = key_total
    sums = token_sums(k_ref[...].astype(F32) * qsum_ref[LEAVES : LEAVES + 1] * key_total)
    tile = jnp.concatenate([qsum_ref[:LEAVES]] + sums, axis=0)
    for i in range(sum_ref.shape[0]):
        sum_ref[i] = tile
    wait_all(copies)


def finish_kernel(
    width, sq_ref, inner_ref, q_ref, k_ref, nqg_ref, nkg_ref,
    dq_ref, dk_ref, results, sems,
):
    rate = rates(width, sq_ref)
    inner = jnp.sum(inner_ref[...], axis=0) / width
    cubed = rate * rate * rate * inner
    copies = []
    gains = sq_ref[lax.axis_index("head"), 8:16]
    for side, (x_ref, grad_ref, out_ref) in enumerate(
        ((q_ref, nqg_ref, dq_ref), (k_ref, nkg_ref, dk_ref))
    ):
        results[side] = (
            spread_tokens(rate, 4 * side) * gains[side : side + 1] * grad_ref[...]
            - x_ref[...].astype(F32) * spread_tokens(cubed, 4 * side)
        ).astype(BF16)
        copies += start_all(
            [
                pltpu.make_async_copy(
                    results.at[side, rows], out_ref.at[rows], sems.at[LEAVES * side + i]
                )
                for i, rows in enumerate(BLOCKS)
            ]
        )
    wait_all(copies)


def call(kernel, outs, args, scratch=(), flops=0, name=None, spaces=None, out_spaces=None, vmem=40):
    many = isinstance(outs, list)
    moved = sum(math.prod(x.shape) * x.dtype.itemsize for x in list(args) + (outs if many else [outs]))
    out_spaces = out_spaces or [pltpu.VMEM] * (len(outs) if many else 1)
    out_specs = [pl.BlockSpec(memory_space=space) for space in out_spaces]
    return pl.pallas_call(
        kernel,
        out_shape=outs,
        in_specs=[pl.BlockSpec(memory_space=space) for space in spaces or [pltpu.VMEM] * len(args)],
        out_specs=out_specs if many else out_specs[0],
        scratch_shapes=list(scratch),
        compiler_params=pltpu.CompilerParams(vmem_limit_bytes=vmem * 1024 * 1024),
        cost_estimate=pl.CostEstimate(flops=flops, bytes_accessed=moved, transcendentals=0),
        name=name,
    )(*args)


def sds(*shape, dtype=BF16):
    return jax.ShapeDtypeStruct(shape, dtype)


ROW_GROUPS = [[8 * y + z for z in range(8)] for y in range(8)]
COLUMN_GROUPS = [[8 * y + z for y in range(8)] for z in range(8)]


def exchange(x, axis, groups=None):
    return lax.all_to_all(x, axis, 0, 0, axis_index_groups=groups, tiled=True)


def local(queries, key_rows, value_rows, query_gain, key_gain, out_grad):
    seq = lax.axis_size("seq")
    heads = lax.axis_size("head")
    width = float(heads * FEAT)
    qg = query_gain.reshape(1, FEAT)
    kg = key_gain.reshape(1, FEAT)
    peer = [(i, i ^ 1) for i in range(seq)]
    beside = [(i, i + 1) for i in range(1, seq - 1, 2)] + [(i + 1, i) for i in range(1, seq - 1, 2)]

    squares = call(
        squares_kernel,
        sds(heads, 16, FEAT, dtype=F32),
        (queries, key_rows, qg, kg),
        scratch=[
            pltpu.VMEM((2 * LEAVES, LEAF, FEAT), BF16),
            pltpu.VMEM((2, 1, FEAT), F32),
            pltpu.SemaphoreType.DMA((2 * LEAVES + 2,)),
        ],
        spaces=[pl.ANY] * 4,
        vmem=60,
        name="squares",
    )
    squares = exchange(squares, "head")
    kv, one, lv, ysend, p1, p2 = call(
        lambda *refs: norm_kernel(width, *refs),
        [sds(ROWS, 256), sds(256, 256), sds(224, 256), sds(8, 16, 256), sds(192, 256), sds(LEAF, 256)],
        (squares, key_rows, value_rows),
        name="norm",
    )
    p1 = lax.ppermute(p1, "seq", peer)
    p2 = lax.ppermute(p2, "seq", beside)
    yrecv = exchange(ysend, "seq", COLUMN_GROUPS)
    zsend = call(
        row_kernel,
        sds(8, SLOT, 256),
        (yrecv, lv),
        scratch=[pltpu.VMEM((8, SLOT, 256), BF16), pltpu.SemaphoreType.DMA((8,))],
        out_spaces=[pl.ANY],
        name="rows",
    )
    zrecv = exchange(zsend, "seq", ROW_GROUPS)
    qn, near = call(
        lambda *refs: near_kernel(width, *refs),
        [sds(ROWS, FEAT), sds(LEAVES, 8, 256, dtype=F32)],
        (squares, queries, kv, one, out_grad),
        flops=14 * 2 * 2 * 256 * LEAF * FEAT,
        name="near",
    )
    stat, cross, halo, p1, p2, zsend = call(
        attend_kernel,
        [sds(LEAVES, 8, 256, dtype=F32), sds(768, 256), sds(2, LEAF, 256)]
        + [sds(192, 256), sds(LEAF, 256), sds(8, SLOT, 256)],
        (qn, out_grad, near, p1, p2, zrecv),
        scratch=[
            pltpu.VMEM((1024, FEAT), BF16),
            pltpu.VMEM((1024, FEAT), BF16),
            pltpu.VMEM((LEAVES, 7, LEAF, 256), F32),
            pltpu.VMEM((LEAVES, 7, LEAF, 256), F32),
            pltpu.VMEM((768, 1024), BF16),
            pltpu.VMEM((768, 1024), BF16),
            pltpu.VMEM((2, LEAF, 256), BF16),
            pltpu.VMEM((384, 256), BF16),
            pltpu.VMEM((8, FAR, 256), BF16),
            pltpu.VMEM((8, 64, 256), BF16),
            pltpu.SemaphoreType.DMA((16,)),
        ],
        out_spaces=[pltpu.VMEM] * 5 + [pl.ANY],
        flops=4 * 4 * 2 * 256 * 768 * FEAT,
        name="attend",
    )
    p1 = lax.ppermute(p1, "seq", peer)
    p2 = lax.ppermute(p2, "seq", beside)
    zrecv = exchange(zsend, "seq", ROW_GROUPS)
    attended, nqg, tok, qsum = call(
        after_kernel,
        [sds(ROWS, FEAT), sds(ROWS, FEAT, dtype=F32), sds(ROWS, 256, dtype=F32)]
        + [sds(8, FEAT, dtype=F32)],
        (stat, qn, kv, one, out_grad, halo, cross, squares, queries),
        scratch=[
            pltpu.VMEM((768, 256), BF16),
            pltpu.VMEM((768, 256), F32),
            pltpu.VMEM((256, 256), F32),
        ],
        flops=4 * 5 * 2 * 256 * KEYS * FEAT,
        name="after",
    )
    ysend = call(
        column_kernel,
        sds(8, 16, 256),
        (zrecv, p1, p2, tok),
        scratch=[pltpu.VMEM((8, FAR, 256), BF16), pltpu.SemaphoreType.DMA],
        spaces=[pl.ANY] * 4,
        name="columns",
    )
    yrecv = exchange(ysend, "seq", COLUMN_GROUPS)
    nkg, value_grad, inner = call(
        total_kernel,
        [sds(ROWS, FEAT, dtype=F32), sds(ROWS, FEAT), sds(heads, 8, FEAT, dtype=F32)],
        (tok, p1, p2, zrecv, yrecv, key_rows, qsum),
        scratch=[
            pltpu.VMEM((ROWS, 256), F32),
            pltpu.VMEM((ROWS, FEAT), BF16),
            pltpu.SemaphoreType.DMA((LEAVES,)),
        ],
        out_spaces=[pltpu.VMEM, pl.ANY, pltpu.VMEM],
        name="total",
    )
    inner = exchange(inner, "head")
    query_grad, key_grad = call(
        lambda *refs: finish_kernel(width, *refs),
        [sds(ROWS, FEAT), sds(ROWS, FEAT)],
        (squares, inner, queries, key_rows, nqg, nkg),
        scratch=[pltpu.VMEM((2, ROWS, FEAT), BF16), pltpu.SemaphoreType.DMA((2 * LEAVES,))],
        out_spaces=[pl.ANY, pl.ANY],
        name="finish",
    )
    return (attended, query_grad, key_grad, value_grad)


def solution(mesh):
    placed = (
        P("seq", "head"),
        P("seq", "head"),
        P("seq", "head"),
        P("head"),
        P("head"),
        P("seq", "head"),
    )
    return jax.shard_map(
        local,
        mesh=mesh,
        in_specs=placed,
        out_specs=(P("seq", "head"), P("seq", "head"), P("seq", "head"), P("seq", "head")),
        check_vma=False,
    )
```

```python
import math

import jax
import jax.numpy as jnp
from jax import lax
from jax.experimental import pallas as pl
from jax.experimental.pallas import tpu as pltpu
from jax.sharding import PartitionSpec as P

ROWS = 512
FEAT = 128
LEAF = 128
LEAVES = 4
HEAD = 64
KEYS = 1280
EPS = 1e-06
LN2 = math.log(2.0)
F32 = jnp.float32
BF16 = jnp.bfloat16
BLOCKS = [pl.ds(i * LEAF, LEAF) for i in range(LEAVES)]
ROW_LEVEL = {1: 2, 2: 3, 3: 3, 4: 4, 5: 4, 6: 4, 7: 4}
COLUMN_LEVEL = {1: 5, 2: 6, 3: 6, 4: 7, 5: 7, 6: 7, 7: 7}
FAR = 48
SLOT = 112


def dot(a, b, dims):
    return lax.dot_general(a, b, ((dims[:1], dims[1:]), ((), ())), preferred_element_type=F32)


def iota(shape, axis):
    return lax.broadcasted_iota(jnp.int32, shape, axis)


def pooling(rows, level):
    token = iota((rows, ROWS), 1)
    hit = jnp.right_shift(token, level) == iota((rows, ROWS), 0)
    return jnp.where(hit, 2.0**-level, 0.0)


def spreading(first, rows, level):
    token = iota((ROWS, rows), 0)
    hit = jnp.right_shift(token, level) == iota((ROWS, rows), 1) + first
    return jnp.where(hit, 2.0**-level, 0.0)


def far_pick(shape, far_axis):
    far = iota(shape, far_axis)
    slot_row = iota(shape, 1 - far_axis)
    mid = far - 16
    low = far - 32
    column = jnp.where(
        far < 16,
        far,
        jnp.where(
            far < 32,
            (1 + jnp.right_shift(mid, 3)) * 16 + jnp.bitwise_and(mid, 7),
            (3 + jnp.right_shift(low, 2)) * 16 + jnp.bitwise_and(low, 3),
        ),
    )
    return jnp.where(column == slot_row, 1.0, 0.0).astype(BF16)


def token_sums(x):
    return [
        jnp.sum(x[i * LEAF : (i + 1) * LEAF].T, axis=0, keepdims=True) for i in range(LEAVES)
    ]


def spread_tokens(tile, first):
    return jnp.concatenate(
        [
            jnp.broadcast_to(tile[first + i : first + i + 1], (LEAF, LEAF)).T
            for i in range(LEAVES)
        ],
        axis=0,
    )


def squares_kernel(q_in, k_in, qg_in, kg_in, out_ref, rows, gains, sems):
    copies = []
    for i in range(2 * LEAVES):
        source = (q_in if i < LEAVES else k_in).at[pl.ds((i % LEAVES) * LEAF, LEAF)]
        copies.append(pltpu.make_async_copy(source, rows.at[i], sems.at[i]))
    for i, source in enumerate((qg_in, kg_in)):
        copies.append(pltpu.make_async_copy(source, gains.at[i], sems.at[2 * LEAVES + i]))
    for copy in copies:
        copy.start()
    sums = []
    for i in range(2 * LEAVES):
        copies[i].wait()
        x = rows[i].astype(F32)
        sums.append(jnp.sum((x * x).T, axis=0, keepdims=True))
    for copy in copies[2 * LEAVES :]:
        copy.wait()
    tile = jnp.concatenate(sums + [gains[0], gains[1], jnp.zeros((6, FEAT), F32)], axis=0)
    for i in range(out_ref.shape[0]):
        out_ref[i] = tile


def rates(width, sum_ref):
    return lax.rsqrt(jnp.sum(sum_ref[:, :8], axis=0) / width + EPS)


def norm_kernel(width, sum_ref, k_ref, v_ref, kv_ref, one_ref, lv_ref, y_ref, p1_ref, p2_ref):
    index = lax.axis_index("seq")
    column = jnp.right_shift(index, 3)
    odd = jnp.bitwise_and(index, 1)
    gain = sum_ref[lax.axis_index("head"), 9:10]
    kv_ref[:, :FEAT] = (
        k_ref[...].astype(F32) * spread_tokens(rates(width, sum_ref), 4) * gain
    ).astype(BF16)
    kv_ref[:, FEAT:] = v_ref[...]
    pool = jnp.concatenate(
        [pooling(ROWS >> level, level) for level in (1, 2, 3, 4)]
        + [pooling(16, COLUMN_LEVEL[d]) for d in range(1, 8)],
        axis=0,
    ).astype(BF16)
    coarse = dot(pool, kv_ref[...], (1, 0)).astype(BF16)
    one_ref[...] = coarse[:256]
    lv_ref[...] = coarse[256:480]
    y_ref[column] = jnp.zeros((16, 2 * FEAT), BF16)
    for d in range(1, 8):
        y_ref[jnp.bitwise_xor(column, d)] = coarse[464 + 16 * d : 480 + 16 * d]
    p1_ref[:LEAF] = kv_ref[pl.ds(pl.multiple_of((1 - odd) * 384, LEAF), LEAF)]
    p1_ref[LEAF:] = coarse[320:384]
    p2_ref[...] = kv_ref[pl.ds(pl.multiple_of(odd * 384, LEAF), LEAF)]


def start_all(copies):
    for copy in copies:
        copy.start()
    return copies


def wait_all(copies):
    for copy in copies:
        copy.wait()


def row_kernel(y_ref, lv_ref, out_ref, far_scr, sems):
    index = lax.axis_index("seq")
    column = jnp.right_shift(index, 3)
    place = jnp.bitwise_and(index, 7)
    copies = []
    for d in range(1, 8):
        first, rows = {1: (0, 64), 2: (128, 64), 3: (128, 64)}.get(d, (192, 32))
        target = out_ref.at[jnp.bitwise_xor(place, d), pl.ds(FAR, rows)]
        copies.append(pltpu.make_async_copy(lv_ref.at[pl.ds(first, rows)], target, sems.at[d]))
    start_all(copies)
    slots = jnp.concatenate([y_ref[jnp.bitwise_xor(column, d)] for d in range(1, 8)], axis=0)
    far_scr[...] = dot(far_pick((FAR, 112), 0), slots, (1, 0)).astype(BF16)
    copies += start_all(
        [
            pltpu.make_async_copy(far_scr, out_ref.at[s, pl.ds(0, FAR)], sems.at[8 + s])
            for s in range(8)
        ]
    )
    wait_all(copies)


def by_head(block):
    lane = iota((LEAF, FEAT), 1)
    zero = jnp.zeros((LEAF, FEAT), BF16)
    return jnp.concatenate(
        [jnp.where(lane < HEAD, block, zero), jnp.where(lane < HEAD, zero, block)], axis=0
    )


def peak(x):
    return jnp.max(x, axis=0, keepdims=True)


def add_up(x):
    return jnp.sum(x, axis=0, keepdims=True)


HALO_PIECE = {0: 0, LEAVES - 1: 2}


def far_bias():
    return jnp.concatenate(
        [jnp.full((LEAF, 2 * LEAF), level * LN2, F32) for level in range(1, 8)], axis=0
    )


def outside_bias():
    index = lax.axis_index("seq")
    last = lax.axis_size("seq") - 1
    return {
        0: jnp.where(index > 0, 0.0, -1e30).astype(F32),
        LEAVES - 1: jnp.where(index < last, 0.0, -1e30).astype(F32),
    }


def weigh(kv, q2, g2):
    score = dot(kv[:, :FEAT], q2, (1, 1))
    top = peak(score)
    weight = jnp.exp(score - top)
    pgrad = dot(kv[:, FEAT:], g2, (1, 1))
    return weight, pgrad, (top, add_up(weight), add_up(weight * pgrad))


def combine(stats):
    top = stats[0][0]
    for stat in stats[1:]:
        top = jnp.maximum(top, stat[0])
    factors = [jnp.exp(stat[0] - top) for stat in stats]
    total = sum(factor * stat[1] for factor, stat in zip(factors, stats))
    mixed = sum(factor * stat[2] for factor, stat in zip(factors, stats))
    return top, total, mixed, factors


def scaled_queries(block):
    return by_head(block) * jnp.asarray(0.125, BF16)


def near_kernel(width, sum_ref, q_ref, kv_ref, one_ref, g_ref, qn_ref, stat_ref):
    gain = sum_ref[lax.axis_index("head"), 8:9]
    qn_ref[...] = (
        q_ref[...].astype(F32) * spread_tokens(rates(width, sum_ref), 0) * gain
    ).astype(BF16)
    for b in range(LEAVES):
        block = slice(b * LEAF, (b + 1) * LEAF)
        q2 = scaled_queries(qn_ref[block])
        g2 = by_head(g_ref[block])
        half = (1 - b // 2) * LEAF
        stats = [
            weigh(kv_ref[(b + i - 1) * LEAF : (b + i) * LEAF], q2, g2)[2]
            for i in range(3)
            if HALO_PIECE.get(b) != i
        ]
        top, total, mixed = weigh(one_ref[half : half + LEAF], q2, g2)[2]
        stats.append((top + LN2, total, mixed))
        top, total, mixed, _ = combine(stats)
        stat_ref[b] = jnp.concatenate([top, total, mixed, jnp.zeros((5, 2 * LEAF), F32)], axis=0)


def attend_kernel(
    qn_ref, g_ref, near_ref, p1_ref, p2_ref, z_ref,
    stat_ref, cross, halo, p1o_ref, p2o_ref, zo_ref,
    q2_scr, g2_scr, weight_scr, pgrad_scr, low_scr, sgrad_scr, rims, mid_grad, far_scr, mid_scr, sems,
):
    index = lax.axis_index("seq")
    place = jnp.bitwise_and(index, 7)
    odd = jnp.bitwise_and(index, 1)
    peer_side = 1 - odd
    halo[peer_side] = p1_ref[:LEAF]
    halo[odd] = p2_ref[...]
    cross[:64] = z_ref[jnp.bitwise_xor(place, 1), FAR:]
    cross[64:128] = p1_ref[LEAF:]
    cross[128:192] = z_ref[jnp.bitwise_xor(place, 2), FAR:]
    cross[192:256] = z_ref[jnp.bitwise_xor(place, 3), FAR:]
    for i in range(4):
        cross[256 + 32 * i : 288 + 32 * i] = z_ref[jnp.bitwise_xor(place, 4 + i), FAR : FAR + 32]
    for s in range(8):
        for j in range(3):
            at = 384 + LEAF * j + 16 * s
            cross[at : at + 16] = z_ref[s, 16 * j : 16 * (j + 1)]

    outside = outside_bias()
    rim_rows = []
    for b in range(LEAVES):
        block = slice(b * LEAF, (b + 1) * LEAF)
        lanes = slice(2 * b * LEAF, 2 * (b + 1) * LEAF)
        q2 = scaled_queries(qn_ref[block])
        g2 = by_head(g_ref[block])
        q2_scr[lanes] = q2
        g2_scr[lanes] = g2
        side = 0 if b == 0 else 1
        pieces = list(range(7 if b in HALO_PIECE else 6))
        stats = [(near_ref[b, 0:1], near_ref[b, 1:2], near_ref[b, 2:3])]
        for i in pieces:
            kv = cross[i * LEAF : (i + 1) * LEAF] if i < 6 else halo[side]
            weight, pgrad, (top, total, mixed) = weigh(kv, q2, g2)
            weight_scr[b, i] = weight
            pgrad_scr[b, i] = pgrad
            bias = (i + 2) * LN2 if i < 6 else outside[b]
            stats.append((top + bias, total, mixed))
        top, total, mixed, factors = combine(stats)
        inverse = 1.0 / total
        delta = mixed * inverse
        stat_ref[b] = jnp.concatenate(
            [top, inverse, delta, jnp.zeros((5, 2 * LEAF), F32)], axis=0
        )
        for i in range(6):
            prob = weight_scr[b, i] * (factors[i + 1] * inverse)
            low_scr[i * LEAF : (i + 1) * LEAF, lanes] = prob.astype(BF16)
            sgrad_scr[i * LEAF : (i + 1) * LEAF, lanes] = (
                prob * (pgrad_scr[b, i] - delta)
            ).astype(BF16)
        if b in HALO_PIECE:
            rim_rows.append((b, side, lanes, factors[7] * inverse, delta))

    def grads(rows):
        keys = dot(sgrad_scr[rows], q2_scr[...], (1, 0))
        values = dot(low_scr[rows], g2_scr[...], (1, 0))
        return jnp.concatenate([keys, values], axis=1).astype(BF16)

    for j in range(3):
        far = grads(slice(384 + LEAF * j, 384 + LEAF * (j + 1)))
        for s in range(8):
            far_scr[s, 16 * j : 16 * (j + 1)] = far[16 * s : 16 * (s + 1)]
    copies = start_all(
        [
            pltpu.make_async_copy(far_scr.at[s], zo_ref.at[s, pl.ds(0, FAR)], sems.at[s])
            for s in range(8)
        ]
    )
    mid_grad[...] = grads(slice(0, 384))
    mid_scr[...] = jnp.zeros_like(mid_scr)
    mid_scr[1] = mid_grad[:64]
    mid_scr[2] = mid_grad[128:192]
    mid_scr[3] = mid_grad[192:256]
    for i in range(4):
        mid_scr[4 + i, :32] = mid_grad[256 + 32 * i : 288 + 32 * i]
    copies += start_all(
        [
            pltpu.make_async_copy(
                mid_scr.at[d],
                zo_ref.at[jnp.bitwise_xor(place, d), pl.ds(FAR, 64)],
                sems.at[8 + d],
            )
            for d in range(8)
        ]
    )
    for b, side, lanes, factor, delta in rim_rows:
        prob = weight_scr[b, 6] * factor
        sgrad = (prob * (pgrad_scr[b, 6] - delta)).astype(BF16)
        rims[side, :, :FEAT] = dot(sgrad, q2_scr[lanes], (1, 0)).astype(BF16)
        rims[side, :, FEAT:] = dot(prob.astype(BF16), g2_scr[lanes], (1, 0)).astype(BF16)
    p1o_ref[:LEAF] = rims[peer_side]
    p1o_ref[LEAF:] = mid_grad[64:128]
    p2o_ref[...] = rims[odd]
    wait_all(copies)


def after_kernel(
    stat_ref, qn_ref, kv_ref, one_ref, g_ref, halo, cross, sum_ref, q_ref,
    att_ref, nqg_ref, tok_ref, qsum_ref, near, near_grad, one_grad,
):
    near[:LEAF] = halo[0]
    near[LEAF : LEAF + ROWS] = kv_ref[...]
    near[LEAF + ROWS :] = halo[1]
    near_grad[...] = jnp.zeros_like(near_grad)
    one_grad[...] = jnp.zeros_like(one_grad)
    feature = iota((FEAT, LEAF), 0)
    bias = far_bias()
    outside = outside_bias()

    def merge_heads(transposed):
        return jnp.where(feature < HEAD, transposed[:, :LEAF], transposed[:, LEAF:]).T

    for b in range(LEAVES):
        rows = slice(b * LEAF, (b + 1) * LEAF)
        near_rows = slice(b * LEAF, (b + 3) * LEAF)
        half = (1 - b // 2) * LEAF
        q2 = scaled_queries(qn_ref[rows])
        g2 = by_head(g_ref[rows])
        kv = jnp.concatenate([near[near_rows], one_ref[half : half + LEAF], cross[...]], axis=0)
        keys = kv[:, :FEAT]
        values = kv[:, FEAT:]
        raw = dot(keys, q2, (1, 1))
        before, after = raw[:LEAF], raw[2 * LEAF : 3 * LEAF]
        if b == 0:
            before = before + outside[b]
        if b == LEAVES - 1:
            after = after + outside[b]
        scores = jnp.concatenate(
            [before, raw[LEAF : 2 * LEAF], after, raw[3 * LEAF :] + bias], axis=0
        )
        probs = jnp.exp(scores - stat_ref[b, 0:1]) * stat_ref[b, 1:2]
        low = probs.astype(BF16)
        score_grad = (probs * (dot(values, g2, (1, 1)) - stat_ref[b, 2:3])).astype(BF16)
        att_ref[rows] = merge_heads(dot(values, low, (0, 0))).astype(BF16)
        nqg_ref[rows] = merge_heads(dot(keys, score_grad, (0, 0))) * 0.125
        for part, lanes in (
            (dot(score_grad[: 4 * LEAF], q2, (1, 0)), slice(0, FEAT)),
            (dot(low[: 4 * LEAF], g2, (1, 0)), slice(FEAT, 2 * FEAT)),
        ):
            near_grad[near_rows, lanes] += part[: 3 * LEAF]
            one_grad[half : half + LEAF, lanes] += part[3 * LEAF :]
    spread = spreading(0, 256, 1).astype(BF16)
    high = one_grad[...].astype(BF16)
    rest = (one_grad[...] - high.astype(F32)).astype(BF16)
    tok_ref[...] = near_grad[LEAF : LEAF + ROWS] + dot(spread, high, (1, 0)) + dot(spread, rest, (1, 0))
    gains = sum_ref[lax.axis_index("head"), 8:16]
    sums = token_sums(q_ref[...].astype(F32) * gains[0:1] * nqg_ref[...])
    qsum_ref[...] = jnp.concatenate(sums + [gains[1:2], jnp.zeros((3, FEAT), F32)], axis=0)


def column_kernel(z_ref, p1_ref, p2_ref, tok_ref, out_ref, far_rows, sem):
    column = jnp.right_shift(lax.axis_index("seq"), 3)
    copy = pltpu.make_async_copy(z_ref.at[:, pl.ds(0, FAR)], far_rows, sem)
    copy.start()
    copy.wait()
    far = jnp.sum(far_rows[...].astype(F32), axis=0).astype(BF16)
    slots = dot(far_pick((112, FAR), 1), far, (1, 0)).astype(BF16)
    out_ref[column] = jnp.zeros((16, 2 * FEAT), BF16)
    for d in range(1, 8):
        out_ref[jnp.bitwise_xor(column, d)] = slots[16 * (d - 1) : 16 * d]


def total_kernel(
    tok_ref, p1_ref, p2_ref, z_ref, y_ref, k_ref, qsum_ref,
    nkg_ref, vg_ref, sum_ref, acc,
):
    index = lax.axis_index("seq")
    column = jnp.right_shift(index, 3)
    place = jnp.bitwise_and(index, 7)
    odd = jnp.bitwise_and(index, 1)
    pieces = [z_ref[jnp.bitwise_xor(place, 1), FAR:], p1_ref[LEAF:]]
    maps = [spreading(0, 64, 2), spreading(64, 64, 2)]
    for d in range(2, 8):
        rows = ROWS >> ROW_LEVEL[d]
        pieces.append(z_ref[jnp.bitwise_xor(place, d), FAR : FAR + rows])
        maps.append(spreading(0, rows, ROW_LEVEL[d]))
    for d in range(1, 8):
        pieces.append(y_ref[jnp.bitwise_xor(column, d)])
        maps.append(spreading(0, 16, COLUMN_LEVEL[d]))
    spread = jnp.concatenate(maps, axis=1).astype(BF16)
    acc[...] = tok_ref[...] + dot(spread, jnp.concatenate(pieces, axis=0), (1, 0))
    acc[pl.ds(pl.multiple_of((1 - odd) * 384, LEAF), LEAF)] += p1_ref[:LEAF].astype(F32)
    acc[pl.ds(pl.multiple_of(odd * 384, LEAF), LEAF)] += p2_ref[...].astype(F32)
    vg_ref[...] = acc[:, FEAT:].astype(BF16)
    key_total = acc[:, :FEAT]
    nkg_ref[...] = key_total
    sums = token_sums(k_ref[...].astype(F32) * qsum_ref[LEAVES : LEAVES + 1] * key_total)
    tile = jnp.concatenate([qsum_ref[:LEAVES]] + sums, axis=0)
    for i in range(sum_ref.shape[0]):
        sum_ref[i] = tile


def finish_kernel(
    width, sq_ref, inner_ref, q_ref, k_ref, nqg_ref, nkg_ref, value_ref,
    dq_ref, dk_ref, vg_ref, results, sems,
):
    copies = start_all([pltpu.make_async_copy(value_ref, vg_ref, sems.at[2 * LEAVES])])
    rate = rates(width, sq_ref)
    inner = jnp.sum(inner_ref[...], axis=0) / width
    cubed = rate * rate * rate * inner
    gains = sq_ref[lax.axis_index("head"), 8:16]
    for side, (x_ref, grad_ref, out_ref) in enumerate(
        ((q_ref, nqg_ref, dq_ref), (k_ref, nkg_ref, dk_ref))
    ):
        results[side] = (
            spread_tokens(rate, 4 * side) * gains[side : side + 1] * grad_ref[...]
            - x_ref[...].astype(F32) * spread_tokens(cubed, 4 * side)
        ).astype(BF16)
        copies += start_all(
            [
                pltpu.make_async_copy(
                    results.at[side, rows], out_ref.at[rows], sems.at[LEAVES * side + i]
                )
                for i, rows in enumerate(BLOCKS)
            ]
        )
    wait_all(copies)


def call(kernel, outs, args, scratch=(), flops=0, name=None, spaces=None, out_spaces=None, vmem=40):
    many = isinstance(outs, list)
    moved = sum(math.prod(x.shape) * x.dtype.itemsize for x in list(args) + (outs if many else [outs]))
    out_spaces = out_spaces or [pltpu.VMEM] * (len(outs) if many else 1)
    out_specs = [pl.BlockSpec(memory_space=space) for space in out_spaces]
    return pl.pallas_call(
        kernel,
        out_shape=outs,
        in_specs=[pl.BlockSpec(memory_space=space) for space in spaces or [pltpu.VMEM] * len(args)],
        out_specs=out_specs if many else out_specs[0],
        scratch_shapes=list(scratch),
        compiler_params=pltpu.CompilerParams(vmem_limit_bytes=vmem * 1024 * 1024),
        cost_estimate=pl.CostEstimate(flops=flops, bytes_accessed=moved, transcendentals=0),
        name=name,
    )(*args)


def sds(*shape, dtype=BF16):
    return jax.ShapeDtypeStruct(shape, dtype)


ROW_GROUPS = [[8 * y + z for z in range(8)] for y in range(8)]
COLUMN_GROUPS = [[8 * y + z for y in range(8)] for z in range(8)]


def exchange(x, axis, groups=None):
    return lax.all_to_all(x, axis, 0, 0, axis_index_groups=groups, tiled=True)


def local(queries, key_rows, value_rows, query_gain, key_gain, out_grad):
    seq = lax.axis_size("seq")
    heads = lax.axis_size("head")
    width = float(heads * FEAT)
    qg = query_gain.reshape(1, FEAT)
    kg = key_gain.reshape(1, FEAT)
    peer = [(i, i ^ 1) for i in range(seq)]
    beside = [(i, i + 1) for i in range(1, seq - 1, 2)] + [(i + 1, i) for i in range(1, seq - 1, 2)]

    squares = call(
        squares_kernel,
        sds(heads, 16, FEAT, dtype=F32),
        (queries, key_rows, qg, kg),
        scratch=[
            pltpu.VMEM((2 * LEAVES, LEAF, FEAT), BF16),
            pltpu.VMEM((2, 1, FEAT), F32),
            pltpu.SemaphoreType.DMA((2 * LEAVES + 2,)),
        ],
        spaces=[pl.ANY] * 4,
        vmem=60,
        name="squares",
    )
    squares = exchange(squares, "head")
    kv, one, lv, ysend, p1, p2 = call(
        lambda *refs: norm_kernel(width, *refs),
        [sds(ROWS, 256), sds(256, 256), sds(224, 256), sds(8, 16, 256), sds(192, 256), sds(LEAF, 256)],
        (squares, key_rows, value_rows),
        name="norm",
    )
    p1 = lax.ppermute(p1, "seq", peer)
    p2 = lax.ppermute(p2, "seq", beside)
    yrecv = exchange(ysend, "seq", COLUMN_GROUPS)
    zsend = call(
        row_kernel,
        sds(8, SLOT, 256),
        (yrecv, lv),
        scratch=[pltpu.VMEM((FAR, 256), BF16), pltpu.SemaphoreType.DMA((16,))],
        out_spaces=[pl.ANY],
        name="rows",
    )
    zrecv = exchange(zsend, "seq", ROW_GROUPS)
    qn, near = call(
        lambda *refs: near_kernel(width, *refs),
        [sds(ROWS, FEAT), sds(LEAVES, 8, 256, dtype=F32)],
        (squares, queries, kv, one, out_grad),
        flops=14 * 2 * 2 * 256 * LEAF * FEAT,
        name="near",
    )
    stat, cross, halo, p1, p2, zsend = call(
        attend_kernel,
        [sds(LEAVES, 8, 256, dtype=F32), sds(768, 256), sds(2, LEAF, 256)]
        + [sds(192, 256), sds(LEAF, 256), sds(8, SLOT, 256)],
        (qn, out_grad, near, p1, p2, zrecv),
        scratch=[
            pltpu.VMEM((1024, FEAT), BF16),
            pltpu.VMEM((1024, FEAT), BF16),
            pltpu.VMEM((LEAVES, 7, LEAF, 256), F32),
            pltpu.VMEM((LEAVES, 7, LEAF, 256), F32),
            pltpu.VMEM((768, 1024), BF16),
            pltpu.VMEM((768, 1024), BF16),
            pltpu.VMEM((2, LEAF, 256), BF16),
            pltpu.VMEM((384, 256), BF16),
            pltpu.VMEM((8, FAR, 256), BF16),
            pltpu.VMEM((8, 64, 256), BF16),
            pltpu.SemaphoreType.DMA((16,)),
        ],
        out_spaces=[pltpu.VMEM] * 5 + [pl.ANY],
        flops=4 * 4 * 2 * 256 * 768 * FEAT,
        name="attend",
    )
    p1 = lax.ppermute(p1, "seq", peer)
    p2 = lax.ppermute(p2, "seq", beside)
    zrecv = exchange(zsend, "seq", ROW_GROUPS)
    attended, nqg, tok, qsum = call(
        after_kernel,
        [sds(ROWS, FEAT), sds(ROWS, FEAT, dtype=F32), sds(ROWS, 256, dtype=F32)]
        + [sds(8, FEAT, dtype=F32)],
        (stat, qn, kv, one, out_grad, halo, cross, squares, queries),
        scratch=[
            pltpu.VMEM((768, 256), BF16),
            pltpu.VMEM((768, 256), F32),
            pltpu.VMEM((256, 256), F32),
        ],
        flops=4 * 5 * 2 * 256 * KEYS * FEAT,
        name="after",
    )
    ysend = call(
        column_kernel,
        sds(8, 16, 256),
        (zrecv, p1, p2, tok),
        scratch=[pltpu.VMEM((8, FAR, 256), BF16), pltpu.SemaphoreType.DMA],
        spaces=[pl.ANY] * 4,
        name="columns",
    )
    yrecv = exchange(ysend, "seq", COLUMN_GROUPS)
    nkg, value_grad, inner = call(
        total_kernel,
        [sds(ROWS, FEAT, dtype=F32), sds(ROWS, FEAT), sds(heads, 8, FEAT, dtype=F32)],
        (tok, p1, p2, zrecv, yrecv, key_rows, qsum),
        scratch=[
            pltpu.VMEM((ROWS, 256), F32),
        ],
        name="total",
    )
    inner = exchange(inner, "head")
    query_grad, key_grad, value_grad = call(
        lambda *refs: finish_kernel(width, *refs),
        [sds(ROWS, FEAT), sds(ROWS, FEAT), sds(ROWS, FEAT)],
        (squares, inner, queries, key_rows, nqg, nkg, value_grad),
        scratch=[pltpu.VMEM((2, ROWS, FEAT), BF16), pltpu.SemaphoreType.DMA((2 * LEAVES + 1,))],
        out_spaces=[pl.ANY] * 3,
        name="finish",
    )
    return (attended, query_grad, key_grad, value_grad)


def solution(mesh):
    placed = (
        P("seq", "head"),
        P("seq", "head"),
        P("seq", "head"),
        P("head"),
        P("head"),
        P("seq", "head"),
    )
    return jax.shard_map(
        local,
        mesh=mesh,
        in_specs=placed,
        out_specs=(P("seq", "head"), P("seq", "head"), P("seq", "head"), P("seq", "head")),
        check_vma=False,
    )
```

```python
import math

import jax
import jax.numpy as jnp
from jax import lax
from jax.experimental import pallas as pl
from jax.experimental.pallas import tpu as pltpu
from jax.sharding import PartitionSpec as P

ROWS = 512
FEAT = 128
LEAF = 128
LEAVES = 4
HEAD = 64
KEYS = 1280
EPS = 1e-06
LN2 = math.log(2.0)
F32 = jnp.float32
BF16 = jnp.bfloat16
BLOCKS = [pl.ds(i * LEAF, LEAF) for i in range(LEAVES)]
ROW_LEVEL = {1: 2, 2: 3, 3: 3, 4: 4, 5: 4, 6: 4, 7: 4}
COLUMN_LEVEL = {1: 5, 2: 6, 3: 6, 4: 7, 5: 7, 6: 7, 7: 7}
FAR = 48
SLOT = 112


def dot(a, b, dims):
    return lax.dot_general(a, b, ((dims[:1], dims[1:]), ((), ())), preferred_element_type=F32)


def iota(shape, axis):
    return lax.broadcasted_iota(jnp.int32, shape, axis)


def pooling(rows, level):
    token = iota((rows, ROWS), 1)
    hit = jnp.right_shift(token, level) == iota((rows, ROWS), 0)
    return jnp.where(hit, 2.0**-level, 0.0)


def spreading(first, rows, level):
    token = iota((ROWS, rows), 0)
    hit = jnp.right_shift(token, level) == iota((ROWS, rows), 1) + first
    return jnp.where(hit, 2.0**-level, 0.0)


def far_pick(shape, far_axis):
    far = iota(shape, far_axis)
    slot_row = iota(shape, 1 - far_axis)
    mid = far - 16
    low = far - 32
    column = jnp.where(
        far < 16,
        far,
        jnp.where(
            far < 32,
            (1 + jnp.right_shift(mid, 3)) * 16 + jnp.bitwise_and(mid, 7),
            (3 + jnp.right_shift(low, 2)) * 16 + jnp.bitwise_and(low, 3),
        ),
    )
    return jnp.where(column == slot_row, 1.0, 0.0).astype(BF16)


def token_sums(x):
    return [
        jnp.sum(x[i * LEAF : (i + 1) * LEAF].T, axis=0, keepdims=True) for i in range(LEAVES)
    ]


def spread_tokens(tile, first):
    return jnp.concatenate(
        [
            jnp.broadcast_to(tile[first + i : first + i + 1], (LEAF, LEAF)).T
            for i in range(LEAVES)
        ],
        axis=0,
    )


def squares_kernel(q_in, k_in, qg_in, kg_in, out_ref, rows, gains, sems):
    copies = []
    for i in range(2 * LEAVES):
        source = (q_in if i < LEAVES else k_in).at[pl.ds((i % LEAVES) * LEAF, LEAF)]
        copies.append(pltpu.make_async_copy(source, rows.at[i], sems.at[i]))
    for i, source in enumerate((qg_in, kg_in)):
        copies.append(pltpu.make_async_copy(source, gains.at[i], sems.at[2 * LEAVES + i]))
    for copy in copies:
        copy.start()
    sums = []
    for i in range(2 * LEAVES):
        copies[i].wait()
        x = rows[i].astype(F32)
        sums.append(jnp.sum((x * x).T, axis=0, keepdims=True))
    for copy in copies[2 * LEAVES :]:
        copy.wait()
    tile = jnp.concatenate(sums + [gains[0], gains[1], jnp.zeros((6, FEAT), F32)], axis=0)
    for i in range(out_ref.shape[0]):
        out_ref[i] = tile


def rates(width, sum_ref):
    return lax.rsqrt(jnp.sum(sum_ref[:, :8], axis=0) / width + EPS)


def norm_kernel(width, sum_ref, k_ref, v_ref, kv_ref, one_ref, lv_ref, y_ref, p1_ref, p2_ref):
    index = lax.axis_index("seq")
    column = jnp.right_shift(index, 3)
    odd = jnp.bitwise_and(index, 1)
    gain = sum_ref[lax.axis_index("head"), 9:10]
    kv_ref[:, :FEAT] = (
        k_ref[...].astype(F32) * spread_tokens(rates(width, sum_ref), 4) * gain
    ).astype(BF16)
    kv_ref[:, FEAT:] = v_ref[...]
    pool = jnp.concatenate(
        [pooling(ROWS >> level, level) for level in (1, 2, 3, 4)]
        + [pooling(16, COLUMN_LEVEL[d]) for d in range(1, 8)],
        axis=0,
    ).astype(BF16)
    coarse = dot(pool, kv_ref[...], (1, 0)).astype(BF16)
    one_ref[...] = coarse[:256]
    lv_ref[...] = coarse[256:480]
    y_ref[column] = jnp.zeros((16, 2 * FEAT), BF16)
    for d in range(1, 8):
        y_ref[jnp.bitwise_xor(column, d)] = coarse[464 + 16 * d : 480 + 16 * d]
    p1_ref[:LEAF] = kv_ref[pl.ds(pl.multiple_of((1 - odd) * 384, LEAF), LEAF)]
    p1_ref[LEAF:] = coarse[320:384]
    p2_ref[...] = kv_ref[pl.ds(pl.multiple_of(odd * 384, LEAF), LEAF)]


def start_all(copies):
    for copy in copies:
        copy.start()
    return copies


def wait_all(copies):
    for copy in copies:
        copy.wait()


def row_kernel(y_ref, lv_ref, out_ref, far_scr, sems):
    index = lax.axis_index("seq")
    column = jnp.right_shift(index, 3)
    place = jnp.bitwise_and(index, 7)
    copies = []
    for d in range(1, 8):
        first, rows = {1: (0, 64), 2: (128, 64), 3: (128, 64)}.get(d, (192, 32))
        target = out_ref.at[jnp.bitwise_xor(place, d), pl.ds(FAR, rows)]
        copies.append(pltpu.make_async_copy(lv_ref.at[pl.ds(first, rows)], target, sems.at[d]))
    start_all(copies)
    slots = jnp.concatenate([y_ref[jnp.bitwise_xor(column, d)] for d in range(1, 8)], axis=0)
    far_scr[...] = dot(far_pick((FAR, 112), 0), slots, (1, 0)).astype(BF16)
    copies += start_all(
        [
            pltpu.make_async_copy(far_scr, out_ref.at[s, pl.ds(0, FAR)], sems.at[8 + s])
            for s in range(8)
        ]
    )
    wait_all(copies)


def by_head(block):
    lane = iota((LEAF, FEAT), 1)
    zero = jnp.zeros((LEAF, FEAT), BF16)
    return jnp.concatenate(
        [jnp.where(lane < HEAD, block, zero), jnp.where(lane < HEAD, zero, block)], axis=0
    )


def peak(x):
    return jnp.max(x, axis=0, keepdims=True)


def add_up(x):
    return jnp.sum(x, axis=0, keepdims=True)


HALO_PIECE = {0: 0, LEAVES - 1: 2}


def far_bias():
    return jnp.concatenate(
        [jnp.full((LEAF, 2 * LEAF), level * LN2, F32) for level in range(1, 8)], axis=0
    )


def outside_bias():
    index = lax.axis_index("seq")
    last = lax.axis_size("seq") - 1
    return {
        0: jnp.where(index > 0, 0.0, -1e30).astype(F32),
        LEAVES - 1: jnp.where(index < last, 0.0, -1e30).astype(F32),
    }


def weigh(kv, q2, g2):
    score = dot(kv[:, :FEAT], q2, (1, 1))
    top = peak(score)
    weight = jnp.exp(score - top)
    pgrad = dot(kv[:, FEAT:], g2, (1, 1))
    return weight, pgrad, (top, add_up(weight), add_up(weight * pgrad))


def combine(stats):
    top = stats[0][0]
    for stat in stats[1:]:
        top = jnp.maximum(top, stat[0])
    factors = [jnp.exp(stat[0] - top) for stat in stats]
    total = sum(factor * stat[1] for factor, stat in zip(factors, stats))
    mixed = sum(factor * stat[2] for factor, stat in zip(factors, stats))
    return top, total, mixed, factors


def scaled_queries(block):
    return by_head(block) * jnp.asarray(0.125, BF16)


def near_kernel(width, sum_ref, q_ref, kv_ref, one_ref, g_ref, qn_ref, stat_ref):
    gain = sum_ref[lax.axis_index("head"), 8:9]
    qn_ref[...] = (
        q_ref[...].astype(F32) * spread_tokens(rates(width, sum_ref), 0) * gain
    ).astype(BF16)
    for b in range(LEAVES):
        block = slice(b * LEAF, (b + 1) * LEAF)
        q2 = scaled_queries(qn_ref[block])
        g2 = by_head(g_ref[block])
        half = (1 - b // 2) * LEAF
        stats = [
            weigh(kv_ref[(b + i - 1) * LEAF : (b + i) * LEAF], q2, g2)[2]
            for i in range(3)
            if HALO_PIECE.get(b) != i
        ]
        top, total, mixed = weigh(one_ref[half : half + LEAF], q2, g2)[2]
        stats.append((top + LN2, total, mixed))
        top, total, mixed, _ = combine(stats)
        stat_ref[b] = jnp.concatenate([top, total, mixed, jnp.zeros((5, 2 * LEAF), F32)], axis=0)


def attend_kernel(
    qn_ref, g_ref, near_ref, p1_ref, p2_ref, z_ref,
    stat_ref, cross, halo, p1o_ref, p2o_ref, zo_ref,
    q2_scr, g2_scr, score_scr, weight_scr, pgrad_scr, low_scr, sgrad_scr, rims, mid_grad, far_scr, mid_scr, sems,
):
    index = lax.axis_index("seq")
    place = jnp.bitwise_and(index, 7)
    odd = jnp.bitwise_and(index, 1)
    peer_side = 1 - odd
    halo[peer_side] = p1_ref[:LEAF]
    halo[odd] = p2_ref[...]
    cross[:64] = z_ref[jnp.bitwise_xor(place, 1), FAR:]
    cross[64:128] = p1_ref[LEAF:]
    cross[128:192] = z_ref[jnp.bitwise_xor(place, 2), FAR:]
    cross[192:256] = z_ref[jnp.bitwise_xor(place, 3), FAR:]
    for i in range(4):
        cross[256 + 32 * i : 288 + 32 * i] = z_ref[jnp.bitwise_xor(place, 4 + i), FAR : FAR + 32]
    for s in range(8):
        for j in range(3):
            at = 384 + LEAF * j + 16 * s
            cross[at : at + 16] = z_ref[s, 16 * j : 16 * (j + 1)]

    outside = outside_bias()
    rim_rows = []
    for b in range(LEAVES):
        block = slice(b * LEAF, (b + 1) * LEAF)
        lanes = slice(2 * b * LEAF, 2 * (b + 1) * LEAF)
        q2 = scaled_queries(qn_ref[block])
        g2 = by_head(g_ref[block])
        q2_scr[lanes] = q2
        g2_scr[lanes] = g2
        side = 0 if b == 0 else 1
        stats = [(near_ref[b, 0:1], near_ref[b, 1:2], near_ref[b, 2:3])]
        score_scr[...] = dot(cross[:, :FEAT], q2, (1, 1))
        pgrad_scr[b, : 6 * LEAF] = dot(cross[:, FEAT:], g2, (1, 1))
        for i in range(6):
            rows = slice(i * LEAF, (i + 1) * LEAF)
            score = score_scr[rows]
            top = peak(score)
            weight = jnp.exp(score - top)
            weight_scr[b, rows] = weight
            mixed = add_up(weight * pgrad_scr[b, rows])
            stats.append((top + (i + 2) * LN2, add_up(weight), mixed))
        if b in HALO_PIECE:
            weight, pgrad, (top, total, mixed) = weigh(halo[side], q2, g2)
            weight_scr[b, 6 * LEAF :] = weight
            pgrad_scr[b, 6 * LEAF :] = pgrad
            stats.append((top + outside[b], total, mixed))
        top, total, mixed, factors = combine(stats)
        inverse = 1.0 / total
        delta = mixed * inverse
        stat_ref[b] = jnp.concatenate(
            [top, inverse, delta, jnp.zeros((5, 2 * LEAF), F32)], axis=0
        )
        for i in range(6):
            rows = slice(i * LEAF, (i + 1) * LEAF)
            prob = weight_scr[b, rows] * (factors[i + 1] * inverse)
            low_scr[rows, lanes] = prob.astype(BF16)
            sgrad_scr[rows, lanes] = (prob * (pgrad_scr[b, rows] - delta)).astype(BF16)
        if b in HALO_PIECE:
            rim_rows.append((b, side, lanes, factors[7] * inverse, delta))

    def grads(rows):
        keys = dot(sgrad_scr[rows], q2_scr[...], (1, 0))
        values = dot(low_scr[rows], g2_scr[...], (1, 0))
        return jnp.concatenate([keys, values], axis=1).astype(BF16)

    far = grads(slice(384, 768))
    for j in range(3):
        for s in range(8):
            at = LEAF * j + 16 * s
            far_scr[s, 16 * j : 16 * (j + 1)] = far[at : at + 16]
    copies = start_all(
        [
            pltpu.make_async_copy(far_scr.at[s], zo_ref.at[s, pl.ds(0, FAR)], sems.at[s])
            for s in range(8)
        ]
    )
    mid_grad[...] = grads(slice(0, 384))
    mid_scr[...] = jnp.zeros_like(mid_scr)
    mid_scr[1] = mid_grad[:64]
    mid_scr[2] = mid_grad[128:192]
    mid_scr[3] = mid_grad[192:256]
    for i in range(4):
        mid_scr[4 + i, :32] = mid_grad[256 + 32 * i : 288 + 32 * i]
    copies += start_all(
        [
            pltpu.make_async_copy(
                mid_scr.at[d],
                zo_ref.at[jnp.bitwise_xor(place, d), pl.ds(FAR, 64)],
                sems.at[8 + d],
            )
            for d in range(8)
        ]
    )
    for b, side, lanes, factor, delta in rim_rows:
        prob = weight_scr[b, 6 * LEAF :] * factor
        sgrad = (prob * (pgrad_scr[b, 6 * LEAF :] - delta)).astype(BF16)
        rims[side, :, :FEAT] = dot(sgrad, q2_scr[lanes], (1, 0)).astype(BF16)
        rims[side, :, FEAT:] = dot(prob.astype(BF16), g2_scr[lanes], (1, 0)).astype(BF16)
    p1o_ref[:LEAF] = rims[peer_side]
    p1o_ref[LEAF:] = mid_grad[64:128]
    p2o_ref[...] = rims[odd]
    wait_all(copies)


def after_kernel(
    stat_ref, qn_ref, kv_ref, one_ref, g_ref, halo, cross, sum_ref, q_ref,
    att_ref, nqg_ref, tok_ref, qsum_ref, near, near_grad, one_grad,
):
    near[:LEAF] = halo[0]
    near[LEAF : LEAF + ROWS] = kv_ref[...]
    near[LEAF + ROWS :] = halo[1]
    near_grad[...] = jnp.zeros_like(near_grad)
    one_grad[...] = jnp.zeros_like(one_grad)
    feature = iota((FEAT, LEAF), 0)
    bias = far_bias()
    outside = outside_bias()

    def merge_heads(transposed):
        return jnp.where(feature < HEAD, transposed[:, :LEAF], transposed[:, LEAF:]).T

    for b in range(LEAVES):
        rows = slice(b * LEAF, (b + 1) * LEAF)
        near_rows = slice(b * LEAF, (b + 3) * LEAF)
        half = (1 - b // 2) * LEAF
        q2 = scaled_queries(qn_ref[rows])
        g2 = by_head(g_ref[rows])
        kv = jnp.concatenate([near[near_rows], one_ref[half : half + LEAF], cross[...]], axis=0)
        keys = kv[:, :FEAT]
        values = kv[:, FEAT:]
        raw = dot(keys, q2, (1, 1))
        before, after = raw[:LEAF], raw[2 * LEAF : 3 * LEAF]
        if b == 0:
            before = before + outside[b]
        if b == LEAVES - 1:
            after = after + outside[b]
        scores = jnp.concatenate(
            [before, raw[LEAF : 2 * LEAF], after, raw[3 * LEAF :] + bias], axis=0
        )
        probs = jnp.exp(scores - stat_ref[b, 0:1]) * stat_ref[b, 1:2]
        low = probs.astype(BF16)
        score_grad = (probs * (dot(values, g2, (1, 1)) - stat_ref[b, 2:3])).astype(BF16)
        att_ref[rows] = merge_heads(dot(values, low, (0, 0))).astype(BF16)
        nqg_ref[rows] = merge_heads(dot(keys, score_grad, (0, 0))) * 0.125
        for part, lanes in (
            (dot(score_grad[: 4 * LEAF], q2, (1, 0)), slice(0, FEAT)),
            (dot(low[: 4 * LEAF], g2, (1, 0)), slice(FEAT, 2 * FEAT)),
        ):
            near_grad[near_rows, lanes] += part[: 3 * LEAF]
            one_grad[half : half + LEAF, lanes] += part[3 * LEAF :]
    spread = spreading(0, 256, 1).astype(BF16)
    high = one_grad[...].astype(BF16)
    rest = (one_grad[...] - high.astype(F32)).astype(BF16)
    tok_ref[...] = near_grad[LEAF : LEAF + ROWS] + dot(spread, high, (1, 0)) + dot(spread, rest, (1, 0))
    gains = sum_ref[lax.axis_index("head"), 8:16]
    sums = token_sums(q_ref[...].astype(F32) * gains[0:1] * nqg_ref[...])
    qsum_ref[...] = jnp.concatenate(sums + [gains[1:2], jnp.zeros((3, FEAT), F32)], axis=0)


def column_kernel(z_ref, p1_ref, p2_ref, tok_ref, out_ref, far_rows, sem):
    column = jnp.right_shift(lax.axis_index("seq"), 3)
    copy = pltpu.make_async_copy(z_ref.at[:, pl.ds(0, FAR)], far_rows, sem)
    copy.start()
    copy.wait()
    far = jnp.sum(far_rows[...].astype(F32), axis=0).astype(BF16)
    slots = dot(far_pick((112, FAR), 1), far, (1, 0)).astype(BF16)
    out_ref[column] = jnp.zeros((16, 2 * FEAT), BF16)
    for d in range(1, 8):
        out_ref[jnp.bitwise_xor(column, d)] = slots[16 * (d - 1) : 16 * d]


def total_kernel(
    tok_ref, p1_ref, p2_ref, z_ref, y_ref, k_ref, qsum_ref,
    nkg_ref, vg_ref, sum_ref, acc,
):
    index = lax.axis_index("seq")
    column = jnp.right_shift(index, 3)
    place = jnp.bitwise_and(index, 7)
    odd = jnp.bitwise_and(index, 1)
    pieces = [z_ref[jnp.bitwise_xor(place, 1), FAR:], p1_ref[LEAF:]]
    maps = [spreading(0, 64, 2), spreading(64, 64, 2)]
    for d in range(2, 8):
        rows = ROWS >> ROW_LEVEL[d]
        pieces.append(z_ref[jnp.bitwise_xor(place, d), FAR : FAR + rows])
        maps.append(spreading(0, rows, ROW_LEVEL[d]))
    for d in range(1, 8):
        pieces.append(y_ref[jnp.bitwise_xor(column, d)])
        maps.append(spreading(0, 16, COLUMN_LEVEL[d]))
    spread = jnp.concatenate(maps, axis=1).astype(BF16)
    acc[...] = tok_ref[...] + dot(spread, jnp.concatenate(pieces, axis=0), (1, 0))
    acc[pl.ds(pl.multiple_of((1 - odd) * 384, LEAF), LEAF)] += p1_ref[:LEAF].astype(F32)
    acc[pl.ds(pl.multiple_of(odd * 384, LEAF), LEAF)] += p2_ref[...].astype(F32)
    vg_ref[...] = acc[:, FEAT:].astype(BF16)
    key_total = acc[:, :FEAT]
    nkg_ref[...] = key_total
    sums = token_sums(k_ref[...].astype(F32) * qsum_ref[LEAVES : LEAVES + 1] * key_total)
    tile = jnp.concatenate([qsum_ref[:LEAVES]] + sums, axis=0)
    for i in range(sum_ref.shape[0]):
        sum_ref[i] = tile


def finish_kernel(
    width, sq_ref, inner_ref, q_ref, k_ref, nqg_ref, nkg_ref, value_ref,
    dq_ref, dk_ref, vg_ref, results, sems,
):
    copies = start_all([pltpu.make_async_copy(value_ref, vg_ref, sems.at[2 * LEAVES])])
    rate = rates(width, sq_ref)
    inner = jnp.sum(inner_ref[...], axis=0) / width
    cubed = rate * rate * rate * inner
    gains = sq_ref[lax.axis_index("head"), 8:16]
    for side, (x_ref, grad_ref, out_ref) in enumerate(
        ((q_ref, nqg_ref, dq_ref), (k_ref, nkg_ref, dk_ref))
    ):
        results[side] = (
            spread_tokens(rate, 4 * side) * gains[side : side + 1] * grad_ref[...]
            - x_ref[...].astype(F32) * spread_tokens(cubed, 4 * side)
        ).astype(BF16)
        copies += start_all(
            [
                pltpu.make_async_copy(
                    results.at[side, rows], out_ref.at[rows], sems.at[LEAVES * side + i]
                )
                for i, rows in enumerate(BLOCKS)
            ]
        )
    wait_all(copies)


def call(kernel, outs, args, scratch=(), flops=0, name=None, spaces=None, out_spaces=None, vmem=40):
    many = isinstance(outs, list)
    moved = sum(math.prod(x.shape) * x.dtype.itemsize for x in list(args) + (outs if many else [outs]))
    out_spaces = out_spaces or [pltpu.VMEM] * (len(outs) if many else 1)
    out_specs = [pl.BlockSpec(memory_space=space) for space in out_spaces]
    return pl.pallas_call(
        kernel,
        out_shape=outs,
        in_specs=[pl.BlockSpec(memory_space=space) for space in spaces or [pltpu.VMEM] * len(args)],
        out_specs=out_specs if many else out_specs[0],
        scratch_shapes=list(scratch),
        compiler_params=pltpu.CompilerParams(vmem_limit_bytes=vmem * 1024 * 1024),
        cost_estimate=pl.CostEstimate(flops=flops, bytes_accessed=moved, transcendentals=0),
        name=name,
    )(*args)


def sds(*shape, dtype=BF16):
    return jax.ShapeDtypeStruct(shape, dtype)


ROW_GROUPS = [[8 * y + z for z in range(8)] for y in range(8)]
COLUMN_GROUPS = [[8 * y + z for y in range(8)] for z in range(8)]


def exchange(x, axis, groups=None):
    return lax.all_to_all(x, axis, 0, 0, axis_index_groups=groups, tiled=True)


def local(queries, key_rows, value_rows, query_gain, key_gain, out_grad):
    seq = lax.axis_size("seq")
    heads = lax.axis_size("head")
    width = float(heads * FEAT)
    qg = query_gain.reshape(1, FEAT)
    kg = key_gain.reshape(1, FEAT)
    peer = [(i, i ^ 1) for i in range(seq)]
    beside = [(i, i + 1) for i in range(1, seq - 1, 2)] + [(i + 1, i) for i in range(1, seq - 1, 2)]

    squares = call(
        squares_kernel,
        sds(heads, 16, FEAT, dtype=F32),
        (queries, key_rows, qg, kg),
        scratch=[
            pltpu.VMEM((2 * LEAVES, LEAF, FEAT), BF16),
            pltpu.VMEM((2, 1, FEAT), F32),
            pltpu.SemaphoreType.DMA((2 * LEAVES + 2,)),
        ],
        spaces=[pl.ANY] * 4,
        vmem=60,
        name="squares",
    )
    squares = exchange(squares, "head")
    kv, one, lv, ysend, p1, p2 = call(
        lambda *refs: norm_kernel(width, *refs),
        [sds(ROWS, 256), sds(256, 256), sds(224, 256), sds(8, 16, 256), sds(192, 256), sds(LEAF, 256)],
        (squares, key_rows, value_rows),
        name="norm",
    )
    p1 = lax.ppermute(p1, "seq", peer)
    p2 = lax.ppermute(p2, "seq", beside)
    yrecv = exchange(ysend, "seq", COLUMN_GROUPS)
    zsend = call(
        row_kernel,
        sds(8, SLOT, 256),
        (yrecv, lv),
        scratch=[pltpu.VMEM((FAR, 256), BF16), pltpu.SemaphoreType.DMA((16,))],
        out_spaces=[pl.ANY],
        name="rows",
    )
    zrecv = exchange(zsend, "seq", ROW_GROUPS)
    qn, near = call(
        lambda *refs: near_kernel(width, *refs),
        [sds(ROWS, FEAT), sds(LEAVES, 8, 256, dtype=F32)],
        (squares, queries, kv, one, out_grad),
        flops=14 * 2 * 2 * 256 * LEAF * FEAT,
        name="near",
    )
    stat, cross, halo, p1, p2, zsend = call(
        attend_kernel,
        [sds(LEAVES, 8, 256, dtype=F32), sds(768, 256), sds(2, LEAF, 256)]
        + [sds(192, 256), sds(LEAF, 256), sds(8, SLOT, 256)],
        (qn, out_grad, near, p1, p2, zrecv),
        scratch=[
            pltpu.VMEM((1024, FEAT), BF16),
            pltpu.VMEM((1024, FEAT), BF16),
            pltpu.VMEM((768, 256), F32),
            pltpu.VMEM((LEAVES, 7 * LEAF, 256), F32),
            pltpu.VMEM((LEAVES, 7 * LEAF, 256), F32),
            pltpu.VMEM((768, 1024), BF16),
            pltpu.VMEM((768, 1024), BF16),
            pltpu.VMEM((2, LEAF, 256), BF16),
            pltpu.VMEM((384, 256), BF16),
            pltpu.VMEM((8, FAR, 256), BF16),
            pltpu.VMEM((8, 64, 256), BF16),
            pltpu.SemaphoreType.DMA((16,)),
        ],
        out_spaces=[pltpu.VMEM] * 5 + [pl.ANY],
        flops=4 * 4 * 2 * 256 * 768 * FEAT,
        name="attend",
    )
    p1 = lax.ppermute(p1, "seq", peer)
    p2 = lax.ppermute(p2, "seq", beside)
    zrecv = exchange(zsend, "seq", ROW_GROUPS)
    attended, nqg, tok, qsum = call(
        after_kernel,
        [sds(ROWS, FEAT), sds(ROWS, FEAT, dtype=F32), sds(ROWS, 256, dtype=F32)]
        + [sds(8, FEAT, dtype=F32)],
        (stat, qn, kv, one, out_grad, halo, cross, squares, queries),
        scratch=[
            pltpu.VMEM((768, 256), BF16),
            pltpu.VMEM((768, 256), F32),
            pltpu.VMEM((256, 256), F32),
        ],
        flops=4 * 5 * 2 * 256 * KEYS * FEAT,
        name="after",
    )
    ysend = call(
        column_kernel,
        sds(8, 16, 256),
        (zrecv, p1, p2, tok),
        scratch=[pltpu.VMEM((8, FAR, 256), BF16), pltpu.SemaphoreType.DMA],
        spaces=[pl.ANY] * 4,
        name="columns",
    )
    yrecv = exchange(ysend, "seq", COLUMN_GROUPS)
    nkg, value_grad, inner = call(
        total_kernel,
        [sds(ROWS, FEAT, dtype=F32), sds(ROWS, FEAT), sds(heads, 8, FEAT, dtype=F32)],
        (tok, p1, p2, zrecv, yrecv, key_rows, qsum),
        scratch=[
            pltpu.VMEM((ROWS, 256), F32),
        ],
        name="total",
    )
    inner = exchange(inner, "head")
    query_grad, key_grad, value_grad = call(
        lambda *refs: finish_kernel(width, *refs),
        [sds(ROWS, FEAT), sds(ROWS, FEAT), sds(ROWS, FEAT)],
        (squares, inner, queries, key_rows, nqg, nkg, value_grad),
        scratch=[pltpu.VMEM((2, ROWS, FEAT), BF16), pltpu.SemaphoreType.DMA((2 * LEAVES + 1,))],
        out_spaces=[pl.ANY] * 3,
        name="finish",
    )
    return (attended, query_grad, key_grad, value_grad)


def solution(mesh):
    placed = (
        P("seq", "head"),
        P("seq", "head"),
        P("seq", "head"),
        P("head"),
        P("head"),
        P("seq", "head"),
    )
    return jax.shard_map(
        local,
        mesh=mesh,
        in_specs=placed,
        out_specs=(P("seq", "head"), P("seq", "head"), P("seq", "head"), P("seq", "head")),
        check_vma=False,
    )
```

```python
import math

import jax
import jax.numpy as jnp
from jax import lax
from jax.experimental import pallas as pl
from jax.experimental.pallas import tpu as pltpu
from jax.sharding import PartitionSpec as P

ROWS = 512
FEAT = 128
LEAF = 128
LEAVES = 4
HEAD = 64
KEYS = 1280
EPS = 1e-06
LN2 = math.log(2.0)
F32 = jnp.float32
BF16 = jnp.bfloat16
ROW_LEVEL = {1: 2, 2: 3, 3: 3, 4: 4, 5: 4, 6: 4, 7: 4}
COLUMN_LEVEL = {1: 5, 2: 6, 3: 6, 4: 7, 5: 7, 6: 7, 7: 7}
FAR = 48
SLOT = 112


def dot(a, b, dims):
    return lax.dot_general(a, b, ((dims[:1], dims[1:]), ((), ())), preferred_element_type=F32)


def iota(shape, axis):
    return lax.broadcasted_iota(jnp.int32, shape, axis)


def pooling(rows, level):
    token = iota((rows, ROWS), 1)
    hit = jnp.right_shift(token, level) == iota((rows, ROWS), 0)
    return jnp.where(hit, 2.0**-level, 0.0)


def spreading(first, rows, level):
    token = iota((ROWS, rows), 0)
    hit = jnp.right_shift(token, level) == iota((ROWS, rows), 1) + first
    return jnp.where(hit, 2.0**-level, 0.0)


def far_pick(shape, far_axis):
    far = iota(shape, far_axis)
    slot_row = iota(shape, 1 - far_axis)
    mid = far - 16
    low = far - 32
    column = jnp.where(
        far < 16,
        far,
        jnp.where(
            far < 32,
            (1 + jnp.right_shift(mid, 3)) * 16 + jnp.bitwise_and(mid, 7),
            (3 + jnp.right_shift(low, 2)) * 16 + jnp.bitwise_and(low, 3),
        ),
    )
    return jnp.where(column == slot_row, 1.0, 0.0).astype(BF16)


def token_sums(x):
    return [
        jnp.sum(x[i * LEAF : (i + 1) * LEAF].T, axis=0, keepdims=True) for i in range(LEAVES)
    ]


def spread_tokens(tile, first):
    return jnp.concatenate(
        [
            jnp.broadcast_to(tile[first + i : first + i + 1], (LEAF, LEAF)).T
            for i in range(LEAVES)
        ],
        axis=0,
    )


def squares_kernel(q_in, k_in, qg_in, kg_in, out_ref, rows, gains, sems):
    copies = [
        pltpu.make_async_copy(source, target, sems.at[i])
        for i, (source, target) in enumerate(
            ((q_in, rows.at[0]), (k_in, rows.at[1]), (qg_in, gains.at[0]), (kg_in, gains.at[1]))
        )
    ]
    for copy in copies:
        copy.start()
    sums = []
    for i in range(2):
        copies[i].wait()
        x = rows[i].astype(F32)
        sums += token_sums(x * x)
    for copy in copies[2:]:
        copy.wait()
    tile = jnp.concatenate(sums + [gains[0], gains[1], jnp.zeros((6, FEAT), F32)], axis=0)
    for i in range(out_ref.shape[0]):
        out_ref[i] = tile


def rates(width, sum_ref):
    return lax.rsqrt(jnp.sum(sum_ref[:, :8], axis=0) / width + EPS)


def norm_kernel(width, sum_ref, k_ref, v_ref, kv_ref, one_ref, lv_ref, y_ref, p1_ref, p2_ref):
    index = lax.axis_index("seq")
    column = jnp.right_shift(index, 3)
    odd = jnp.bitwise_and(index, 1)
    gain = sum_ref[lax.axis_index("head"), 9:10]
    kv_ref[:, :FEAT] = (
        k_ref[...].astype(F32) * spread_tokens(rates(width, sum_ref), 4) * gain
    ).astype(BF16)
    kv_ref[:, FEAT:] = v_ref[...]
    pool = jnp.concatenate(
        [pooling(ROWS >> level, level) for level in (1, 2, 3, 4)]
        + [pooling(16, COLUMN_LEVEL[d]) for d in range(1, 8)],
        axis=0,
    ).astype(BF16)
    coarse = dot(pool, kv_ref[...], (1, 0)).astype(BF16)
    one_ref[...] = coarse[:256]
    lv_ref[...] = coarse[256:480]
    y_ref[column] = jnp.zeros((16, 2 * FEAT), BF16)
    for d in range(1, 8):
        y_ref[jnp.bitwise_xor(column, d)] = coarse[464 + 16 * d : 480 + 16 * d]
    p1_ref[:LEAF] = kv_ref[pl.ds(pl.multiple_of((1 - odd) * 384, LEAF), LEAF)]
    p1_ref[LEAF:] = coarse[320:384]
    p2_ref[...] = kv_ref[pl.ds(pl.multiple_of(odd * 384, LEAF), LEAF)]


def start_all(copies):
    for copy in copies:
        copy.start()
    return copies


def wait_all(copies):
    for copy in copies:
        copy.wait()


def row_kernel(y_ref, lv_ref, out_ref, far_scr, mid_scr, sems):
    index = lax.axis_index("seq")
    column = jnp.right_shift(index, 3)
    place = jnp.bitwise_and(index, 7)
    mid_scr[place] = jnp.zeros((64, 2 * FEAT), BF16)
    for d in range(1, 8):
        other = jnp.bitwise_xor(place, d)
        if d < 4:
            mid_scr[other] = lv_ref[:64] if d == 1 else lv_ref[128:192]
        else:
            mid_scr[other, :32] = lv_ref[192:224]
            mid_scr[other, 32:] = jnp.zeros((32, 2 * FEAT), BF16)
    copies = start_all([pltpu.make_async_copy(mid_scr, out_ref.at[:, pl.ds(FAR, 64)], sems.at[0])])
    slots = jnp.concatenate([y_ref[jnp.bitwise_xor(column, d)] for d in range(1, 8)], axis=0)
    far = dot(far_pick((FAR, 112), 0), slots, (1, 0)).astype(BF16)
    for s in range(8):
        far_scr[s] = far
    copies += start_all([pltpu.make_async_copy(far_scr, out_ref.at[:, pl.ds(0, FAR)], sems.at[1])])
    wait_all(copies)


def by_head(block):
    lane = iota((LEAF, FEAT), 1)
    zero = jnp.zeros((LEAF, FEAT), BF16)
    return jnp.concatenate(
        [jnp.where(lane < HEAD, block, zero), jnp.where(lane < HEAD, zero, block)], axis=0
    )


def peak(x):
    return jnp.max(x, axis=0, keepdims=True)


def add_up(x):
    return jnp.sum(x, axis=0, keepdims=True)


HALO_PIECE = {0: 0, LEAVES - 1: 2}


def far_bias():
    return jnp.concatenate(
        [jnp.full((LEAF, 2 * LEAF), level * LN2, F32) for level in range(1, 8)], axis=0
    )


def outside_bias():
    index = lax.axis_index("seq")
    last = lax.axis_size("seq") - 1
    return {
        0: jnp.where(index > 0, 0.0, -1e30).astype(F32),
        LEAVES - 1: jnp.where(index < last, 0.0, -1e30).astype(F32),
    }


def weigh(kv, q2, g2):
    score = dot(kv[:, :FEAT], q2, (1, 1))
    top = peak(score)
    weight = jnp.exp(score - top)
    pgrad = dot(kv[:, FEAT:], g2, (1, 1))
    return weight, pgrad, (top, add_up(weight), add_up(weight * pgrad))


def combine(stats):
    top = stats[0][0]
    for stat in stats[1:]:
        top = jnp.maximum(top, stat[0])
    factors = [jnp.exp(stat[0] - top) for stat in stats]
    total = sum(factor * stat[1] for factor, stat in zip(factors, stats))
    mixed = sum(factor * stat[2] for factor, stat in zip(factors, stats))
    return top, total, mixed, factors


def scaled_queries(block):
    return by_head(block) * jnp.asarray(0.125, BF16)


def near_kernel(width, sum_ref, q_ref, kv_ref, one_ref, g_ref, qn_ref, stat_ref):
    gain = sum_ref[lax.axis_index("head"), 8:9]
    qn_ref[...] = (
        q_ref[...].astype(F32) * spread_tokens(rates(width, sum_ref), 0) * gain
    ).astype(BF16)
    for b in range(LEAVES):
        block = slice(b * LEAF, (b + 1) * LEAF)
        q2 = scaled_queries(qn_ref[block])
        g2 = by_head(g_ref[block])
        half = (1 - b // 2) * LEAF
        stats = [
            weigh(kv_ref[(b + i - 1) * LEAF : (b + i) * LEAF], q2, g2)[2]
            for i in range(3)
            if HALO_PIECE.get(b) != i
        ]
        top, total, mixed = weigh(one_ref[half : half + LEAF], q2, g2)[2]
        stats.append((top + LN2, total, mixed))
        top, total, mixed, _ = combine(stats)
        stat_ref[b] = jnp.concatenate([top, total, mixed, jnp.zeros((5, 2 * LEAF), F32)], axis=0)


def attend_kernel(
    qn_ref, g_ref, near_ref, p1_ref, p2_ref, z_ref,
    stat_ref, cross, halo, p1o_ref, p2o_ref, zo_ref,
    q2_scr, g2_scr, score_scr, weight_scr, pgrad_scr, low_scr, sgrad_scr, rims, mid_grad, far_scr, mid_scr, sems,
):
    index = lax.axis_index("seq")
    place = jnp.bitwise_and(index, 7)
    odd = jnp.bitwise_and(index, 1)
    peer_side = 1 - odd
    halo[peer_side] = p1_ref[:LEAF]
    halo[odd] = p2_ref[...]
    cross[:64] = z_ref[jnp.bitwise_xor(place, 1), FAR:]
    cross[64:128] = p1_ref[LEAF:]
    cross[128:192] = z_ref[jnp.bitwise_xor(place, 2), FAR:]
    cross[192:256] = z_ref[jnp.bitwise_xor(place, 3), FAR:]
    for i in range(4):
        cross[256 + 32 * i : 288 + 32 * i] = z_ref[jnp.bitwise_xor(place, 4 + i), FAR : FAR + 32]
    for s in range(8):
        for j in range(3):
            at = 384 + LEAF * j + 16 * s
            cross[at : at + 16] = z_ref[s, 16 * j : 16 * (j + 1)]

    outside = outside_bias()
    rim_rows = []
    for b in range(LEAVES):
        block = slice(b * LEAF, (b + 1) * LEAF)
        lanes = slice(2 * b * LEAF, 2 * (b + 1) * LEAF)
        q2 = scaled_queries(qn_ref[block])
        g2 = by_head(g_ref[block])
        q2_scr[lanes] = q2
        g2_scr[lanes] = g2
        side = 0 if b == 0 else 1
        stats = [(near_ref[b, 0:1], near_ref[b, 1:2], near_ref[b, 2:3])]
        score_scr[...] = dot(cross[:, :FEAT], q2, (1, 1))
        pgrad_scr[b, : 6 * LEAF] = dot(cross[:, FEAT:], g2, (1, 1))
        for i in range(6):
            rows = slice(i * LEAF, (i + 1) * LEAF)
            score = score_scr[rows]
            top = peak(score)
            weight = jnp.exp(score - top)
            weight_scr[b, rows] = weight
            mixed = add_up(weight * pgrad_scr[b, rows])
            stats.append((top + (i + 2) * LN2, add_up(weight), mixed))
        if b in HALO_PIECE:
            weight, pgrad, (top, total, mixed) = weigh(halo[side], q2, g2)
            weight_scr[b, 6 * LEAF :] = weight
            pgrad_scr[b, 6 * LEAF :] = pgrad
            stats.append((top + outside[b], total, mixed))
        top, total, mixed, factors = combine(stats)
        inverse = 1.0 / total
        delta = mixed * inverse
        stat_ref[b] = jnp.concatenate(
            [top, inverse, delta, jnp.zeros((5, 2 * LEAF), F32)], axis=0
        )
        for i in range(6):
            rows = slice(i * LEAF, (i + 1) * LEAF)
            prob = weight_scr[b, rows] * (factors[i + 1] * inverse)
            low_scr[rows, lanes] = prob.astype(BF16)
            sgrad_scr[rows, lanes] = (prob * (pgrad_scr[b, rows] - delta)).astype(BF16)
        if b in HALO_PIECE:
            rim_rows.append((b, side, lanes, factors[7] * inverse, delta))

    def grads(rows):
        keys = dot(sgrad_scr[rows], q2_scr[...], (1, 0))
        values = dot(low_scr[rows], g2_scr[...], (1, 0))
        return jnp.concatenate([keys, values], axis=1).astype(BF16)

    far = grads(slice(384, 768))
    for j in range(3):
        for s in range(8):
            at = LEAF * j + 16 * s
            far_scr[s, 16 * j : 16 * (j + 1)] = far[at : at + 16]
    copies = start_all([pltpu.make_async_copy(far_scr, zo_ref.at[:, pl.ds(0, FAR)], sems.at[0])])
    mid_grad[...] = grads(slice(0, 384))
    mid_scr[place] = jnp.zeros((64, 2 * FEAT), BF16)
    mid_scr[jnp.bitwise_xor(place, 1)] = mid_grad[:64]
    mid_scr[jnp.bitwise_xor(place, 2)] = mid_grad[128:192]
    mid_scr[jnp.bitwise_xor(place, 3)] = mid_grad[192:256]
    for i in range(4):
        other = jnp.bitwise_xor(place, 4 + i)
        mid_scr[other, :32] = mid_grad[256 + 32 * i : 288 + 32 * i]
        mid_scr[other, 32:] = jnp.zeros((32, 2 * FEAT), BF16)
    copies += start_all([pltpu.make_async_copy(mid_scr, zo_ref.at[:, pl.ds(FAR, 64)], sems.at[1])])
    for b, side, lanes, factor, delta in rim_rows:
        prob = weight_scr[b, 6 * LEAF :] * factor
        sgrad = (prob * (pgrad_scr[b, 6 * LEAF :] - delta)).astype(BF16)
        rims[side, :, :FEAT] = dot(sgrad, q2_scr[lanes], (1, 0)).astype(BF16)
        rims[side, :, FEAT:] = dot(prob.astype(BF16), g2_scr[lanes], (1, 0)).astype(BF16)
    p1o_ref[:LEAF] = rims[peer_side]
    p1o_ref[LEAF:] = mid_grad[64:128]
    p2o_ref[...] = rims[odd]
    wait_all(copies)


def after_kernel(
    stat_ref, qn_ref, kv_ref, one_ref, g_ref, halo, cross, sum_ref, q_ref,
    att_ref, nqg_ref, tok_ref, qsum_ref, near, near_grad, one_grad,
):
    near[:LEAF] = halo[0]
    near[LEAF : LEAF + ROWS] = kv_ref[...]
    near[LEAF + ROWS :] = halo[1]
    near_grad[...] = jnp.zeros_like(near_grad)
    one_grad[...] = jnp.zeros_like(one_grad)
    feature = iota((FEAT, LEAF), 0)
    bias = far_bias()
    outside = outside_bias()

    def merge_heads(transposed):
        return jnp.where(feature < HEAD, transposed[:, :LEAF], transposed[:, LEAF:]).T

    for b in range(LEAVES):
        rows = slice(b * LEAF, (b + 1) * LEAF)
        near_rows = slice(b * LEAF, (b + 3) * LEAF)
        half = (1 - b // 2) * LEAF
        q2 = scaled_queries(qn_ref[rows])
        g2 = by_head(g_ref[rows])
        kv = jnp.concatenate([near[near_rows], one_ref[half : half + LEAF], cross[...]], axis=0)
        keys = kv[:, :FEAT]
        values = kv[:, FEAT:]
        raw = dot(keys, q2, (1, 1))
        before, after = raw[:LEAF], raw[2 * LEAF : 3 * LEAF]
        if b == 0:
            before = before + outside[b]
        if b == LEAVES - 1:
            after = after + outside[b]
        scores = jnp.concatenate(
            [before, raw[LEAF : 2 * LEAF], after, raw[3 * LEAF :] + bias], axis=0
        )
        probs = jnp.exp(scores - stat_ref[b, 0:1]) * stat_ref[b, 1:2]
        low = probs.astype(BF16)
        score_grad = (probs * (dot(values, g2, (1, 1)) - stat_ref[b, 2:3])).astype(BF16)
        att_ref[rows] = merge_heads(dot(values, low, (0, 0))).astype(BF16)
        nqg_ref[rows] = merge_heads(dot(keys, score_grad, (0, 0))) * 0.125
        for part, lanes in (
            (dot(score_grad[: 4 * LEAF], q2, (1, 0)), slice(0, FEAT)),
            (dot(low[: 4 * LEAF], g2, (1, 0)), slice(FEAT, 2 * FEAT)),
        ):
            near_grad[near_rows, lanes] += part[: 3 * LEAF]
            one_grad[half : half + LEAF, lanes] += part[3 * LEAF :]
    spread = spreading(0, 256, 1).astype(BF16)
    high = one_grad[...].astype(BF16)
    rest = (one_grad[...] - high.astype(F32)).astype(BF16)
    tok_ref[...] = near_grad[LEAF : LEAF + ROWS] + dot(spread, high, (1, 0)) + dot(spread, rest, (1, 0))
    gains = sum_ref[lax.axis_index("head"), 8:16]
    sums = token_sums(q_ref[...].astype(F32) * gains[0:1] * nqg_ref[...])
    qsum_ref[...] = jnp.concatenate(sums + [gains[1:2], jnp.zeros((3, FEAT), F32)], axis=0)


def column_kernel(z_ref, p1_ref, p2_ref, tok_ref, out_ref, far_rows, sem):
    column = jnp.right_shift(lax.axis_index("seq"), 3)
    copy = pltpu.make_async_copy(z_ref.at[:, pl.ds(0, FAR)], far_rows, sem)
    copy.start()
    copy.wait()
    far = jnp.sum(far_rows[...].astype(F32), axis=0).astype(BF16)
    slots = dot(far_pick((112, FAR), 1), far, (1, 0)).astype(BF16)
    out_ref[column] = jnp.zeros((16, 2 * FEAT), BF16)
    for d in range(1, 8):
        out_ref[jnp.bitwise_xor(column, d)] = slots[16 * (d - 1) : 16 * d]


def total_kernel(
    tok_ref, p1_ref, p2_ref, z_ref, y_ref, k_ref, qsum_ref,
    nkg_ref, vg_ref, sum_ref, acc,
):
    index = lax.axis_index("seq")
    column = jnp.right_shift(index, 3)
    place = jnp.bitwise_and(index, 7)
    odd = jnp.bitwise_and(index, 1)
    pieces = [z_ref[jnp.bitwise_xor(place, 1), FAR:], p1_ref[LEAF:]]
    maps = [spreading(0, 64, 2), spreading(64, 64, 2)]
    for d in range(2, 8):
        rows = ROWS >> ROW_LEVEL[d]
        pieces.append(z_ref[jnp.bitwise_xor(place, d), FAR : FAR + rows])
        maps.append(spreading(0, rows, ROW_LEVEL[d]))
    for d in range(1, 8):
        pieces.append(y_ref[jnp.bitwise_xor(column, d)])
        maps.append(spreading(0, 16, COLUMN_LEVEL[d]))
    spread = jnp.concatenate(maps, axis=1).astype(BF16)
    acc[...] = tok_ref[...] + dot(spread, jnp.concatenate(pieces, axis=0), (1, 0))
    acc[pl.ds(pl.multiple_of((1 - odd) * 384, LEAF), LEAF)] += p1_ref[:LEAF].astype(F32)
    acc[pl.ds(pl.multiple_of(odd * 384, LEAF), LEAF)] += p2_ref[...].astype(F32)
    vg_ref[...] = acc[:, FEAT:].astype(BF16)
    key_total = acc[:, :FEAT]
    nkg_ref[...] = key_total
    sums = token_sums(k_ref[...].astype(F32) * qsum_ref[LEAVES : LEAVES + 1] * key_total)
    tile = jnp.concatenate([qsum_ref[:LEAVES]] + sums, axis=0)
    for i in range(sum_ref.shape[0]):
        sum_ref[i] = tile


def finish_kernel(
    width, sq_ref, inner_ref, q_ref, k_ref, nqg_ref, nkg_ref, value_ref,
    dq_ref, dk_ref, vg_ref, results, sems,
):
    copies = start_all([pltpu.make_async_copy(value_ref, vg_ref, sems.at[2])])
    rate = rates(width, sq_ref)
    inner = jnp.sum(inner_ref[...], axis=0) / width
    cubed = rate * rate * rate * inner
    gains = sq_ref[lax.axis_index("head"), 8:16]
    for side, (x_ref, grad_ref, out_ref) in enumerate(
        ((q_ref, nqg_ref, dq_ref), (k_ref, nkg_ref, dk_ref))
    ):
        results[side] = (
            spread_tokens(rate, 4 * side) * gains[side : side + 1] * grad_ref[...]
            - x_ref[...].astype(F32) * spread_tokens(cubed, 4 * side)
        ).astype(BF16)
        copies += start_all([pltpu.make_async_copy(results.at[side], out_ref, sems.at[side])])
    wait_all(copies)


def call(kernel, outs, args, scratch=(), flops=0, name=None, spaces=None, out_spaces=None, vmem=40):
    many = isinstance(outs, list)
    moved = sum(math.prod(x.shape) * x.dtype.itemsize for x in list(args) + (outs if many else [outs]))
    out_spaces = out_spaces or [pltpu.VMEM] * (len(outs) if many else 1)
    out_specs = [pl.BlockSpec(memory_space=space) for space in out_spaces]
    return pl.pallas_call(
        kernel,
        out_shape=outs,
        in_specs=[pl.BlockSpec(memory_space=space) for space in spaces or [pltpu.VMEM] * len(args)],
        out_specs=out_specs if many else out_specs[0],
        scratch_shapes=list(scratch),
        compiler_params=pltpu.CompilerParams(vmem_limit_bytes=vmem * 1024 * 1024),
        cost_estimate=pl.CostEstimate(flops=flops, bytes_accessed=moved, transcendentals=0),
        name=name,
    )(*args)


def sds(*shape, dtype=BF16):
    return jax.ShapeDtypeStruct(shape, dtype)


ROW_GROUPS = [[8 * y + z for z in range(8)] for y in range(8)]
COLUMN_GROUPS = [[8 * y + z for y in range(8)] for z in range(8)]


def exchange(x, axis, groups=None):
    return lax.all_to_all(x, axis, 0, 0, axis_index_groups=groups, tiled=True)


def local(queries, key_rows, value_rows, query_gain, key_gain, out_grad):
    seq = lax.axis_size("seq")
    heads = lax.axis_size("head")
    width = float(heads * FEAT)
    qg = query_gain.reshape(1, FEAT)
    kg = key_gain.reshape(1, FEAT)
    peer = [(i, i ^ 1) for i in range(seq)]
    beside = [(i, i + 1) for i in range(1, seq - 1, 2)] + [(i + 1, i) for i in range(1, seq - 1, 2)]

    squares = call(
        squares_kernel,
        sds(heads, 16, FEAT, dtype=F32),
        (queries, key_rows, qg, kg),
        scratch=[
            pltpu.VMEM((2, ROWS, FEAT), BF16),
            pltpu.VMEM((2, 1, FEAT), F32),
            pltpu.SemaphoreType.DMA((4,)),
        ],
        spaces=[pl.ANY] * 4,
        vmem=60,
        name="squares",
    )
    squares = exchange(squares, "head")
    kv, one, lv, ysend, p1, p2 = call(
        lambda *refs: norm_kernel(width, *refs),
        [sds(ROWS, 256), sds(256, 256), sds(224, 256), sds(8, 16, 256), sds(192, 256), sds(LEAF, 256)],
        (squares, key_rows, value_rows),
        name="norm",
    )
    p1 = lax.ppermute(p1, "seq", peer)
    p2 = lax.ppermute(p2, "seq", beside)
    yrecv = exchange(ysend, "seq", COLUMN_GROUPS)
    zsend = call(
        row_kernel,
        sds(8, SLOT, 256),
        (yrecv, lv),
        scratch=[
            pltpu.VMEM((8, FAR, 256), BF16),
            pltpu.VMEM((8, 64, 256), BF16),
            pltpu.SemaphoreType.DMA((2,)),
        ],
        out_spaces=[pl.ANY],
        name="rows",
    )
    zrecv = exchange(zsend, "seq", ROW_GROUPS)
    qn, near = call(
        lambda *refs: near_kernel(width, *refs),
        [sds(ROWS, FEAT), sds(LEAVES, 8, 256, dtype=F32)],
        (squares, queries, kv, one, out_grad),
        flops=14 * 2 * 2 * 256 * LEAF * FEAT,
        name="near",
    )
    stat, cross, halo, p1, p2, zsend = call(
        attend_kernel,
        [sds(LEAVES, 8, 256, dtype=F32), sds(768, 256), sds(2, LEAF, 256)]
        + [sds(192, 256), sds(LEAF, 256), sds(8, SLOT, 256)],
        (qn, out_grad, near, p1, p2, zrecv),
        scratch=[
            pltpu.VMEM((1024, FEAT), BF16),
            pltpu.VMEM((1024, FEAT), BF16),
            pltpu.VMEM((768, 256), F32),
            pltpu.VMEM((LEAVES, 7 * LEAF, 256), F32),
            pltpu.VMEM((LEAVES, 7 * LEAF, 256), F32),
            pltpu.VMEM((768, 1024), BF16),
            pltpu.VMEM((768, 1024), BF16),
            pltpu.VMEM((2, LEAF, 256), BF16),
            pltpu.VMEM((384, 256), BF16),
            pltpu.VMEM((8, FAR, 256), BF16),
            pltpu.VMEM((8, 64, 256), BF16),
            pltpu.SemaphoreType.DMA((2,)),
        ],
        out_spaces=[pltpu.VMEM] * 5 + [pl.ANY],
        flops=4 * 4 * 2 * 256 * 768 * FEAT,
        name="attend",
    )
    p1 = lax.ppermute(p1, "seq", peer)
    p2 = lax.ppermute(p2, "seq", beside)
    zrecv = exchange(zsend, "seq", ROW_GROUPS)
    attended, nqg, tok, qsum = call(
        after_kernel,
        [sds(ROWS, FEAT), sds(ROWS, FEAT, dtype=F32), sds(ROWS, 256, dtype=F32)]
        + [sds(8, FEAT, dtype=F32)],
        (stat, qn, kv, one, out_grad, halo, cross, squares, queries),
        scratch=[
            pltpu.VMEM((768, 256), BF16),
            pltpu.VMEM((768, 256), F32),
            pltpu.VMEM((256, 256), F32),
        ],
        flops=4 * 5 * 2 * 256 * KEYS * FEAT,
        name="after",
    )
    ysend = call(
        column_kernel,
        sds(8, 16, 256),
        (zrecv, p1, p2, tok),
        scratch=[pltpu.VMEM((8, FAR, 256), BF16), pltpu.SemaphoreType.DMA],
        spaces=[pl.ANY] * 4,
        name="columns",
    )
    yrecv = exchange(ysend, "seq", COLUMN_GROUPS)
    nkg, value_grad, inner = call(
        total_kernel,
        [sds(ROWS, FEAT, dtype=F32), sds(ROWS, FEAT), sds(heads, 8, FEAT, dtype=F32)],
        (tok, p1, p2, zrecv, yrecv, key_rows, qsum),
        scratch=[
            pltpu.VMEM((ROWS, 256), F32),
        ],
        name="total",
    )
    inner = exchange(inner, "head")
    query_grad, key_grad, value_grad = call(
        lambda *refs: finish_kernel(width, *refs),
        [sds(ROWS, FEAT), sds(ROWS, FEAT), sds(ROWS, FEAT)],
        (squares, inner, queries, key_rows, nqg, nkg, value_grad),
        scratch=[pltpu.VMEM((2, ROWS, FEAT), BF16), pltpu.SemaphoreType.DMA((3,))],
        out_spaces=[pl.ANY] * 3,
        name="finish",
    )
    return (attended, query_grad, key_grad, value_grad)


def solution(mesh):
    placed = (
        P("seq", "head"),
        P("seq", "head"),
        P("seq", "head"),
        P("head"),
        P("head"),
        P("seq", "head"),
    )
    return jax.shard_map(
        local,
        mesh=mesh,
        in_specs=placed,
        out_specs=(P("seq", "head"), P("seq", "head"), P("seq", "head"), P("seq", "head")),
        check_vma=False,
    )
```

```python
import math

import jax
import jax.numpy as jnp
from jax import lax
from jax.experimental import pallas as pl
from jax.experimental.pallas import tpu as pltpu
from jax.sharding import PartitionSpec as P

ROWS = 512
FEAT = 128
LEAF = 128
LEAVES = 4
HEAD = 64
KEYS = 1280
EPS = 1e-06
LN2 = math.log(2.0)
F32 = jnp.float32
BF16 = jnp.bfloat16
ROW_LEVEL = {1: 2, 2: 3, 3: 3, 4: 4, 5: 4, 6: 4, 7: 4}
COLUMN_LEVEL = {1: 5, 2: 6, 3: 6, 4: 7, 5: 7, 6: 7, 7: 7}
FAR = 48
SLOT = 112


def dot(a, b, dims):
    return lax.dot_general(a, b, ((dims[:1], dims[1:]), ((), ())), preferred_element_type=F32)


def iota(shape, axis):
    return lax.broadcasted_iota(jnp.int32, shape, axis)


def pooling(rows, level):
    token = iota((rows, ROWS), 1)
    hit = jnp.right_shift(token, level) == iota((rows, ROWS), 0)
    return jnp.where(hit, 2.0**-level, 0.0)


def spreading(first, rows, level):
    token = iota((ROWS, rows), 0)
    hit = jnp.right_shift(token, level) == iota((ROWS, rows), 1) + first
    return jnp.where(hit, 2.0**-level, 0.0)


def far_pick(shape, far_axis):
    far = iota(shape, far_axis)
    slot_row = iota(shape, 1 - far_axis)
    mid = far - 16
    low = far - 32
    column = jnp.where(
        far < 16,
        far,
        jnp.where(
            far < 32,
            (1 + jnp.right_shift(mid, 3)) * 16 + jnp.bitwise_and(mid, 7),
            (3 + jnp.right_shift(low, 2)) * 16 + jnp.bitwise_and(low, 3),
        ),
    )
    return jnp.where(column == slot_row, 1.0, 0.0).astype(BF16)


def token_sums(x):
    return [
        jnp.sum(x[i * LEAF : (i + 1) * LEAF].T, axis=0, keepdims=True) for i in range(LEAVES)
    ]


def spread_tokens(tile, first):
    return jnp.concatenate(
        [
            jnp.broadcast_to(tile[first + i : first + i + 1], (LEAF, LEAF)).T
            for i in range(LEAVES)
        ],
        axis=0,
    )


def squares_kernel(q_in, k_in, qg_in, kg_in, out_ref, rows, gains, sems):
    copies = [
        pltpu.make_async_copy(source, target, sems.at[i])
        for i, (source, target) in enumerate(
            ((q_in, rows.at[0]), (k_in, rows.at[1]), (qg_in, gains.at[0]), (kg_in, gains.at[1]))
        )
    ]
    for copy in copies:
        copy.start()
    sums = []
    for i in range(2):
        copies[i].wait()
        x = rows[i].astype(F32)
        sums += token_sums(x * x)
    for copy in copies[2:]:
        copy.wait()
    tile = jnp.concatenate(sums + [gains[0], gains[1], jnp.zeros((6, FEAT), F32)], axis=0)
    for i in range(out_ref.shape[0]):
        out_ref[i] = tile


def rates(width, sum_ref):
    return lax.rsqrt(jnp.sum(sum_ref[:, :8], axis=0) / width + EPS)


def norm_kernel(width, sum_ref, k_ref, v_ref, kv_ref, one_ref, lv_ref, y_ref, p1_ref, p2_ref):
    index = lax.axis_index("seq")
    column = jnp.right_shift(index, 3)
    odd = jnp.bitwise_and(index, 1)
    gain = sum_ref[lax.axis_index("head"), 9:10]
    kv_ref[:, :FEAT] = (
        k_ref[...].astype(F32) * spread_tokens(rates(width, sum_ref), 4) * gain
    ).astype(BF16)
    kv_ref[:, FEAT:] = v_ref[...]
    pool = jnp.concatenate(
        [pooling(ROWS >> level, level) for level in (1, 2, 3, 4)]
        + [pooling(16, COLUMN_LEVEL[d]) for d in range(1, 8)],
        axis=0,
    ).astype(BF16)
    coarse = dot(pool, kv_ref[...], (1, 0)).astype(BF16)
    one_ref[...] = coarse[:256]
    lv_ref[...] = coarse[256:480]
    y_ref[column] = jnp.zeros((16, 2 * FEAT), BF16)
    for d in range(1, 8):
        y_ref[jnp.bitwise_xor(column, d)] = coarse[464 + 16 * d : 480 + 16 * d]
    p1_ref[:LEAF] = kv_ref[pl.ds(pl.multiple_of((1 - odd) * 384, LEAF), LEAF)]
    p1_ref[LEAF:] = coarse[320:384]
    p2_ref[...] = kv_ref[pl.ds(pl.multiple_of(odd * 384, LEAF), LEAF)]


def start_all(copies):
    for copy in copies:
        copy.start()
    return copies


def wait_all(copies):
    for copy in copies:
        copy.wait()


def row_kernel(y_ref, lv_ref, out_ref, far_scr, mid_scr, sems):
    index = lax.axis_index("seq")
    column = jnp.right_shift(index, 3)
    place = jnp.bitwise_and(index, 7)
    mid_scr[place] = jnp.zeros((64, 2 * FEAT), BF16)
    for d in range(1, 8):
        other = jnp.bitwise_xor(place, d)
        if d < 4:
            mid_scr[other] = lv_ref[:64] if d == 1 else lv_ref[128:192]
        else:
            mid_scr[other, :32] = lv_ref[192:224]
            mid_scr[other, 32:] = jnp.zeros((32, 2 * FEAT), BF16)
    copies = start_all([pltpu.make_async_copy(mid_scr, out_ref.at[:, pl.ds(FAR, 64)], sems.at[0])])
    slots = jnp.concatenate([y_ref[jnp.bitwise_xor(column, d)] for d in range(1, 8)], axis=0)
    far = dot(far_pick((FAR, 112), 0), slots, (1, 0)).astype(BF16)
    for s in range(8):
        far_scr[s] = far
    copies += start_all([pltpu.make_async_copy(far_scr, out_ref.at[:, pl.ds(0, FAR)], sems.at[1])])
    wait_all(copies)


def by_head(block):
    lane = iota((LEAF, FEAT), 1)
    zero = jnp.zeros((LEAF, FEAT), BF16)
    return jnp.concatenate(
        [jnp.where(lane < HEAD, block, zero), jnp.where(lane < HEAD, zero, block)], axis=0
    )


def peak(x):
    return jnp.max(x, axis=0, keepdims=True)


def add_up(x):
    return jnp.sum(x, axis=0, keepdims=True)


HALO_PIECE = {0: 0, LEAVES - 1: 2}


def far_bias():
    return jnp.concatenate(
        [jnp.full((LEAF, 2 * LEAF), level * LN2, F32) for level in range(1, 8)], axis=0
    )


def outside_bias():
    index = lax.axis_index("seq")
    last = lax.axis_size("seq") - 1
    return {
        0: jnp.where(index > 0, 0.0, -1e30).astype(F32),
        LEAVES - 1: jnp.where(index < last, 0.0, -1e30).astype(F32),
    }


def weigh(kv, q2, g2):
    score = dot(kv[:, :FEAT], q2, (1, 1))
    top = peak(score)
    weight = jnp.exp(score - top)
    pgrad = dot(kv[:, FEAT:], g2, (1, 1))
    return weight, pgrad, (top, add_up(weight), add_up(weight * pgrad))


def combine(stats):
    top = stats[0][0]
    for stat in stats[1:]:
        top = jnp.maximum(top, stat[0])
    factors = [jnp.exp(stat[0] - top) for stat in stats]
    total = sum(factor * stat[1] for factor, stat in zip(factors, stats))
    mixed = sum(factor * stat[2] for factor, stat in zip(factors, stats))
    return top, total, mixed, factors


def scaled_queries(block):
    return by_head(block) * jnp.asarray(0.125, BF16)


def near_kernel(width, sum_ref, q_ref, kv_ref, one_ref, g_ref, qn_ref, stat_ref):
    gain = sum_ref[lax.axis_index("head"), 8:9]
    qn_ref[...] = (
        q_ref[...].astype(F32) * spread_tokens(rates(width, sum_ref), 0) * gain
    ).astype(BF16)
    for b in range(LEAVES):
        block = slice(b * LEAF, (b + 1) * LEAF)
        q2 = scaled_queries(qn_ref[block])
        g2 = by_head(g_ref[block])
        half = (1 - b // 2) * LEAF
        stats = [
            weigh(kv_ref[(b + i - 1) * LEAF : (b + i) * LEAF], q2, g2)[2]
            for i in range(3)
            if HALO_PIECE.get(b) != i
        ]
        top, total, mixed = weigh(one_ref[half : half + LEAF], q2, g2)[2]
        stats.append((top + LN2, total, mixed))
        top, total, mixed, _ = combine(stats)
        stat_ref[b] = jnp.concatenate([top, total, mixed, jnp.zeros((5, 2 * LEAF), F32)], axis=0)


def attend_kernel(
    qn_ref, g_ref, near_ref, p1_ref, p2_ref, z_ref,
    stat_ref, cross, halo, p1o_ref, p2o_ref, zo_ref,
    q2_scr, g2_scr, score_scr, weight_scr, pgrad_scr, low_scr, sgrad_scr, half_scr, rims, mid_grad,
    far_scr, mid_scr, sems,
):
    index = lax.axis_index("seq")
    place = jnp.bitwise_and(index, 7)
    odd = jnp.bitwise_and(index, 1)
    peer_side = 1 - odd
    halo[peer_side] = p1_ref[:LEAF]
    halo[odd] = p2_ref[...]
    cross[:64] = z_ref[jnp.bitwise_xor(place, 1), FAR:]
    cross[64:128] = p1_ref[LEAF:]
    cross[128:192] = z_ref[jnp.bitwise_xor(place, 2), FAR:]
    cross[192:256] = z_ref[jnp.bitwise_xor(place, 3), FAR:]
    for i in range(4):
        cross[256 + 32 * i : 288 + 32 * i] = z_ref[jnp.bitwise_xor(place, 4 + i), FAR : FAR + 32]
    for s in range(8):
        for j in range(3):
            at = 384 + LEAF * j + 16 * s
            cross[at : at + 16] = z_ref[s, 16 * j : 16 * (j + 1)]

    outside = outside_bias()
    rim_rows = []
    for b in range(LEAVES):
        block = slice(b * LEAF, (b + 1) * LEAF)
        lanes = slice(2 * b * LEAF, 2 * (b + 1) * LEAF)
        q2 = scaled_queries(qn_ref[block])
        g2 = by_head(g_ref[block])
        q2_scr[lanes] = q2
        g2_scr[lanes] = g2
        side = 0 if b == 0 else 1
        stats = [(near_ref[b, 0:1], near_ref[b, 1:2], near_ref[b, 2:3])]
        score_scr[b] = dot(cross[:, :FEAT], q2, (1, 1))
        pgrad_scr[b, : 6 * LEAF] = dot(cross[:, FEAT:], g2, (1, 1))
        for i in range(6):
            rows = slice(i * LEAF, (i + 1) * LEAF)
            score = score_scr[b, rows]
            top = peak(score)
            weight = jnp.exp(score - top)
            weight_scr[b, rows] = weight
            mixed = add_up(weight * pgrad_scr[b, rows])
            stats.append((top + (i + 2) * LN2, add_up(weight), mixed))
        if b in HALO_PIECE:
            weight, pgrad, (top, total, mixed) = weigh(halo[side], q2, g2)
            weight_scr[b, 6 * LEAF :] = weight
            pgrad_scr[b, 6 * LEAF :] = pgrad
            stats.append((top + outside[b], total, mixed))
        top, total, mixed, factors = combine(stats)
        inverse = 1.0 / total
        delta = mixed * inverse
        stat_ref[b] = jnp.concatenate(
            [top, inverse, delta, jnp.zeros((5, 2 * LEAF), F32)], axis=0
        )
        for i in range(6):
            rows = slice(i * LEAF, (i + 1) * LEAF)
            prob = weight_scr[b, rows] * (factors[i + 1] * inverse)
            low_scr[rows, lanes] = prob.astype(BF16)
            sgrad_scr[rows, lanes] = (prob * (pgrad_scr[b, rows] - delta)).astype(BF16)
        if b in HALO_PIECE:
            rim_rows.append((b, side, lanes, factors[7] * inverse, delta))
        if b == 1:
            half_scr[:, :FEAT] = dot(sgrad_scr[:, :512], q2_scr[:512], (1, 0))
            half_scr[:, FEAT:] = dot(low_scr[:, :512], g2_scr[:512], (1, 0))

    def grads(rows):
        keys = half_scr[rows, :FEAT] + dot(sgrad_scr[rows, 512:], q2_scr[512:], (1, 0))
        values = half_scr[rows, FEAT:] + dot(low_scr[rows, 512:], g2_scr[512:], (1, 0))
        return jnp.concatenate([keys, values], axis=1).astype(BF16)

    far = grads(slice(384, 768))
    for j in range(3):
        for s in range(8):
            at = LEAF * j + 16 * s
            far_scr[s, 16 * j : 16 * (j + 1)] = far[at : at + 16]
    copies = start_all([pltpu.make_async_copy(far_scr, zo_ref.at[:, pl.ds(0, FAR)], sems.at[0])])
    mid_grad[...] = grads(slice(0, 384))
    mid_scr[place] = jnp.zeros((64, 2 * FEAT), BF16)
    mid_scr[jnp.bitwise_xor(place, 1)] = mid_grad[:64]
    mid_scr[jnp.bitwise_xor(place, 2)] = mid_grad[128:192]
    mid_scr[jnp.bitwise_xor(place, 3)] = mid_grad[192:256]
    for i in range(4):
        other = jnp.bitwise_xor(place, 4 + i)
        mid_scr[other, :32] = mid_grad[256 + 32 * i : 288 + 32 * i]
        mid_scr[other, 32:] = jnp.zeros((32, 2 * FEAT), BF16)
    copies += start_all([pltpu.make_async_copy(mid_scr, zo_ref.at[:, pl.ds(FAR, 64)], sems.at[1])])
    for b, side, lanes, factor, delta in rim_rows:
        prob = weight_scr[b, 6 * LEAF :] * factor
        sgrad = (prob * (pgrad_scr[b, 6 * LEAF :] - delta)).astype(BF16)
        rims[side, :, :FEAT] = dot(sgrad, q2_scr[lanes], (1, 0)).astype(BF16)
        rims[side, :, FEAT:] = dot(prob.astype(BF16), g2_scr[lanes], (1, 0)).astype(BF16)
    p1o_ref[:LEAF] = rims[peer_side]
    p1o_ref[LEAF:] = mid_grad[64:128]
    p2o_ref[...] = rims[odd]
    wait_all(copies)


def after_kernel(
    stat_ref, qn_ref, kv_ref, one_ref, g_ref, halo, cross, sum_ref, q_ref,
    att_ref, nqg_ref, tok_ref, qsum_ref, near, near_grad, one_grad,
):
    near[:LEAF] = halo[0]
    near[LEAF : LEAF + ROWS] = kv_ref[...]
    near[LEAF + ROWS :] = halo[1]
    near_grad[...] = jnp.zeros_like(near_grad)
    one_grad[...] = jnp.zeros_like(one_grad)
    feature = iota((FEAT, LEAF), 0)
    bias = far_bias()
    outside = outside_bias()

    def merge_heads(transposed):
        return jnp.where(feature < HEAD, transposed[:, :LEAF], transposed[:, LEAF:]).T

    for b in range(LEAVES):
        rows = slice(b * LEAF, (b + 1) * LEAF)
        near_rows = slice(b * LEAF, (b + 3) * LEAF)
        half = (1 - b // 2) * LEAF
        q2 = scaled_queries(qn_ref[rows])
        g2 = by_head(g_ref[rows])
        kv = jnp.concatenate([near[near_rows], one_ref[half : half + LEAF], cross[...]], axis=0)
        keys = kv[:, :FEAT]
        values = kv[:, FEAT:]
        raw = dot(keys, q2, (1, 1))
        before, after = raw[:LEAF], raw[2 * LEAF : 3 * LEAF]
        if b == 0:
            before = before + outside[b]
        if b == LEAVES - 1:
            after = after + outside[b]
        scores = jnp.concatenate(
            [before, raw[LEAF : 2 * LEAF], after, raw[3 * LEAF :] + bias], axis=0
        )
        probs = jnp.exp(scores - stat_ref[b, 0:1]) * stat_ref[b, 1:2]
        low = probs.astype(BF16)
        score_grad = (probs * (dot(values, g2, (1, 1)) - stat_ref[b, 2:3])).astype(BF16)
        att_ref[rows] = merge_heads(dot(values, low, (0, 0))).astype(BF16)
        nqg_ref[rows] = merge_heads(dot(keys, score_grad, (0, 0))) * 0.125
        for part, lanes in (
            (dot(score_grad[: 4 * LEAF], q2, (1, 0)), slice(0, FEAT)),
            (dot(low[: 4 * LEAF], g2, (1, 0)), slice(FEAT, 2 * FEAT)),
        ):
            near_grad[near_rows, lanes] += part[: 3 * LEAF]
            one_grad[half : half + LEAF, lanes] += part[3 * LEAF :]
    spread = spreading(0, 256, 1).astype(BF16)
    high = one_grad[...].astype(BF16)
    rest = (one_grad[...] - high.astype(F32)).astype(BF16)
    tok_ref[...] = near_grad[LEAF : LEAF + ROWS] + dot(spread, high, (1, 0)) + dot(spread, rest, (1, 0))
    gains = sum_ref[lax.axis_index("head"), 8:16]
    sums = token_sums(q_ref[...].astype(F32) * gains[0:1] * nqg_ref[...])
    qsum_ref[...] = jnp.concatenate(sums + [gains[1:2], jnp.zeros((3, FEAT), F32)], axis=0)


def column_kernel(z_ref, p1_ref, p2_ref, tok_ref, out_ref, far_rows, sem):
    column = jnp.right_shift(lax.axis_index("seq"), 3)
    copy = pltpu.make_async_copy(z_ref.at[:, pl.ds(0, FAR)], far_rows, sem)
    copy.start()
    copy.wait()
    far = jnp.sum(far_rows[...].astype(F32), axis=0).astype(BF16)
    slots = dot(far_pick((112, FAR), 1), far, (1, 0)).astype(BF16)
    out_ref[column] = jnp.zeros((16, 2 * FEAT), BF16)
    for d in range(1, 8):
        out_ref[jnp.bitwise_xor(column, d)] = slots[16 * (d - 1) : 16 * d]


def total_kernel(
    tok_ref, p1_ref, p2_ref, z_ref, y_ref, k_ref, qsum_ref,
    nkg_ref, vg_ref, sum_ref, acc,
):
    index = lax.axis_index("seq")
    column = jnp.right_shift(index, 3)
    place = jnp.bitwise_and(index, 7)
    odd = jnp.bitwise_and(index, 1)
    pieces = [z_ref[jnp.bitwise_xor(place, 1), FAR:], p1_ref[LEAF:]]
    maps = [spreading(0, 64, 2), spreading(64, 64, 2)]
    for d in range(2, 8):
        rows = ROWS >> ROW_LEVEL[d]
        pieces.append(z_ref[jnp.bitwise_xor(place, d), FAR : FAR + rows])
        maps.append(spreading(0, rows, ROW_LEVEL[d]))
    for d in range(1, 8):
        pieces.append(y_ref[jnp.bitwise_xor(column, d)])
        maps.append(spreading(0, 16, COLUMN_LEVEL[d]))
    spread = jnp.concatenate(maps, axis=1).astype(BF16)
    acc[...] = tok_ref[...] + dot(spread, jnp.concatenate(pieces, axis=0), (1, 0))
    acc[pl.ds(pl.multiple_of((1 - odd) * 384, LEAF), LEAF)] += p1_ref[:LEAF].astype(F32)
    acc[pl.ds(pl.multiple_of(odd * 384, LEAF), LEAF)] += p2_ref[...].astype(F32)
    vg_ref[...] = acc[:, FEAT:].astype(BF16)
    key_total = acc[:, :FEAT]
    nkg_ref[...] = key_total
    sums = token_sums(k_ref[...].astype(F32) * qsum_ref[LEAVES : LEAVES + 1] * key_total)
    tile = jnp.concatenate([qsum_ref[:LEAVES]] + sums, axis=0)
    for i in range(sum_ref.shape[0]):
        sum_ref[i] = tile


def finish_kernel(
    width, sq_ref, inner_ref, q_ref, k_ref, nqg_ref, nkg_ref, value_ref,
    dq_ref, dk_ref, vg_ref, results, sems,
):
    copies = start_all([pltpu.make_async_copy(value_ref, vg_ref, sems.at[2])])
    rate = rates(width, sq_ref)
    inner = jnp.sum(inner_ref[...], axis=0) / width
    cubed = rate * rate * rate * inner
    gains = sq_ref[lax.axis_index("head"), 8:16]
    for side, (x_ref, grad_ref, out_ref) in enumerate(
        ((q_ref, nqg_ref, dq_ref), (k_ref, nkg_ref, dk_ref))
    ):
        results[side] = (
            spread_tokens(rate, 4 * side) * gains[side : side + 1] * grad_ref[...]
            - x_ref[...].astype(F32) * spread_tokens(cubed, 4 * side)
        ).astype(BF16)
        copies += start_all([pltpu.make_async_copy(results.at[side], out_ref, sems.at[side])])
    wait_all(copies)


def call(kernel, outs, args, scratch=(), flops=0, name=None, spaces=None, out_spaces=None, vmem=40):
    many = isinstance(outs, list)
    moved = sum(math.prod(x.shape) * x.dtype.itemsize for x in list(args) + (outs if many else [outs]))
    out_spaces = out_spaces or [pltpu.VMEM] * (len(outs) if many else 1)
    out_specs = [pl.BlockSpec(memory_space=space) for space in out_spaces]
    return pl.pallas_call(
        kernel,
        out_shape=outs,
        in_specs=[pl.BlockSpec(memory_space=space) for space in spaces or [pltpu.VMEM] * len(args)],
        out_specs=out_specs if many else out_specs[0],
        scratch_shapes=list(scratch),
        compiler_params=pltpu.CompilerParams(vmem_limit_bytes=vmem * 1024 * 1024),
        cost_estimate=pl.CostEstimate(flops=flops, bytes_accessed=moved, transcendentals=0),
        name=name,
    )(*args)


def sds(*shape, dtype=BF16):
    return jax.ShapeDtypeStruct(shape, dtype)


ROW_GROUPS = [[8 * y + z for z in range(8)] for y in range(8)]
COLUMN_GROUPS = [[8 * y + z for y in range(8)] for z in range(8)]


def exchange(x, axis, groups=None):
    return lax.all_to_all(x, axis, 0, 0, axis_index_groups=groups, tiled=True)


def local(queries, key_rows, value_rows, query_gain, key_gain, out_grad):
    seq = lax.axis_size("seq")
    heads = lax.axis_size("head")
    width = float(heads * FEAT)
    qg = query_gain.reshape(1, FEAT)
    kg = key_gain.reshape(1, FEAT)
    peer = [(i, i ^ 1) for i in range(seq)]
    beside = [(i, i + 1) for i in range(1, seq - 1, 2)] + [(i + 1, i) for i in range(1, seq - 1, 2)]

    squares = call(
        squares_kernel,
        sds(heads, 16, FEAT, dtype=F32),
        (queries, key_rows, qg, kg),
        scratch=[
            pltpu.VMEM((2, ROWS, FEAT), BF16),
            pltpu.VMEM((2, 1, FEAT), F32),
            pltpu.SemaphoreType.DMA((4,)),
        ],
        spaces=[pl.ANY] * 4,
        vmem=60,
        name="squares",
    )
    squares = exchange(squares, "head")
    kv, one, lv, ysend, p1, p2 = call(
        lambda *refs: norm_kernel(width, *refs),
        [sds(ROWS, 256), sds(256, 256), sds(224, 256), sds(8, 16, 256), sds(192, 256), sds(LEAF, 256)],
        (squares, key_rows, value_rows),
        name="norm",
    )
    p1 = lax.ppermute(p1, "seq", peer)
    p2 = lax.ppermute(p2, "seq", beside)
    yrecv = exchange(ysend, "seq", COLUMN_GROUPS)
    zsend = call(
        row_kernel,
        sds(8, SLOT, 256),
        (yrecv, lv),
        scratch=[
            pltpu.VMEM((8, FAR, 256), BF16),
            pltpu.VMEM((8, 64, 256), BF16),
            pltpu.SemaphoreType.DMA((2,)),
        ],
        out_spaces=[pl.ANY],
        name="rows",
    )
    zrecv = exchange(zsend, "seq", ROW_GROUPS)
    qn, near = call(
        lambda *refs: near_kernel(width, *refs),
        [sds(ROWS, FEAT), sds(LEAVES, 8, 256, dtype=F32)],
        (squares, queries, kv, one, out_grad),
        flops=14 * 2 * 2 * 256 * LEAF * FEAT,
        name="near",
    )
    stat, cross, halo, p1, p2, zsend = call(
        attend_kernel,
        [sds(LEAVES, 8, 256, dtype=F32), sds(768, 256), sds(2, LEAF, 256)]
        + [sds(192, 256), sds(LEAF, 256), sds(8, SLOT, 256)],
        (qn, out_grad, near, p1, p2, zrecv),
        scratch=[
            pltpu.VMEM((1024, FEAT), BF16),
            pltpu.VMEM((1024, FEAT), BF16),
            pltpu.VMEM((LEAVES, 768, 256), F32),
            pltpu.VMEM((LEAVES, 7 * LEAF, 256), F32),
            pltpu.VMEM((LEAVES, 7 * LEAF, 256), F32),
            pltpu.VMEM((768, 1024), BF16),
            pltpu.VMEM((768, 1024), BF16),
            pltpu.VMEM((768, 256), F32),
            pltpu.VMEM((2, LEAF, 256), BF16),
            pltpu.VMEM((384, 256), BF16),
            pltpu.VMEM((8, FAR, 256), BF16),
            pltpu.VMEM((8, 64, 256), BF16),
            pltpu.SemaphoreType.DMA((2,)),
        ],
        out_spaces=[pltpu.VMEM] * 5 + [pl.ANY],
        flops=4 * 4 * 2 * 256 * 768 * FEAT,
        name="attend",
    )
    p1 = lax.ppermute(p1, "seq", peer)
    p2 = lax.ppermute(p2, "seq", beside)
    zrecv = exchange(zsend, "seq", ROW_GROUPS)
    attended, nqg, tok, qsum = call(
        after_kernel,
        [sds(ROWS, FEAT), sds(ROWS, FEAT, dtype=F32), sds(ROWS, 256, dtype=F32)]
        + [sds(8, FEAT, dtype=F32)],
        (stat, qn, kv, one, out_grad, halo, cross, squares, queries),
        scratch=[
            pltpu.VMEM((768, 256), BF16),
            pltpu.VMEM((768, 256), F32),
            pltpu.VMEM((256, 256), F32),
        ],
        flops=4 * 5 * 2 * 256 * KEYS * FEAT,
        name="after",
    )
    ysend = call(
        column_kernel,
        sds(8, 16, 256),
        (zrecv, p1, p2, tok),
        scratch=[pltpu.VMEM((8, FAR, 256), BF16), pltpu.SemaphoreType.DMA],
        spaces=[pl.ANY] * 4,
        name="columns",
    )
    yrecv = exchange(ysend, "seq", COLUMN_GROUPS)
    nkg, value_grad, inner = call(
        total_kernel,
        [sds(ROWS, FEAT, dtype=F32), sds(ROWS, FEAT), sds(heads, 8, FEAT, dtype=F32)],
        (tok, p1, p2, zrecv, yrecv, key_rows, qsum),
        scratch=[
            pltpu.VMEM((ROWS, 256), F32),
        ],
        name="total",
    )
    inner = exchange(inner, "head")
    query_grad, key_grad, value_grad = call(
        lambda *refs: finish_kernel(width, *refs),
        [sds(ROWS, FEAT), sds(ROWS, FEAT), sds(ROWS, FEAT)],
        (squares, inner, queries, key_rows, nqg, nkg, value_grad),
        scratch=[pltpu.VMEM((2, ROWS, FEAT), BF16), pltpu.SemaphoreType.DMA((3,))],
        out_spaces=[pl.ANY] * 3,
        name="finish",
    )
    return (attended, query_grad, key_grad, value_grad)


def solution(mesh):
    placed = (
        P("seq", "head"),
        P("seq", "head"),
        P("seq", "head"),
        P("head"),
        P("head"),
        P("seq", "head"),
    )
    return jax.shard_map(
        local,
        mesh=mesh,
        in_specs=placed,
        out_specs=(P("seq", "head"), P("seq", "head"), P("seq", "head"), P("seq", "head")),
        check_vma=False,
    )
```

```python
import math

import jax
import jax.numpy as jnp
from jax import lax
from jax.experimental import pallas as pl
from jax.experimental.pallas import tpu as pltpu
from jax.sharding import PartitionSpec as P

ROWS = 512
FEAT = 128
LEAF = 128
LEAVES = 4
HEAD = 64
KEYS = 1280
EPS = 1e-06
LN2 = math.log(2.0)
F32 = jnp.float32
BF16 = jnp.bfloat16
ROW_LEVEL = {1: 2, 2: 3, 3: 3, 4: 4, 5: 4, 6: 4, 7: 4}
COLUMN_LEVEL = {1: 5, 2: 6, 3: 6, 4: 7, 5: 7, 6: 7, 7: 7}
FAR = 48
SLOT = 112


def dot(a, b, dims):
    return lax.dot_general(a, b, ((dims[:1], dims[1:]), ((), ())), preferred_element_type=F32)


def iota(shape, axis):
    return lax.broadcasted_iota(jnp.int32, shape, axis)


def pooling(rows, level, tokens=ROWS):
    token = iota((rows, tokens), 1)
    hit = jnp.right_shift(token, level) == iota((rows, tokens), 0)
    return jnp.where(hit, 2.0**-level, 0.0)


def spreading(first, rows, level, tokens=ROWS):
    token = iota((tokens, rows), 0)
    hit = jnp.right_shift(token, level) == iota((tokens, rows), 1) + first
    return jnp.where(hit, 2.0**-level, 0.0)


def far_pick(shape, far_axis):
    far = iota(shape, far_axis)
    slot_row = iota(shape, 1 - far_axis)
    mid = far - 16
    low = far - 32
    column = jnp.where(
        far < 16,
        far,
        jnp.where(
            far < 32,
            (1 + jnp.right_shift(mid, 3)) * 16 + jnp.bitwise_and(mid, 7),
            (3 + jnp.right_shift(low, 2)) * 16 + jnp.bitwise_and(low, 3),
        ),
    )
    return jnp.where(column == slot_row, 1.0, 0.0).astype(BF16)


def token_sums(x):
    return [
        jnp.sum(x[i * LEAF : (i + 1) * LEAF].T, axis=0, keepdims=True) for i in range(LEAVES)
    ]


def spread_tokens(tile, first):
    return jnp.concatenate(
        [
            jnp.broadcast_to(tile[first + i : first + i + 1], (LEAF, LEAF)).T
            for i in range(LEAVES)
        ],
        axis=0,
    )


def squares_kernel(q_in, k_in, qg_in, kg_in, out_ref, rows, gains, sems):
    copies = [
        pltpu.make_async_copy(source, target, sems.at[i])
        for i, (source, target) in enumerate(
            ((q_in, rows.at[0]), (k_in, rows.at[1]), (qg_in, gains.at[0]), (kg_in, gains.at[1]))
        )
    ]
    for copy in copies:
        copy.start()
    sums = []
    for i in range(2):
        copies[i].wait()
        x = rows[i].astype(F32)
        sums += token_sums(x * x)
    for copy in copies[2:]:
        copy.wait()
    tile = jnp.concatenate(sums + [gains[0], gains[1], jnp.zeros((6, FEAT), F32)], axis=0)
    for i in range(out_ref.shape[0]):
        out_ref[i] = tile


def rates(width, sum_ref):
    return lax.rsqrt(jnp.sum(sum_ref[:, :8], axis=0) / width + EPS)


def norm_kernel(width, sum_ref, k_ref, v_ref, kv_ref, one_ref, lv_ref, y_ref, p1_ref, p2_ref):
    index = lax.axis_index("seq")
    column = jnp.right_shift(index, 3)
    odd = jnp.bitwise_and(index, 1)
    gain = sum_ref[lax.axis_index("head"), 9:10]
    kv_ref[:, :FEAT] = (
        k_ref[...].astype(F32) * spread_tokens(rates(width, sum_ref), 4) * gain
    ).astype(BF16)
    kv_ref[:, FEAT:] = v_ref[...]
    pool = jnp.concatenate(
        [pooling(ROWS >> level, level) for level in (1, 2, 3, 4)]
        + [pooling(16, COLUMN_LEVEL[d]) for d in range(1, 8)],
        axis=0,
    ).astype(BF16)
    coarse = dot(pool, kv_ref[...], (1, 0)).astype(BF16)
    one_ref[...] = coarse[:256]
    lv_ref[...] = coarse[256:480]
    y_ref[column] = jnp.zeros((16, 2 * FEAT), BF16)
    for d in range(1, 8):
        y_ref[jnp.bitwise_xor(column, d)] = coarse[464 + 16 * d : 480 + 16 * d]
    p1_ref[:LEAF] = kv_ref[pl.ds(pl.multiple_of((1 - odd) * 384, LEAF), LEAF)]
    p1_ref[LEAF:] = lv_ref[pl.ds(pl.multiple_of(64 + 32 * odd, 32), 32)]
    p2_ref[...] = kv_ref[pl.ds(pl.multiple_of(odd * 384, LEAF), LEAF)]


def start_all(copies):
    for copy in copies:
        copy.start()
    return copies


def wait_all(copies):
    for copy in copies:
        copy.wait()


def row_kernel(y_ref, lv_ref, out_ref, far_scr, mid_scr, sems):
    index = lax.axis_index("seq")
    column = jnp.right_shift(index, 3)
    place = jnp.bitwise_and(index, 7)
    odd = jnp.bitwise_and(index, 1)
    mid_scr[place] = jnp.zeros((64, 2 * FEAT), BF16)
    for d in range(1, 8):
        other = jnp.bitwise_xor(place, d)
        if d < 4:
            first = pl.multiple_of(32 * odd, 32) if d == 1 else 128
            mid_scr[other] = lv_ref[pl.ds(first, 64)]
        else:
            mid_scr[other, :32] = lv_ref[192:224]
            mid_scr[other, 32:] = jnp.zeros((32, 2 * FEAT), BF16)
    copies = start_all([pltpu.make_async_copy(mid_scr, out_ref.at[:, pl.ds(FAR, 64)], sems.at[0])])
    slots = jnp.concatenate([y_ref[jnp.bitwise_xor(column, d)] for d in range(1, 8)], axis=0)
    far = dot(far_pick((FAR, 112), 0), slots, (1, 0)).astype(BF16)
    for s in range(8):
        far_scr[s] = far
    copies += start_all([pltpu.make_async_copy(far_scr, out_ref.at[:, pl.ds(0, FAR)], sems.at[1])])
    wait_all(copies)


def by_head(block):
    lane = iota((LEAF, FEAT), 1)
    zero = jnp.zeros((LEAF, FEAT), BF16)
    return jnp.concatenate(
        [jnp.where(lane < HEAD, block, zero), jnp.where(lane < HEAD, zero, block)], axis=0
    )


def peak(x):
    return jnp.max(x, axis=0, keepdims=True)


def add_up(x):
    return jnp.sum(x, axis=0, keepdims=True)


HALO_PIECE = {0: 0, LEAVES - 1: 2}


def far_bias():
    return jnp.concatenate(
        [jnp.full((LEAF, 2 * LEAF), level * LN2, F32) for level in range(1, 8)], axis=0
    )


def outside_bias():
    index = lax.axis_index("seq")
    last = lax.axis_size("seq") - 1
    return {
        0: jnp.where(index > 0, 0.0, -1e30).astype(F32),
        LEAVES - 1: jnp.where(index < last, 0.0, -1e30).astype(F32),
    }


def weigh(kv, q2, g2):
    score = dot(kv[:, :FEAT], q2, (1, 1))
    top = peak(score)
    weight = jnp.exp(score - top)
    pgrad = dot(kv[:, FEAT:], g2, (1, 1))
    return weight, pgrad, (top, add_up(weight), add_up(weight * pgrad))


def combine(stats):
    top = stats[0][0]
    for stat in stats[1:]:
        top = jnp.maximum(top, stat[0])
    factors = [jnp.exp(stat[0] - top) for stat in stats]
    total = sum(factor * stat[1] for factor, stat in zip(factors, stats))
    mixed = sum(factor * stat[2] for factor, stat in zip(factors, stats))
    return top, total, mixed, factors


def scaled_queries(block):
    return by_head(block) * jnp.asarray(0.125, BF16)


def near_kernel(width, sum_ref, q_ref, kv_ref, one_ref, g_ref, qn_ref, stat_ref):
    gain = sum_ref[lax.axis_index("head"), 8:9]
    qn_ref[...] = (
        q_ref[...].astype(F32) * spread_tokens(rates(width, sum_ref), 0) * gain
    ).astype(BF16)
    for b in range(LEAVES):
        block = slice(b * LEAF, (b + 1) * LEAF)
        q2 = scaled_queries(qn_ref[block])
        g2 = by_head(g_ref[block])
        half = (1 - b // 2) * LEAF
        stats = [
            weigh(kv_ref[(b + i - 1) * LEAF : (b + i) * LEAF], q2, g2)[2]
            for i in range(3)
            if HALO_PIECE.get(b) != i
        ]
        top, total, mixed = weigh(one_ref[half : half + LEAF], q2, g2)[2]
        stats.append((top + LN2, total, mixed))
        top, total, mixed, _ = combine(stats)
        stat_ref[b] = jnp.concatenate([top, total, mixed, jnp.zeros((5, 2 * LEAF), F32)], axis=0)


def attend_kernel(
    qn_ref, g_ref, near_ref, p1_ref, p2_ref, z_ref,
    stat_ref, cross, halo, p1o_ref, p2o_ref, zo_ref,
    q2_scr, g2_scr, score_scr, weight_scr, pgrad_scr, low_scr, sgrad_scr, rims, mid_grad, far_scr, mid_scr, sems,
):
    index = lax.axis_index("seq")
    place = jnp.bitwise_and(index, 7)
    odd = jnp.bitwise_and(index, 1)
    peer_side = 1 - odd
    halo[peer_side] = p1_ref[:LEAF]
    halo[odd] = p2_ref[...]
    cross[:64] = z_ref[jnp.bitwise_xor(place, 1), FAR:]
    cross[64:96] = p1_ref[LEAF:]
    cross[96:128] = dot(pooling(32, 2, LEAF).astype(BF16), p1_ref[:LEAF], (1, 0)).astype(BF16)
    cross[128:192] = z_ref[jnp.bitwise_xor(place, 2), FAR:]
    cross[192:256] = z_ref[jnp.bitwise_xor(place, 3), FAR:]
    for i in range(4):
        cross[256 + 32 * i : 288 + 32 * i] = z_ref[jnp.bitwise_xor(place, 4 + i), FAR : FAR + 32]
    for s in range(8):
        for j in range(3):
            at = 384 + LEAF * j + 16 * s
            cross[at : at + 16] = z_ref[s, 16 * j : 16 * (j + 1)]

    outside = outside_bias()
    rim_rows = []
    for b in range(LEAVES):
        block = slice(b * LEAF, (b + 1) * LEAF)
        lanes = slice(2 * b * LEAF, 2 * (b + 1) * LEAF)
        q2 = scaled_queries(qn_ref[block])
        g2 = by_head(g_ref[block])
        q2_scr[lanes] = q2
        g2_scr[lanes] = g2
        side = 0 if b == 0 else 1
        stats = [(near_ref[b, 0:1], near_ref[b, 1:2], near_ref[b, 2:3])]
        score_scr[...] = dot(cross[:, :FEAT], q2, (1, 1))
        pgrad_scr[b, : 6 * LEAF] = dot(cross[:, FEAT:], g2, (1, 1))
        for i in range(6):
            rows = slice(i * LEAF, (i + 1) * LEAF)
            score = score_scr[rows]
            top = peak(score)
            weight = jnp.exp(score - top)
            weight_scr[b, rows] = weight
            mixed = add_up(weight * pgrad_scr[b, rows])
            stats.append((top + (i + 2) * LN2, add_up(weight), mixed))
        if b in HALO_PIECE:
            weight, pgrad, (top, total, mixed) = weigh(halo[side], q2, g2)
            weight_scr[b, 6 * LEAF :] = weight
            pgrad_scr[b, 6 * LEAF :] = pgrad
            stats.append((top + outside[b], total, mixed))
        top, total, mixed, factors = combine(stats)
        inverse = 1.0 / total
        delta = mixed * inverse
        stat_ref[b] = jnp.concatenate(
            [top, inverse, delta, jnp.zeros((5, 2 * LEAF), F32)], axis=0
        )
        for i in range(6):
            rows = slice(i * LEAF, (i + 1) * LEAF)
            prob = weight_scr[b, rows] * (factors[i + 1] * inverse)
            low_scr[rows, lanes] = prob.astype(BF16)
            sgrad_scr[rows, lanes] = (prob * (pgrad_scr[b, rows] - delta)).astype(BF16)
        if b in HALO_PIECE:
            rim_rows.append((b, side, lanes, factors[7] * inverse, delta))

    def grads(rows):
        keys = dot(sgrad_scr[rows], q2_scr[...], (1, 0))
        values = dot(low_scr[rows], g2_scr[...], (1, 0))
        return jnp.concatenate([keys, values], axis=1).astype(BF16)

    far = grads(slice(384, 768))
    for j in range(3):
        for s in range(8):
            at = LEAF * j + 16 * s
            far_scr[s, 16 * j : 16 * (j + 1)] = far[at : at + 16]
    copies = start_all([pltpu.make_async_copy(far_scr, zo_ref.at[:, pl.ds(0, FAR)], sems.at[0])])
    mid_grad[...] = grads(slice(0, 384))
    mid_scr[place] = jnp.zeros((64, 2 * FEAT), BF16)
    mid_scr[jnp.bitwise_xor(place, 1)] = mid_grad[:64]
    mid_scr[jnp.bitwise_xor(place, 2)] = mid_grad[128:192]
    mid_scr[jnp.bitwise_xor(place, 3)] = mid_grad[192:256]
    for i in range(4):
        other = jnp.bitwise_xor(place, 4 + i)
        mid_scr[other, :32] = mid_grad[256 + 32 * i : 288 + 32 * i]
        mid_scr[other, 32:] = jnp.zeros((32, 2 * FEAT), BF16)
    copies += start_all([pltpu.make_async_copy(mid_scr, zo_ref.at[:, pl.ds(FAR, 64)], sems.at[1])])
    for b, side, lanes, factor, delta in rim_rows:
        prob = weight_scr[b, 6 * LEAF :] * factor
        sgrad = (prob * (pgrad_scr[b, 6 * LEAF :] - delta)).astype(BF16)
        rims[side, :, :FEAT] = dot(sgrad, q2_scr[lanes], (1, 0))
        rims[side, :, FEAT:] = dot(prob.astype(BF16), g2_scr[lanes], (1, 0))
    own_rows = dot(spreading(0, 32, 2, LEAF).astype(BF16), mid_grad[96:128], (1, 0))
    p1o_ref[:LEAF] = (rims[peer_side] + own_rows).astype(BF16)
    p1o_ref[LEAF:] = mid_grad[64:96]
    p2o_ref[...] = rims[odd].astype(BF16)
    wait_all(copies)


def after_kernel(
    stat_ref, qn_ref, kv_ref, one_ref, g_ref, halo, cross, sum_ref, q_ref,
    att_ref, nqg_ref, tok_ref, qsum_ref, near, near_grad, one_grad,
):
    near[:LEAF] = halo[0]
    near[LEAF : LEAF + ROWS] = kv_ref[...]
    near[LEAF + ROWS :] = halo[1]
    near_grad[...] = jnp.zeros_like(near_grad)
    one_grad[...] = jnp.zeros_like(one_grad)
    feature = iota((FEAT, LEAF), 0)
    bias = far_bias()
    outside = outside_bias()

    def merge_heads(transposed):
        return jnp.where(feature < HEAD, transposed[:, :LEAF], transposed[:, LEAF:]).T

    for b in range(LEAVES):
        rows = slice(b * LEAF, (b + 1) * LEAF)
        near_rows = slice(b * LEAF, (b + 3) * LEAF)
        half = (1 - b // 2) * LEAF
        q2 = scaled_queries(qn_ref[rows])
        g2 = by_head(g_ref[rows])
        kv = jnp.concatenate([near[near_rows], one_ref[half : half + LEAF], cross[...]], axis=0)
        keys = kv[:, :FEAT]
        values = kv[:, FEAT:]
        raw = dot(keys, q2, (1, 1))
        before, after = raw[:LEAF], raw[2 * LEAF : 3 * LEAF]
        if b == 0:
            before = before + outside[b]
        if b == LEAVES - 1:
            after = after + outside[b]
        scores = jnp.concatenate(
            [before, raw[LEAF : 2 * LEAF], after, raw[3 * LEAF :] + bias], axis=0
        )
        probs = jnp.exp(scores - stat_ref[b, 0:1]) * stat_ref[b, 1:2]
        low = probs.astype(BF16)
        score_grad = (probs * (dot(values, g2, (1, 1)) - stat_ref[b, 2:3])).astype(BF16)
        att_ref[rows] = merge_heads(dot(values, low, (0, 0))).astype(BF16)
        nqg_ref[rows] = merge_heads(dot(keys, score_grad, (0, 0))) * 0.125
        for part, lanes in (
            (dot(score_grad[: 4 * LEAF], q2, (1, 0)), slice(0, FEAT)),
            (dot(low[: 4 * LEAF], g2, (1, 0)), slice(FEAT, 2 * FEAT)),
        ):
            near_grad[near_rows, lanes] += part[: 3 * LEAF]
            one_grad[half : half + LEAF, lanes] += part[3 * LEAF :]
    spread = spreading(0, 256, 1).astype(BF16)
    high = one_grad[...].astype(BF16)
    rest = (one_grad[...] - high.astype(F32)).astype(BF16)
    tok_ref[...] = near_grad[LEAF : LEAF + ROWS] + dot(spread, high, (1, 0)) + dot(spread, rest, (1, 0))
    gains = sum_ref[lax.axis_index("head"), 8:16]
    sums = token_sums(q_ref[...].astype(F32) * gains[0:1] * nqg_ref[...])
    qsum_ref[...] = jnp.concatenate(sums + [gains[1:2], jnp.zeros((3, FEAT), F32)], axis=0)


def column_kernel(z_ref, p1_ref, p2_ref, tok_ref, out_ref, far_rows, sem):
    column = jnp.right_shift(lax.axis_index("seq"), 3)
    copy = pltpu.make_async_copy(z_ref.at[:, pl.ds(0, FAR)], far_rows, sem)
    copy.start()
    copy.wait()
    far = jnp.sum(far_rows[...].astype(F32), axis=0).astype(BF16)
    slots = dot(far_pick((112, FAR), 1), far, (1, 0)).astype(BF16)
    out_ref[column] = jnp.zeros((16, 2 * FEAT), BF16)
    for d in range(1, 8):
        out_ref[jnp.bitwise_xor(column, d)] = slots[16 * (d - 1) : 16 * d]


def total_kernel(
    tok_ref, p1_ref, p2_ref, z_ref, y_ref, k_ref, qsum_ref,
    nkg_ref, vg_ref, sum_ref, acc,
):
    index = lax.axis_index("seq")
    column = jnp.right_shift(index, 3)
    place = jnp.bitwise_and(index, 7)
    odd = jnp.bitwise_and(index, 1)
    pieces = [z_ref[jnp.bitwise_xor(place, 1), FAR:], p1_ref[LEAF:]]
    maps = [spreading(32 * odd, 64, 2), spreading(64 + 32 * odd, 32, 2)]
    for d in range(2, 8):
        rows = ROWS >> ROW_LEVEL[d]
        pieces.append(z_ref[jnp.bitwise_xor(place, d), FAR : FAR + rows])
        maps.append(spreading(0, rows, ROW_LEVEL[d]))
    for d in range(1, 8):
        pieces.append(y_ref[jnp.bitwise_xor(column, d)])
        maps.append(spreading(0, 16, COLUMN_LEVEL[d]))
    spread = jnp.concatenate(maps, axis=1).astype(BF16)
    acc[...] = tok_ref[...] + dot(spread, jnp.concatenate(pieces, axis=0), (1, 0))
    acc[pl.ds(pl.multiple_of((1 - odd) * 384, LEAF), LEAF)] += p1_ref[:LEAF].astype(F32)
    acc[pl.ds(pl.multiple_of(odd * 384, LEAF), LEAF)] += p2_ref[...].astype(F32)
    vg_ref[...] = acc[:, FEAT:].astype(BF16)
    key_total = acc[:, :FEAT]
    nkg_ref[...] = key_total
    sums = token_sums(k_ref[...].astype(F32) * qsum_ref[LEAVES : LEAVES + 1] * key_total)
    tile = jnp.concatenate([qsum_ref[:LEAVES]] + sums, axis=0)
    for i in range(sum_ref.shape[0]):
        sum_ref[i] = tile


def finish_kernel(
    width, sq_ref, inner_ref, q_ref, k_ref, nqg_ref, nkg_ref, value_ref,
    dq_ref, dk_ref, vg_ref, results, sems,
):
    copies = start_all([pltpu.make_async_copy(value_ref, vg_ref, sems.at[2])])
    rate = rates(width, sq_ref)
    inner = jnp.sum(inner_ref[...], axis=0) / width
    cubed = rate * rate * rate * inner
    gains = sq_ref[lax.axis_index("head"), 8:16]
    for side, (x_ref, grad_ref, out_ref) in enumerate(
        ((q_ref, nqg_ref, dq_ref), (k_ref, nkg_ref, dk_ref))
    ):
        results[side] = (
            spread_tokens(rate, 4 * side) * gains[side : side + 1] * grad_ref[...]
            - x_ref[...].astype(F32) * spread_tokens(cubed, 4 * side)
        ).astype(BF16)
        copies += start_all([pltpu.make_async_copy(results.at[side], out_ref, sems.at[side])])
    wait_all(copies)


def call(kernel, outs, args, scratch=(), flops=0, name=None, spaces=None, out_spaces=None, vmem=40):
    many = isinstance(outs, list)
    moved = sum(math.prod(x.shape) * x.dtype.itemsize for x in list(args) + (outs if many else [outs]))
    out_spaces = out_spaces or [pltpu.VMEM] * (len(outs) if many else 1)
    out_specs = [pl.BlockSpec(memory_space=space) for space in out_spaces]
    return pl.pallas_call(
        kernel,
        out_shape=outs,
        in_specs=[pl.BlockSpec(memory_space=space) for space in spaces or [pltpu.VMEM] * len(args)],
        out_specs=out_specs if many else out_specs[0],
        scratch_shapes=list(scratch),
        compiler_params=pltpu.CompilerParams(vmem_limit_bytes=vmem * 1024 * 1024),
        cost_estimate=pl.CostEstimate(flops=flops, bytes_accessed=moved, transcendentals=0),
        name=name,
    )(*args)


def sds(*shape, dtype=BF16):
    return jax.ShapeDtypeStruct(shape, dtype)


ROW_GROUPS = [[8 * y + z for z in range(8)] for y in range(8)]
COLUMN_GROUPS = [[8 * y + z for y in range(8)] for z in range(8)]


def exchange(x, axis, groups=None):
    return lax.all_to_all(x, axis, 0, 0, axis_index_groups=groups, tiled=True)


def local(queries, key_rows, value_rows, query_gain, key_gain, out_grad):
    seq = lax.axis_size("seq")
    heads = lax.axis_size("head")
    width = float(heads * FEAT)
    qg = query_gain.reshape(1, FEAT)
    kg = key_gain.reshape(1, FEAT)
    peer = [(i, i ^ 1) for i in range(seq)]
    beside = [(i, i + 1) for i in range(1, seq - 1, 2)] + [(i + 1, i) for i in range(1, seq - 1, 2)]

    squares = call(
        squares_kernel,
        sds(heads, 16, FEAT, dtype=F32),
        (queries, key_rows, qg, kg),
        scratch=[
            pltpu.VMEM((2, ROWS, FEAT), BF16),
            pltpu.VMEM((2, 1, FEAT), F32),
            pltpu.SemaphoreType.DMA((4,)),
        ],
        spaces=[pl.ANY] * 4,
        vmem=60,
        name="squares",
    )
    squares = exchange(squares, "head")
    kv, one, lv, ysend, p1, p2 = call(
        lambda *refs: norm_kernel(width, *refs),
        [sds(ROWS, 256), sds(256, 256), sds(224, 256), sds(8, 16, 256), sds(160, 256), sds(LEAF, 256)],
        (squares, key_rows, value_rows),
        name="norm",
    )
    p1 = lax.ppermute(p1, "seq", peer)
    p2 = lax.ppermute(p2, "seq", beside)
    yrecv = exchange(ysend, "seq", COLUMN_GROUPS)
    zsend = call(
        row_kernel,
        sds(8, SLOT, 256),
        (yrecv, lv),
        scratch=[
            pltpu.VMEM((8, FAR, 256), BF16),
            pltpu.VMEM((8, 64, 256), BF16),
            pltpu.SemaphoreType.DMA((2,)),
        ],
        out_spaces=[pl.ANY],
        name="rows",
    )
    zrecv = exchange(zsend, "seq", ROW_GROUPS)
    qn, near = call(
        lambda *refs: near_kernel(width, *refs),
        [sds(ROWS, FEAT), sds(LEAVES, 8, 256, dtype=F32)],
        (squares, queries, kv, one, out_grad),
        flops=14 * 2 * 2 * 256 * LEAF * FEAT,
        name="near",
    )
    stat, cross, halo, p1, p2, zsend = call(
        attend_kernel,
        [sds(LEAVES, 8, 256, dtype=F32), sds(768, 256), sds(2, LEAF, 256)]
        + [sds(160, 256), sds(LEAF, 256), sds(8, SLOT, 256)],
        (qn, out_grad, near, p1, p2, zrecv),
        scratch=[
            pltpu.VMEM((1024, FEAT), BF16),
            pltpu.VMEM((1024, FEAT), BF16),
            pltpu.VMEM((768, 256), F32),
            pltpu.VMEM((LEAVES, 7 * LEAF, 256), F32),
            pltpu.VMEM((LEAVES, 7 * LEAF, 256), F32),
            pltpu.VMEM((768, 1024), BF16),
            pltpu.VMEM((768, 1024), BF16),
            pltpu.VMEM((2, LEAF, 256), F32),
            pltpu.VMEM((384, 256), BF16),
            pltpu.VMEM((8, FAR, 256), BF16),
            pltpu.VMEM((8, 64, 256), BF16),
            pltpu.SemaphoreType.DMA((2,)),
        ],
        out_spaces=[pltpu.VMEM] * 5 + [pl.ANY],
        flops=4 * 4 * 2 * 256 * 768 * FEAT,
        name="attend",
    )
    p1 = lax.ppermute(p1, "seq", peer)
    p2 = lax.ppermute(p2, "seq", beside)
    zrecv = exchange(zsend, "seq", ROW_GROUPS)
    attended, nqg, tok, qsum = call(
        after_kernel,
        [sds(ROWS, FEAT), sds(ROWS, FEAT, dtype=F32), sds(ROWS, 256, dtype=F32)]
        + [sds(8, FEAT, dtype=F32)],
        (stat, qn, kv, one, out_grad, halo, cross, squares, queries),
        scratch=[
            pltpu.VMEM((768, 256), BF16),
            pltpu.VMEM((768, 256), F32),
            pltpu.VMEM((256, 256), F32),
        ],
        flops=4 * 5 * 2 * 256 * KEYS * FEAT,
        name="after",
    )
    ysend = call(
        column_kernel,
        sds(8, 16, 256),
        (zrecv, p1, p2, tok),
        scratch=[pltpu.VMEM((8, FAR, 256), BF16), pltpu.SemaphoreType.DMA],
        spaces=[pl.ANY] * 4,
        name="columns",
    )
    yrecv = exchange(ysend, "seq", COLUMN_GROUPS)
    nkg, value_grad, inner = call(
        total_kernel,
        [sds(ROWS, FEAT, dtype=F32), sds(ROWS, FEAT), sds(heads, 8, FEAT, dtype=F32)],
        (tok, p1, p2, zrecv, yrecv, key_rows, qsum),
        scratch=[
            pltpu.VMEM((ROWS, 256), F32),
        ],
        name="total",
    )
    inner = exchange(inner, "head")
    query_grad, key_grad, value_grad = call(
        lambda *refs: finish_kernel(width, *refs),
        [sds(ROWS, FEAT), sds(ROWS, FEAT), sds(ROWS, FEAT)],
        (squares, inner, queries, key_rows, nqg, nkg, value_grad),
        scratch=[pltpu.VMEM((2, ROWS, FEAT), BF16), pltpu.SemaphoreType.DMA((3,))],
        out_spaces=[pl.ANY] * 3,
        name="finish",
    )
    return (attended, query_grad, key_grad, value_grad)


def solution(mesh):
    placed = (
        P("seq", "head"),
        P("seq", "head"),
        P("seq", "head"),
        P("head"),
        P("head"),
        P("seq", "head"),
    )
    return jax.shard_map(
        local,
        mesh=mesh,
        in_specs=placed,
        out_specs=(P("seq", "head"), P("seq", "head"), P("seq", "head"), P("seq", "head")),
        check_vma=False,
    )
```

```python
import math

import jax
import jax.numpy as jnp
from jax import lax
from jax.experimental import pallas as pl
from jax.experimental.pallas import tpu as pltpu
from jax.sharding import PartitionSpec as P

ROWS = 512
FEAT = 128
LEAF = 128
LEAVES = 4
HEAD = 64
KEYS = 1280
EPS = 1e-06
LN2 = math.log(2.0)
F32 = jnp.float32
BF16 = jnp.bfloat16
ROW_LEVEL = {1: 2, 2: 3, 3: 3, 4: 4, 5: 4, 6: 4, 7: 4}
COLUMN_LEVEL = {1: 5, 2: 6, 3: 6, 4: 7, 5: 7, 6: 7, 7: 7}
FAR = 48
SLOT = 112


def dot(a, b, dims):
    return lax.dot_general(a, b, ((dims[:1], dims[1:]), ((), ())), preferred_element_type=F32)


def iota(shape, axis):
    return lax.broadcasted_iota(jnp.int32, shape, axis)


def pooling(rows, level):
    token = iota((rows, ROWS), 1)
    hit = jnp.right_shift(token, level) == iota((rows, ROWS), 0)
    return jnp.where(hit, 2.0**-level, 0.0)


def spreading(first, rows, level):
    token = iota((ROWS, rows), 0)
    hit = jnp.right_shift(token, level) == iota((ROWS, rows), 1) + first
    return jnp.where(hit, 2.0**-level, 0.0)


def far_pick(shape, far_axis):
    far = iota(shape, far_axis)
    slot_row = iota(shape, 1 - far_axis)
    mid = far - 16
    low = far - 32
    column = jnp.where(
        far < 16,
        far,
        jnp.where(
            far < 32,
            (1 + jnp.right_shift(mid, 3)) * 16 + jnp.bitwise_and(mid, 7),
            (3 + jnp.right_shift(low, 2)) * 16 + jnp.bitwise_and(low, 3),
        ),
    )
    return jnp.where(column == slot_row, 1.0, 0.0).astype(BF16)


def token_sums(x):
    return [
        jnp.sum(x[i * LEAF : (i + 1) * LEAF].T, axis=0, keepdims=True) for i in range(LEAVES)
    ]


def spread_tokens(tile, first):
    return jnp.concatenate(
        [
            jnp.broadcast_to(tile[first + i : first + i + 1], (LEAF, LEAF)).T
            for i in range(LEAVES)
        ],
        axis=0,
    )


def squares_kernel(q_in, k_in, qg_in, kg_in, out_ref, rows, gains, sems):
    copies = [
        pltpu.make_async_copy(source, target, sems.at[i])
        for i, (source, target) in enumerate(
            ((q_in, rows.at[0]), (k_in, rows.at[1]), (qg_in, gains.at[0]), (kg_in, gains.at[1]))
        )
    ]
    for copy in copies:
        copy.start()
    sums = []
    for i in range(2):
        copies[i].wait()
        x = rows[i].astype(F32)
        sums += token_sums(x * x)
    for copy in copies[2:]:
        copy.wait()
    tile = jnp.concatenate(sums + [gains[0], gains[1], jnp.zeros((6, FEAT), F32)], axis=0)
    for i in range(out_ref.shape[0]):
        out_ref[i] = tile


def rates(width, sum_ref):
    return lax.rsqrt(jnp.sum(sum_ref[:, :8], axis=0) / width + EPS)


def norm_kernel(width, sum_ref, k_ref, v_ref, kv_ref, one_ref, lv_ref, y_ref, p1_ref, p2_ref):
    index = lax.axis_index("seq")
    column = jnp.right_shift(index, 3)
    odd = jnp.bitwise_and(index, 1)
    gain = sum_ref[lax.axis_index("head"), 9:10]
    kv_ref[:, :FEAT] = (
        k_ref[...].astype(F32) * spread_tokens(rates(width, sum_ref), 4) * gain
    ).astype(BF16)
    kv_ref[:, FEAT:] = v_ref[...]
    pool = jnp.concatenate(
        [pooling(ROWS >> level, level) for level in (1, 2, 3, 4)]
        + [pooling(16, COLUMN_LEVEL[d]) for d in range(1, 8)],
        axis=0,
    ).astype(BF16)
    coarse = dot(pool, kv_ref[...], (1, 0)).astype(BF16)
    one_ref[...] = coarse[:256]
    lv_ref[...] = coarse[256:480]
    y_ref[column] = jnp.zeros((16, 2 * FEAT), BF16)
    for d in range(1, 8):
        y_ref[jnp.bitwise_xor(column, d)] = coarse[464 + 16 * d : 480 + 16 * d]
    p1_ref[:LEAF] = kv_ref[pl.ds(pl.multiple_of((1 - odd) * 384, LEAF), LEAF)]
    p1_ref[LEAF:] = coarse[320:384]
    p2_ref[...] = kv_ref[pl.ds(pl.multiple_of(odd * 384, LEAF), LEAF)]


def start_all(copies):
    for copy in copies:
        copy.start()
    return copies


def wait_all(copies):
    for copy in copies:
        copy.wait()


def row_kernel(y_ref, lv_ref, out_ref, far_scr, mid_scr, sems):
    index = lax.axis_index("seq")
    column = jnp.right_shift(index, 3)
    place = jnp.bitwise_and(index, 7)
    mid_scr[place] = jnp.zeros((64, 2 * FEAT), BF16)
    for d in range(1, 8):
        other = jnp.bitwise_xor(place, d)
        if d < 4:
            mid_scr[other] = lv_ref[:64] if d == 1 else lv_ref[128:192]
        else:
            mid_scr[other, :32] = lv_ref[192:224]
            mid_scr[other, 32:] = jnp.zeros((32, 2 * FEAT), BF16)
    copies = start_all([pltpu.make_async_copy(mid_scr, out_ref.at[:, pl.ds(FAR, 64)], sems.at[0])])
    slots = jnp.concatenate([y_ref[jnp.bitwise_xor(column, d)] for d in range(1, 8)], axis=0)
    far = dot(far_pick((FAR, 112), 0), slots, (1, 0)).astype(BF16)
    for s in range(8):
        far_scr[s] = far
    copies += start_all([pltpu.make_async_copy(far_scr, out_ref.at[:, pl.ds(0, FAR)], sems.at[1])])
    wait_all(copies)


def by_head(block):
    lane = iota((LEAF, FEAT), 1)
    zero = jnp.zeros((LEAF, FEAT), BF16)
    return jnp.concatenate(
        [jnp.where(lane < HEAD, block, zero), jnp.where(lane < HEAD, zero, block)], axis=0
    )


def peak(x):
    return jnp.max(x, axis=0, keepdims=True)


def add_up(x):
    return jnp.sum(x, axis=0, keepdims=True)


HALO_PIECE = {0: 0, LEAVES - 1: 2}


def far_bias():
    return jnp.concatenate(
        [jnp.full((LEAF, 2 * LEAF), level * LN2, F32) for level in range(1, 8)], axis=0
    )


def outside_bias():
    index = lax.axis_index("seq")
    last = lax.axis_size("seq") - 1
    return {
        0: jnp.where(index > 0, 0.0, -1e30).astype(F32),
        LEAVES - 1: jnp.where(index < last, 0.0, -1e30).astype(F32),
    }


def weigh(kv, q2, g2):
    score = dot(kv[:, :FEAT], q2, (1, 1))
    top = peak(score)
    weight = jnp.exp(score - top)
    pgrad = dot(kv[:, FEAT:], g2, (1, 1))
    return weight, pgrad, (top, add_up(weight), add_up(weight * pgrad))


def combine(stats):
    top = stats[0][0]
    for stat in stats[1:]:
        top = jnp.maximum(top, stat[0])
    factors = [jnp.exp(stat[0] - top) for stat in stats]
    total = sum(factor * stat[1] for factor, stat in zip(factors, stats))
    mixed = sum(factor * stat[2] for factor, stat in zip(factors, stats))
    return top, total, mixed, factors


def scaled_queries(block):
    return by_head(block) * jnp.asarray(0.125, BF16)


def near_kernel(width, sum_ref, q_ref, kv_ref, one_ref, g_ref, qn_ref, stat_ref):
    gain = sum_ref[lax.axis_index("head"), 8:9]
    qn_ref[...] = (
        q_ref[...].astype(F32) * spread_tokens(rates(width, sum_ref), 0) * gain
    ).astype(BF16)
    for b in range(LEAVES):
        block = slice(b * LEAF, (b + 1) * LEAF)
        q2 = scaled_queries(qn_ref[block])
        g2 = by_head(g_ref[block])
        half = (1 - b // 2) * LEAF
        stats = [
            weigh(kv_ref[(b + i - 1) * LEAF : (b + i) * LEAF], q2, g2)[2]
            for i in range(3)
            if HALO_PIECE.get(b) != i
        ]
        top, total, mixed = weigh(one_ref[half : half + LEAF], q2, g2)[2]
        stats.append((top + LN2, total, mixed))
        top, total, mixed, _ = combine(stats)
        stat_ref[b] = jnp.concatenate([top, total, mixed, jnp.zeros((5, 2 * LEAF), F32)], axis=0)


def attend_kernel(
    qn_ref, g_ref, near_ref, p1_ref, p2_ref, z_ref,
    stat_ref, cross, halo, p1o_ref, p2o_ref, zo_ref,
    q2_scr, g2_scr, score_scr, weight_scr, pgrad_scr, low_scr, sgrad_scr, rims, cross_grad, far_scr, mid_scr, sems,
):
    index = lax.axis_index("seq")
    place = jnp.bitwise_and(index, 7)
    odd = jnp.bitwise_and(index, 1)
    peer_side = 1 - odd
    halo[peer_side] = p1_ref[:LEAF]
    halo[odd] = p2_ref[...]
    cross[:64] = z_ref[jnp.bitwise_xor(place, 1), FAR:]
    cross[64:128] = p1_ref[LEAF:]
    cross[128:192] = z_ref[jnp.bitwise_xor(place, 2), FAR:]
    cross[192:256] = z_ref[jnp.bitwise_xor(place, 3), FAR:]
    for i in range(4):
        cross[256 + 32 * i : 288 + 32 * i] = z_ref[jnp.bitwise_xor(place, 4 + i), FAR : FAR + 32]
    for s in range(8):
        for j in range(3):
            at = 384 + LEAF * j + 16 * s
            cross[at : at + 16] = z_ref[s, 16 * j : 16 * (j + 1)]

    outside = outside_bias()
    rim_rows = []
    for b in range(LEAVES):
        block = slice(b * LEAF, (b + 1) * LEAF)
        lanes = slice(2 * b * LEAF, 2 * (b + 1) * LEAF)
        q2 = scaled_queries(qn_ref[block])
        g2 = by_head(g_ref[block])
        q2_scr[lanes] = q2
        g2_scr[lanes] = g2
        side = 0 if b == 0 else 1
        stats = [(near_ref[b, 0:1], near_ref[b, 1:2], near_ref[b, 2:3])]
        score_scr[b] = dot(cross[:, :FEAT], q2, (1, 1))
        pgrad_scr[b, : 6 * LEAF] = dot(cross[:, FEAT:], g2, (1, 1))
        for i in range(6):
            rows = slice(i * LEAF, (i + 1) * LEAF)
            score = score_scr[b, rows]
            top = peak(score)
            weight = jnp.exp(score - top)
            weight_scr[b, rows] = weight
            mixed = add_up(weight * pgrad_scr[b, rows])
            stats.append((top + (i + 2) * LN2, add_up(weight), mixed))
        if b in HALO_PIECE:
            weight, pgrad, (top, total, mixed) = weigh(halo[side], q2, g2)
            weight_scr[b, 6 * LEAF :] = weight
            pgrad_scr[b, 6 * LEAF :] = pgrad
            stats.append((top + outside[b], total, mixed))
        top, total, mixed, factors = combine(stats)
        inverse = 1.0 / total
        delta = mixed * inverse
        stat_ref[b] = jnp.concatenate(
            [top, inverse, delta, jnp.zeros((5, 2 * LEAF), F32)], axis=0
        )
        for i in range(6):
            rows = slice(i * LEAF, (i + 1) * LEAF)
            prob = weight_scr[b, rows] * (factors[i + 1] * inverse)
            low_scr[rows, lanes] = prob.astype(BF16)
            sgrad_scr[rows, lanes] = (prob * (pgrad_scr[b, rows] - delta)).astype(BF16)
        if b in HALO_PIECE:
            rim_rows.append((b, side, lanes, factors[7] * inverse, delta))

    cross_grad[:, :FEAT] = dot(sgrad_scr[...], q2_scr[...], (1, 0)).astype(BF16)
    cross_grad[:, FEAT:] = dot(low_scr[...], g2_scr[...], (1, 0)).astype(BF16)
    for j in range(3):
        for s in range(8):
            at = 384 + LEAF * j + 16 * s
            far_scr[s, 16 * j : 16 * (j + 1)] = cross_grad[at : at + 16]
    copies = start_all([pltpu.make_async_copy(far_scr, zo_ref.at[:, pl.ds(0, FAR)], sems.at[0])])
    mid_scr[place] = jnp.zeros((64, 2 * FEAT), BF16)
    mid_scr[jnp.bitwise_xor(place, 1)] = cross_grad[:64]
    mid_scr[jnp.bitwise_xor(place, 2)] = cross_grad[128:192]
    mid_scr[jnp.bitwise_xor(place, 3)] = cross_grad[192:256]
    for i in range(4):
        other = jnp.bitwise_xor(place, 4 + i)
        mid_scr[other, :32] = cross_grad[256 + 32 * i : 288 + 32 * i]
        mid_scr[other, 32:] = jnp.zeros((32, 2 * FEAT), BF16)
    copies += start_all([pltpu.make_async_copy(mid_scr, zo_ref.at[:, pl.ds(FAR, 64)], sems.at[1])])
    for b, side, lanes, factor, delta in rim_rows:
        prob = weight_scr[b, 6 * LEAF :] * factor
        sgrad = (prob * (pgrad_scr[b, 6 * LEAF :] - delta)).astype(BF16)
        rims[side, :, :FEAT] = dot(sgrad, q2_scr[lanes], (1, 0)).astype(BF16)
        rims[side, :, FEAT:] = dot(prob.astype(BF16), g2_scr[lanes], (1, 0)).astype(BF16)
    p1o_ref[:LEAF] = rims[peer_side]
    p1o_ref[LEAF:] = cross_grad[64:128]
    p2o_ref[...] = rims[odd]
    wait_all(copies)


def after_kernel(
    stat_ref, qn_ref, kv_ref, one_ref, g_ref, halo, cross, sum_ref, q_ref,
    att_ref, nqg_ref, tok_ref, qsum_ref, near, near_grad, one_grad,
):
    near[:LEAF] = halo[0]
    near[LEAF : LEAF + ROWS] = kv_ref[...]
    near[LEAF + ROWS :] = halo[1]
    near_grad[...] = jnp.zeros_like(near_grad)
    one_grad[...] = jnp.zeros_like(one_grad)
    feature = iota((FEAT, LEAF), 0)
    bias = far_bias()
    outside = outside_bias()

    def merge_heads(transposed):
        return jnp.where(feature < HEAD, transposed[:, :LEAF], transposed[:, LEAF:]).T

    for b in range(LEAVES):
        rows = slice(b * LEAF, (b + 1) * LEAF)
        near_rows = slice(b * LEAF, (b + 3) * LEAF)
        half = (1 - b // 2) * LEAF
        q2 = scaled_queries(qn_ref[rows])
        g2 = by_head(g_ref[rows])
        kv = jnp.concatenate([near[near_rows], one_ref[half : half + LEAF], cross[...]], axis=0)
        keys = kv[:, :FEAT]
        values = kv[:, FEAT:]
        raw = dot(keys, q2, (1, 1))
        before, after = raw[:LEAF], raw[2 * LEAF : 3 * LEAF]
        if b == 0:
            before = before + outside[b]
        if b == LEAVES - 1:
            after = after + outside[b]
        scores = jnp.concatenate(
            [before, raw[LEAF : 2 * LEAF], after, raw[3 * LEAF :] + bias], axis=0
        )
        probs = jnp.exp(scores - stat_ref[b, 0:1]) * stat_ref[b, 1:2]
        low = probs.astype(BF16)
        score_grad = (probs * (dot(values, g2, (1, 1)) - stat_ref[b, 2:3])).astype(BF16)
        att_ref[rows] = merge_heads(dot(values, low, (0, 0))).astype(BF16)
        nqg_ref[rows] = merge_heads(dot(keys, score_grad, (0, 0))) * 0.125
        for part, lanes in (
            (dot(score_grad[: 4 * LEAF], q2, (1, 0)), slice(0, FEAT)),
            (dot(low[: 4 * LEAF], g2, (1, 0)), slice(FEAT, 2 * FEAT)),
        ):
            near_grad[near_rows, lanes] += part[: 3 * LEAF]
            one_grad[half : half + LEAF, lanes] += part[3 * LEAF :]
    spread = spreading(0, 256, 1).astype(BF16)
    high = one_grad[...].astype(BF16)
    rest = (one_grad[...] - high.astype(F32)).astype(BF16)
    tok_ref[...] = near_grad[LEAF : LEAF + ROWS] + dot(spread, high, (1, 0)) + dot(spread, rest, (1, 0))
    gains = sum_ref[lax.axis_index("head"), 8:16]
    sums = token_sums(q_ref[...].astype(F32) * gains[0:1] * nqg_ref[...])
    qsum_ref[...] = jnp.concatenate(sums + [gains[1:2], jnp.zeros((3, FEAT), F32)], axis=0)


def column_kernel(z_ref, p1_ref, p2_ref, tok_ref, out_ref, far_rows, sem):
    column = jnp.right_shift(lax.axis_index("seq"), 3)
    copy = pltpu.make_async_copy(z_ref.at[:, pl.ds(0, FAR)], far_rows, sem)
    copy.start()
    copy.wait()
    far = jnp.sum(far_rows[...].astype(F32), axis=0).astype(BF16)
    slots = dot(far_pick((112, FAR), 1), far, (1, 0)).astype(BF16)
    out_ref[column] = jnp.zeros((16, 2 * FEAT), BF16)
    for d in range(1, 8):
        out_ref[jnp.bitwise_xor(column, d)] = slots[16 * (d - 1) : 16 * d]


def total_kernel(
    tok_ref, p1_ref, p2_ref, z_ref, y_ref, k_ref, qsum_ref,
    nkg_ref, vg_ref, sum_ref, acc,
):
    index = lax.axis_index("seq")
    column = jnp.right_shift(index, 3)
    place = jnp.bitwise_and(index, 7)
    odd = jnp.bitwise_and(index, 1)
    pieces = [z_ref[jnp.bitwise_xor(place, 1), FAR:], p1_ref[LEAF:]]
    maps = [spreading(0, 64, 2), spreading(64, 64, 2)]
    for d in range(2, 8):
        rows = ROWS >> ROW_LEVEL[d]
        pieces.append(z_ref[jnp.bitwise_xor(place, d), FAR : FAR + rows])
        maps.append(spreading(0, rows, ROW_LEVEL[d]))
    for d in range(1, 8):
        pieces.append(y_ref[jnp.bitwise_xor(column, d)])
        maps.append(spreading(0, 16, COLUMN_LEVEL[d]))
    spread = jnp.concatenate(maps, axis=1).astype(BF16)
    acc[...] = tok_ref[...] + dot(spread, jnp.concatenate(pieces, axis=0), (1, 0))
    acc[pl.ds(pl.multiple_of((1 - odd) * 384, LEAF), LEAF)] += p1_ref[:LEAF].astype(F32)
    acc[pl.ds(pl.multiple_of(odd * 384, LEAF), LEAF)] += p2_ref[...].astype(F32)
    vg_ref[...] = acc[:, FEAT:].astype(BF16)
    key_total = acc[:, :FEAT]
    nkg_ref[...] = key_total
    sums = token_sums(k_ref[...].astype(F32) * qsum_ref[LEAVES : LEAVES + 1] * key_total)
    tile = jnp.concatenate([qsum_ref[:LEAVES]] + sums, axis=0)
    for i in range(sum_ref.shape[0]):
        sum_ref[i] = tile


def finish_kernel(
    width, sq_ref, inner_ref, q_ref, k_ref, nqg_ref, nkg_ref, value_ref,
    dq_ref, dk_ref, vg_ref, results, sems,
):
    copies = start_all([pltpu.make_async_copy(value_ref, vg_ref, sems.at[2])])
    rate = rates(width, sq_ref)
    inner = jnp.sum(inner_ref[...], axis=0) / width
    cubed = rate * rate * rate * inner
    gains = sq_ref[lax.axis_index("head"), 8:16]
    for side, (x_ref, grad_ref, out_ref) in enumerate(
        ((q_ref, nqg_ref, dq_ref), (k_ref, nkg_ref, dk_ref))
    ):
        results[side] = (
            spread_tokens(rate, 4 * side) * gains[side : side + 1] * grad_ref[...]
            - x_ref[...].astype(F32) * spread_tokens(cubed, 4 * side)
        ).astype(BF16)
        copies += start_all([pltpu.make_async_copy(results.at[side], out_ref, sems.at[side])])
    wait_all(copies)


def call(kernel, outs, args, scratch=(), flops=0, name=None, spaces=None, out_spaces=None, vmem=40):
    many = isinstance(outs, list)
    moved = sum(math.prod(x.shape) * x.dtype.itemsize for x in list(args) + (outs if many else [outs]))
    out_spaces = out_spaces or [pltpu.VMEM] * (len(outs) if many else 1)
    out_specs = [pl.BlockSpec(memory_space=space) for space in out_spaces]
    return pl.pallas_call(
        kernel,
        out_shape=outs,
        in_specs=[pl.BlockSpec(memory_space=space) for space in spaces or [pltpu.VMEM] * len(args)],
        out_specs=out_specs if many else out_specs[0],
        scratch_shapes=list(scratch),
        compiler_params=pltpu.CompilerParams(vmem_limit_bytes=vmem * 1024 * 1024),
        cost_estimate=pl.CostEstimate(flops=flops, bytes_accessed=moved, transcendentals=0),
        name=name,
    )(*args)


def sds(*shape, dtype=BF16):
    return jax.ShapeDtypeStruct(shape, dtype)


ROW_GROUPS = [[8 * y + z for z in range(8)] for y in range(8)]
COLUMN_GROUPS = [[8 * y + z for y in range(8)] for z in range(8)]


def exchange(x, axis, groups=None):
    return lax.all_to_all(x, axis, 0, 0, axis_index_groups=groups, tiled=True)


def local(queries, key_rows, value_rows, query_gain, key_gain, out_grad):
    seq = lax.axis_size("seq")
    heads = lax.axis_size("head")
    width = float(heads * FEAT)
    qg = query_gain.reshape(1, FEAT)
    kg = key_gain.reshape(1, FEAT)
    peer = [(i, i ^ 1) for i in range(seq)]
    beside = [(i, i + 1) for i in range(1, seq - 1, 2)] + [(i + 1, i) for i in range(1, seq - 1, 2)]

    squares = call(
        squares_kernel,
        sds(heads, 16, FEAT, dtype=F32),
        (queries, key_rows, qg, kg),
        scratch=[
            pltpu.VMEM((2, ROWS, FEAT), BF16),
            pltpu.VMEM((2, 1, FEAT), F32),
            pltpu.SemaphoreType.DMA((4,)),
        ],
        spaces=[pl.ANY] * 4,
        vmem=60,
        name="squares",
    )
    squares = exchange(squares, "head")
    kv, one, lv, ysend, p1, p2 = call(
        lambda *refs: norm_kernel(width, *refs),
        [sds(ROWS, 256), sds(256, 256), sds(224, 256), sds(8, 16, 256), sds(192, 256), sds(LEAF, 256)],
        (squares, key_rows, value_rows),
        name="norm",
    )
    p1 = lax.ppermute(p1, "seq", peer)
    p2 = lax.ppermute(p2, "seq", beside)
    yrecv = exchange(ysend, "seq", COLUMN_GROUPS)
    zsend = call(
        row_kernel,
        sds(8, SLOT, 256),
        (yrecv, lv),
        scratch=[
            pltpu.VMEM((8, FAR, 256), BF16),
            pltpu.VMEM((8, 64, 256), BF16),
            pltpu.SemaphoreType.DMA((2,)),
        ],
        out_spaces=[pl.ANY],
        name="rows",
    )
    zrecv = exchange(zsend, "seq", ROW_GROUPS)
    qn, near = call(
        lambda *refs: near_kernel(width, *refs),
        [sds(ROWS, FEAT), sds(LEAVES, 8, 256, dtype=F32)],
        (squares, queries, kv, one, out_grad),
        flops=14 * 2 * 2 * 256 * LEAF * FEAT,
        name="near",
    )
    stat, cross, halo, p1, p2, zsend = call(
        attend_kernel,
        [sds(LEAVES, 8, 256, dtype=F32), sds(768, 256), sds(2, LEAF, 256)]
        + [sds(192, 256), sds(LEAF, 256), sds(8, SLOT, 256)],
        (qn, out_grad, near, p1, p2, zrecv),
        scratch=[
            pltpu.VMEM((1024, FEAT), BF16),
            pltpu.VMEM((1024, FEAT), BF16),
            pltpu.VMEM((LEAVES, 768, 256), F32),
            pltpu.VMEM((LEAVES, 7 * LEAF, 256), F32),
            pltpu.VMEM((LEAVES, 7 * LEAF, 256), F32),
            pltpu.VMEM((768, 1024), BF16),
            pltpu.VMEM((768, 1024), BF16),
            pltpu.VMEM((2, LEAF, 256), BF16),
            pltpu.VMEM((768, 256), BF16),
            pltpu.VMEM((8, FAR, 256), BF16),
            pltpu.VMEM((8, 64, 256), BF16),
            pltpu.SemaphoreType.DMA((2,)),
        ],
        out_spaces=[pltpu.VMEM] * 5 + [pl.ANY],
        flops=4 * 4 * 2 * 256 * 768 * FEAT,
        name="attend",
    )
    p1 = lax.ppermute(p1, "seq", peer)
    p2 = lax.ppermute(p2, "seq", beside)
    zrecv = exchange(zsend, "seq", ROW_GROUPS)
    attended, nqg, tok, qsum = call(
        after_kernel,
        [sds(ROWS, FEAT), sds(ROWS, FEAT, dtype=F32), sds(ROWS, 256, dtype=F32)]
        + [sds(8, FEAT, dtype=F32)],
        (stat, qn, kv, one, out_grad, halo, cross, squares, queries),
        scratch=[
            pltpu.VMEM((768, 256), BF16),
            pltpu.VMEM((768, 256), F32),
            pltpu.VMEM((256, 256), F32),
        ],
        flops=4 * 5 * 2 * 256 * KEYS * FEAT,
        name="after",
    )
    ysend = call(
        column_kernel,
        sds(8, 16, 256),
        (zrecv, p1, p2, tok),
        scratch=[pltpu.VMEM((8, FAR, 256), BF16), pltpu.SemaphoreType.DMA],
        spaces=[pl.ANY] * 4,
        name="columns",
    )
    yrecv = exchange(ysend, "seq", COLUMN_GROUPS)
    nkg, value_grad, inner = call(
        total_kernel,
        [sds(ROWS, FEAT, dtype=F32), sds(ROWS, FEAT), sds(heads, 8, FEAT, dtype=F32)],
        (tok, p1, p2, zrecv, yrecv, key_rows, qsum),
        scratch=[
            pltpu.VMEM((ROWS, 256), F32),
        ],
        name="total",
    )
    inner = exchange(inner, "head")
    query_grad, key_grad, value_grad = call(
        lambda *refs: finish_kernel(width, *refs),
        [sds(ROWS, FEAT), sds(ROWS, FEAT), sds(ROWS, FEAT)],
        (squares, inner, queries, key_rows, nqg, nkg, value_grad),
        scratch=[pltpu.VMEM((2, ROWS, FEAT), BF16), pltpu.SemaphoreType.DMA((3,))],
        out_spaces=[pl.ANY] * 3,
        name="finish",
    )
    return (attended, query_grad, key_grad, value_grad)


def solution(mesh):
    placed = (
        P("seq", "head"),
        P("seq", "head"),
        P("seq", "head"),
        P("head"),
        P("head"),
        P("seq", "head"),
    )
    return jax.shard_map(
        local,
        mesh=mesh,
        in_specs=placed,
        out_specs=(P("seq", "head"), P("seq", "head"), P("seq", "head"), P("seq", "head")),
        check_vma=False,
    )
```

```python
import math

import jax
import jax.numpy as jnp
from jax import lax
from jax.experimental import pallas as pl
from jax.experimental.pallas import tpu as pltpu
from jax.sharding import PartitionSpec as P

ROWS = 512
FEAT = 128
LEAF = 128
LEAVES = 4
HEAD = 64
KEYS = 1280
EPS = 1e-06
LN2 = math.log(2.0)
F32 = jnp.float32
BF16 = jnp.bfloat16
ROW_LEVEL = {1: 2, 2: 3, 3: 3, 4: 4, 5: 4, 6: 4, 7: 4}
COLUMN_LEVEL = {1: 5, 2: 6, 3: 6, 4: 7, 5: 7, 6: 7, 7: 7}
FAR = 48
SLOT = 112
FIRST_Z = 7
FIRST_Y = 4


def dot(a, b, dims):
    return lax.dot_general(a, b, ((dims[:1], dims[1:]), ((), ())), preferred_element_type=F32)


def iota(shape, axis):
    return lax.broadcasted_iota(jnp.int32, shape, axis)


def pooling(rows, level):
    token = iota((rows, ROWS), 1)
    hit = jnp.right_shift(token, level) == iota((rows, ROWS), 0)
    return jnp.where(hit, 2.0**-level, 0.0)


def spreading(first, rows, level):
    token = iota((ROWS, rows), 0)
    hit = jnp.right_shift(token, level) == iota((ROWS, rows), 1) + first
    return jnp.where(hit, 2.0**-level, 0.0)


def far_pick(shape, far_axis):
    far = iota(shape, far_axis)
    slot_row = iota(shape, 1 - far_axis)
    mid = far - 16
    low = far - 32
    column = jnp.where(
        far < 16,
        far,
        jnp.where(
            far < 32,
            (1 + jnp.right_shift(mid, 3)) * 16 + jnp.bitwise_and(mid, 7),
            (3 + jnp.right_shift(low, 2)) * 16 + jnp.bitwise_and(low, 3),
        ),
    )
    return jnp.where(column == slot_row, 1.0, 0.0).astype(BF16)


def token_sums(x):
    return [
        jnp.sum(x[i * LEAF : (i + 1) * LEAF].T, axis=0, keepdims=True) for i in range(LEAVES)
    ]


def spread_tokens(tile, first):
    return jnp.concatenate(
        [
            jnp.broadcast_to(tile[first + i : first + i + 1], (LEAF, LEAF)).T
            for i in range(LEAVES)
        ],
        axis=0,
    )


def squares_kernel(q_in, k_in, qg_in, kg_in, out_ref, rows, gains, sems):
    copies = [
        pltpu.make_async_copy(source, target, sems.at[i])
        for i, (source, target) in enumerate(
            ((q_in, rows.at[0]), (k_in, rows.at[1]), (qg_in, gains.at[0]), (kg_in, gains.at[1]))
        )
    ]
    for copy in copies:
        copy.start()
    sums = []
    for i in range(2):
        copies[i].wait()
        x = rows[i].astype(F32)
        sums += token_sums(x * x)
    for copy in copies[2:]:
        copy.wait()
    tile = jnp.concatenate(sums + [gains[0], gains[1], jnp.zeros((6, FEAT), F32)], axis=0)
    for i in range(out_ref.shape[0]):
        out_ref[i] = tile


def rates(width, sum_ref):
    return lax.rsqrt(jnp.sum(sum_ref[:, :8], axis=0) / width + EPS)


def norm_kernel(width, sum_ref, k_ref, v_ref, kv_ref, one_ref, lv_ref, y_ref, p1_ref, p2_ref):
    index = lax.axis_index("seq")
    column = jnp.bitwise_xor(jnp.right_shift(index, 3), FIRST_Y)
    odd = jnp.bitwise_and(index, 1)
    gain = sum_ref[lax.axis_index("head"), 9:10]
    kv_ref[:, :FEAT] = (
        k_ref[...].astype(F32) * spread_tokens(rates(width, sum_ref), 4) * gain
    ).astype(BF16)
    kv_ref[:, FEAT:] = v_ref[...]
    pool = jnp.concatenate(
        [pooling(ROWS >> level, level) for level in (1, 2, 3, 4)]
        + [pooling(16, COLUMN_LEVEL[d]) for d in range(1, 8)],
        axis=0,
    ).astype(BF16)
    coarse = dot(pool, kv_ref[...], (1, 0)).astype(BF16)
    one_ref[...] = coarse[:256]
    lv_ref[...] = coarse[256:480]
    y_ref[column] = jnp.zeros((16, 2 * FEAT), BF16)
    for d in range(1, 8):
        y_ref[jnp.bitwise_xor(column, d)] = coarse[464 + 16 * d : 480 + 16 * d]
    p1_ref[:LEAF] = kv_ref[pl.ds(pl.multiple_of((1 - odd) * 384, LEAF), LEAF)]
    p1_ref[LEAF:] = coarse[320:384]
    p2_ref[...] = kv_ref[pl.ds(pl.multiple_of(odd * 384, LEAF), LEAF)]


def start_all(copies):
    for copy in copies:
        copy.start()
    return copies


def wait_all(copies):
    for copy in copies:
        copy.wait()


def row_kernel(y_ref, lv_ref, out_ref, far_scr, mid_scr, sems):
    index = lax.axis_index("seq")
    column = jnp.bitwise_xor(jnp.right_shift(index, 3), FIRST_Y)
    place = jnp.bitwise_xor(jnp.bitwise_and(index, 7), FIRST_Z)
    mid_scr[place] = jnp.zeros((64, 2 * FEAT), BF16)
    for d in range(1, 8):
        other = jnp.bitwise_xor(place, d)
        if d < 4:
            mid_scr[other] = lv_ref[:64] if d == 1 else lv_ref[128:192]
        else:
            mid_scr[other, :32] = lv_ref[192:224]
            mid_scr[other, 32:] = jnp.zeros((32, 2 * FEAT), BF16)
    copies = start_all([pltpu.make_async_copy(mid_scr, out_ref.at[:, pl.ds(FAR, 64)], sems.at[0])])
    slots = jnp.concatenate([y_ref[jnp.bitwise_xor(column, d)] for d in range(1, 8)], axis=0)
    far = dot(far_pick((FAR, 112), 0), slots, (1, 0)).astype(BF16)
    for s in range(8):
        far_scr[s] = far
    copies += start_all([pltpu.make_async_copy(far_scr, out_ref.at[:, pl.ds(0, FAR)], sems.at[1])])
    wait_all(copies)


def by_head(block):
    lane = iota((LEAF, FEAT), 1)
    zero = jnp.zeros((LEAF, FEAT), BF16)
    return jnp.concatenate(
        [jnp.where(lane < HEAD, block, zero), jnp.where(lane < HEAD, zero, block)], axis=0
    )


def peak(x):
    return jnp.max(x, axis=0, keepdims=True)


def add_up(x):
    return jnp.sum(x, axis=0, keepdims=True)


HALO_PIECE = {0: 0, LEAVES - 1: 2}


def far_bias():
    return jnp.concatenate(
        [jnp.full((LEAF, 2 * LEAF), level * LN2, F32) for level in range(1, 8)], axis=0
    )


def outside_bias():
    index = lax.axis_index("seq")
    last = lax.axis_size("seq") - 1
    return {
        0: jnp.where(index > 0, 0.0, -1e30).astype(F32),
        LEAVES - 1: jnp.where(index < last, 0.0, -1e30).astype(F32),
    }


def weigh(kv, q2, g2):
    score = dot(kv[:, :FEAT], q2, (1, 1))
    top = peak(score)
    weight = jnp.exp(score - top)
    pgrad = dot(kv[:, FEAT:], g2, (1, 1))
    return weight, pgrad, (top, add_up(weight), add_up(weight * pgrad))


def combine(stats):
    top = stats[0][0]
    for stat in stats[1:]:
        top = jnp.maximum(top, stat[0])
    factors = [jnp.exp(stat[0] - top) for stat in stats]
    total = sum(factor * stat[1] for factor, stat in zip(factors, stats))
    mixed = sum(factor * stat[2] for factor, stat in zip(factors, stats))
    return top, total, mixed, factors


def scaled_queries(block):
    return by_head(block) * jnp.asarray(0.125, BF16)


def near_kernel(width, sum_ref, q_ref, kv_ref, one_ref, g_ref, qn_ref, stat_ref):
    gain = sum_ref[lax.axis_index("head"), 8:9]
    qn_ref[...] = (
        q_ref[...].astype(F32) * spread_tokens(rates(width, sum_ref), 0) * gain
    ).astype(BF16)
    for b in range(LEAVES):
        block = slice(b * LEAF, (b + 1) * LEAF)
        q2 = scaled_queries(qn_ref[block])
        g2 = by_head(g_ref[block])
        half = (1 - b // 2) * LEAF
        stats = [
            weigh(kv_ref[(b + i - 1) * LEAF : (b + i) * LEAF], q2, g2)[2]
            for i in range(3)
            if HALO_PIECE.get(b) != i
        ]
        top, total, mixed = weigh(one_ref[half : half + LEAF], q2, g2)[2]
        stats.append((top + LN2, total, mixed))
        top, total, mixed, _ = combine(stats)
        stat_ref[b] = jnp.concatenate([top, total, mixed, jnp.zeros((5, 2 * LEAF), F32)], axis=0)


def attend_kernel(
    qn_ref, g_ref, near_ref, p1_ref, p2_ref, z_ref,
    stat_ref, cross, halo, p1o_ref, p2o_ref, zo_ref,
    q2_scr, g2_scr, score_scr, weight_scr, pgrad_scr, low_scr, sgrad_scr, rims, cross_grad, far_scr, mid_scr, sems,
):
    index = lax.axis_index("seq")
    place = jnp.bitwise_and(index, 7)
    slot = jnp.bitwise_xor(place, FIRST_Z)
    odd = jnp.bitwise_and(index, 1)
    peer_side = 1 - odd
    halo[peer_side] = p1_ref[:LEAF]
    halo[odd] = p2_ref[...]
    cross[:64] = z_ref[jnp.bitwise_xor(slot, 1), FAR:]
    cross[64:128] = p1_ref[LEAF:]
    cross[128:192] = z_ref[jnp.bitwise_xor(slot, 2), FAR:]
    cross[192:256] = z_ref[jnp.bitwise_xor(slot, 3), FAR:]
    for i in range(4):
        cross[256 + 32 * i : 288 + 32 * i] = z_ref[jnp.bitwise_xor(slot, 4 + i), FAR : FAR + 32]
    for s in range(8):
        for j in range(3):
            at = 384 + LEAF * j + 16 * s
            cross[at : at + 16] = z_ref[s, 16 * j : 16 * (j + 1)]

    outside = outside_bias()
    rim_rows = []
    for b in range(LEAVES):
        block = slice(b * LEAF, (b + 1) * LEAF)
        lanes = slice(2 * b * LEAF, 2 * (b + 1) * LEAF)
        q2 = scaled_queries(qn_ref[block])
        g2 = by_head(g_ref[block])
        q2_scr[lanes] = q2
        g2_scr[lanes] = g2
        side = 0 if b == 0 else 1
        stats = [(near_ref[b, 0:1], near_ref[b, 1:2], near_ref[b, 2:3])]
        score_scr[b] = dot(cross[:, :FEAT], q2, (1, 1))
        pgrad_scr[b, : 6 * LEAF] = dot(cross[:, FEAT:], g2, (1, 1))
        for i in range(6):
            rows = slice(i * LEAF, (i + 1) * LEAF)
            score = score_scr[b, rows]
            top = peak(score)
            weight = jnp.exp(score - top)
            weight_scr[b, rows] = weight
            mixed = add_up(weight * pgrad_scr[b, rows])
            stats.append((top + (i + 2) * LN2, add_up(weight), mixed))
        if b in HALO_PIECE:
            weight, pgrad, (top, total, mixed) = weigh(halo[side], q2, g2)
            weight_scr[b, 6 * LEAF :] = weight
            pgrad_scr[b, 6 * LEAF :] = pgrad
            stats.append((top + outside[b], total, mixed))
        top, total, mixed, factors = combine(stats)
        inverse = 1.0 / total
        delta = mixed * inverse
        stat_ref[b] = jnp.concatenate(
            [top, inverse, delta, jnp.zeros((5, 2 * LEAF), F32)], axis=0
        )
        for i in range(6):
            rows = slice(i * LEAF, (i + 1) * LEAF)
            prob = weight_scr[b, rows] * (factors[i + 1] * inverse)
            low_scr[rows, lanes] = prob.astype(BF16)
            sgrad_scr[rows, lanes] = (prob * (pgrad_scr[b, rows] - delta)).astype(BF16)
        if b in HALO_PIECE:
            rim_rows.append((b, side, lanes, factors[7] * inverse, delta))

    cross_grad[:, :FEAT] = dot(sgrad_scr[...], q2_scr[...], (1, 0)).astype(BF16)
    cross_grad[:, FEAT:] = dot(low_scr[...], g2_scr[...], (1, 0)).astype(BF16)
    for j in range(3):
        for s in range(8):
            at = 384 + LEAF * j + 16 * s
            far_scr[s ^ FIRST_Z, 16 * j : 16 * (j + 1)] = cross_grad[at : at + 16]
    copies = start_all([pltpu.make_async_copy(far_scr, zo_ref.at[:, pl.ds(0, FAR)], sems.at[0])])
    mid_scr[place] = jnp.zeros((64, 2 * FEAT), BF16)
    mid_scr[jnp.bitwise_xor(place, 1)] = cross_grad[:64]
    mid_scr[jnp.bitwise_xor(place, 2)] = cross_grad[128:192]
    mid_scr[jnp.bitwise_xor(place, 3)] = cross_grad[192:256]
    for i in range(4):
        other = jnp.bitwise_xor(place, 4 + i)
        mid_scr[other, :32] = cross_grad[256 + 32 * i : 288 + 32 * i]
        mid_scr[other, 32:] = jnp.zeros((32, 2 * FEAT), BF16)
    copies += start_all([pltpu.make_async_copy(mid_scr, zo_ref.at[:, pl.ds(FAR, 64)], sems.at[1])])
    for b, side, lanes, factor, delta in rim_rows:
        prob = weight_scr[b, 6 * LEAF :] * factor
        sgrad = (prob * (pgrad_scr[b, 6 * LEAF :] - delta)).astype(BF16)
        rims[side, :, :FEAT] = dot(sgrad, q2_scr[lanes], (1, 0)).astype(BF16)
        rims[side, :, FEAT:] = dot(prob.astype(BF16), g2_scr[lanes], (1, 0)).astype(BF16)
    p1o_ref[:LEAF] = rims[peer_side]
    p1o_ref[LEAF:] = cross_grad[64:128]
    p2o_ref[...] = rims[odd]
    wait_all(copies)


def after_kernel(
    stat_ref, qn_ref, kv_ref, one_ref, g_ref, halo, cross, sum_ref, q_ref,
    att_ref, nqg_ref, tok_ref, qsum_ref, near, near_grad, one_grad,
):
    near[:LEAF] = halo[0]
    near[LEAF : LEAF + ROWS] = kv_ref[...]
    near[LEAF + ROWS :] = halo[1]
    near_grad[...] = jnp.zeros_like(near_grad)
    one_grad[...] = jnp.zeros_like(one_grad)
    feature = iota((FEAT, LEAF), 0)
    bias = far_bias()
    outside = outside_bias()

    def merge_heads(transposed):
        return jnp.where(feature < HEAD, transposed[:, :LEAF], transposed[:, LEAF:]).T

    for b in range(LEAVES):
        rows = slice(b * LEAF, (b + 1) * LEAF)
        near_rows = slice(b * LEAF, (b + 3) * LEAF)
        half = (1 - b // 2) * LEAF
        q2 = scaled_queries(qn_ref[rows])
        g2 = by_head(g_ref[rows])
        kv = jnp.concatenate([near[near_rows], one_ref[half : half + LEAF], cross[...]], axis=0)
        keys = kv[:, :FEAT]
        values = kv[:, FEAT:]
        raw = dot(keys, q2, (1, 1))
        before, after = raw[:LEAF], raw[2 * LEAF : 3 * LEAF]
        if b == 0:
            before = before + outside[b]
        if b == LEAVES - 1:
            after = after + outside[b]
        scores = jnp.concatenate(
            [before, raw[LEAF : 2 * LEAF], after, raw[3 * LEAF :] + bias], axis=0
        )
        probs = jnp.exp(scores - stat_ref[b, 0:1]) * stat_ref[b, 1:2]
        low = probs.astype(BF16)
        score_grad = (probs * (dot(values, g2, (1, 1)) - stat_ref[b, 2:3])).astype(BF16)
        att_ref[rows] = merge_heads(dot(values, low, (0, 0))).astype(BF16)
        nqg_ref[rows] = merge_heads(dot(keys, score_grad, (0, 0))) * 0.125
        for part, lanes in (
            (dot(score_grad[: 4 * LEAF], q2, (1, 0)), slice(0, FEAT)),
            (dot(low[: 4 * LEAF], g2, (1, 0)), slice(FEAT, 2 * FEAT)),
        ):
            near_grad[near_rows, lanes] += part[: 3 * LEAF]
            one_grad[half : half + LEAF, lanes] += part[3 * LEAF :]
    spread = spreading(0, 256, 1).astype(BF16)
    high = one_grad[...].astype(BF16)
    rest = (one_grad[...] - high.astype(F32)).astype(BF16)
    tok_ref[...] = near_grad[LEAF : LEAF + ROWS] + dot(spread, high, (1, 0)) + dot(spread, rest, (1, 0))
    gains = sum_ref[lax.axis_index("head"), 8:16]
    sums = token_sums(q_ref[...].astype(F32) * gains[0:1] * nqg_ref[...])
    qsum_ref[...] = jnp.concatenate(sums + [gains[1:2], jnp.zeros((3, FEAT), F32)], axis=0)


def column_kernel(z_ref, p1_ref, p2_ref, tok_ref, out_ref, far_rows, sem):
    column = jnp.right_shift(lax.axis_index("seq"), 3)
    copy = pltpu.make_async_copy(z_ref.at[:, pl.ds(0, FAR)], far_rows, sem)
    copy.start()
    copy.wait()
    far = jnp.sum(far_rows[...].astype(F32), axis=0).astype(BF16)
    slots = dot(far_pick((112, FAR), 1), far, (1, 0)).astype(BF16)
    out_ref[column] = jnp.zeros((16, 2 * FEAT), BF16)
    for d in range(1, 8):
        out_ref[jnp.bitwise_xor(column, d)] = slots[16 * (d - 1) : 16 * d]


def total_kernel(
    tok_ref, p1_ref, p2_ref, z_ref, y_ref, k_ref, qsum_ref,
    nkg_ref, vg_ref, sum_ref, acc,
):
    index = lax.axis_index("seq")
    column = jnp.right_shift(index, 3)
    place = jnp.bitwise_and(index, 7)
    odd = jnp.bitwise_and(index, 1)
    pieces = [z_ref[jnp.bitwise_xor(place, 1), FAR:], p1_ref[LEAF:]]
    maps = [spreading(0, 64, 2), spreading(64, 64, 2)]
    for d in range(2, 8):
        rows = ROWS >> ROW_LEVEL[d]
        pieces.append(z_ref[jnp.bitwise_xor(place, d), FAR : FAR + rows])
        maps.append(spreading(0, rows, ROW_LEVEL[d]))
    for d in range(1, 8):
        pieces.append(y_ref[jnp.bitwise_xor(column, d)])
        maps.append(spreading(0, 16, COLUMN_LEVEL[d]))
    spread = jnp.concatenate(maps, axis=1).astype(BF16)
    acc[...] = tok_ref[...] + dot(spread, jnp.concatenate(pieces, axis=0), (1, 0))
    acc[pl.ds(pl.multiple_of((1 - odd) * 384, LEAF), LEAF)] += p1_ref[:LEAF].astype(F32)
    acc[pl.ds(pl.multiple_of(odd * 384, LEAF), LEAF)] += p2_ref[...].astype(F32)
    vg_ref[...] = acc[:, FEAT:].astype(BF16)
    key_total = acc[:, :FEAT]
    nkg_ref[...] = key_total
    sums = token_sums(k_ref[...].astype(F32) * qsum_ref[LEAVES : LEAVES + 1] * key_total)
    tile = jnp.concatenate([qsum_ref[:LEAVES]] + sums, axis=0)
    for i in range(sum_ref.shape[0]):
        sum_ref[i] = tile


def finish_kernel(
    width, sq_ref, inner_ref, q_ref, k_ref, nqg_ref, nkg_ref, value_ref,
    dq_ref, dk_ref, vg_ref, results, sems,
):
    copies = start_all([pltpu.make_async_copy(value_ref, vg_ref, sems.at[2])])
    rate = rates(width, sq_ref)
    inner = jnp.sum(inner_ref[...], axis=0) / width
    cubed = rate * rate * rate * inner
    gains = sq_ref[lax.axis_index("head"), 8:16]
    for side, (x_ref, grad_ref, out_ref) in enumerate(
        ((q_ref, nqg_ref, dq_ref), (k_ref, nkg_ref, dk_ref))
    ):
        results[side] = (
            spread_tokens(rate, 4 * side) * gains[side : side + 1] * grad_ref[...]
            - x_ref[...].astype(F32) * spread_tokens(cubed, 4 * side)
        ).astype(BF16)
        copies += start_all([pltpu.make_async_copy(results.at[side], out_ref, sems.at[side])])
    wait_all(copies)


def call(kernel, outs, args, scratch=(), flops=0, name=None, spaces=None, out_spaces=None, vmem=40):
    many = isinstance(outs, list)
    moved = sum(math.prod(x.shape) * x.dtype.itemsize for x in list(args) + (outs if many else [outs]))
    out_spaces = out_spaces or [pltpu.VMEM] * (len(outs) if many else 1)
    out_specs = [pl.BlockSpec(memory_space=space) for space in out_spaces]
    return pl.pallas_call(
        kernel,
        out_shape=outs,
        in_specs=[pl.BlockSpec(memory_space=space) for space in spaces or [pltpu.VMEM] * len(args)],
        out_specs=out_specs if many else out_specs[0],
        scratch_shapes=list(scratch),
        compiler_params=pltpu.CompilerParams(vmem_limit_bytes=vmem * 1024 * 1024),
        cost_estimate=pl.CostEstimate(flops=flops, bytes_accessed=moved, transcendentals=0),
        name=name,
    )(*args)


def sds(*shape, dtype=BF16):
    return jax.ShapeDtypeStruct(shape, dtype)


FORWARD_ROWS = [[8 * y + (p ^ FIRST_Z) for p in range(8)] for y in range(8)]
FORWARD_COLUMNS = [[8 * (p ^ FIRST_Y) + z for p in range(8)] for z in range(8)]
ROW_GROUPS = [[8 * y + z for z in range(8)] for y in range(8)]
COLUMN_GROUPS = [[8 * y + z for y in range(8)] for z in range(8)]


def exchange(x, axis, groups=None):
    return lax.all_to_all(x, axis, 0, 0, axis_index_groups=groups, tiled=True)


def local(queries, key_rows, value_rows, query_gain, key_gain, out_grad):
    seq = lax.axis_size("seq")
    heads = lax.axis_size("head")
    width = float(heads * FEAT)
    qg = query_gain.reshape(1, FEAT)
    kg = key_gain.reshape(1, FEAT)
    peer = [(i, i ^ 1) for i in range(seq)]
    beside = [(i, i + 1) for i in range(1, seq - 1, 2)] + [(i + 1, i) for i in range(1, seq - 1, 2)]

    squares = call(
        squares_kernel,
        sds(heads, 16, FEAT, dtype=F32),
        (queries, key_rows, qg, kg),
        scratch=[
            pltpu.VMEM((2, ROWS, FEAT), BF16),
            pltpu.VMEM((2, 1, FEAT), F32),
            pltpu.SemaphoreType.DMA((4,)),
        ],
        spaces=[pl.ANY] * 4,
        vmem=60,
        name="squares",
    )
    squares = exchange(squares, "head")
    kv, one, lv, ysend, p1, p2 = call(
        lambda *refs: norm_kernel(width, *refs),
        [sds(ROWS, 256), sds(256, 256), sds(224, 256), sds(8, 16, 256), sds(192, 256), sds(LEAF, 256)],
        (squares, key_rows, value_rows),
        name="norm",
    )
    p1 = lax.ppermute(p1, "seq", peer)
    p2 = lax.ppermute(p2, "seq", beside)
    yrecv = exchange(ysend, "seq", FORWARD_COLUMNS)
    zsend = call(
        row_kernel,
        sds(8, SLOT, 256),
        (yrecv, lv),
        scratch=[
            pltpu.VMEM((8, FAR, 256), BF16),
            pltpu.VMEM((8, 64, 256), BF16),
            pltpu.SemaphoreType.DMA((2,)),
        ],
        out_spaces=[pl.ANY],
        name="rows",
    )
    zrecv = exchange(zsend, "seq", FORWARD_ROWS)
    qn, near = call(
        lambda *refs: near_kernel(width, *refs),
        [sds(ROWS, FEAT), sds(LEAVES, 8, 256, dtype=F32)],
        (squares, queries, kv, one, out_grad),
        flops=14 * 2 * 2 * 256 * LEAF * FEAT,
        name="near",
    )
    stat, cross, halo, p1, p2, zsend = call(
        attend_kernel,
        [sds(LEAVES, 8, 256, dtype=F32), sds(768, 256), sds(2, LEAF, 256)]
        + [sds(192, 256), sds(LEAF, 256), sds(8, SLOT, 256)],
        (qn, out_grad, near, p1, p2, zrecv),
        scratch=[
            pltpu.VMEM((1024, FEAT), BF16),
            pltpu.VMEM((1024, FEAT), BF16),
            pltpu.VMEM((LEAVES, 768, 256), F32),
            pltpu.VMEM((LEAVES, 7 * LEAF, 256), F32),
            pltpu.VMEM((LEAVES, 7 * LEAF, 256), F32),
            pltpu.VMEM((768, 1024), BF16),
            pltpu.VMEM((768, 1024), BF16),
            pltpu.VMEM((2, LEAF, 256), BF16),
            pltpu.VMEM((768, 256), BF16),
            pltpu.VMEM((8, FAR, 256), BF16),
            pltpu.VMEM((8, 64, 256), BF16),
            pltpu.SemaphoreType.DMA((2,)),
        ],
        out_spaces=[pltpu.VMEM] * 5 + [pl.ANY],
        flops=4 * 4 * 2 * 256 * 768 * FEAT,
        name="attend",
    )
    p1 = lax.ppermute(p1, "seq", peer)
    p2 = lax.ppermute(p2, "seq", beside)
    zrecv = exchange(zsend, "seq", ROW_GROUPS)
    attended, nqg, tok, qsum = call(
        after_kernel,
        [sds(ROWS, FEAT), sds(ROWS, FEAT, dtype=F32), sds(ROWS, 256, dtype=F32)]
        + [sds(8, FEAT, dtype=F32)],
        (stat, qn, kv, one, out_grad, halo, cross, squares, queries),
        scratch=[
            pltpu.VMEM((768, 256), BF16),
            pltpu.VMEM((768, 256), F32),
            pltpu.VMEM((256, 256), F32),
        ],
        flops=4 * 5 * 2 * 256 * KEYS * FEAT,
        name="after",
    )
    ysend = call(
        column_kernel,
        sds(8, 16, 256),
        (zrecv, p1, p2, tok),
        scratch=[pltpu.VMEM((8, FAR, 256), BF16), pltpu.SemaphoreType.DMA],
        spaces=[pl.ANY] * 4,
        name="columns",
    )
    yrecv = exchange(ysend, "seq", COLUMN_GROUPS)
    nkg, value_grad, inner = call(
        total_kernel,
        [sds(ROWS, FEAT, dtype=F32), sds(ROWS, FEAT), sds(heads, 8, FEAT, dtype=F32)],
        (tok, p1, p2, zrecv, yrecv, key_rows, qsum),
        scratch=[
            pltpu.VMEM((ROWS, 256), F32),
        ],
        name="total",
    )
    inner = exchange(inner, "head")
    query_grad, key_grad, value_grad = call(
        lambda *refs: finish_kernel(width, *refs),
        [sds(ROWS, FEAT), sds(ROWS, FEAT), sds(ROWS, FEAT)],
        (squares, inner, queries, key_rows, nqg, nkg, value_grad),
        scratch=[pltpu.VMEM((2, ROWS, FEAT), BF16), pltpu.SemaphoreType.DMA((3,))],
        out_spaces=[pl.ANY] * 3,
        name="finish",
    )
    return (attended, query_grad, key_grad, value_grad)


def solution(mesh):
    placed = (
        P("seq", "head"),
        P("seq", "head"),
        P("seq", "head"),
        P("head"),
        P("head"),
        P("seq", "head"),
    )
    return jax.shard_map(
        local,
        mesh=mesh,
        in_specs=placed,
        out_specs=(P("seq", "head"), P("seq", "head"), P("seq", "head"), P("seq", "head")),
        check_vma=False,
    )
```

```python
import math

import jax
import jax.numpy as jnp
from jax import lax
from jax.experimental import pallas as pl
from jax.experimental.pallas import tpu as pltpu
from jax.sharding import PartitionSpec as P

ROWS = 512
FEAT = 128
LEAF = 128
LEAVES = 4
HEAD = 64
KEYS = 1280
EPS = 1e-06
LN2 = math.log(2.0)
F32 = jnp.float32
BF16 = jnp.bfloat16
ROW_LEVEL = {1: 2, 2: 3, 3: 3, 4: 4, 5: 4, 6: 4, 7: 4}
COLUMN_LEVEL = {1: 5, 2: 6, 3: 6, 4: 7, 5: 7, 6: 7, 7: 7}
FAR = 48
SLOT = 112
FIRST_Z = 7


def dot(a, b, dims):
    return lax.dot_general(a, b, ((dims[:1], dims[1:]), ((), ())), preferred_element_type=F32)


def iota(shape, axis):
    return lax.broadcasted_iota(jnp.int32, shape, axis)


def pooling(rows, level):
    token = iota((rows, ROWS), 1)
    hit = jnp.right_shift(token, level) == iota((rows, ROWS), 0)
    return jnp.where(hit, 2.0**-level, 0.0)


def spreading(first, rows, level):
    token = iota((ROWS, rows), 0)
    hit = jnp.right_shift(token, level) == iota((ROWS, rows), 1) + first
    return jnp.where(hit, 2.0**-level, 0.0)


def far_pick(shape, far_axis):
    far = iota(shape, far_axis)
    slot_row = iota(shape, 1 - far_axis)
    mid = far - 16
    low = far - 32
    column = jnp.where(
        far < 16,
        far,
        jnp.where(
            far < 32,
            (1 + jnp.right_shift(mid, 3)) * 16 + jnp.bitwise_and(mid, 7),
            (3 + jnp.right_shift(low, 2)) * 16 + jnp.bitwise_and(low, 3),
        ),
    )
    return jnp.where(column == slot_row, 1.0, 0.0).astype(BF16)


def token_sums(x):
    return [
        jnp.sum(x[i * LEAF : (i + 1) * LEAF].T, axis=0, keepdims=True) for i in range(LEAVES)
    ]


def spread_tokens(tile, first):
    return jnp.concatenate(
        [
            jnp.broadcast_to(tile[first + i : first + i + 1], (LEAF, LEAF)).T
            for i in range(LEAVES)
        ],
        axis=0,
    )


def squares_kernel(q_in, k_in, qg_in, kg_in, out_ref, rows, gains, sems):
    copies = [
        pltpu.make_async_copy(source, target, sems.at[i])
        for i, (source, target) in enumerate(
            ((q_in, rows.at[0]), (k_in, rows.at[1]), (qg_in, gains.at[0]), (kg_in, gains.at[1]))
        )
    ]
    for copy in copies:
        copy.start()
    sums = []
    for i in range(2):
        copies[i].wait()
        x = rows[i].astype(F32)
        sums += token_sums(x * x)
    for copy in copies[2:]:
        copy.wait()
    tile = jnp.concatenate(sums + [gains[0], gains[1], jnp.zeros((6, FEAT), F32)], axis=0)
    for i in range(out_ref.shape[0]):
        out_ref[i] = tile


def rates(width, sum_ref):
    return lax.rsqrt(jnp.sum(sum_ref[:, :8], axis=0) / width + EPS)


def norm_kernel(width, sum_ref, k_ref, v_ref, kv_ref, one_ref, lv_ref, y_ref, p1_ref, p2_ref):
    index = lax.axis_index("seq")
    column = jnp.right_shift(index, 3)
    odd = jnp.bitwise_and(index, 1)
    gain = sum_ref[lax.axis_index("head"), 9:10]
    kv_ref[:, :FEAT] = (
        k_ref[...].astype(F32) * spread_tokens(rates(width, sum_ref), 4) * gain
    ).astype(BF16)
    kv_ref[:, FEAT:] = v_ref[...]
    pool = jnp.concatenate(
        [pooling(ROWS >> level, level) for level in (1, 2, 3, 4)]
        + [pooling(16, COLUMN_LEVEL[d]) for d in range(1, 8)],
        axis=0,
    ).astype(BF16)
    coarse = dot(pool, kv_ref[...], (1, 0)).astype(BF16)
    one_ref[...] = coarse[:256]
    lv_ref[...] = coarse[256:480]
    y_ref[column] = jnp.zeros((16, 2 * FEAT), BF16)
    for d in range(1, 8):
        y_ref[jnp.bitwise_xor(column, d)] = coarse[464 + 16 * d : 480 + 16 * d]
    p1_ref[:LEAF] = kv_ref[pl.ds(pl.multiple_of((1 - odd) * 384, LEAF), LEAF)]
    p1_ref[LEAF:] = coarse[320:384]
    p2_ref[...] = kv_ref[pl.ds(pl.multiple_of(odd * 384, LEAF), LEAF)]


def start_all(copies):
    for copy in copies:
        copy.start()
    return copies


def wait_all(copies):
    for copy in copies:
        copy.wait()


def row_kernel(y_ref, lv_ref, out_ref, far_scr, mid_scr, sems):
    index = lax.axis_index("seq")
    column = jnp.right_shift(index, 3)
    place = jnp.bitwise_and(index, 7)
    mid_scr[place] = jnp.zeros((64, 2 * FEAT), BF16)
    for d in range(1, 8):
        other = jnp.bitwise_xor(place, d)
        if d < 4:
            mid_scr[other] = lv_ref[:64] if d == 1 else lv_ref[128:192]
        else:
            mid_scr[other, :32] = lv_ref[192:224]
            mid_scr[other, 32:] = jnp.zeros((32, 2 * FEAT), BF16)
    copies = start_all([pltpu.make_async_copy(mid_scr, out_ref.at[:, pl.ds(FAR, 64)], sems.at[0])])
    slots = jnp.concatenate([y_ref[jnp.bitwise_xor(column, d)] for d in range(1, 8)], axis=0)
    far = dot(far_pick((FAR, 112), 0), slots, (1, 0)).astype(BF16)
    for s in range(8):
        far_scr[s] = far
    copies += start_all([pltpu.make_async_copy(far_scr, out_ref.at[:, pl.ds(0, FAR)], sems.at[1])])
    wait_all(copies)


def by_head(block):
    lane = iota((LEAF, FEAT), 1)
    zero = jnp.zeros((LEAF, FEAT), BF16)
    return jnp.concatenate(
        [jnp.where(lane < HEAD, block, zero), jnp.where(lane < HEAD, zero, block)], axis=0
    )


def peak(x):
    return jnp.max(x, axis=0, keepdims=True)


def add_up(x):
    return jnp.sum(x, axis=0, keepdims=True)


HALO_PIECE = {0: 0, LEAVES - 1: 2}


def far_bias():
    return jnp.concatenate(
        [jnp.full((LEAF, 2 * LEAF), level * LN2, F32) for level in range(1, 8)], axis=0
    )


def outside_bias():
    index = lax.axis_index("seq")
    last = lax.axis_size("seq") - 1
    return {
        0: jnp.where(index > 0, 0.0, -1e30).astype(F32),
        LEAVES - 1: jnp.where(index < last, 0.0, -1e30).astype(F32),
    }


def weigh(kv, q2, g2):
    score = dot(kv[:, :FEAT], q2, (1, 1))
    top = peak(score)
    weight = jnp.exp(score - top)
    pgrad = dot(kv[:, FEAT:], g2, (1, 1))
    return weight, pgrad, (top, add_up(weight), add_up(weight * pgrad))


def combine(stats):
    top = stats[0][0]
    for stat in stats[1:]:
        top = jnp.maximum(top, stat[0])
    factors = [jnp.exp(stat[0] - top) for stat in stats]
    total = sum(factor * stat[1] for factor, stat in zip(factors, stats))
    mixed = sum(factor * stat[2] for factor, stat in zip(factors, stats))
    return top, total, mixed, factors


def scaled_queries(block):
    return by_head(block) * jnp.asarray(0.125, BF16)


def near_kernel(width, sum_ref, q_ref, kv_ref, one_ref, g_ref, qn_ref, stat_ref):
    gain = sum_ref[lax.axis_index("head"), 8:9]
    qn_ref[...] = (
        q_ref[...].astype(F32) * spread_tokens(rates(width, sum_ref), 0) * gain
    ).astype(BF16)
    for b in range(LEAVES):
        block = slice(b * LEAF, (b + 1) * LEAF)
        q2 = scaled_queries(qn_ref[block])
        g2 = by_head(g_ref[block])
        half = (1 - b // 2) * LEAF
        stats = [
            weigh(kv_ref[(b + i - 1) * LEAF : (b + i) * LEAF], q2, g2)[2]
            for i in range(3)
            if HALO_PIECE.get(b) != i
        ]
        top, total, mixed = weigh(one_ref[half : half + LEAF], q2, g2)[2]
        stats.append((top + LN2, total, mixed))
        top, total, mixed, _ = combine(stats)
        stat_ref[b] = jnp.concatenate([top, total, mixed, jnp.zeros((5, 2 * LEAF), F32)], axis=0)


def attend_kernel(
    qn_ref, g_ref, near_ref, p1_ref, p2_ref, z_ref,
    stat_ref, cross, halo, p1o_ref, p2o_ref, zo_ref,
    q2_scr, g2_scr, score_scr, weight_scr, pgrad_scr, low_scr, sgrad_scr, rims, cross_grad, far_scr, mid_scr, sems,
):
    index = lax.axis_index("seq")
    place = jnp.bitwise_and(index, 7)
    slot = jnp.bitwise_xor(place, FIRST_Z)
    odd = jnp.bitwise_and(index, 1)
    peer_side = 1 - odd
    halo[peer_side] = p1_ref[:LEAF]
    halo[odd] = p2_ref[...]
    cross[:64] = z_ref[jnp.bitwise_xor(place, 1), FAR:]
    cross[64:128] = p1_ref[LEAF:]
    cross[128:192] = z_ref[jnp.bitwise_xor(place, 2), FAR:]
    cross[192:256] = z_ref[jnp.bitwise_xor(place, 3), FAR:]
    for i in range(4):
        cross[256 + 32 * i : 288 + 32 * i] = z_ref[jnp.bitwise_xor(place, 4 + i), FAR : FAR + 32]
    for s in range(8):
        for j in range(3):
            at = 384 + LEAF * j + 16 * s
            cross[at : at + 16] = z_ref[s, 16 * j : 16 * (j + 1)]

    outside = outside_bias()
    rim_rows = []
    for b in range(LEAVES):
        block = slice(b * LEAF, (b + 1) * LEAF)
        lanes = slice(2 * b * LEAF, 2 * (b + 1) * LEAF)
        q2 = scaled_queries(qn_ref[block])
        g2 = by_head(g_ref[block])
        q2_scr[lanes] = q2
        g2_scr[lanes] = g2
        side = 0 if b == 0 else 1
        stats = [(near_ref[b, 0:1], near_ref[b, 1:2], near_ref[b, 2:3])]
        score_scr[b] = dot(cross[:, :FEAT], q2, (1, 1))
        pgrad_scr[b, : 6 * LEAF] = dot(cross[:, FEAT:], g2, (1, 1))
        for i in range(6):
            rows = slice(i * LEAF, (i + 1) * LEAF)
            score = score_scr[b, rows]
            top = peak(score)
            weight = jnp.exp(score - top)
            weight_scr[b, rows] = weight
            mixed = add_up(weight * pgrad_scr[b, rows])
            stats.append((top + (i + 2) * LN2, add_up(weight), mixed))
        if b in HALO_PIECE:
            weight, pgrad, (top, total, mixed) = weigh(halo[side], q2, g2)
            weight_scr[b, 6 * LEAF :] = weight
            pgrad_scr[b, 6 * LEAF :] = pgrad
            stats.append((top + outside[b], total, mixed))
        top, total, mixed, factors = combine(stats)
        inverse = 1.0 / total
        delta = mixed * inverse
        stat_ref[b] = jnp.concatenate(
            [top, inverse, delta, jnp.zeros((5, 2 * LEAF), F32)], axis=0
        )
        for i in range(6):
            rows = slice(i * LEAF, (i + 1) * LEAF)
            prob = weight_scr[b, rows] * (factors[i + 1] * inverse)
            low_scr[rows, lanes] = prob.astype(BF16)
            sgrad_scr[rows, lanes] = (prob * (pgrad_scr[b, rows] - delta)).astype(BF16)
        if b in HALO_PIECE:
            rim_rows.append((b, side, lanes, factors[7] * inverse, delta))

    cross_grad[:, :FEAT] = dot(sgrad_scr[...], q2_scr[...], (1, 0)).astype(BF16)
    cross_grad[:, FEAT:] = dot(low_scr[...], g2_scr[...], (1, 0)).astype(BF16)
    for j in range(3):
        for s in range(8):
            at = 384 + LEAF * j + 16 * s
            far_scr[s ^ FIRST_Z, 16 * j : 16 * (j + 1)] = cross_grad[at : at + 16]
    copies = start_all([pltpu.make_async_copy(far_scr, zo_ref.at[:, pl.ds(0, FAR)], sems.at[0])])
    mid_scr[slot] = jnp.zeros((64, 2 * FEAT), BF16)
    mid_scr[jnp.bitwise_xor(slot, 1)] = cross_grad[:64]
    mid_scr[jnp.bitwise_xor(slot, 2)] = cross_grad[128:192]
    mid_scr[jnp.bitwise_xor(slot, 3)] = cross_grad[192:256]
    for i in range(4):
        other = jnp.bitwise_xor(slot, 4 + i)
        mid_scr[other, :32] = cross_grad[256 + 32 * i : 288 + 32 * i]
        mid_scr[other, 32:] = jnp.zeros((32, 2 * FEAT), BF16)
    copies += start_all([pltpu.make_async_copy(mid_scr, zo_ref.at[:, pl.ds(FAR, 64)], sems.at[1])])
    for b, side, lanes, factor, delta in rim_rows:
        prob = weight_scr[b, 6 * LEAF :] * factor
        sgrad = (prob * (pgrad_scr[b, 6 * LEAF :] - delta)).astype(BF16)
        rims[side, :, :FEAT] = dot(sgrad, q2_scr[lanes], (1, 0)).astype(BF16)
        rims[side, :, FEAT:] = dot(prob.astype(BF16), g2_scr[lanes], (1, 0)).astype(BF16)
    p1o_ref[:LEAF] = rims[peer_side]
    p1o_ref[LEAF:] = cross_grad[64:128]
    p2o_ref[...] = rims[odd]
    wait_all(copies)


def after_kernel(
    stat_ref, qn_ref, kv_ref, one_ref, g_ref, halo, cross, sum_ref, q_ref,
    att_ref, nqg_ref, tok_ref, qsum_ref, near, near_grad, one_grad,
):
    near[:LEAF] = halo[0]
    near[LEAF : LEAF + ROWS] = kv_ref[...]
    near[LEAF + ROWS :] = halo[1]
    near_grad[...] = jnp.zeros_like(near_grad)
    one_grad[...] = jnp.zeros_like(one_grad)
    feature = iota((FEAT, LEAF), 0)
    bias = far_bias()
    outside = outside_bias()

    def merge_heads(transposed):
        return jnp.where(feature < HEAD, transposed[:, :LEAF], transposed[:, LEAF:]).T

    for b in range(LEAVES):
        rows = slice(b * LEAF, (b + 1) * LEAF)
        near_rows = slice(b * LEAF, (b + 3) * LEAF)
        half = (1 - b // 2) * LEAF
        q2 = scaled_queries(qn_ref[rows])
        g2 = by_head(g_ref[rows])
        kv = jnp.concatenate([near[near_rows], one_ref[half : half + LEAF], cross[...]], axis=0)
        keys = kv[:, :FEAT]
        values = kv[:, FEAT:]
        raw = dot(keys, q2, (1, 1))
        before, after = raw[:LEAF], raw[2 * LEAF : 3 * LEAF]
        if b == 0:
            before = before + outside[b]
        if b == LEAVES - 1:
            after = after + outside[b]
        scores = jnp.concatenate(
            [before, raw[LEAF : 2 * LEAF], after, raw[3 * LEAF :] + bias], axis=0
        )
        probs = jnp.exp(scores - stat_ref[b, 0:1]) * stat_ref[b, 1:2]
        low = probs.astype(BF16)
        score_grad = (probs * (dot(values, g2, (1, 1)) - stat_ref[b, 2:3])).astype(BF16)
        att_ref[rows] = merge_heads(dot(values, low, (0, 0))).astype(BF16)
        nqg_ref[rows] = merge_heads(dot(keys, score_grad, (0, 0))) * 0.125
        for part, lanes in (
            (dot(score_grad[: 4 * LEAF], q2, (1, 0)), slice(0, FEAT)),
            (dot(low[: 4 * LEAF], g2, (1, 0)), slice(FEAT, 2 * FEAT)),
        ):
            near_grad[near_rows, lanes] += part[: 3 * LEAF]
            one_grad[half : half + LEAF, lanes] += part[3 * LEAF :]
    spread = spreading(0, 256, 1).astype(BF16)
    high = one_grad[...].astype(BF16)
    rest = (one_grad[...] - high.astype(F32)).astype(BF16)
    tok_ref[...] = near_grad[LEAF : LEAF + ROWS] + dot(spread, high, (1, 0)) + dot(spread, rest, (1, 0))
    gains = sum_ref[lax.axis_index("head"), 8:16]
    sums = token_sums(q_ref[...].astype(F32) * gains[0:1] * nqg_ref[...])
    qsum_ref[...] = jnp.concatenate(sums + [gains[1:2], jnp.zeros((3, FEAT), F32)], axis=0)


def column_kernel(z_ref, p1_ref, p2_ref, tok_ref, out_ref, far_rows, sem):
    column = jnp.right_shift(lax.axis_index("seq"), 3)
    copy = pltpu.make_async_copy(z_ref.at[:, pl.ds(0, FAR)], far_rows, sem)
    copy.start()
    copy.wait()
    far = jnp.sum(far_rows[...].astype(F32), axis=0).astype(BF16)
    slots = dot(far_pick((112, FAR), 1), far, (1, 0)).astype(BF16)
    out_ref[column] = jnp.zeros((16, 2 * FEAT), BF16)
    for d in range(1, 8):
        out_ref[jnp.bitwise_xor(column, d)] = slots[16 * (d - 1) : 16 * d]


def total_kernel(
    tok_ref, p1_ref, p2_ref, z_ref, y_ref, k_ref, qsum_ref,
    nkg_ref, vg_ref, sum_ref, acc,
):
    index = lax.axis_index("seq")
    column = jnp.right_shift(index, 3)
    place = jnp.bitwise_xor(jnp.bitwise_and(index, 7), FIRST_Z)
    odd = jnp.bitwise_and(index, 1)
    pieces = [z_ref[jnp.bitwise_xor(place, 1), FAR:], p1_ref[LEAF:]]
    maps = [spreading(0, 64, 2), spreading(64, 64, 2)]
    for d in range(2, 8):
        rows = ROWS >> ROW_LEVEL[d]
        pieces.append(z_ref[jnp.bitwise_xor(place, d), FAR : FAR + rows])
        maps.append(spreading(0, rows, ROW_LEVEL[d]))
    for d in range(1, 8):
        pieces.append(y_ref[jnp.bitwise_xor(column, d)])
        maps.append(spreading(0, 16, COLUMN_LEVEL[d]))
    spread = jnp.concatenate(maps, axis=1).astype(BF16)
    acc[...] = tok_ref[...] + dot(spread, jnp.concatenate(pieces, axis=0), (1, 0))
    acc[pl.ds(pl.multiple_of((1 - odd) * 384, LEAF), LEAF)] += p1_ref[:LEAF].astype(F32)
    acc[pl.ds(pl.multiple_of(odd * 384, LEAF), LEAF)] += p2_ref[...].astype(F32)
    vg_ref[...] = acc[:, FEAT:].astype(BF16)
    key_total = acc[:, :FEAT]
    nkg_ref[...] = key_total
    sums = token_sums(k_ref[...].astype(F32) * qsum_ref[LEAVES : LEAVES + 1] * key_total)
    tile = jnp.concatenate([qsum_ref[:LEAVES]] + sums, axis=0)
    for i in range(sum_ref.shape[0]):
        sum_ref[i] = tile


def finish_kernel(
    width, sq_ref, inner_ref, q_ref, k_ref, nqg_ref, nkg_ref, value_ref,
    dq_ref, dk_ref, vg_ref, results, sems,
):
    copies = start_all([pltpu.make_async_copy(value_ref, vg_ref, sems.at[2])])
    rate = rates(width, sq_ref)
    inner = jnp.sum(inner_ref[...], axis=0) / width
    cubed = rate * rate * rate * inner
    gains = sq_ref[lax.axis_index("head"), 8:16]
    for side, (x_ref, grad_ref, out_ref) in enumerate(
        ((q_ref, nqg_ref, dq_ref), (k_ref, nkg_ref, dk_ref))
    ):
        results[side] = (
            spread_tokens(rate, 4 * side) * gains[side : side + 1] * grad_ref[...]
            - x_ref[...].astype(F32) * spread_tokens(cubed, 4 * side)
        ).astype(BF16)
        copies += start_all([pltpu.make_async_copy(results.at[side], out_ref, sems.at[side])])
    wait_all(copies)


def call(kernel, outs, args, scratch=(), flops=0, name=None, spaces=None, out_spaces=None, vmem=40):
    many = isinstance(outs, list)
    moved = sum(math.prod(x.shape) * x.dtype.itemsize for x in list(args) + (outs if many else [outs]))
    out_spaces = out_spaces or [pltpu.VMEM] * (len(outs) if many else 1)
    out_specs = [pl.BlockSpec(memory_space=space) for space in out_spaces]
    return pl.pallas_call(
        kernel,
        out_shape=outs,
        in_specs=[pl.BlockSpec(memory_space=space) for space in spaces or [pltpu.VMEM] * len(args)],
        out_specs=out_specs if many else out_specs[0],
        scratch_shapes=list(scratch),
        compiler_params=pltpu.CompilerParams(vmem_limit_bytes=vmem * 1024 * 1024),
        cost_estimate=pl.CostEstimate(flops=flops, bytes_accessed=moved, transcendentals=0),
        name=name,
    )(*args)


def sds(*shape, dtype=BF16):
    return jax.ShapeDtypeStruct(shape, dtype)


BACKWARD_ROWS = [[8 * y + (p ^ FIRST_Z) for p in range(8)] for y in range(8)]
ROW_GROUPS = [[8 * y + z for z in range(8)] for y in range(8)]
COLUMN_GROUPS = [[8 * y + z for y in range(8)] for z in range(8)]


def exchange(x, axis, groups=None):
    return lax.all_to_all(x, axis, 0, 0, axis_index_groups=groups, tiled=True)


def local(queries, key_rows, value_rows, query_gain, key_gain, out_grad):
    seq = lax.axis_size("seq")
    heads = lax.axis_size("head")
    width = float(heads * FEAT)
    qg = query_gain.reshape(1, FEAT)
    kg = key_gain.reshape(1, FEAT)
    peer = [(i, i ^ 1) for i in range(seq)]
    beside = [(i, i + 1) for i in range(1, seq - 1, 2)] + [(i + 1, i) for i in range(1, seq - 1, 2)]

    squares = call(
        squares_kernel,
        sds(heads, 16, FEAT, dtype=F32),
        (queries, key_rows, qg, kg),
        scratch=[
            pltpu.VMEM((2, ROWS, FEAT), BF16),
            pltpu.VMEM((2, 1, FEAT), F32),
            pltpu.SemaphoreType.DMA((4,)),
        ],
        spaces=[pl.ANY] * 4,
        vmem=60,
        name="squares",
    )
    squares = exchange(squares, "head")
    kv, one, lv, ysend, p1, p2 = call(
        lambda *refs: norm_kernel(width, *refs),
        [sds(ROWS, 256), sds(256, 256), sds(224, 256), sds(8, 16, 256), sds(192, 256), sds(LEAF, 256)],
        (squares, key_rows, value_rows),
        name="norm",
    )
    p1 = lax.ppermute(p1, "seq", peer)
    p2 = lax.ppermute(p2, "seq", beside)
    yrecv = exchange(ysend, "seq", COLUMN_GROUPS)
    zsend = call(
        row_kernel,
        sds(8, SLOT, 256),
        (yrecv, lv),
        scratch=[
            pltpu.VMEM((8, FAR, 256), BF16),
            pltpu.VMEM((8, 64, 256), BF16),
            pltpu.SemaphoreType.DMA((2,)),
        ],
        out_spaces=[pl.ANY],
        name="rows",
    )
    zrecv = exchange(zsend, "seq", ROW_GROUPS)
    qn, near = call(
        lambda *refs: near_kernel(width, *refs),
        [sds(ROWS, FEAT), sds(LEAVES, 8, 256, dtype=F32)],
        (squares, queries, kv, one, out_grad),
        flops=14 * 2 * 2 * 256 * LEAF * FEAT,
        name="near",
    )
    stat, cross, halo, p1, p2, zsend = call(
        attend_kernel,
        [sds(LEAVES, 8, 256, dtype=F32), sds(768, 256), sds(2, LEAF, 256)]
        + [sds(192, 256), sds(LEAF, 256), sds(8, SLOT, 256)],
        (qn, out_grad, near, p1, p2, zrecv),
        scratch=[
            pltpu.VMEM((1024, FEAT), BF16),
            pltpu.VMEM((1024, FEAT), BF16),
            pltpu.VMEM((LEAVES, 768, 256), F32),
            pltpu.VMEM((LEAVES, 7 * LEAF, 256), F32),
            pltpu.VMEM((LEAVES, 7 * LEAF, 256), F32),
            pltpu.VMEM((768, 1024), BF16),
            pltpu.VMEM((768, 1024), BF16),
            pltpu.VMEM((2, LEAF, 256), BF16),
            pltpu.VMEM((768, 256), BF16),
            pltpu.VMEM((8, FAR, 256), BF16),
            pltpu.VMEM((8, 64, 256), BF16),
            pltpu.SemaphoreType.DMA((2,)),
        ],
        out_spaces=[pltpu.VMEM] * 5 + [pl.ANY],
        flops=4 * 4 * 2 * 256 * 768 * FEAT,
        name="attend",
    )
    p1 = lax.ppermute(p1, "seq", peer)
    p2 = lax.ppermute(p2, "seq", beside)
    zrecv = exchange(zsend, "seq", BACKWARD_ROWS)
    attended, nqg, tok, qsum = call(
        after_kernel,
        [sds(ROWS, FEAT), sds(ROWS, FEAT, dtype=F32), sds(ROWS, 256, dtype=F32)]
        + [sds(8, FEAT, dtype=F32)],
        (stat, qn, kv, one, out_grad, halo, cross, squares, queries),
        scratch=[
            pltpu.VMEM((768, 256), BF16),
            pltpu.VMEM((768, 256), F32),
            pltpu.VMEM((256, 256), F32),
        ],
        flops=4 * 5 * 2 * 256 * KEYS * FEAT,
        name="after",
    )
    ysend = call(
        column_kernel,
        sds(8, 16, 256),
        (zrecv, p1, p2, tok),
        scratch=[pltpu.VMEM((8, FAR, 256), BF16), pltpu.SemaphoreType.DMA],
        spaces=[pl.ANY] * 4,
        name="columns",
    )
    yrecv = exchange(ysend, "seq", COLUMN_GROUPS)
    nkg, value_grad, inner = call(
        total_kernel,
        [sds(ROWS, FEAT, dtype=F32), sds(ROWS, FEAT), sds(heads, 8, FEAT, dtype=F32)],
        (tok, p1, p2, zrecv, yrecv, key_rows, qsum),
        scratch=[
            pltpu.VMEM((ROWS, 256), F32),
        ],
        name="total",
    )
    inner = exchange(inner, "head")
    query_grad, key_grad, value_grad = call(
        lambda *refs: finish_kernel(width, *refs),
        [sds(ROWS, FEAT), sds(ROWS, FEAT), sds(ROWS, FEAT)],
        (squares, inner, queries, key_rows, nqg, nkg, value_grad),
        scratch=[pltpu.VMEM((2, ROWS, FEAT), BF16), pltpu.SemaphoreType.DMA((3,))],
        out_spaces=[pl.ANY] * 3,
        name="finish",
    )
    return (attended, query_grad, key_grad, value_grad)


def solution(mesh):
    placed = (
        P("seq", "head"),
        P("seq", "head"),
        P("seq", "head"),
        P("head"),
        P("head"),
        P("seq", "head"),
    )
    return jax.shard_map(
        local,
        mesh=mesh,
        in_specs=placed,
        out_specs=(P("seq", "head"), P("seq", "head"), P("seq", "head"), P("seq", "head")),
        check_vma=False,
    )
```

```python
import math

import jax
import jax.numpy as jnp
from jax import lax
from jax.experimental import pallas as pl
from jax.experimental.pallas import tpu as pltpu
from jax.sharding import PartitionSpec as P

ROWS = 512
FEAT = 128
LEAF = 128
LEAVES = 4
HEAD = 64
KEYS = 1280
EPS = 1e-06
LN2 = math.log(2.0)
F32 = jnp.float32
BF16 = jnp.bfloat16
ROW_LEVEL = {1: 2, 2: 3, 3: 3, 4: 4, 5: 4, 6: 4, 7: 4}
COLUMN_LEVEL = {1: 5, 2: 6, 3: 6, 4: 7, 5: 7, 6: 7, 7: 7}
FAR = 48
SLOT = 112
FIRST_Z = 7


def dot(a, b, dims):
    return lax.dot_general(a, b, ((dims[:1], dims[1:]), ((), ())), preferred_element_type=F32)


def iota(shape, axis):
    return lax.broadcasted_iota(jnp.int32, shape, axis)


def pooling(rows, level):
    token = iota((rows, ROWS), 1)
    hit = jnp.right_shift(token, level) == iota((rows, ROWS), 0)
    return jnp.where(hit, 2.0**-level, 0.0)


def spreading(first, rows, level):
    token = iota((ROWS, rows), 0)
    hit = jnp.right_shift(token, level) == iota((ROWS, rows), 1) + first
    return jnp.where(hit, 2.0**-level, 0.0)


def far_pick(shape, far_axis):
    far = iota(shape, far_axis)
    slot_row = iota(shape, 1 - far_axis)
    mid = far - 16
    low = far - 32
    column = jnp.where(
        far < 16,
        far,
        jnp.where(
            far < 32,
            (1 + jnp.right_shift(mid, 3)) * 16 + jnp.bitwise_and(mid, 7),
            (3 + jnp.right_shift(low, 2)) * 16 + jnp.bitwise_and(low, 3),
        ),
    )
    return jnp.where(column == slot_row, 1.0, 0.0).astype(BF16)


def token_sums(x):
    return [
        jnp.sum(x[i * LEAF : (i + 1) * LEAF].T, axis=0, keepdims=True) for i in range(LEAVES)
    ]


def spread_tokens(tile, first):
    return jnp.concatenate(
        [
            jnp.broadcast_to(tile[first + i : first + i + 1], (LEAF, LEAF)).T
            for i in range(LEAVES)
        ],
        axis=0,
    )


def squares_kernel(q_in, k_in, qg_in, kg_in, out_ref, rows, gains, sems):
    copies = [
        pltpu.make_async_copy(source, target, sems.at[i])
        for i, (source, target) in enumerate(
            ((q_in, rows.at[0]), (k_in, rows.at[1]), (qg_in, gains.at[0]), (kg_in, gains.at[1]))
        )
    ]
    for copy in copies:
        copy.start()
    sums = []
    for i in range(2):
        copies[i].wait()
        x = rows[i].astype(F32)
        sums += token_sums(x * x)
    for copy in copies[2:]:
        copy.wait()
    tile = jnp.concatenate(sums + [gains[0], gains[1], jnp.zeros((6, FEAT), F32)], axis=0)
    for i in range(out_ref.shape[0]):
        out_ref[i] = tile


def rates(width, sum_ref):
    return lax.rsqrt(jnp.sum(sum_ref[:, :8], axis=0) / width + EPS)


def norm_kernel(width, sum_ref, k_ref, v_ref, kv_ref, one_ref, lv_ref, y_ref, p1_ref, p2_ref):
    index = lax.axis_index("seq")
    column = jnp.right_shift(index, 3)
    odd = jnp.bitwise_and(index, 1)
    gain = sum_ref[lax.axis_index("head"), 9:10]
    kv_ref[:, :FEAT] = (
        k_ref[...].astype(F32) * spread_tokens(rates(width, sum_ref), 4) * gain
    ).astype(BF16)
    kv_ref[:, FEAT:] = v_ref[...]
    pool = jnp.concatenate(
        [pooling(ROWS >> level, level) for level in (1, 2, 3, 4)]
        + [pooling(16, COLUMN_LEVEL[d]) for d in range(1, 8)],
        axis=0,
    ).astype(BF16)
    coarse = dot(pool, kv_ref[...], (1, 0)).astype(BF16)
    one_ref[...] = coarse[:256]
    lv_ref[...] = coarse[256:480]
    y_ref[column] = jnp.zeros((16, 2 * FEAT), BF16)
    for d in range(1, 8):
        y_ref[jnp.bitwise_xor(column, d)] = coarse[464 + 16 * d : 480 + 16 * d]
    p1_ref[:LEAF] = kv_ref[pl.ds(pl.multiple_of((1 - odd) * 384, LEAF), LEAF)]
    p1_ref[LEAF:] = coarse[320:384]
    p2_ref[...] = kv_ref[pl.ds(pl.multiple_of(odd * 384, LEAF), LEAF)]


def start_all(copies):
    for copy in copies:
        copy.start()
    return copies


def wait_all(copies):
    for copy in copies:
        copy.wait()


def row_kernel(y_ref, lv_ref, out_ref, far_scr, mid_scr, sems):
    index = lax.axis_index("seq")
    column = jnp.right_shift(index, 3)
    place = jnp.bitwise_and(index, 7)
    mid_scr[place] = jnp.zeros((64, 2 * FEAT), BF16)
    for d in range(1, 8):
        other = jnp.bitwise_xor(place, d)
        if d < 4:
            mid_scr[other] = lv_ref[:64] if d == 1 else lv_ref[128:192]
        else:
            mid_scr[other, :32] = lv_ref[192:224]
            mid_scr[other, 32:] = jnp.zeros((32, 2 * FEAT), BF16)
    copies = start_all([pltpu.make_async_copy(mid_scr, out_ref.at[:, pl.ds(FAR, 64)], sems.at[0])])
    slots = jnp.concatenate([y_ref[jnp.bitwise_xor(column, d)] for d in range(1, 8)], axis=0)
    far = dot(far_pick((FAR, 112), 0), slots, (1, 0)).astype(BF16)
    for s in range(8):
        far_scr[s] = far
    copies += start_all([pltpu.make_async_copy(far_scr, out_ref.at[:, pl.ds(0, FAR)], sems.at[1])])
    wait_all(copies)


def by_head(block):
    lane = iota((LEAF, FEAT), 1)
    zero = jnp.zeros((LEAF, FEAT), BF16)
    return jnp.concatenate(
        [jnp.where(lane < HEAD, block, zero), jnp.where(lane < HEAD, zero, block)], axis=0
    )


def peak(x):
    return jnp.max(x, axis=0, keepdims=True)


def add_up(x):
    return jnp.sum(x, axis=0, keepdims=True)


HALO_PIECE = {0: 0, LEAVES - 1: 2}


def far_bias():
    return jnp.concatenate(
        [jnp.full((LEAF, 2 * LEAF), level * LN2, F32) for level in range(1, 8)], axis=0
    )


def outside_bias():
    index = lax.axis_index("seq")
    last = lax.axis_size("seq") - 1
    return {
        0: jnp.where(index > 0, 0.0, -1e30).astype(F32),
        LEAVES - 1: jnp.where(index < last, 0.0, -1e30).astype(F32),
    }


def weigh(kv, q2, g2):
    score = dot(kv[:, :FEAT], q2, (1, 1))
    top = peak(score)
    weight = jnp.exp(score - top)
    pgrad = dot(kv[:, FEAT:], g2, (1, 1))
    return weight, pgrad, (top, add_up(weight), add_up(weight * pgrad))


def combine(stats):
    top = stats[0][0]
    for stat in stats[1:]:
        top = jnp.maximum(top, stat[0])
    factors = [jnp.exp(stat[0] - top) for stat in stats]
    total = sum(factor * stat[1] for factor, stat in zip(factors, stats))
    mixed = sum(factor * stat[2] for factor, stat in zip(factors, stats))
    return top, total, mixed, factors


def scaled_queries(block):
    return by_head(block) * jnp.asarray(0.125, BF16)


def near_kernel(width, sum_ref, q_ref, kv_ref, one_ref, g_ref, qn_ref, stat_ref):
    gain = sum_ref[lax.axis_index("head"), 8:9]
    qn_ref[...] = (
        q_ref[...].astype(F32) * spread_tokens(rates(width, sum_ref), 0) * gain
    ).astype(BF16)
    for b in range(LEAVES):
        block = slice(b * LEAF, (b + 1) * LEAF)
        q2 = scaled_queries(qn_ref[block])
        g2 = by_head(g_ref[block])
        half = (1 - b // 2) * LEAF
        stats = [
            weigh(kv_ref[(b + i - 1) * LEAF : (b + i) * LEAF], q2, g2)[2]
            for i in range(3)
            if HALO_PIECE.get(b) != i
        ]
        top, total, mixed = weigh(one_ref[half : half + LEAF], q2, g2)[2]
        stats.append((top + LN2, total, mixed))
        top, total, mixed, _ = combine(stats)
        stat_ref[b] = jnp.concatenate([top, total, mixed, jnp.zeros((5, 2 * LEAF), F32)], axis=0)


def attend_kernel(
    qn_ref, g_ref, near_ref, p1_ref, p2_ref, z_ref,
    stat_ref, cross, halo, p1o_ref, p2o_ref, zo_ref,
    q2_scr, g2_scr, score_scr, weight_scr, pgrad_scr, low_scr, sgrad_scr, rims, cross_grad, far_scr, mid_scr, sems,
):
    index = lax.axis_index("seq")
    place = jnp.bitwise_and(index, 7)
    slot = jnp.bitwise_xor(place, FIRST_Z)
    odd = jnp.bitwise_and(index, 1)
    peer_side = 1 - odd
    halo[peer_side] = p1_ref[:LEAF]
    halo[odd] = p2_ref[...]
    cross[:64] = z_ref[jnp.bitwise_xor(place, 1), FAR:]
    cross[64:128] = p1_ref[LEAF:]
    cross[128:192] = z_ref[jnp.bitwise_xor(place, 2), FAR:]
    cross[192:256] = z_ref[jnp.bitwise_xor(place, 3), FAR:]
    for i in range(4):
        cross[256 + 32 * i : 288 + 32 * i] = z_ref[jnp.bitwise_xor(place, 4 + i), FAR : FAR + 32]
    for s in range(8):
        for j in range(3):
            at = 384 + LEAF * j + 16 * s
            cross[at : at + 16] = z_ref[s, 16 * j : 16 * (j + 1)]

    outside = outside_bias()
    rim_rows = []
    for b in range(LEAVES):
        block = slice(b * LEAF, (b + 1) * LEAF)
        lanes = slice(2 * b * LEAF, 2 * (b + 1) * LEAF)
        q2 = scaled_queries(qn_ref[block])
        g2 = by_head(g_ref[block])
        q2_scr[lanes] = q2
        g2_scr[lanes] = g2
        side = 0 if b == 0 else 1
        stats = [(near_ref[b, 0:1], near_ref[b, 1:2], near_ref[b, 2:3])]
        score_scr[b] = dot(cross[:, :FEAT], q2, (1, 1))
        pgrad_scr[b, : 6 * LEAF] = dot(cross[:, FEAT:], g2, (1, 1))
        for i in range(6):
            rows = slice(i * LEAF, (i + 1) * LEAF)
            score = score_scr[b, rows]
            top = peak(score)
            weight = jnp.exp(score - top)
            weight_scr[b, rows] = weight
            mixed = add_up(weight * pgrad_scr[b, rows])
            stats.append((top + (i + 2) * LN2, add_up(weight), mixed))
        if b in HALO_PIECE:
            weight, pgrad, (top, total, mixed) = weigh(halo[side], q2, g2)
            weight_scr[b, 6 * LEAF :] = weight
            pgrad_scr[b, 6 * LEAF :] = pgrad
            stats.append((top + outside[b], total, mixed))
        top, total, mixed, factors = combine(stats)
        inverse = 1.0 / total
        delta = mixed * inverse
        stat_ref[b] = jnp.concatenate(
            [top, inverse, delta, jnp.zeros((5, 2 * LEAF), F32)], axis=0
        )
        for i in range(6):
            rows = slice(i * LEAF, (i + 1) * LEAF)
            prob = weight_scr[b, rows] * (factors[i + 1] * inverse)
            low_scr[rows, lanes] = prob.astype(BF16)
            sgrad_scr[rows, lanes] = (prob * (pgrad_scr[b, rows] - delta)).astype(BF16)
        if b in HALO_PIECE:
            rim_rows.append((b, side, lanes, factors[7] * inverse, delta))

    cross_grad[:, :FEAT] = dot(sgrad_scr[...], q2_scr[...], (1, 0)).astype(BF16)
    cross_grad[:, FEAT:] = dot(low_scr[...], g2_scr[...], (1, 0)).astype(BF16)
    for j in range(3):
        for s in range(8):
            at = 384 + LEAF * j + 16 * s
            far_scr[s ^ FIRST_Z, 16 * j : 16 * (j + 1)] = cross_grad[at : at + 16]
    copies = start_all([pltpu.make_async_copy(far_scr, zo_ref.at[:, pl.ds(0, FAR)], sems.at[0])])
    mid_scr[slot] = jnp.zeros((64, 2 * FEAT), BF16)
    mid_scr[jnp.bitwise_xor(slot, 1)] = cross_grad[:64]
    mid_scr[jnp.bitwise_xor(slot, 2)] = cross_grad[128:192]
    mid_scr[jnp.bitwise_xor(slot, 3)] = cross_grad[192:256]
    for i in range(4):
        other = jnp.bitwise_xor(slot, 4 + i)
        mid_scr[other, :32] = cross_grad[256 + 32 * i : 288 + 32 * i]
        mid_scr[other, 32:] = jnp.zeros((32, 2 * FEAT), BF16)
    copies += start_all([pltpu.make_async_copy(mid_scr, zo_ref.at[:, pl.ds(FAR, 64)], sems.at[1])])
    for b, side, lanes, factor, delta in rim_rows:
        prob = weight_scr[b, 6 * LEAF :] * factor
        sgrad = (prob * (pgrad_scr[b, 6 * LEAF :] - delta)).astype(BF16)
        rims[side, :, :FEAT] = dot(sgrad, q2_scr[lanes], (1, 0)).astype(BF16)
        rims[side, :, FEAT:] = dot(prob.astype(BF16), g2_scr[lanes], (1, 0)).astype(BF16)
    p1o_ref[:LEAF] = rims[peer_side]
    p1o_ref[LEAF:] = cross_grad[64:128]
    p2o_ref[...] = rims[odd]
    wait_all(copies)


def after_kernel(
    stat_ref, qn_ref, kv_ref, one_ref, g_ref, halo, cross, sum_ref, q_ref,
    att_ref, nqg_ref, tok_ref, qsum_ref, near, near_grad, one_grad,
):
    near[:LEAF] = halo[0]
    near[LEAF : LEAF + ROWS] = kv_ref[...]
    near[LEAF + ROWS :] = halo[1]
    near_grad[...] = jnp.zeros_like(near_grad)
    one_grad[...] = jnp.zeros_like(one_grad)
    feature = iota((FEAT, LEAF), 0)
    bias = far_bias()
    outside = outside_bias()

    def merge_heads(transposed):
        return jnp.where(feature < HEAD, transposed[:, :LEAF], transposed[:, LEAF:]).T

    for b in range(LEAVES):
        rows = slice(b * LEAF, (b + 1) * LEAF)
        near_rows = slice(b * LEAF, (b + 3) * LEAF)
        half = (1 - b // 2) * LEAF
        q2 = scaled_queries(qn_ref[rows])
        g2 = by_head(g_ref[rows])
        kv = jnp.concatenate([near[near_rows], one_ref[half : half + LEAF], cross[...]], axis=0)
        keys = kv[:, :FEAT]
        values = kv[:, FEAT:]
        raw = dot(keys, q2, (1, 1))
        before, after = raw[:LEAF], raw[2 * LEAF : 3 * LEAF]
        if b == 0:
            before = before + outside[b]
        if b == LEAVES - 1:
            after = after + outside[b]
        scores = jnp.concatenate(
            [before, raw[LEAF : 2 * LEAF], after, raw[3 * LEAF :] + bias], axis=0
        )
        probs = jnp.exp(scores - stat_ref[b, 0:1]) * stat_ref[b, 1:2]
        low = probs.astype(BF16)
        score_grad = (probs * (dot(values, g2, (1, 1)) - stat_ref[b, 2:3])).astype(BF16)
        att_ref[rows] = merge_heads(dot(values, low, (0, 0))).astype(BF16)
        nqg_ref[rows] = merge_heads(dot(keys, score_grad, (0, 0))) * 0.125
        for part, lanes in (
            (dot(score_grad[: 4 * LEAF], q2, (1, 0)), slice(0, FEAT)),
            (dot(low[: 4 * LEAF], g2, (1, 0)), slice(FEAT, 2 * FEAT)),
        ):
            near_grad[near_rows, lanes] += part[: 3 * LEAF]
            one_grad[half : half + LEAF, lanes] += part[3 * LEAF :]
    spread = spreading(0, 256, 1).astype(BF16)
    high = one_grad[...].astype(BF16)
    rest = (one_grad[...] - high.astype(F32)).astype(BF16)
    tok_ref[...] = near_grad[LEAF : LEAF + ROWS] + dot(spread, high, (1, 0)) + dot(spread, rest, (1, 0))
    gains = sum_ref[lax.axis_index("head"), 8:16]
    sums = token_sums(q_ref[...].astype(F32) * gains[0:1] * nqg_ref[...])
    qsum_ref[...] = jnp.concatenate(sums + [gains[1:2], jnp.zeros((3, FEAT), F32)], axis=0)


def column_kernel(z_ref, p1_ref, p2_ref, tok_ref, out_ref, far_rows, sem):
    column = jnp.right_shift(lax.axis_index("seq"), 3)
    copy = pltpu.make_async_copy(z_ref.at[:, pl.ds(0, FAR)], far_rows, sem)
    copy.start()
    copy.wait()
    far = jnp.sum(far_rows[...].astype(F32), axis=0).astype(BF16)
    slots = dot(far_pick((112, FAR), 1), far, (1, 0)).astype(BF16)
    out_ref[column] = jnp.zeros((16, 2 * FEAT), BF16)
    for d in range(1, 8):
        out_ref[jnp.bitwise_xor(column, d)] = slots[16 * (d - 1) : 16 * d]


def total_kernel(
    tok_ref, p1_ref, p2_ref, z_ref, y_ref, k_ref, qsum_ref,
    nkg_ref, vg_ref, sum_ref, acc,
):
    index = lax.axis_index("seq")
    column = jnp.right_shift(index, 3)
    place = jnp.bitwise_xor(jnp.bitwise_and(index, 7), FIRST_Z)
    odd = jnp.bitwise_and(index, 1)
    pieces = [z_ref[jnp.bitwise_xor(place, 1), FAR:], p1_ref[LEAF:]]
    maps = [spreading(0, 64, 2), spreading(64, 64, 2)]
    for d in range(2, 8):
        rows = ROWS >> ROW_LEVEL[d]
        pieces.append(z_ref[jnp.bitwise_xor(place, d), FAR : FAR + rows])
        maps.append(spreading(0, rows, ROW_LEVEL[d]))
    for d in range(1, 8):
        pieces.append(y_ref[jnp.bitwise_xor(column, d)])
        maps.append(spreading(0, 16, COLUMN_LEVEL[d]))
    spread = jnp.concatenate(maps, axis=1).astype(BF16)
    acc[...] = tok_ref[...] + dot(spread, jnp.concatenate(pieces, axis=0), (1, 0))
    acc[pl.ds(pl.multiple_of((1 - odd) * 384, LEAF), LEAF)] += p1_ref[:LEAF].astype(F32)
    acc[pl.ds(pl.multiple_of(odd * 384, LEAF), LEAF)] += p2_ref[...].astype(F32)
    vg_ref[...] = acc[:, FEAT:].astype(BF16)
    key_total = acc[:, :FEAT]
    nkg_ref[...] = key_total
    sums = token_sums(k_ref[...].astype(F32) * qsum_ref[LEAVES : LEAVES + 1] * key_total)
    tile = jnp.concatenate([qsum_ref[:LEAVES]] + sums, axis=0)
    for i in range(sum_ref.shape[0]):
        sum_ref[i] = tile


def finish_kernel(
    width, sq_ref, inner_ref, q_ref, k_ref, nqg_ref, nkg_ref, value_ref,
    dq_ref, dk_ref, vg_ref, results, sems,
):
    copies = start_all([pltpu.make_async_copy(value_ref, vg_ref, sems.at[2])])
    rate = rates(width, sq_ref)
    inner = jnp.sum(inner_ref[...], axis=0) / width
    cubed = rate * rate * rate * inner
    gains = sq_ref[lax.axis_index("head"), 8:16]
    for side, (x_ref, grad_ref, out_ref) in enumerate(
        ((q_ref, nqg_ref, dq_ref), (k_ref, nkg_ref, dk_ref))
    ):
        results[side] = (
            spread_tokens(rate, 4 * side) * gains[side : side + 1] * grad_ref[...]
            - x_ref[...].astype(F32) * spread_tokens(cubed, 4 * side)
        ).astype(BF16)
        copies += start_all([pltpu.make_async_copy(results.at[side], out_ref, sems.at[side])])
    wait_all(copies)


def call(kernel, outs, args, scratch=(), flops=0, name=None, spaces=None, out_spaces=None, vmem=40):
    many = isinstance(outs, list)
    moved = sum(math.prod(x.shape) * x.dtype.itemsize for x in list(args) + (outs if many else [outs]))
    out_spaces = out_spaces or [pltpu.VMEM] * (len(outs) if many else 1)
    out_specs = [pl.BlockSpec(memory_space=space) for space in out_spaces]
    return pl.pallas_call(
        kernel,
        out_shape=outs,
        in_specs=[pl.BlockSpec(memory_space=space) for space in spaces or [pltpu.VMEM] * len(args)],
        out_specs=out_specs if many else out_specs[0],
        scratch_shapes=list(scratch),
        compiler_params=pltpu.CompilerParams(vmem_limit_bytes=vmem * 1024 * 1024),
        cost_estimate=pl.CostEstimate(flops=flops, bytes_accessed=moved, transcendentals=0),
        name=name,
    )(*args)


def sds(*shape, dtype=BF16):
    return jax.ShapeDtypeStruct(shape, dtype)


BACKWARD_ROWS = [[8 * y + (p ^ FIRST_Z) for p in range(8)] for y in range(8)]
ROW_GROUPS = [[8 * y + z for z in range(8)] for y in range(8)]
COLUMN_GROUPS = [[8 * y + z for y in range(8)] for z in range(8)]


def exchange(x, axis, groups=None):
    return lax.all_to_all(x, axis, 0, 0, axis_index_groups=groups, tiled=True)


def local(queries, key_rows, value_rows, query_gain, key_gain, out_grad):
    seq = lax.axis_size("seq")
    heads = lax.axis_size("head")
    width = float(heads * FEAT)
    qg = query_gain.reshape(1, FEAT)
    kg = key_gain.reshape(1, FEAT)
    peer = [(i, i ^ 1) for i in range(seq)]
    beside = [(i, i + 1) for i in range(1, seq - 1, 2)] + [(i + 1, i) for i in range(1, seq - 1, 2)]

    squares = call(
        squares_kernel,
        sds(heads, 16, FEAT, dtype=F32),
        (queries, key_rows, qg, kg),
        scratch=[
            pltpu.VMEM((2, ROWS, FEAT), BF16),
            pltpu.VMEM((2, 1, FEAT), F32),
            pltpu.SemaphoreType.DMA((4,)),
        ],
        spaces=[pl.ANY] * 4,
        vmem=60,
        name="squares",
    )
    squares = exchange(squares, "head")
    kv, one, lv, ysend, p1, p2 = call(
        lambda *refs: norm_kernel(width, *refs),
        [sds(ROWS, 256), sds(256, 256), sds(224, 256), sds(8, 16, 256), sds(192, 256), sds(LEAF, 256)],
        (squares, key_rows, value_rows),
        name="norm",
    )
    p1 = lax.ppermute(p1, "seq", peer)
    p2 = lax.ppermute(p2, "seq", beside)
    yrecv = exchange(ysend, "seq", COLUMN_GROUPS)
    zsend = call(
        row_kernel,
        sds(8, SLOT, 256),
        (yrecv, lv),
        scratch=[
            pltpu.VMEM((8, FAR, 256), BF16),
            pltpu.VMEM((8, 64, 256), BF16),
            pltpu.SemaphoreType.DMA((2,)),
        ],
        out_spaces=[pl.ANY],
        name="rows",
    )
    zrecv = exchange(zsend, "seq", ROW_GROUPS)
    qn, near = call(
        lambda *refs: near_kernel(width, *refs),
        [sds(ROWS, FEAT), sds(LEAVES, 8, 256, dtype=F32)],
        (squares, queries, kv, one, out_grad),
        flops=14 * 2 * 2 * 256 * LEAF * FEAT,
        name="near",
    )
    stat, cross, halo, p1, p2, zsend = call(
        attend_kernel,
        [sds(LEAVES, 8, 256, dtype=F32), sds(768, 256), sds(2, LEAF, 256)]
        + [sds(192, 256), sds(LEAF, 256), sds(8, SLOT, 256)],
        (qn, out_grad, near, p1, p2, zrecv),
        scratch=[
            pltpu.VMEM((1024, FEAT), BF16),
            pltpu.VMEM((1024, FEAT), BF16),
            pltpu.VMEM((LEAVES, 768, 256), F32),
            pltpu.VMEM((LEAVES, 7 * LEAF, 256), F32),
            pltpu.VMEM((LEAVES, 7 * LEAF, 256), F32),
            pltpu.VMEM((768, 1024), BF16),
            pltpu.VMEM((768, 1024), BF16),
            pltpu.VMEM((2, LEAF, 256), BF16),
            pltpu.VMEM((768, 256), BF16),
            pltpu.VMEM((8, FAR, 256), BF16),
            pltpu.VMEM((8, 64, 256), BF16),
            pltpu.SemaphoreType.DMA((2,)),
        ],
        out_spaces=[pltpu.VMEM] * 5 + [pl.ANY],
        flops=4 * 4 * 2 * 256 * 768 * FEAT,
        name="attend",
    )
    p1 = lax.ppermute(p1, "seq", peer)
    p2 = lax.ppermute(p2, "seq", beside)
    zrecv = exchange(zsend, "seq", BACKWARD_ROWS)
    attended, nqg, tok, qsum = call(
        after_kernel,
        [sds(ROWS, FEAT), sds(ROWS, FEAT, dtype=F32), sds(ROWS, 256, dtype=F32)]
        + [sds(8, FEAT, dtype=F32)],
        (stat, qn, kv, one, out_grad, halo, cross, squares, queries),
        scratch=[
            pltpu.VMEM((768, 256), BF16),
            pltpu.VMEM((768, 256), F32),
            pltpu.VMEM((256, 256), F32),
        ],
        flops=4 * 5 * 2 * 256 * KEYS * FEAT,
        name="after",
    )
    ysend = call(
        column_kernel,
        sds(8, 16, 256),
        (zrecv, p1, p2, tok),
        scratch=[pltpu.VMEM((8, FAR, 256), BF16), pltpu.SemaphoreType.DMA],
        spaces=[pl.ANY] * 4,
        name="columns",
    )
    yrecv = exchange(ysend, "seq", COLUMN_GROUPS)
    nkg, value_grad, inner = call(
        total_kernel,
        [sds(ROWS, FEAT, dtype=F32), sds(ROWS, FEAT), sds(heads, 8, FEAT, dtype=F32)],
        (tok, p1, p2, zrecv, yrecv, key_rows, qsum),
        scratch=[
            pltpu.VMEM((ROWS, 256), F32),
        ],
        name="total",
    )
    odd_first = [[p ^ 1 for p in range(heads)]] if heads > 1 else None
    inner = exchange(inner, "head", odd_first)
    query_grad, key_grad, value_grad = call(
        lambda *refs: finish_kernel(width, *refs),
        [sds(ROWS, FEAT), sds(ROWS, FEAT), sds(ROWS, FEAT)],
        (squares, inner, queries, key_rows, nqg, nkg, value_grad),
        scratch=[pltpu.VMEM((2, ROWS, FEAT), BF16), pltpu.SemaphoreType.DMA((3,))],
        out_spaces=[pl.ANY] * 3,
        name="finish",
    )
    return (attended, query_grad, key_grad, value_grad)


def solution(mesh):
    placed = (
        P("seq", "head"),
        P("seq", "head"),
        P("seq", "head"),
        P("head"),
        P("head"),
        P("seq", "head"),
    )
    return jax.shard_map(
        local,
        mesh=mesh,
        in_specs=placed,
        out_specs=(P("seq", "head"), P("seq", "head"), P("seq", "head"), P("seq", "head")),
        check_vma=False,
    )
```

```python
import math

import jax
import jax.numpy as jnp
from jax import lax
from jax.experimental import pallas as pl
from jax.experimental.pallas import tpu as pltpu
from jax.sharding import PartitionSpec as P

ROWS = 512
FEAT = 128
LEAF = 128
LEAVES = 4
HEAD = 64
KEYS = 1280
EPS = 1e-06
LN2 = math.log(2.0)
F32 = jnp.float32
BF16 = jnp.bfloat16
ROW_LEVEL = {1: 2, 2: 3, 3: 3, 4: 4, 5: 4, 6: 4, 7: 4}
COLUMN_LEVEL = {1: 5, 2: 6, 3: 6, 4: 7, 5: 7, 6: 7, 7: 7}
FAR = 48
SLOT = 112
FIRST_Z = 7
FIRST_Y = 5


def dot(a, b, dims):
    return lax.dot_general(a, b, ((dims[:1], dims[1:]), ((), ())), preferred_element_type=F32)


def iota(shape, axis):
    return lax.broadcasted_iota(jnp.int32, shape, axis)


def pooling(rows, level):
    token = iota((rows, ROWS), 1)
    hit = jnp.right_shift(token, level) == iota((rows, ROWS), 0)
    return jnp.where(hit, 2.0**-level, 0.0)


def spreading(first, rows, level):
    token = iota((ROWS, rows), 0)
    hit = jnp.right_shift(token, level) == iota((ROWS, rows), 1) + first
    return jnp.where(hit, 2.0**-level, 0.0)


def far_pick(shape, far_axis):
    far = iota(shape, far_axis)
    slot_row = iota(shape, 1 - far_axis)
    mid = far - 16
    low = far - 32
    column = jnp.where(
        far < 16,
        far,
        jnp.where(
            far < 32,
            (1 + jnp.right_shift(mid, 3)) * 16 + jnp.bitwise_and(mid, 7),
            (3 + jnp.right_shift(low, 2)) * 16 + jnp.bitwise_and(low, 3),
        ),
    )
    return jnp.where(column == slot_row, 1.0, 0.0).astype(BF16)


def token_sums(x):
    return [
        jnp.sum(x[i * LEAF : (i + 1) * LEAF].T, axis=0, keepdims=True) for i in range(LEAVES)
    ]


def spread_tokens(tile, first):
    return jnp.concatenate(
        [
            jnp.broadcast_to(tile[first + i : first + i + 1], (LEAF, LEAF)).T
            for i in range(LEAVES)
        ],
        axis=0,
    )


def squares_kernel(q_in, k_in, qg_in, kg_in, out_ref, rows, gains, sems):
    copies = [
        pltpu.make_async_copy(source, target, sems.at[i])
        for i, (source, target) in enumerate(
            ((q_in, rows.at[0]), (k_in, rows.at[1]), (qg_in, gains.at[0]), (kg_in, gains.at[1]))
        )
    ]
    for copy in copies:
        copy.start()
    sums = []
    for i in range(2):
        copies[i].wait()
        x = rows[i].astype(F32)
        sums += token_sums(x * x)
    for copy in copies[2:]:
        copy.wait()
    tile = jnp.concatenate(sums + [gains[0], gains[1], jnp.zeros((6, FEAT), F32)], axis=0)
    for i in range(out_ref.shape[0]):
        out_ref[i] = tile


def rates(width, sum_ref):
    return lax.rsqrt(jnp.sum(sum_ref[:, :8], axis=0) / width + EPS)


def norm_kernel(width, sum_ref, k_ref, v_ref, kv_ref, one_ref, lv_ref, y_ref, p1_ref, p2_ref):
    index = lax.axis_index("seq")
    column = jnp.bitwise_xor(jnp.right_shift(index, 3), FIRST_Y)
    odd = jnp.bitwise_and(index, 1)
    gain = sum_ref[lax.axis_index("head"), 9:10]
    kv_ref[:, :FEAT] = (
        k_ref[...].astype(F32) * spread_tokens(rates(width, sum_ref), 4) * gain
    ).astype(BF16)
    kv_ref[:, FEAT:] = v_ref[...]
    pool = jnp.concatenate(
        [pooling(ROWS >> level, level) for level in (1, 2, 3, 4)]
        + [pooling(16, COLUMN_LEVEL[d]) for d in range(1, 8)],
        axis=0,
    ).astype(BF16)
    coarse = dot(pool, kv_ref[...], (1, 0)).astype(BF16)
    one_ref[...] = coarse[:256]
    lv_ref[...] = coarse[256:480]
    y_ref[column] = jnp.zeros((16, 2 * FEAT), BF16)
    for d in range(1, 8):
        y_ref[jnp.bitwise_xor(column, d)] = coarse[464 + 16 * d : 480 + 16 * d]
    p1_ref[:LEAF] = kv_ref[pl.ds(pl.multiple_of((1 - odd) * 384, LEAF), LEAF)]
    p1_ref[LEAF:] = coarse[320:384]
    p2_ref[...] = kv_ref[pl.ds(pl.multiple_of(odd * 384, LEAF), LEAF)]


def start_all(copies):
    for copy in copies:
        copy.start()
    return copies


def wait_all(copies):
    for copy in copies:
        copy.wait()


def row_kernel(y_ref, lv_ref, out_ref, far_scr, mid_scr, sems):
    index = lax.axis_index("seq")
    column = jnp.bitwise_xor(jnp.right_shift(index, 3), FIRST_Y)
    place = jnp.bitwise_and(index, 7)
    mid_scr[place] = jnp.zeros((64, 2 * FEAT), BF16)
    for d in range(1, 8):
        other = jnp.bitwise_xor(place, d)
        if d < 4:
            mid_scr[other] = lv_ref[:64] if d == 1 else lv_ref[128:192]
        else:
            mid_scr[other, :32] = lv_ref[192:224]
            mid_scr[other, 32:] = jnp.zeros((32, 2 * FEAT), BF16)
    copies = start_all([pltpu.make_async_copy(mid_scr, out_ref.at[:, pl.ds(FAR, 64)], sems.at[0])])
    slots = jnp.concatenate([y_ref[jnp.bitwise_xor(column, d)] for d in range(1, 8)], axis=0)
    far = dot(far_pick((FAR, 112), 0), slots, (1, 0)).astype(BF16)
    for s in range(8):
        far_scr[s] = far
    copies += start_all([pltpu.make_async_copy(far_scr, out_ref.at[:, pl.ds(0, FAR)], sems.at[1])])
    wait_all(copies)


def by_head(block):
    lane = iota((LEAF, FEAT), 1)
    zero = jnp.zeros((LEAF, FEAT), BF16)
    return jnp.concatenate(
        [jnp.where(lane < HEAD, block, zero), jnp.where(lane < HEAD, zero, block)], axis=0
    )


def peak(x):
    return jnp.max(x, axis=0, keepdims=True)


def add_up(x):
    return jnp.sum(x, axis=0, keepdims=True)


HALO_PIECE = {0: 0, LEAVES - 1: 2}


def far_bias():
    return jnp.concatenate(
        [jnp.full((LEAF, 2 * LEAF), level * LN2, F32) for level in range(1, 8)], axis=0
    )


def outside_bias():
    index = lax.axis_index("seq")
    last = lax.axis_size("seq") - 1
    return {
        0: jnp.where(index > 0, 0.0, -1e30).astype(F32),
        LEAVES - 1: jnp.where(index < last, 0.0, -1e30).astype(F32),
    }


def weigh(kv, q2, g2):
    score = dot(kv[:, :FEAT], q2, (1, 1))
    top = peak(score)
    weight = jnp.exp(score - top)
    pgrad = dot(kv[:, FEAT:], g2, (1, 1))
    return weight, pgrad, (top, add_up(weight), add_up(weight * pgrad))


def combine(stats):
    top = stats[0][0]
    for stat in stats[1:]:
        top = jnp.maximum(top, stat[0])
    factors = [jnp.exp(stat[0] - top) for stat in stats]
    total = sum(factor * stat[1] for factor, stat in zip(factors, stats))
    mixed = sum(factor * stat[2] for factor, stat in zip(factors, stats))
    return top, total, mixed, factors


def scaled_queries(block):
    return by_head(block) * jnp.asarray(0.125, BF16)


def near_kernel(width, sum_ref, q_ref, kv_ref, one_ref, g_ref, qn_ref, stat_ref):
    gain = sum_ref[lax.axis_index("head"), 8:9]
    qn_ref[...] = (
        q_ref[...].astype(F32) * spread_tokens(rates(width, sum_ref), 0) * gain
    ).astype(BF16)
    for b in range(LEAVES):
        block = slice(b * LEAF, (b + 1) * LEAF)
        q2 = scaled_queries(qn_ref[block])
        g2 = by_head(g_ref[block])
        half = (1 - b // 2) * LEAF
        stats = [
            weigh(kv_ref[(b + i - 1) * LEAF : (b + i) * LEAF], q2, g2)[2]
            for i in range(3)
            if HALO_PIECE.get(b) != i
        ]
        top, total, mixed = weigh(one_ref[half : half + LEAF], q2, g2)[2]
        stats.append((top + LN2, total, mixed))
        top, total, mixed, _ = combine(stats)
        stat_ref[b] = jnp.concatenate([top, total, mixed, jnp.zeros((5, 2 * LEAF), F32)], axis=0)


def attend_kernel(
    qn_ref, g_ref, near_ref, p1_ref, p2_ref, z_ref,
    stat_ref, cross, halo, p1o_ref, p2o_ref, zo_ref,
    q2_scr, g2_scr, score_scr, weight_scr, pgrad_scr, low_scr, sgrad_scr, rims, cross_grad, far_scr, mid_scr, sems,
):
    index = lax.axis_index("seq")
    place = jnp.bitwise_and(index, 7)
    slot = jnp.bitwise_xor(place, FIRST_Z)
    odd = jnp.bitwise_and(index, 1)
    peer_side = 1 - odd
    halo[peer_side] = p1_ref[:LEAF]
    halo[odd] = p2_ref[...]
    cross[:64] = z_ref[jnp.bitwise_xor(place, 1), FAR:]
    cross[64:128] = p1_ref[LEAF:]
    cross[128:192] = z_ref[jnp.bitwise_xor(place, 2), FAR:]
    cross[192:256] = z_ref[jnp.bitwise_xor(place, 3), FAR:]
    for i in range(4):
        cross[256 + 32 * i : 288 + 32 * i] = z_ref[jnp.bitwise_xor(place, 4 + i), FAR : FAR + 32]
    for s in range(8):
        for j in range(3):
            at = 384 + LEAF * j + 16 * s
            cross[at : at + 16] = z_ref[s, 16 * j : 16 * (j + 1)]

    outside = outside_bias()
    rim_rows = []
    for b in range(LEAVES):
        block = slice(b * LEAF, (b + 1) * LEAF)
        lanes = slice(2 * b * LEAF, 2 * (b + 1) * LEAF)
        q2 = scaled_queries(qn_ref[block])
        g2 = by_head(g_ref[block])
        q2_scr[lanes] = q2
        g2_scr[lanes] = g2
        side = 0 if b == 0 else 1
        stats = [(near_ref[b, 0:1], near_ref[b, 1:2], near_ref[b, 2:3])]
        score_scr[b] = dot(cross[:, :FEAT], q2, (1, 1))
        pgrad_scr[b, : 6 * LEAF] = dot(cross[:, FEAT:], g2, (1, 1))
        for i in range(6):
            rows = slice(i * LEAF, (i + 1) * LEAF)
            score = score_scr[b, rows]
            top = peak(score)
            weight = jnp.exp(score - top)
            weight_scr[b, rows] = weight
            mixed = add_up(weight * pgrad_scr[b, rows])
            stats.append((top + (i + 2) * LN2, add_up(weight), mixed))
        if b in HALO_PIECE:
            weight, pgrad, (top, total, mixed) = weigh(halo[side], q2, g2)
            weight_scr[b, 6 * LEAF :] = weight
            pgrad_scr[b, 6 * LEAF :] = pgrad
            stats.append((top + outside[b], total, mixed))
        top, total, mixed, factors = combine(stats)
        inverse = 1.0 / total
        delta = mixed * inverse
        stat_ref[b] = jnp.concatenate(
            [top, inverse, delta, jnp.zeros((5, 2 * LEAF), F32)], axis=0
        )
        for i in range(6):
            rows = slice(i * LEAF, (i + 1) * LEAF)
            prob = weight_scr[b, rows] * (factors[i + 1] * inverse)
            low_scr[rows, lanes] = prob.astype(BF16)
            sgrad_scr[rows, lanes] = (prob * (pgrad_scr[b, rows] - delta)).astype(BF16)
        if b in HALO_PIECE:
            rim_rows.append((b, side, lanes, factors[7] * inverse, delta))

    cross_grad[:, :FEAT] = dot(sgrad_scr[...], q2_scr[...], (1, 0)).astype(BF16)
    cross_grad[:, FEAT:] = dot(low_scr[...], g2_scr[...], (1, 0)).astype(BF16)
    for j in range(3):
        for s in range(8):
            at = 384 + LEAF * j + 16 * s
            far_scr[s ^ FIRST_Z, 16 * j : 16 * (j + 1)] = cross_grad[at : at + 16]
    copies = start_all([pltpu.make_async_copy(far_scr, zo_ref.at[:, pl.ds(0, FAR)], sems.at[0])])
    mid_scr[slot] = jnp.zeros((64, 2 * FEAT), BF16)
    mid_scr[jnp.bitwise_xor(slot, 1)] = cross_grad[:64]
    mid_scr[jnp.bitwise_xor(slot, 2)] = cross_grad[128:192]
    mid_scr[jnp.bitwise_xor(slot, 3)] = cross_grad[192:256]
    for i in range(4):
        other = jnp.bitwise_xor(slot, 4 + i)
        mid_scr[other, :32] = cross_grad[256 + 32 * i : 288 + 32 * i]
        mid_scr[other, 32:] = jnp.zeros((32, 2 * FEAT), BF16)
    copies += start_all([pltpu.make_async_copy(mid_scr, zo_ref.at[:, pl.ds(FAR, 64)], sems.at[1])])
    for b, side, lanes, factor, delta in rim_rows:
        prob = weight_scr[b, 6 * LEAF :] * factor
        sgrad = (prob * (pgrad_scr[b, 6 * LEAF :] - delta)).astype(BF16)
        rims[side, :, :FEAT] = dot(sgrad, q2_scr[lanes], (1, 0)).astype(BF16)
        rims[side, :, FEAT:] = dot(prob.astype(BF16), g2_scr[lanes], (1, 0)).astype(BF16)
    p1o_ref[:LEAF] = rims[peer_side]
    p1o_ref[LEAF:] = cross_grad[64:128]
    p2o_ref[...] = rims[odd]
    wait_all(copies)


def after_kernel(
    stat_ref, qn_ref, kv_ref, one_ref, g_ref, halo, cross, sum_ref, q_ref,
    att_ref, nqg_ref, tok_ref, qsum_ref, near, near_grad, one_grad,
):
    near[:LEAF] = halo[0]
    near[LEAF : LEAF + ROWS] = kv_ref[...]
    near[LEAF + ROWS :] = halo[1]
    near_grad[...] = jnp.zeros_like(near_grad)
    one_grad[...] = jnp.zeros_like(one_grad)
    feature = iota((FEAT, LEAF), 0)
    bias = far_bias()
    outside = outside_bias()

    def merge_heads(transposed):
        return jnp.where(feature < HEAD, transposed[:, :LEAF], transposed[:, LEAF:]).T

    for b in range(LEAVES):
        rows = slice(b * LEAF, (b + 1) * LEAF)
        near_rows = slice(b * LEAF, (b + 3) * LEAF)
        half = (1 - b // 2) * LEAF
        q2 = scaled_queries(qn_ref[rows])
        g2 = by_head(g_ref[rows])
        kv = jnp.concatenate([near[near_rows], one_ref[half : half + LEAF], cross[...]], axis=0)
        keys = kv[:, :FEAT]
        values = kv[:, FEAT:]
        raw = dot(keys, q2, (1, 1))
        before, after = raw[:LEAF], raw[2 * LEAF : 3 * LEAF]
        if b == 0:
            before = before + outside[b]
        if b == LEAVES - 1:
            after = after + outside[b]
        scores = jnp.concatenate(
            [before, raw[LEAF : 2 * LEAF], after, raw[3 * LEAF :] + bias], axis=0
        )
        probs = jnp.exp(scores - stat_ref[b, 0:1]) * stat_ref[b, 1:2]
        low = probs.astype(BF16)
        score_grad = (probs * (dot(values, g2, (1, 1)) - stat_ref[b, 2:3])).astype(BF16)
        att_ref[rows] = merge_heads(dot(values, low, (0, 0))).astype(BF16)
        nqg_ref[rows] = merge_heads(dot(keys, score_grad, (0, 0))) * 0.125
        for part, lanes in (
            (dot(score_grad[: 4 * LEAF], q2, (1, 0)), slice(0, FEAT)),
            (dot(low[: 4 * LEAF], g2, (1, 0)), slice(FEAT, 2 * FEAT)),
        ):
            near_grad[near_rows, lanes] += part[: 3 * LEAF]
            one_grad[half : half + LEAF, lanes] += part[3 * LEAF :]
    spread = spreading(0, 256, 1).astype(BF16)
    high = one_grad[...].astype(BF16)
    rest = (one_grad[...] - high.astype(F32)).astype(BF16)
    tok_ref[...] = near_grad[LEAF : LEAF + ROWS] + dot(spread, high, (1, 0)) + dot(spread, rest, (1, 0))
    gains = sum_ref[lax.axis_index("head"), 8:16]
    sums = token_sums(q_ref[...].astype(F32) * gains[0:1] * nqg_ref[...])
    qsum_ref[...] = jnp.concatenate(sums + [gains[1:2], jnp.zeros((3, FEAT), F32)], axis=0)


def column_kernel(z_ref, p1_ref, p2_ref, tok_ref, out_ref, far_rows, sem):
    column = jnp.bitwise_xor(jnp.right_shift(lax.axis_index("seq"), 3), FIRST_Y)
    copy = pltpu.make_async_copy(z_ref.at[:, pl.ds(0, FAR)], far_rows, sem)
    copy.start()
    copy.wait()
    far = jnp.sum(far_rows[...].astype(F32), axis=0).astype(BF16)
    slots = dot(far_pick((112, FAR), 1), far, (1, 0)).astype(BF16)
    out_ref[column] = jnp.zeros((16, 2 * FEAT), BF16)
    for d in range(1, 8):
        out_ref[jnp.bitwise_xor(column, d)] = slots[16 * (d - 1) : 16 * d]


def total_kernel(
    tok_ref, p1_ref, p2_ref, z_ref, y_ref, k_ref, qsum_ref,
    nkg_ref, vg_ref, sum_ref, acc,
):
    index = lax.axis_index("seq")
    column = jnp.bitwise_xor(jnp.right_shift(index, 3), FIRST_Y)
    place = jnp.bitwise_xor(jnp.bitwise_and(index, 7), FIRST_Z)
    odd = jnp.bitwise_and(index, 1)
    pieces = [z_ref[jnp.bitwise_xor(place, 1), FAR:], p1_ref[LEAF:]]
    maps = [spreading(0, 64, 2), spreading(64, 64, 2)]
    for d in range(2, 8):
        rows = ROWS >> ROW_LEVEL[d]
        pieces.append(z_ref[jnp.bitwise_xor(place, d), FAR : FAR + rows])
        maps.append(spreading(0, rows, ROW_LEVEL[d]))
    for d in range(1, 8):
        pieces.append(y_ref[jnp.bitwise_xor(column, d)])
        maps.append(spreading(0, 16, COLUMN_LEVEL[d]))
    spread = jnp.concatenate(maps, axis=1).astype(BF16)
    acc[...] = tok_ref[...] + dot(spread, jnp.concatenate(pieces, axis=0), (1, 0))
    acc[pl.ds(pl.multiple_of((1 - odd) * 384, LEAF), LEAF)] += p1_ref[:LEAF].astype(F32)
    acc[pl.ds(pl.multiple_of(odd * 384, LEAF), LEAF)] += p2_ref[...].astype(F32)
    vg_ref[...] = acc[:, FEAT:].astype(BF16)
    key_total = acc[:, :FEAT]
    nkg_ref[...] = key_total
    sums = token_sums(k_ref[...].astype(F32) * qsum_ref[LEAVES : LEAVES + 1] * key_total)
    tile = jnp.concatenate([qsum_ref[:LEAVES]] + sums, axis=0)
    for i in range(sum_ref.shape[0]):
        sum_ref[i] = tile


def finish_kernel(
    width, sq_ref, inner_ref, q_ref, k_ref, nqg_ref, nkg_ref, value_ref,
    dq_ref, dk_ref, vg_ref, results, sems,
):
    copies = start_all([pltpu.make_async_copy(value_ref, vg_ref, sems.at[2])])
    rate = rates(width, sq_ref)
    inner = jnp.sum(inner_ref[...], axis=0) / width
    cubed = rate * rate * rate * inner
    gains = sq_ref[lax.axis_index("head"), 8:16]
    for side, (x_ref, grad_ref, out_ref) in enumerate(
        ((q_ref, nqg_ref, dq_ref), (k_ref, nkg_ref, dk_ref))
    ):
        results[side] = (
            spread_tokens(rate, 4 * side) * gains[side : side + 1] * grad_ref[...]
            - x_ref[...].astype(F32) * spread_tokens(cubed, 4 * side)
        ).astype(BF16)
        copies += start_all([pltpu.make_async_copy(results.at[side], out_ref, sems.at[side])])
    wait_all(copies)


def call(kernel, outs, args, scratch=(), flops=0, name=None, spaces=None, out_spaces=None, vmem=40):
    many = isinstance(outs, list)
    moved = sum(math.prod(x.shape) * x.dtype.itemsize for x in list(args) + (outs if many else [outs]))
    out_spaces = out_spaces or [pltpu.VMEM] * (len(outs) if many else 1)
    out_specs = [pl.BlockSpec(memory_space=space) for space in out_spaces]
    return pl.pallas_call(
        kernel,
        out_shape=outs,
        in_specs=[pl.BlockSpec(memory_space=space) for space in spaces or [pltpu.VMEM] * len(args)],
        out_specs=out_specs if many else out_specs[0],
        scratch_shapes=list(scratch),
        compiler_params=pltpu.CompilerParams(vmem_limit_bytes=vmem * 1024 * 1024),
        cost_estimate=pl.CostEstimate(flops=flops, bytes_accessed=moved, transcendentals=0),
        name=name,
    )(*args)


def sds(*shape, dtype=BF16):
    return jax.ShapeDtypeStruct(shape, dtype)


BACKWARD_ROWS = [[8 * y + (p ^ FIRST_Z) for p in range(8)] for y in range(8)]
ROW_GROUPS = [[8 * y + z for z in range(8)] for y in range(8)]
COLUMN_GROUPS = [[8 * (p ^ FIRST_Y) + z for p in range(8)] for z in range(8)]


def exchange(x, axis, groups=None):
    return lax.all_to_all(x, axis, 0, 0, axis_index_groups=groups, tiled=True)


def local(queries, key_rows, value_rows, query_gain, key_gain, out_grad):
    seq = lax.axis_size("seq")
    heads = lax.axis_size("head")
    width = float(heads * FEAT)
    qg = query_gain.reshape(1, FEAT)
    kg = key_gain.reshape(1, FEAT)
    peer = [(i, i ^ 1) for i in range(seq)]
    beside = [(i, i + 1) for i in range(1, seq - 1, 2)] + [(i + 1, i) for i in range(1, seq - 1, 2)]

    squares = call(
        squares_kernel,
        sds(heads, 16, FEAT, dtype=F32),
        (queries, key_rows, qg, kg),
        scratch=[
            pltpu.VMEM((2, ROWS, FEAT), BF16),
            pltpu.VMEM((2, 1, FEAT), F32),
            pltpu.SemaphoreType.DMA((4,)),
        ],
        spaces=[pl.ANY] * 4,
        vmem=60,
        name="squares",
    )
    squares = exchange(squares, "head")
    kv, one, lv, ysend, p1, p2 = call(
        lambda *refs: norm_kernel(width, *refs),
        [sds(ROWS, 256), sds(256, 256), sds(224, 256), sds(8, 16, 256), sds(192, 256), sds(LEAF, 256)],
        (squares, key_rows, value_rows),
        name="norm",
    )
    p1 = lax.ppermute(p1, "seq", peer)
    p2 = lax.ppermute(p2, "seq", beside)
    yrecv = exchange(ysend, "seq", COLUMN_GROUPS)
    zsend = call(
        row_kernel,
        sds(8, SLOT, 256),
        (yrecv, lv),
        scratch=[
            pltpu.VMEM((8, FAR, 256), BF16),
            pltpu.VMEM((8, 64, 256), BF16),
            pltpu.SemaphoreType.DMA((2,)),
        ],
        out_spaces=[pl.ANY],
        name="rows",
    )
    zrecv = exchange(zsend, "seq", ROW_GROUPS)
    qn, near = call(
        lambda *refs: near_kernel(width, *refs),
        [sds(ROWS, FEAT), sds(LEAVES, 8, 256, dtype=F32)],
        (squares, queries, kv, one, out_grad),
        flops=14 * 2 * 2 * 256 * LEAF * FEAT,
        name="near",
    )
    stat, cross, halo, p1, p2, zsend = call(
        attend_kernel,
        [sds(LEAVES, 8, 256, dtype=F32), sds(768, 256), sds(2, LEAF, 256)]
        + [sds(192, 256), sds(LEAF, 256), sds(8, SLOT, 256)],
        (qn, out_grad, near, p1, p2, zrecv),
        scratch=[
            pltpu.VMEM((1024, FEAT), BF16),
            pltpu.VMEM((1024, FEAT), BF16),
            pltpu.VMEM((LEAVES, 768, 256), F32),
            pltpu.VMEM((LEAVES, 7 * LEAF, 256), F32),
            pltpu.VMEM((LEAVES, 7 * LEAF, 256), F32),
            pltpu.VMEM((768, 1024), BF16),
            pltpu.VMEM((768, 1024), BF16),
            pltpu.VMEM((2, LEAF, 256), BF16),
            pltpu.VMEM((768, 256), BF16),
            pltpu.VMEM((8, FAR, 256), BF16),
            pltpu.VMEM((8, 64, 256), BF16),
            pltpu.SemaphoreType.DMA((2,)),
        ],
        out_spaces=[pltpu.VMEM] * 5 + [pl.ANY],
        flops=4 * 4 * 2 * 256 * 768 * FEAT,
        name="attend",
    )
    p1 = lax.ppermute(p1, "seq", peer)
    p2 = lax.ppermute(p2, "seq", beside)
    zrecv = exchange(zsend, "seq", BACKWARD_ROWS)
    attended, nqg, tok, qsum = call(
        after_kernel,
        [sds(ROWS, FEAT), sds(ROWS, FEAT, dtype=F32), sds(ROWS, 256, dtype=F32)]
        + [sds(8, FEAT, dtype=F32)],
        (stat, qn, kv, one, out_grad, halo, cross, squares, queries),
        scratch=[
            pltpu.VMEM((768, 256), BF16),
            pltpu.VMEM((768, 256), F32),
            pltpu.VMEM((256, 256), F32),
        ],
        flops=4 * 5 * 2 * 256 * KEYS * FEAT,
        name="after",
    )
    ysend = call(
        column_kernel,
        sds(8, 16, 256),
        (zrecv, p1, p2, tok),
        scratch=[pltpu.VMEM((8, FAR, 256), BF16), pltpu.SemaphoreType.DMA],
        spaces=[pl.ANY] * 4,
        name="columns",
    )
    yrecv = exchange(ysend, "seq", COLUMN_GROUPS)
    nkg, value_grad, inner = call(
        total_kernel,
        [sds(ROWS, FEAT, dtype=F32), sds(ROWS, FEAT), sds(heads, 8, FEAT, dtype=F32)],
        (tok, p1, p2, zrecv, yrecv, key_rows, qsum),
        scratch=[
            pltpu.VMEM((ROWS, 256), F32),
        ],
        name="total",
    )
    odd_first = [[p ^ 1 for p in range(heads)]] if heads > 1 else None
    inner = exchange(inner, "head", odd_first)
    query_grad, key_grad, value_grad = call(
        lambda *refs: finish_kernel(width, *refs),
        [sds(ROWS, FEAT), sds(ROWS, FEAT), sds(ROWS, FEAT)],
        (squares, inner, queries, key_rows, nqg, nkg, value_grad),
        scratch=[pltpu.VMEM((2, ROWS, FEAT), BF16), pltpu.SemaphoreType.DMA((3,))],
        out_spaces=[pl.ANY] * 3,
        name="finish",
    )
    return (attended, query_grad, key_grad, value_grad)


def solution(mesh):
    placed = (
        P("seq", "head"),
        P("seq", "head"),
        P("seq", "head"),
        P("head"),
        P("head"),
        P("seq", "head"),
    )
    return jax.shard_map(
        local,
        mesh=mesh,
        in_specs=placed,
        out_specs=(P("seq", "head"), P("seq", "head"), P("seq", "head"), P("seq", "head")),
        check_vma=False,
    )
```

```python
import math

import jax
import jax.numpy as jnp
from jax import lax
from jax.experimental import pallas as pl
from jax.experimental.pallas import tpu as pltpu
from jax.sharding import PartitionSpec as P

ROWS = 512
FEAT = 128
LEAF = 128
LEAVES = 4
HEAD = 64
KEYS = 1280
EPS = 1e-06
LN2 = math.log(2.0)
F32 = jnp.float32
BF16 = jnp.bfloat16
ROW_LEVEL = {1: 2, 2: 3, 3: 3, 4: 4, 5: 4, 6: 4, 7: 4}
COLUMN_LEVEL = {1: 5, 2: 6, 3: 6, 4: 7, 5: 7, 6: 7, 7: 7}
FAR = 48
SLOT = 112
FIRST_Z = 7
FIRST_Y = 5
FIRST_HEAD = 3


def dot(a, b, dims):
    return lax.dot_general(a, b, ((dims[:1], dims[1:]), ((), ())), preferred_element_type=F32)


def iota(shape, axis):
    return lax.broadcasted_iota(jnp.int32, shape, axis)


def pooling(rows, level):
    token = iota((rows, ROWS), 1)
    hit = jnp.right_shift(token, level) == iota((rows, ROWS), 0)
    return jnp.where(hit, 2.0**-level, 0.0)


def spreading(first, rows, level):
    token = iota((ROWS, rows), 0)
    hit = jnp.right_shift(token, level) == iota((ROWS, rows), 1) + first
    return jnp.where(hit, 2.0**-level, 0.0)


def far_pick(shape, far_axis):
    far = iota(shape, far_axis)
    slot_row = iota(shape, 1 - far_axis)
    mid = far - 16
    low = far - 32
    column = jnp.where(
        far < 16,
        far,
        jnp.where(
            far < 32,
            (1 + jnp.right_shift(mid, 3)) * 16 + jnp.bitwise_and(mid, 7),
            (3 + jnp.right_shift(low, 2)) * 16 + jnp.bitwise_and(low, 3),
        ),
    )
    return jnp.where(column == slot_row, 1.0, 0.0).astype(BF16)


def token_sums(x):
    return [
        jnp.sum(x[i * LEAF : (i + 1) * LEAF].T, axis=0, keepdims=True) for i in range(LEAVES)
    ]


def spread_tokens(tile, first):
    return jnp.concatenate(
        [
            jnp.broadcast_to(tile[first + i : first + i + 1], (LEAF, LEAF)).T
            for i in range(LEAVES)
        ],
        axis=0,
    )


def squares_kernel(q_in, k_in, qg_in, kg_in, out_ref, rows, gains, sems):
    copies = [
        pltpu.make_async_copy(source, target, sems.at[i])
        for i, (source, target) in enumerate(
            ((q_in, rows.at[0]), (k_in, rows.at[1]), (qg_in, gains.at[0]), (kg_in, gains.at[1]))
        )
    ]
    for copy in copies:
        copy.start()
    sums = []
    for i in range(2):
        copies[i].wait()
        x = rows[i].astype(F32)
        sums += token_sums(x * x)
    for copy in copies[2:]:
        copy.wait()
    tile = jnp.concatenate(sums + [gains[0], gains[1], jnp.zeros((6, FEAT), F32)], axis=0)
    for i in range(out_ref.shape[0]):
        out_ref[i] = tile


def own_slot():
    head = lax.axis_index("head")
    return jnp.bitwise_xor(head, FIRST_HEAD) if lax.axis_size("head") > 1 else head


def rates(width, sum_ref):
    return lax.rsqrt(jnp.sum(sum_ref[:, :8], axis=0) / width + EPS)


def norm_kernel(width, sum_ref, k_ref, v_ref, kv_ref, one_ref, lv_ref, y_ref, p1_ref, p2_ref):
    index = lax.axis_index("seq")
    column = jnp.bitwise_xor(jnp.right_shift(index, 3), FIRST_Y)
    odd = jnp.bitwise_and(index, 1)
    gain = sum_ref[own_slot(), 9:10]
    kv_ref[:, :FEAT] = (
        k_ref[...].astype(F32) * spread_tokens(rates(width, sum_ref), 4) * gain
    ).astype(BF16)
    kv_ref[:, FEAT:] = v_ref[...]
    pool = jnp.concatenate(
        [pooling(ROWS >> level, level) for level in (1, 2, 3, 4)]
        + [pooling(16, COLUMN_LEVEL[d]) for d in range(1, 8)],
        axis=0,
    ).astype(BF16)
    coarse = dot(pool, kv_ref[...], (1, 0)).astype(BF16)
    one_ref[...] = coarse[:256]
    lv_ref[...] = coarse[256:480]
    y_ref[column] = jnp.zeros((16, 2 * FEAT), BF16)
    for d in range(1, 8):
        y_ref[jnp.bitwise_xor(column, d)] = coarse[464 + 16 * d : 480 + 16 * d]
    p1_ref[:LEAF] = kv_ref[pl.ds(pl.multiple_of((1 - odd) * 384, LEAF), LEAF)]
    p1_ref[LEAF:] = coarse[320:384]
    p2_ref[...] = kv_ref[pl.ds(pl.multiple_of(odd * 384, LEAF), LEAF)]


def start_all(copies):
    for copy in copies:
        copy.start()
    return copies


def wait_all(copies):
    for copy in copies:
        copy.wait()


def row_kernel(y_ref, lv_ref, out_ref, far_scr, mid_scr, sems):
    index = lax.axis_index("seq")
    column = jnp.bitwise_xor(jnp.right_shift(index, 3), FIRST_Y)
    place = jnp.bitwise_and(index, 7)
    mid_scr[place] = jnp.zeros((64, 2 * FEAT), BF16)
    for d in range(1, 8):
        other = jnp.bitwise_xor(place, d)
        if d < 4:
            mid_scr[other] = lv_ref[:64] if d == 1 else lv_ref[128:192]
        else:
            mid_scr[other, :32] = lv_ref[192:224]
            mid_scr[other, 32:] = jnp.zeros((32, 2 * FEAT), BF16)
    copies = start_all([pltpu.make_async_copy(mid_scr, out_ref.at[:, pl.ds(FAR, 64)], sems.at[0])])
    slots = jnp.concatenate([y_ref[jnp.bitwise_xor(column, d)] for d in range(1, 8)], axis=0)
    far = dot(far_pick((FAR, 112), 0), slots, (1, 0)).astype(BF16)
    for s in range(8):
        far_scr[s] = far
    copies += start_all([pltpu.make_async_copy(far_scr, out_ref.at[:, pl.ds(0, FAR)], sems.at[1])])
    wait_all(copies)


def by_head(block):
    lane = iota((LEAF, FEAT), 1)
    zero = jnp.zeros((LEAF, FEAT), BF16)
    return jnp.concatenate(
        [jnp.where(lane < HEAD, block, zero), jnp.where(lane < HEAD, zero, block)], axis=0
    )


def peak(x):
    return jnp.max(x, axis=0, keepdims=True)


def add_up(x):
    return jnp.sum(x, axis=0, keepdims=True)


HALO_PIECE = {0: 0, LEAVES - 1: 2}


def far_bias():
    return jnp.concatenate(
        [jnp.full((LEAF, 2 * LEAF), level * LN2, F32) for level in range(1, 8)], axis=0
    )


def outside_bias():
    index = lax.axis_index("seq")
    last = lax.axis_size("seq") - 1
    return {
        0: jnp.where(index > 0, 0.0, -1e30).astype(F32),
        LEAVES - 1: jnp.where(index < last, 0.0, -1e30).astype(F32),
    }


def weigh(kv, q2, g2):
    score = dot(kv[:, :FEAT], q2, (1, 1))
    top = peak(score)
    weight = jnp.exp(score - top)
    pgrad = dot(kv[:, FEAT:], g2, (1, 1))
    return weight, pgrad, (top, add_up(weight), add_up(weight * pgrad))


def combine(stats):
    top = stats[0][0]
    for stat in stats[1:]:
        top = jnp.maximum(top, stat[0])
    factors = [jnp.exp(stat[0] - top) for stat in stats]
    total = sum(factor * stat[1] for factor, stat in zip(factors, stats))
    mixed = sum(factor * stat[2] for factor, stat in zip(factors, stats))
    return top, total, mixed, factors


def scaled_queries(block):
    return by_head(block) * jnp.asarray(0.125, BF16)


def near_kernel(width, sum_ref, q_ref, kv_ref, one_ref, g_ref, qn_ref, stat_ref):
    gain = sum_ref[own_slot(), 8:9]
    qn_ref[...] = (
        q_ref[...].astype(F32) * spread_tokens(rates(width, sum_ref), 0) * gain
    ).astype(BF16)
    for b in range(LEAVES):
        block = slice(b * LEAF, (b + 1) * LEAF)
        q2 = scaled_queries(qn_ref[block])
        g2 = by_head(g_ref[block])
        half = (1 - b // 2) * LEAF
        stats = [
            weigh(kv_ref[(b + i - 1) * LEAF : (b + i) * LEAF], q2, g2)[2]
            for i in range(3)
            if HALO_PIECE.get(b) != i
        ]
        top, total, mixed = weigh(one_ref[half : half + LEAF], q2, g2)[2]
        stats.append((top + LN2, total, mixed))
        top, total, mixed, _ = combine(stats)
        stat_ref[b] = jnp.concatenate([top, total, mixed, jnp.zeros((5, 2 * LEAF), F32)], axis=0)


def attend_kernel(
    qn_ref, g_ref, near_ref, p1_ref, p2_ref, z_ref,
    stat_ref, cross, halo, p1o_ref, p2o_ref, zo_ref,
    q2_scr, g2_scr, score_scr, weight_scr, pgrad_scr, low_scr, sgrad_scr, rims, cross_grad, far_scr, mid_scr, sems,
):
    index = lax.axis_index("seq")
    place = jnp.bitwise_and(index, 7)
    slot = jnp.bitwise_xor(place, FIRST_Z)
    odd = jnp.bitwise_and(index, 1)
    peer_side = 1 - odd
    halo[peer_side] = p1_ref[:LEAF]
    halo[odd] = p2_ref[...]
    cross[:64] = z_ref[jnp.bitwise_xor(place, 1), FAR:]
    cross[64:128] = p1_ref[LEAF:]
    cross[128:192] = z_ref[jnp.bitwise_xor(place, 2), FAR:]
    cross[192:256] = z_ref[jnp.bitwise_xor(place, 3), FAR:]
    for i in range(4):
        cross[256 + 32 * i : 288 + 32 * i] = z_ref[jnp.bitwise_xor(place, 4 + i), FAR : FAR + 32]
    for s in range(8):
        for j in range(3):
            at = 384 + LEAF * j + 16 * s
            cross[at : at + 16] = z_ref[s, 16 * j : 16 * (j + 1)]

    outside = outside_bias()
    rim_rows = []
    for b in range(LEAVES):
        block = slice(b * LEAF, (b + 1) * LEAF)
        lanes = slice(2 * b * LEAF, 2 * (b + 1) * LEAF)
        q2 = scaled_queries(qn_ref[block])
        g2 = by_head(g_ref[block])
        q2_scr[lanes] = q2
        g2_scr[lanes] = g2
        side = 0 if b == 0 else 1
        stats = [(near_ref[b, 0:1], near_ref[b, 1:2], near_ref[b, 2:3])]
        score_scr[b] = dot(cross[:, :FEAT], q2, (1, 1))
        pgrad_scr[b, : 6 * LEAF] = dot(cross[:, FEAT:], g2, (1, 1))
        for i in range(6):
            rows = slice(i * LEAF, (i + 1) * LEAF)
            score = score_scr[b, rows]
            top = peak(score)
            weight = jnp.exp(score - top)
            weight_scr[b, rows] = weight
            mixed = add_up(weight * pgrad_scr[b, rows])
            stats.append((top + (i + 2) * LN2, add_up(weight), mixed))
        if b in HALO_PIECE:
            weight, pgrad, (top, total, mixed) = weigh(halo[side], q2, g2)
            weight_scr[b, 6 * LEAF :] = weight
            pgrad_scr[b, 6 * LEAF :] = pgrad
            stats.append((top + outside[b], total, mixed))
        top, total, mixed, factors = combine(stats)
        inverse = 1.0 / total
        delta = mixed * inverse
        stat_ref[b] = jnp.concatenate(
            [top, inverse, delta, jnp.zeros((5, 2 * LEAF), F32)], axis=0
        )
        for i in range(6):
            rows = slice(i * LEAF, (i + 1) * LEAF)
            prob = weight_scr[b, rows] * (factors[i + 1] * inverse)
            low_scr[rows, lanes] = prob.astype(BF16)
            sgrad_scr[rows, lanes] = (prob * (pgrad_scr[b, rows] - delta)).astype(BF16)
        if b in HALO_PIECE:
            rim_rows.append((b, side, lanes, factors[7] * inverse, delta))

    cross_grad[:, :FEAT] = dot(sgrad_scr[...], q2_scr[...], (1, 0)).astype(BF16)
    cross_grad[:, FEAT:] = dot(low_scr[...], g2_scr[...], (1, 0)).astype(BF16)
    for j in range(3):
        for s in range(8):
            at = 384 + LEAF * j + 16 * s
            far_scr[s ^ FIRST_Z, 16 * j : 16 * (j + 1)] = cross_grad[at : at + 16]
    copies = start_all([pltpu.make_async_copy(far_scr, zo_ref.at[:, pl.ds(0, FAR)], sems.at[0])])
    mid_scr[slot] = jnp.zeros((64, 2 * FEAT), BF16)
    mid_scr[jnp.bitwise_xor(slot, 1)] = cross_grad[:64]
    mid_scr[jnp.bitwise_xor(slot, 2)] = cross_grad[128:192]
    mid_scr[jnp.bitwise_xor(slot, 3)] = cross_grad[192:256]
    for i in range(4):
        other = jnp.bitwise_xor(slot, 4 + i)
        mid_scr[other, :32] = cross_grad[256 + 32 * i : 288 + 32 * i]
        mid_scr[other, 32:] = jnp.zeros((32, 2 * FEAT), BF16)
    copies += start_all([pltpu.make_async_copy(mid_scr, zo_ref.at[:, pl.ds(FAR, 64)], sems.at[1])])
    for b, side, lanes, factor, delta in rim_rows:
        prob = weight_scr[b, 6 * LEAF :] * factor
        sgrad = (prob * (pgrad_scr[b, 6 * LEAF :] - delta)).astype(BF16)
        rims[side, :, :FEAT] = dot(sgrad, q2_scr[lanes], (1, 0)).astype(BF16)
        rims[side, :, FEAT:] = dot(prob.astype(BF16), g2_scr[lanes], (1, 0)).astype(BF16)
    p1o_ref[:LEAF] = rims[peer_side]
    p1o_ref[LEAF:] = cross_grad[64:128]
    p2o_ref[...] = rims[odd]
    wait_all(copies)


def after_kernel(
    stat_ref, qn_ref, kv_ref, one_ref, g_ref, halo, cross, sum_ref, q_ref,
    att_ref, nqg_ref, tok_ref, qsum_ref, near, near_grad, one_grad,
):
    near[:LEAF] = halo[0]
    near[LEAF : LEAF + ROWS] = kv_ref[...]
    near[LEAF + ROWS :] = halo[1]
    near_grad[...] = jnp.zeros_like(near_grad)
    one_grad[...] = jnp.zeros_like(one_grad)
    feature = iota((FEAT, LEAF), 0)
    bias = far_bias()
    outside = outside_bias()

    def merge_heads(transposed):
        return jnp.where(feature < HEAD, transposed[:, :LEAF], transposed[:, LEAF:]).T

    for b in range(LEAVES):
        rows = slice(b * LEAF, (b + 1) * LEAF)
        near_rows = slice(b * LEAF, (b + 3) * LEAF)
        half = (1 - b // 2) * LEAF
        q2 = scaled_queries(qn_ref[rows])
        g2 = by_head(g_ref[rows])
        kv = jnp.concatenate([near[near_rows], one_ref[half : half + LEAF], cross[...]], axis=0)
        keys = kv[:, :FEAT]
        values = kv[:, FEAT:]
        raw = dot(keys, q2, (1, 1))
        before, after = raw[:LEAF], raw[2 * LEAF : 3 * LEAF]
        if b == 0:
            before = before + outside[b]
        if b == LEAVES - 1:
            after = after + outside[b]
        scores = jnp.concatenate(
            [before, raw[LEAF : 2 * LEAF], after, raw[3 * LEAF :] + bias], axis=0
        )
        probs = jnp.exp(scores - stat_ref[b, 0:1]) * stat_ref[b, 1:2]
        low = probs.astype(BF16)
        score_grad = (probs * (dot(values, g2, (1, 1)) - stat_ref[b, 2:3])).astype(BF16)
        att_ref[rows] = merge_heads(dot(values, low, (0, 0))).astype(BF16)
        nqg_ref[rows] = merge_heads(dot(keys, score_grad, (0, 0))) * 0.125
        for part, lanes in (
            (dot(score_grad[: 4 * LEAF], q2, (1, 0)), slice(0, FEAT)),
            (dot(low[: 4 * LEAF], g2, (1, 0)), slice(FEAT, 2 * FEAT)),
        ):
            near_grad[near_rows, lanes] += part[: 3 * LEAF]
            one_grad[half : half + LEAF, lanes] += part[3 * LEAF :]
    spread = spreading(0, 256, 1).astype(BF16)
    high = one_grad[...].astype(BF16)
    rest = (one_grad[...] - high.astype(F32)).astype(BF16)
    tok_ref[...] = near_grad[LEAF : LEAF + ROWS] + dot(spread, high, (1, 0)) + dot(spread, rest, (1, 0))
    gains = sum_ref[own_slot(), 8:16]
    sums = token_sums(q_ref[...].astype(F32) * gains[0:1] * nqg_ref[...])
    qsum_ref[...] = jnp.concatenate(sums + [gains[1:2], jnp.zeros((3, FEAT), F32)], axis=0)


def column_kernel(z_ref, p1_ref, p2_ref, tok_ref, out_ref, far_rows, sem):
    column = jnp.bitwise_xor(jnp.right_shift(lax.axis_index("seq"), 3), FIRST_Y)
    copy = pltpu.make_async_copy(z_ref.at[:, pl.ds(0, FAR)], far_rows, sem)
    copy.start()
    copy.wait()
    far = jnp.sum(far_rows[...].astype(F32), axis=0).astype(BF16)
    slots = dot(far_pick((112, FAR), 1), far, (1, 0)).astype(BF16)
    out_ref[column] = jnp.zeros((16, 2 * FEAT), BF16)
    for d in range(1, 8):
        out_ref[jnp.bitwise_xor(column, d)] = slots[16 * (d - 1) : 16 * d]


def total_kernel(
    tok_ref, p1_ref, p2_ref, z_ref, y_ref, k_ref, qsum_ref,
    nkg_ref, vg_ref, sum_ref, acc,
):
    index = lax.axis_index("seq")
    column = jnp.bitwise_xor(jnp.right_shift(index, 3), FIRST_Y)
    place = jnp.bitwise_xor(jnp.bitwise_and(index, 7), FIRST_Z)
    odd = jnp.bitwise_and(index, 1)
    pieces = [z_ref[jnp.bitwise_xor(place, 1), FAR:], p1_ref[LEAF:]]
    maps = [spreading(0, 64, 2), spreading(64, 64, 2)]
    for d in range(2, 8):
        rows = ROWS >> ROW_LEVEL[d]
        pieces.append(z_ref[jnp.bitwise_xor(place, d), FAR : FAR + rows])
        maps.append(spreading(0, rows, ROW_LEVEL[d]))
    for d in range(1, 8):
        pieces.append(y_ref[jnp.bitwise_xor(column, d)])
        maps.append(spreading(0, 16, COLUMN_LEVEL[d]))
    spread = jnp.concatenate(maps, axis=1).astype(BF16)
    acc[...] = tok_ref[...] + dot(spread, jnp.concatenate(pieces, axis=0), (1, 0))
    acc[pl.ds(pl.multiple_of((1 - odd) * 384, LEAF), LEAF)] += p1_ref[:LEAF].astype(F32)
    acc[pl.ds(pl.multiple_of(odd * 384, LEAF), LEAF)] += p2_ref[...].astype(F32)
    vg_ref[...] = acc[:, FEAT:].astype(BF16)
    key_total = acc[:, :FEAT]
    nkg_ref[...] = key_total
    sums = token_sums(k_ref[...].astype(F32) * qsum_ref[LEAVES : LEAVES + 1] * key_total)
    tile = jnp.concatenate([qsum_ref[:LEAVES]] + sums, axis=0)
    for i in range(sum_ref.shape[0]):
        sum_ref[i] = tile


def finish_kernel(
    width, sq_ref, inner_ref, q_ref, k_ref, nqg_ref, nkg_ref, value_ref,
    dq_ref, dk_ref, vg_ref, results, sems,
):
    copies = start_all([pltpu.make_async_copy(value_ref, vg_ref, sems.at[2])])
    rate = rates(width, sq_ref)
    inner = jnp.sum(inner_ref[...], axis=0) / width
    cubed = rate * rate * rate * inner
    gains = sq_ref[own_slot(), 8:16]
    for side, (x_ref, grad_ref, out_ref) in enumerate(
        ((q_ref, nqg_ref, dq_ref), (k_ref, nkg_ref, dk_ref))
    ):
        results[side] = (
            spread_tokens(rate, 4 * side) * gains[side : side + 1] * grad_ref[...]
            - x_ref[...].astype(F32) * spread_tokens(cubed, 4 * side)
        ).astype(BF16)
        copies += start_all([pltpu.make_async_copy(results.at[side], out_ref, sems.at[side])])
    wait_all(copies)


def call(kernel, outs, args, scratch=(), flops=0, name=None, spaces=None, out_spaces=None, vmem=40):
    many = isinstance(outs, list)
    moved = sum(math.prod(x.shape) * x.dtype.itemsize for x in list(args) + (outs if many else [outs]))
    out_spaces = out_spaces or [pltpu.VMEM] * (len(outs) if many else 1)
    out_specs = [pl.BlockSpec(memory_space=space) for space in out_spaces]
    return pl.pallas_call(
        kernel,
        out_shape=outs,
        in_specs=[pl.BlockSpec(memory_space=space) for space in spaces or [pltpu.VMEM] * len(args)],
        out_specs=out_specs if many else out_specs[0],
        scratch_shapes=list(scratch),
        compiler_params=pltpu.CompilerParams(vmem_limit_bytes=vmem * 1024 * 1024),
        cost_estimate=pl.CostEstimate(flops=flops, bytes_accessed=moved, transcendentals=0),
        name=name,
    )(*args)


def sds(*shape, dtype=BF16):
    return jax.ShapeDtypeStruct(shape, dtype)


BACKWARD_ROWS = [[8 * y + (p ^ FIRST_Z) for p in range(8)] for y in range(8)]
ROW_GROUPS = [[8 * y + z for z in range(8)] for y in range(8)]
COLUMN_GROUPS = [[8 * (p ^ FIRST_Y) + z for p in range(8)] for z in range(8)]


def exchange(x, axis, groups=None):
    return lax.all_to_all(x, axis, 0, 0, axis_index_groups=groups, tiled=True)


def local(queries, key_rows, value_rows, query_gain, key_gain, out_grad):
    seq = lax.axis_size("seq")
    heads = lax.axis_size("head")
    width = float(heads * FEAT)
    qg = query_gain.reshape(1, FEAT)
    kg = key_gain.reshape(1, FEAT)
    peer = [(i, i ^ 1) for i in range(seq)]
    beside = [(i, i + 1) for i in range(1, seq - 1, 2)] + [(i + 1, i) for i in range(1, seq - 1, 2)]

    squares = call(
        squares_kernel,
        sds(heads, 16, FEAT, dtype=F32),
        (queries, key_rows, qg, kg),
        scratch=[
            pltpu.VMEM((2, ROWS, FEAT), BF16),
            pltpu.VMEM((2, 1, FEAT), F32),
            pltpu.SemaphoreType.DMA((4,)),
        ],
        spaces=[pl.ANY] * 4,
        vmem=60,
        name="squares",
    )
    head_group = [[p ^ FIRST_HEAD for p in range(heads)]] if heads > 1 else None
    squares = exchange(squares, "head", head_group)
    kv, one, lv, ysend, p1, p2 = call(
        lambda *refs: norm_kernel(width, *refs),
        [sds(ROWS, 256), sds(256, 256), sds(224, 256), sds(8, 16, 256), sds(192, 256), sds(LEAF, 256)],
        (squares, key_rows, value_rows),
        name="norm",
    )
    p1 = lax.ppermute(p1, "seq", peer)
    p2 = lax.ppermute(p2, "seq", beside)
    yrecv = exchange(ysend, "seq", COLUMN_GROUPS)
    zsend = call(
        row_kernel,
        sds(8, SLOT, 256),
        (yrecv, lv),
        scratch=[
            pltpu.VMEM((8, FAR, 256), BF16),
            pltpu.VMEM((8, 64, 256), BF16),
            pltpu.SemaphoreType.DMA((2,)),
        ],
        out_spaces=[pl.ANY],
        name="rows",
    )
    zrecv = exchange(zsend, "seq", ROW_GROUPS)
    qn, near = call(
        lambda *refs: near_kernel(width, *refs),
        [sds(ROWS, FEAT), sds(LEAVES, 8, 256, dtype=F32)],
        (squares, queries, kv, one, out_grad),
        flops=14 * 2 * 2 * 256 * LEAF * FEAT,
        name="near",
    )
    stat, cross, halo, p1, p2, zsend = call(
        attend_kernel,
        [sds(LEAVES, 8, 256, dtype=F32), sds(768, 256), sds(2, LEAF, 256)]
        + [sds(192, 256), sds(LEAF, 256), sds(8, SLOT, 256)],
        (qn, out_grad, near, p1, p2, zrecv),
        scratch=[
            pltpu.VMEM((1024, FEAT), BF16),
            pltpu.VMEM((1024, FEAT), BF16),
            pltpu.VMEM((LEAVES, 768, 256), F32),
            pltpu.VMEM((LEAVES, 7 * LEAF, 256), F32),
            pltpu.VMEM((LEAVES, 7 * LEAF, 256), F32),
            pltpu.VMEM((768, 1024), BF16),
            pltpu.VMEM((768, 1024), BF16),
            pltpu.VMEM((2, LEAF, 256), BF16),
            pltpu.VMEM((768, 256), BF16),
            pltpu.VMEM((8, FAR, 256), BF16),
            pltpu.VMEM((8, 64, 256), BF16),
            pltpu.SemaphoreType.DMA((2,)),
        ],
        out_spaces=[pltpu.VMEM] * 5 + [pl.ANY],
        flops=4 * 4 * 2 * 256 * 768 * FEAT,
        name="attend",
    )
    p1 = lax.ppermute(p1, "seq", peer)
    p2 = lax.ppermute(p2, "seq", beside)
    zrecv = exchange(zsend, "seq", BACKWARD_ROWS)
    attended, nqg, tok, qsum = call(
        after_kernel,
        [sds(ROWS, FEAT), sds(ROWS, FEAT, dtype=F32), sds(ROWS, 256, dtype=F32)]
        + [sds(8, FEAT, dtype=F32)],
        (stat, qn, kv, one, out_grad, halo, cross, squares, queries),
        scratch=[
            pltpu.VMEM((768, 256), BF16),
            pltpu.VMEM((768, 256), F32),
            pltpu.VMEM((256, 256), F32),
        ],
        flops=4 * 5 * 2 * 256 * KEYS * FEAT,
        name="after",
    )
    ysend = call(
        column_kernel,
        sds(8, 16, 256),
        (zrecv, p1, p2, tok),
        scratch=[pltpu.VMEM((8, FAR, 256), BF16), pltpu.SemaphoreType.DMA],
        spaces=[pl.ANY] * 4,
        name="columns",
    )
    yrecv = exchange(ysend, "seq", COLUMN_GROUPS)
    nkg, value_grad, inner = call(
        total_kernel,
        [sds(ROWS, FEAT, dtype=F32), sds(ROWS, FEAT), sds(heads, 8, FEAT, dtype=F32)],
        (tok, p1, p2, zrecv, yrecv, key_rows, qsum),
        scratch=[
            pltpu.VMEM((ROWS, 256), F32),
        ],
        name="total",
    )
    inner = exchange(inner, "head", head_group)
    query_grad, key_grad, value_grad = call(
        lambda *refs: finish_kernel(width, *refs),
        [sds(ROWS, FEAT), sds(ROWS, FEAT), sds(ROWS, FEAT)],
        (squares, inner, queries, key_rows, nqg, nkg, value_grad),
        scratch=[pltpu.VMEM((2, ROWS, FEAT), BF16), pltpu.SemaphoreType.DMA((3,))],
        out_spaces=[pl.ANY] * 3,
        name="finish",
    )
    return (attended, query_grad, key_grad, value_grad)


def solution(mesh):
    placed = (
        P("seq", "head"),
        P("seq", "head"),
        P("seq", "head"),
        P("head"),
        P("head"),
        P("seq", "head"),
    )
    return jax.shard_map(
        local,
        mesh=mesh,
        in_specs=placed,
        out_specs=(P("seq", "head"), P("seq", "head"), P("seq", "head"), P("seq", "head")),
        check_vma=False,
    )
```
